32 devices in a mesh: pipe: 4 (over y, core), seq: 8 (over z, x).
Axes of the slice: x: 2, y: 2, z: 4, core: 2. Of those that a mesh axis runs over, the one named last changes fastest.
Arguments:
- hidden: bfloat16 [2, 192, 3072], P(None, 'seq'), may hold values from -8 to 8
- mod_shift: float32 [4, 3072], P('pipe'), may hold values from -0.3 to 0.3
- mod_scale: float32 [4, 3072], P('pipe'), may hold values from -3 to 3
- mod_gate: float32 [4, 3072], P('pipe'), may hold values from 0.5 to 2.5
- norm_gain: float32 [4, 2, 128], P('pipe'), may hold values from 0.5 to 1.5
- input_proj: bfloat16 [4, 3072, 3, 2048], P('pipe', None, None, 'seq'), may hold values from -0.109375 to 0.109375
- output_proj: bfloat16 [4, 2048, 3072], P('pipe', 'seq'), may hold values from -0.5 to 0.5
- stale_cache: bfloat16 [4, 2, 192, 2, 2048], P('pipe', None, 'seq'), may hold values from -6 to 6
Outputs:
- block_output: bfloat16 [4, 2, 192, 3072], P('pipe', None, 'seq')
- fresh_cache: bfloat16 [4, 2, 192, 2, 2048], P('pipe', None, 'seq')
The draws below stay inside these ranges and needn't reach their ends.
All inputs are finite; a program needn't handle non-finite values.
Results may differ from the reference program's by a relative error of at most 0.019.
Values may be sent and summed in bfloat16 or wider, within the bound.
No kernel may reach another device: no remote copies, remote signals or barrier semaphores. Data moves between devices by JAX's collectives and lax.ppermute only.
A program may use at most 64 MiB of HBM per device.

```python
import math
import jax
import jax.numpy as jnp
from jax import lax

D = 3072
HS = 128
HEADS = 16
PATCHES = 2
LAYERS = 4
PATCH_TOK = 192


def shard_levels(rng, extent, shards, least, high):
    def one(position, blocks):
        heights = jax.random.uniform(jax.random.fold_in(jax.random.fold_in(rng, 6), position), (blocks,), jnp.float32, least / len(shards), high / len(shards))
        return jnp.repeat(jnp.exp(heights), extent[position] // blocks).reshape((-1,) + (1,) * (len(extent) - position - 1))

    level = one(*shards[0])
    for cut in shards[1:]:
        level = level * one(*cut)
    return level


def noise(own_key, shape, scale, limit, shards=(), held_as=jnp.bfloat16):
    loudness = shard_levels(own_key, shape, shards, -0.22, 0.18) if shards else 1.0
    values = jax.random.normal(own_key, shape, jnp.float32) * scale * loudness
    return jnp.minimum(jnp.maximum(values, -limit), limit).astype(held_as)


def setup_inputs(seed: int = 0) -> dict:
    splits = jax.random.split(jax.random.key(seed), 9)
    hidden = noise(splits[0], (PATCHES, PATCH_TOK, D), 2.0, 8.0, ((1, 8),))
    mod_shift = noise(splits[1], (LAYERS, D), 0.05, 0.3, ((0, 4),), jnp.float32)
    mod_scale = noise(splits[2], (LAYERS, D), 0.5, 3.0, ((0, 4),), jnp.float32)
    mod_gate = jnp.clip(0.5 + 2.0 * jax.random.uniform(splits[3], (LAYERS, D), jnp.float32) ** shard_levels(splits[3], (LAYERS, D), ((0, 4),), -0.2, 0.2), 0.5, 2.5)
    norm_gain = jnp.clip(1.0 + 0.1 * jax.random.normal(splits[4], (LAYERS, 2, HS), jnp.float32), 0.5, 1.5)
    input_proj = noise(splits[5], (LAYERS, D, 3, HEADS * HS), D ** -0.5, 0.109375, ((0, 4), (3, 8)))
    output_proj = noise(splits[6], (LAYERS, HEADS * HS, D), HS ** -0.5, 0.5, ((0, 4), (1, 8)))
    stale_cache = noise(splits[7], (LAYERS, PATCHES, PATCH_TOK, 2, HEADS * HS), 1.0, 6.0, ((0, 4), (2, 8)))
    return dict(hidden=hidden, mod_shift=mod_shift, mod_scale=mod_scale, mod_gate=mod_gate, norm_gain=norm_gain, input_proj=input_proj, output_proj=output_proj, stale_cache=stale_cache)


def layer_norm(values, shift_row, scale_row):
    widened = values.astype(jnp.float32)
    centered = widened - lax.optimization_barrier(jnp.mean(widened, axis=-1, keepdims=True))
    spread = lax.optimization_barrier(jnp.mean(centered * centered, axis=-1, keepdims=True))
    return (centered / jnp.sqrt(spread + 1e-06) * (1.0 + scale_row) + shift_row).astype(jnp.bfloat16)

def head_norm(values, gain_row, head_size):
    row_count = values.shape[0]
    split = values.reshape(row_count, values.shape[1] // head_size, head_size)
    square = lax.optimization_barrier(jnp.mean(split * split, axis=-1, keepdims=True))
    return (split / jnp.sqrt(square + 1e-06) * gain_row).reshape(row_count, values.shape[1]).astype(jnp.bfloat16)

def attend(queries, own_keys, own_values, far_keys, far_values, head_size):
    row_count = queries.shape[0]
    head_count = queries.shape[1] // head_size
    shaped = lambda array: array.reshape(array.shape[0], head_count, head_size).astype(jnp.float32)
    query_heads = shaped(queries)
    factor = 1.0 / math.sqrt(head_size)
    near_scores = jnp.einsum('thd,shd->hts', query_heads, shaped(own_keys)) * factor
    far_scores = jnp.einsum('thd,shd->hts', query_heads, shaped(far_keys)) * factor
    near_exp = jnp.exp(near_scores)
    far_exp = jnp.exp(far_scores)
    denominator = lax.optimization_barrier(jnp.sum(near_exp, axis=-1, keepdims=True)) + lax.optimization_barrier(jnp.sum(far_exp, axis=-1, keepdims=True))
    near_prob = (near_exp / denominator).astype(jnp.bfloat16).astype(jnp.float32)
    far_prob = (far_exp / denominator).astype(jnp.bfloat16).astype(jnp.float32)
    mixed = jnp.einsum('hts,shd->thd', near_prob, shaped(own_values)) + jnp.einsum('hts,shd->thd', far_prob, shaped(far_values))
    return mixed.reshape(row_count, head_count * head_size).astype(jnp.bfloat16)

def reference(hidden, mod_shift, mod_scale, mod_gate, norm_gain, input_proj, output_proj, stale_cache):
    channels = HEADS * HS
    current = hidden
    outputs = []
    caches = []
    for layer_index in range(LAYERS):
        weight_flat = input_proj[layer_index].reshape(D, 3 * channels)

        def run_block(block_in, far_keys, far_values):
            normed = layer_norm(block_in, mod_shift[layer_index], mod_scale[layer_index])
            projected = jnp.dot(normed, weight_flat, preferred_element_type=jnp.float32)
            queries = head_norm(projected[:, :channels], norm_gain[layer_index, 0], HS)
            fresh_keys = head_norm(projected[:, channels:2 * channels], norm_gain[layer_index, 1], HS)
            values = projected[:, 2 * channels:].astype(jnp.bfloat16)
            attended = attend(queries, fresh_keys, values, far_keys, far_values, HS)
            update = jnp.dot(attended, output_proj[layer_index], preferred_element_type=jnp.float32)
            result = (block_in.astype(jnp.float32) + mod_gate[layer_index] * update).astype(jnp.bfloat16)
            return (result, fresh_keys, values)
        stale_pair = stale_cache[layer_index, 1]
        first_out, first_keys, first_values = run_block(current[0], stale_pair[:, 0], stale_pair[:, 1])
        second_out, second_keys, second_values = run_block(current[1], first_keys, first_values)
        current = jnp.stack([first_out, second_out])
        first_pair = jnp.stack([first_keys, first_values], axis=1)
        second_pair = jnp.stack([second_keys, second_values], axis=1)
        caches.append(jnp.stack([first_pair, second_pair]))
        outputs.append(current)
    return (jnp.stack(outputs), jnp.stack(caches))
```

```python
import functools
import math

import jax
import jax.numpy as jnp
from jax import lax
from jax.experimental import pallas as pl
from jax.experimental.pallas import tpu as pltpu
from jax.sharding import PartitionSpec as P

AXES = ("pipe", "seq")
VMEM = pl.BlockSpec(memory_space=pltpu.VMEM)
ANY = pl.BlockSpec(memory_space=pl.ANY)


def ring_order(count):
    fast = 1
    while fast * fast * 4 <= count and count % (fast * 2) == 0:
        fast *= 2
    slow = count // fast
    if fast == 1 or slow % 2:
        return list(range(count))
    cells = [(0, 0)]
    for row in range(slow):
        columns = range(1, fast) if row % 2 == 0 else range(fast - 1, 0, -1)
        cells += [(row, column) for column in columns]
    cells += [(row, 0) for row in range(slow - 1, 0, -1)]
    return [row * fast + column for row, column in cells]


def normalise(values, shift_row, scale_row):
    centered = values - jnp.mean(values, axis=-1, keepdims=True)
    spread = jnp.mean(centered * centered, axis=-1, keepdims=True)
    return (centered * lax.rsqrt(spread + 1e-06) * (1.0 + scale_row) + shift_row).astype(
        jnp.bfloat16
    )


def norm_kernel(params_ref, x_ref, normed_ref):
    normed_ref[...] = normalise(
        x_ref[...].astype(jnp.float32), params_ref[0:1, :], params_ref[1:2, :]
    )


def finish_kernel(params_ref, next_ref, x_ref, own_ref, right_ref, left_ref, out_ref, normed_ref):
    update = (
        own_ref[...].astype(jnp.float32)
        + right_ref[...].astype(jnp.float32)
        + left_ref[...].astype(jnp.float32)
    )
    result = (x_ref[...].astype(jnp.float32) + params_ref[2:3, :] * update).astype(jnp.bfloat16)
    out_ref[...] = result
    normed_ref[...] = normalise(
        result.astype(jnp.float32), next_ref[0:1, :], next_ref[1:2, :]
    )


def weight_copies(turn, own_ref, other_ref, buffer, sems, parts):
    mine = lax.rem(lax.axis_index("pipe"), 2) == turn

    @pl.when(mine)
    def _():
        for part in range(parts):
            pltpu.make_async_copy(own_ref.at[part], buffer.at[part], sems.at[part]).start()

    @pl.when(jnp.logical_not(mine))
    def _():
        for part in range(parts):
            pltpu.make_async_copy(other_ref.at[part], buffer.at[part], sems.at[part]).start()


def project_kernel(turn, count, head_size, gain_ref, own_ref, other_ref, *refs):
    blocks = refs[:count]
    q_ref, kv_ref, wide, weights, sems = refs[count:]
    weight_copies(turn, own_ref, other_ref, weights, sems, 3)
    rows = blocks[0].shape[0]
    for index, block in enumerate(blocks):
        wide[index * rows : (index + 1) * rows, :] = block[...].astype(jnp.float32)
    tokens = wide[...].astype(jnp.bfloat16)
    channels = weights.shape[2]
    for part in (1, 2, 0):
        pltpu.make_async_copy(own_ref.at[part], weights.at[part], sems.at[part]).wait()
        projected = jnp.dot(tokens, weights[part], preferred_element_type=jnp.float32)
        if part == 2:
            kv_ref[1] = projected.astype(jnp.bfloat16)
            continue
        for start in range(0, channels, head_size):
            head = projected[:, start : start + head_size]
            square = jnp.mean(head * head, axis=-1, keepdims=True)
            head = (head * lax.rsqrt(square + 1e-06) * gain_ref[part : part + 1, :]).astype(
                jnp.bfloat16
            )
            if part == 0:
                q_ref[:, start : start + head_size] = head
            else:
                kv_ref[0, :, start : start + head_size] = head


def attend_kernel(turn, count, head_size, own_ref, other_ref, q_ref, kv_ref, stale_ref, fresh_ref, *refs):
    parts = refs[:count]
    weights, sems = refs[count:]
    weight_copies(turn, own_ref, other_ref, weights, sems, 1)
    early = lax.rem(lax.axis_index("pipe"), 2) == 0
    factor = 1.0 / math.sqrt(head_size)
    channels = q_ref.shape[1]
    heads = []
    across = (((1,), (1,)), ((), ()))
    for start in range(0, channels, head_size):
        cut = slice(start, start + head_size)
        query = q_ref[:, cut]
        far_keys = jnp.where(early, stale_ref[0, :, cut], fresh_ref[0, :, cut])
        far_values = jnp.where(early, stale_ref[1, :, cut], fresh_ref[1, :, cut])
        near = lax.dot_general(query, kv_ref[0, :, cut], across, preferred_element_type=jnp.float32)
        far = lax.dot_general(query, far_keys, across, preferred_element_type=jnp.float32)
        near = jnp.exp(near * factor)
        far = jnp.exp(far * factor)
        total = jnp.sum(near, axis=-1, keepdims=True) + jnp.sum(far, axis=-1, keepdims=True)
        near = (near / total).astype(jnp.bfloat16)
        far = (far / total).astype(jnp.bfloat16)
        mixed = jnp.dot(near, kv_ref[1, :, cut], preferred_element_type=jnp.float32)
        mixed = mixed + jnp.dot(far, far_values, preferred_element_type=jnp.float32)
        heads.append(mixed.astype(jnp.bfloat16))
    attended = jnp.concatenate(heads, axis=1)
    pltpu.make_async_copy(own_ref.at[0], weights.at[0], sems.at[0]).wait()
    rows = parts[0].shape[0]
    update = jnp.dot(attended, weights[0], preferred_element_type=jnp.float32)
    for index, part in enumerate(parts):
        part[...] = update[index * rows : (index + 1) * rows, :].astype(jnp.bfloat16)


def params_of(limit):
    return pltpu.CompilerParams(vmem_limit_bytes=limit << 20)


def body(hidden, mod_shift, mod_scale, mod_gate, norm_gain, input_proj, output_proj, stale_cache):
    sections = lax.axis_size("pipe")
    seq = lax.axis_size("seq")
    pipe = lax.axis_index("pipe")
    core = lax.rem(pipe, 2)
    plane = pipe // 2
    ring = ring_order(seq)
    half = seq // 2
    rows, width = hidden.shape[1:]
    head_size = norm_gain.shape[2]
    channels = input_proj.shape[3]
    tokens = rows * seq

    place = lambda row, position: row * seq + position
    swap = [(place(row, s), place(row ^ 1, s)) for row in range(sections) for s in range(seq)]

    def around(value, level, step):
        pairs = [
            (place(row, ring[i]), place(row, ring[(i + step) % seq]))
            for row in (2 * level, 2 * level + 1)
            for i in range(seq)
        ]
        return lax.ppermute(value, AXES, pairs)

    def upward(value, level):
        pairs = [
            (place(row, s), place(row + 2, s))
            for row in (2 * level, 2 * level + 1)
            for s in range(seq)
        ]
        return lax.ppermute(value, AXES, pairs)

    def gather(block, level):
        right, left = [block], [block]
        for hop in range(1, half + 1):
            right.append(around(right[-1], level, 1))
            if hop < half:
                left.append(around(left[-1], level, -1))
        return [block] + right[1:] + left[1:]

    def scatter(parts, level):
        add = lambda one, two: (one.astype(jnp.float32) + two.astype(jnp.float32)).astype(
            jnp.bfloat16
        )
        right = around(parts[half], level, 1)
        left = around(parts[half - 1], level, -1)
        for hop in range(half - 1, 0, -1):
            right = around(add(right, parts[half + hop]), level, 1)
            if hop > 1:
                left = around(add(left, parts[hop - 1]), level, -1)
        return right, left

    gains = jnp.pad(norm_gain[0].reshape(1, -1), ((0, 0), (0, width - 2 * head_size)))
    own_params = jnp.concatenate([mod_shift, mod_scale, mod_gate, gains], axis=0)
    own_in = jnp.transpose(input_proj[0], (1, 0, 2))
    own_out = output_proj
    other_params = lax.ppermute(own_params, AXES, swap)
    other_in = lax.ppermute(own_in, AXES, swap)
    other_out = lax.ppermute(own_out, AXES, swap)
    params = [jnp.where(core == turn, own_params, other_params) for turn in range(2)]
    gain_rows = [p[3, : 2 * head_size].reshape(2, head_size) for p in params]

    stale = lax.all_to_all(stale_cache[0, 1], "seq", split_axis=2, concat_axis=0, tiled=True)
    stale = jnp.transpose(stale, (1, 0, 2))
    stale_pair = [stale, lax.ppermute(stale, AXES, swap)]

    block_shape = jax.ShapeDtypeStruct((rows, width), jnp.bfloat16)

    def norm(x, turn):
        return pl.pallas_call(
            norm_kernel, out_shape=block_shape, in_specs=[VMEM] * 2, out_specs=VMEM,
            compiler_params=params_of(16),
        )(params[turn], x)

    def project(blocks, turn):
        return pl.pallas_call(
            functools.partial(project_kernel, turn, seq, head_size),
            out_shape=(
                jax.ShapeDtypeStruct((tokens, channels), jnp.bfloat16),
                jax.ShapeDtypeStruct((2, tokens, channels), jnp.bfloat16),
            ),
            in_specs=[VMEM, ANY, ANY] + [VMEM] * seq,
            out_specs=(VMEM, VMEM),
            scratch_shapes=[
                pltpu.VMEM((tokens, width), jnp.float32),
                pltpu.VMEM(own_in.shape, jnp.bfloat16),
                pltpu.SemaphoreType.DMA((3,)),
            ],
            compiler_params=params_of(32),
        )(gain_rows[turn], own_in, other_in, *blocks)

    def attend(queries, pair, fresh, turn):
        return pl.pallas_call(
            functools.partial(attend_kernel, turn, seq, head_size),
            out_shape=(block_shape,) * seq,
            in_specs=[ANY, ANY] + [VMEM] * 4,
            out_specs=(VMEM,) * seq,
            scratch_shapes=[
                pltpu.VMEM(own_out.shape, jnp.bfloat16),
                pltpu.SemaphoreType.DMA((1,)),
            ],
            compiler_params=params_of(32),
        )(own_out, other_out, queries, pair, stale_pair[turn], fresh)

    def finish(x, own, right, left, turn):
        return pl.pallas_call(
            finish_kernel, out_shape=(block_shape,) * 2, in_specs=[VMEM] * 6, out_specs=(VMEM,) * 2,
            compiler_params=params_of(16),
        )(params[turn], params[1 - turn], x, own, right, left)

    outputs = [None, None]
    pairs = [None, None]
    freshes = [None, None]
    x = lax.dynamic_index_in_dim(hidden, core, 0, keepdims=False)
    for level in range(sections // 2):
        if level:
            x = upward(x, level - 1)
        normed = norm(x, 0)
        for turn in range(2):
            blocks = gather(normed, level)
            queries, pair = project(blocks, turn)
            fresh = lax.ppermute(pair, AXES, swap)
            parts = attend(queries, pair, fresh, turn)
            right, left = scatter(parts, level)
            x, normed = finish(x, parts[0], right, left, turn)
            here = plane == level
            keep = lambda new, old: new if old is None else jnp.where(here, new, old)
            outputs[turn] = keep(x, outputs[turn])
            pairs[turn] = keep(pair, pairs[turn])
            freshes[turn] = keep(fresh, freshes[turn])

    mine = jnp.where(core == 0, outputs[0], outputs[1])
    theirs = lax.ppermute(jnp.where(core == 0, outputs[1], outputs[0]), AXES, swap)
    block_output = jnp.stack(
        [jnp.where(core == 0, mine, theirs), jnp.where(core == 0, theirs, mine)]
    )
    cache = jnp.stack(
        [jnp.where(core == 0, pairs[0], freshes[1]), jnp.where(core == 0, freshes[0], pairs[1])]
    )
    cache = cache.reshape(2, 2, seq, rows, channels)
    spot = [0] * seq
    for index, position in enumerate(ring):
        spot[position] = index
    spot = jnp.array(spot, jnp.int32)
    away = jnp.remainder(spot[lax.axis_index("seq")] - spot, seq)
    cache = jnp.take(cache, jnp.where(away <= half, away, half + seq - away), axis=2)
    cache = lax.all_to_all(cache, "seq", split_axis=2, concat_axis=4, tiled=True)
    cache = jnp.transpose(cache[:, :, 0], (0, 2, 1, 3))
    return block_output[None], cache[None]


def solution(mesh):
    in_specs = (
        P(None, "seq", None),
        P("pipe", None),
        P("pipe", None),
        P("pipe", None),
        P("pipe", None, None),
        P("pipe", None, None, "seq"),
        P("pipe", "seq", None),
        P("pipe", None, "seq", None, None),
    )
    out_specs = (P("pipe", None, "seq", None), P("pipe", None, "seq", None, None))
    return jax.shard_map(body, mesh=mesh, in_specs=in_specs, out_specs=out_specs, check_vma=False)
```

```python
import functools
import math

import jax
import jax.numpy as jnp
from jax import lax
from jax.experimental import pallas as pl
from jax.experimental.pallas import tpu as pltpu
from jax.sharding import PartitionSpec as P

AXES = ("pipe", "seq")
VMEM = pl.BlockSpec(memory_space=pltpu.VMEM)
ANY = pl.BlockSpec(memory_space=pl.ANY)


def ring_order(count):
    fast = 1
    while fast * fast * 4 <= count and count % (fast * 2) == 0:
        fast *= 2
    slow = count // fast
    if fast == 1 or slow % 2:
        return list(range(count))
    cells = [(0, 0)]
    for row in range(slow):
        columns = range(1, fast) if row % 2 == 0 else range(fast - 1, 0, -1)
        cells += [(row, column) for column in columns]
    cells += [(row, 0) for row in range(slow - 1, 0, -1)]
    return [row * fast + column for row, column in cells]


def normalise(values, shift_row, scale_row):
    centered = values - jnp.mean(values, axis=-1, keepdims=True)
    spread = jnp.mean(centered * centered, axis=-1, keepdims=True)
    return (centered * lax.rsqrt(spread + 1e-06) * (1.0 + scale_row) + shift_row).astype(
        jnp.bfloat16
    )


def norm_kernel(params_ref, x_ref, normed_ref):
    normed_ref[...] = normalise(
        x_ref[...].astype(jnp.float32), params_ref[0:1, :], params_ref[1:2, :]
    )


def finish_kernel(params_ref, next_ref, x_ref, own_ref, last_ref, out_ref, normed_ref):
    update = own_ref[...] + last_ref[...].astype(jnp.float32)
    result = (x_ref[...].astype(jnp.float32) + params_ref[2:3, :] * update).astype(jnp.bfloat16)
    out_ref[...] = result
    normed_ref[...] = normalise(
        result.astype(jnp.float32), next_ref[0:1, :], next_ref[1:2, :]
    )


def load_kernel(turn, own_ref, other_ref, out_ref, sem):
    mine = lax.rem(lax.axis_index("pipe"), 2) == turn

    @pl.when(mine)
    def _():
        pltpu.make_async_copy(own_ref, out_ref, sem).start()

    @pl.when(jnp.logical_not(mine))
    def _():
        pltpu.make_async_copy(other_ref, out_ref, sem).start()

    pltpu.make_async_copy(own_ref, out_ref, sem).wait()


def split_kernel(cache_ref, out_ref):
    channels = out_ref.shape[3]
    for kind in range(2):
        rows = cache_ref[:, kind, :]
        for shard in range(out_ref.shape[0]):
            out_ref[shard, kind] = rows[:, shard * channels : (shard + 1) * channels]


def project_kernel(head_size, gain_ref, weights_ref, *refs):
    groups, (q_ref, kv_ref, tokens_ref) = refs[:-3], refs[-3:]
    rows = groups[0].shape[0]
    for index, group in enumerate(groups):
        tokens_ref[index * rows : (index + 1) * rows, :] = group[...]
    tokens = tokens_ref[...]
    channels = weights_ref.shape[2]
    for part in (1, 2, 0):
        projected = jnp.dot(tokens, weights_ref[part], preferred_element_type=jnp.float32)
        if part == 2:
            kv_ref[1] = projected.astype(jnp.bfloat16)
            continue
        for start in range(0, channels, head_size):
            head = projected[:, start : start + head_size]
            square = jnp.mean(head * head, axis=-1, keepdims=True)
            head = (head * lax.rsqrt(square + 1e-06) * gain_ref[part : part + 1, :]).astype(
                jnp.bfloat16
            )
            if part == 0:
                q_ref[:, start : start + head_size] = head
            else:
                kv_ref[0, :, start : start + head_size] = head


def attend_kernel(turn, head_size, own_ref, other_ref, q_ref, kv_ref, stale_ref, fresh_ref, *refs):
    parts, (weights, sem) = refs[:-2], refs[-2:]
    early = lax.rem(lax.axis_index("pipe"), 2) == 0
    mine = lax.rem(lax.axis_index("pipe"), 2) == turn

    @pl.when(mine)
    def _():
        pltpu.make_async_copy(own_ref, weights, sem).start()

    @pl.when(jnp.logical_not(mine))
    def _():
        pltpu.make_async_copy(other_ref, weights, sem).start()

    factor = 1.0 / math.sqrt(head_size)
    tokens, channels = q_ref.shape
    heads = []
    across = (((1,), (1,)), ((), ()))

    def far_of(kind, cut):
        stale = stale_ref[:, kind, :, cut].astype(jnp.float32).reshape(tokens, head_size)
        return jnp.where(early, stale, fresh_ref[kind, :, cut].astype(jnp.float32)).astype(
            jnp.bfloat16
        )

    for start in range(0, channels, head_size):
        cut = slice(start, start + head_size)
        query = q_ref[:, cut]
        near = lax.dot_general(query, kv_ref[0, :, cut], across, preferred_element_type=jnp.float32)
        far = lax.dot_general(query, far_of(0, cut), across, preferred_element_type=jnp.float32)
        near = jnp.exp(near * factor)
        far = jnp.exp(far * factor)
        total = jnp.sum(near, axis=-1, keepdims=True) + jnp.sum(far, axis=-1, keepdims=True)
        near = (near / total).astype(jnp.bfloat16)
        far = (far / total).astype(jnp.bfloat16)
        mixed = jnp.dot(near, kv_ref[1, :, cut], preferred_element_type=jnp.float32)
        mixed = mixed + jnp.dot(far, far_of(1, cut), preferred_element_type=jnp.float32)
        heads.append(mixed.astype(jnp.bfloat16))
    attended = jnp.concatenate(heads, axis=1)
    pltpu.make_async_copy(own_ref, weights, sem).wait()
    rows = parts[0].shape[0]
    update = jnp.dot(attended, weights[...], preferred_element_type=jnp.float32)
    for index, part in enumerate(parts):
        part[...] = update[index * rows : (index + 1) * rows, :].astype(jnp.bfloat16)


def params_of(limit):
    return pltpu.CompilerParams(vmem_limit_bytes=limit << 20)


def body(hidden, mod_shift, mod_scale, mod_gate, norm_gain, input_proj, output_proj, stale_cache):
    sections = lax.axis_size("pipe")
    seq = lax.axis_size("seq")
    pipe = lax.axis_index("pipe")
    core = lax.rem(pipe, 2)
    plane = pipe // 2
    ring = ring_order(seq)
    half = seq // 2
    rows, width = hidden.shape[1:]
    head_size = norm_gain.shape[2]
    channels = input_proj.shape[3]
    tokens = rows * seq

    place = lambda row, position: row * seq + position
    swap = [(place(row, s), place(row ^ 1, s)) for row in range(sections) for s in range(seq)]

    def exchange(value, level, side):
        pairs = []
        for row in (2 * level, 2 * level + 1):
            for i in range((side + row) % 2, seq, 2):
                one, two = place(row, ring[i]), place(row, ring[(i + 1) % seq])
                pairs += [(one, two), (two, one)]
        return lax.ppermute(value, AXES, pairs)

    def upward(value, level):
        pairs = [
            (place(row, s), place(row + 2, s))
            for row in (2 * level, 2 * level + 1)
            for s in range(seq)
        ]
        return lax.ppermute(value, AXES, pairs)

    def gather(block, level, turn):
        groups = [jnp.concatenate([block, exchange(block, level, 0)], axis=0)]
        for step in range(1, half):
            if step == half - 1:
                groups[-1], late = lax.optimization_barrier((groups[-1], own_in))
            groups.append(exchange(groups[-1], level, step % 2))
        return groups, load(late, turn)

    def scatter(parts, level):
        wide = lambda value: value.astype(jnp.float32)
        got = exchange(parts[-1], level, (half - 1) % 2)
        for step in range(half - 2, 0, -1):
            got = exchange((wide(parts[step]) + wide(got)).astype(jnp.bfloat16), level, step % 2)
        own = wide(parts[0][:rows]) + wide(got[:rows])
        sent = (wide(parts[0][rows:]) + wide(got[rows:])).astype(jnp.bfloat16)
        return own, exchange(sent, level, 0)

    gains = jnp.pad(norm_gain[0].reshape(1, -1), ((0, 0), (0, width - 2 * head_size)))
    own_params = jnp.concatenate([mod_shift, mod_scale, mod_gate, gains], axis=0)
    own_in = jnp.transpose(input_proj[0], (1, 0, 2))
    own_out = output_proj[0]
    other_params = lax.ppermute(own_params, AXES, swap)
    own_in, own_out, other_params = lax.optimization_barrier((own_in, own_out, other_params))
    other_in = lax.ppermute(own_in, AXES, swap)
    other_out = lax.ppermute(own_out, AXES, swap)
    params = [jnp.where(core == turn, own_params, other_params) for turn in range(2)]
    gain_rows = [p[3, : 2 * head_size].reshape(2, head_size) for p in params]

    stale = pl.pallas_call(
        split_kernel,
        out_shape=jax.ShapeDtypeStruct((seq, 2, rows, channels), jnp.bfloat16),
        in_specs=[VMEM], out_specs=VMEM, compiler_params=params_of(16),
    )(stale_cache[0, 1])
    stale, hidden = lax.optimization_barrier((stale, hidden))
    stale = lax.all_to_all(stale, "seq", split_axis=0, concat_axis=0, tiled=True)
    stale_pair = [stale, lax.ppermute(stale, AXES, swap)]

    block_shape = jax.ShapeDtypeStruct((rows, width), jnp.bfloat16)

    def norm(x, turn):
        return pl.pallas_call(
            norm_kernel, out_shape=block_shape, in_specs=[VMEM] * 2, out_specs=VMEM,
            compiler_params=params_of(16),
        )(params[turn], x)

    def load(late, turn):
        return pl.pallas_call(
            functools.partial(load_kernel, turn),
            out_shape=jax.ShapeDtypeStruct(own_in.shape, jnp.bfloat16),
            in_specs=[ANY, ANY], out_specs=VMEM,
            scratch_shapes=[pltpu.SemaphoreType.DMA],
            compiler_params=params_of(16),
        )(late, other_in)

    def project(groups, weights, turn):
        return pl.pallas_call(
            functools.partial(project_kernel, head_size),
            out_shape=(
                jax.ShapeDtypeStruct((tokens, channels), jnp.bfloat16),
                jax.ShapeDtypeStruct((2, tokens, channels), jnp.bfloat16),
            ),
            in_specs=[VMEM] * (2 + half),
            out_specs=(VMEM, VMEM),
            scratch_shapes=[pltpu.VMEM((tokens, width), jnp.bfloat16)],
            compiler_params=params_of(32),
        )(gain_rows[turn], weights, *groups)

    def attend(queries, pair, fresh, turn):
        return pl.pallas_call(
            functools.partial(attend_kernel, turn, head_size),
            out_shape=(jax.ShapeDtypeStruct((2 * rows, width), jnp.bfloat16),) * half,
            in_specs=[ANY, ANY] + [VMEM] * 4,
            out_specs=(VMEM,) * half,
            scratch_shapes=[pltpu.VMEM(own_out.shape, jnp.bfloat16), pltpu.SemaphoreType.DMA],
            compiler_params=params_of(32),
        )(own_out, other_out, queries, pair, stale_pair[turn], fresh)

    def finish(x, own, last, turn):
        return pl.pallas_call(
            finish_kernel, out_shape=(block_shape,) * 2, in_specs=[VMEM] * 5, out_specs=(VMEM,) * 2,
            compiler_params=params_of(16),
        )(params[turn], params[1 - turn], x, own, last)

    outputs = [None, None]
    pairs = [None, None]
    freshes = [None, None]
    x = lax.dynamic_index_in_dim(hidden, core, 0, keepdims=False)
    for level in range(sections // 2):
        if level:
            x = upward(x, level - 1)
        normed = norm(x, 0)
        for turn in range(2):
            groups, weights = gather(normed, level, turn)
            queries, pair = project(groups, weights, turn)
            fresh = lax.ppermute(pair, AXES, swap)
            parts = attend(queries, pair, fresh, turn)
            own, last = scatter(parts, level)
            x, normed = finish(x, own, last, turn)
            here = plane == level
            keep = lambda new, old: new if old is None else jnp.where(here, new, old)
            outputs[turn] = keep(x, outputs[turn])
            pairs[turn] = keep(pair, pairs[turn])
            freshes[turn] = keep(fresh, freshes[turn])

    mine = jnp.where(core == 0, outputs[0], outputs[1])
    theirs = lax.ppermute(jnp.where(core == 0, outputs[1], outputs[0]), AXES, swap)
    block_output = jnp.stack(
        [jnp.where(core == 0, mine, theirs), jnp.where(core == 0, theirs, mine)]
    )
    cache = jnp.stack(
        [jnp.where(core == 0, pairs[0], freshes[1]), jnp.where(core == 0, freshes[0], pairs[1])]
    )
    cache = cache.reshape(2, 2, seq, rows, channels)
    spot = [0] * seq
    for index, position in enumerate(ring):
        spot[position] = index
    spot = jnp.array(spot, jnp.int32)
    steps = [0, 1]
    for group in range(1, half):
        steps += [-group, -group - 1] if group % 2 else [group, group + 1]
    held = [0] * seq
    for index, step in enumerate(steps):
        held[step % seq] = index
    held = jnp.array(held, jnp.int32)
    me = spot[lax.axis_index("seq")]
    cache = jnp.stack(
        [
            jnp.take(
                cache[patch],
                held[jnp.remainder((spot - me) * (1 - 2 * lax.rem(me + patch, 2)), seq)],
                axis=1,
            )
            for patch in range(2)
        ]
    )
    cache = lax.all_to_all(cache, "seq", split_axis=2, concat_axis=4, tiled=True)
    cache = jnp.transpose(cache[:, :, 0], (0, 2, 1, 3))
    return block_output[None], cache[None]


def solution(mesh):
    in_specs = (
        P(None, "seq", None),
        P("pipe", None),
        P("pipe", None),
        P("pipe", None),
        P("pipe", None, None),
        P("pipe", None, None, "seq"),
        P("pipe", "seq", None),
        P("pipe", None, "seq", None, None),
    )
    out_specs = (P("pipe", None, "seq", None), P("pipe", None, "seq", None, None))
    return jax.shard_map(body, mesh=mesh, in_specs=in_specs, out_specs=out_specs, check_vma=False)
```

```python
import functools
import math

import jax
import jax.numpy as jnp
from jax import lax
from jax.experimental import pallas as pl
from jax.experimental.pallas import tpu as pltpu
from jax.sharding import PartitionSpec as P

AXES = ("pipe", "seq")
VMEM = pl.BlockSpec(memory_space=pltpu.VMEM)
ANY = pl.BlockSpec(memory_space=pl.ANY)


def normalise(values, shift_row, scale_row):
    centered = values - jnp.mean(values, axis=-1, keepdims=True)
    spread = jnp.mean(centered * centered, axis=-1, keepdims=True)
    return (centered * lax.rsqrt(spread + 1e-06) * (1.0 + scale_row) + shift_row).astype(
        jnp.bfloat16
    )


def norm_kernel(params_ref, x_ref, normed_ref):
    normed_ref[...] = normalise(
        x_ref[...].astype(jnp.float32), params_ref[0:1, :], params_ref[1:2, :]
    )


def finish_kernel(params_ref, next_ref, x_ref, parts_ref, out_ref, normed_ref):
    update = jnp.sum(parts_ref[...].astype(jnp.float32), axis=0)
    result = (x_ref[...].astype(jnp.float32) + params_ref[2:3, :] * update).astype(jnp.bfloat16)
    out_ref[...] = result
    normed_ref[...] = normalise(
        result.astype(jnp.float32), next_ref[0:1, :], next_ref[1:2, :]
    )


def load_kernel(turn, own_ref, other_ref, out_ref, sem):
    mine = lax.rem(lax.axis_index("pipe"), 2) == turn

    @pl.when(mine)
    def _():
        pltpu.make_async_copy(own_ref, out_ref, sem).start()

    @pl.when(jnp.logical_not(mine))
    def _():
        pltpu.make_async_copy(other_ref, out_ref, sem).start()

    pltpu.make_async_copy(own_ref, out_ref, sem).wait()


def split_kernel(cache_ref, out_ref):
    channels = out_ref.shape[3]
    for kind in range(2):
        rows = cache_ref[:, kind, :]
        for shard in range(out_ref.shape[0]):
            out_ref[shard, kind] = rows[:, shard * channels : (shard + 1) * channels]


def project_kernel(head_size, gain_ref, weights_ref, blocks_ref, q_ref, kv_ref):
    count, rows, width = blocks_ref.shape
    tokens = blocks_ref[...].astype(jnp.float32).reshape(count * rows, width).astype(jnp.bfloat16)
    channels = weights_ref.shape[2]
    for part in (1, 2, 0):
        projected = jnp.dot(tokens, weights_ref[part], preferred_element_type=jnp.float32)
        if part == 2:
            kv_ref[1] = projected.astype(jnp.bfloat16)
            continue
        for start in range(0, channels, head_size):
            head = projected[:, start : start + head_size]
            square = jnp.mean(head * head, axis=-1, keepdims=True)
            head = (head * lax.rsqrt(square + 1e-06) * gain_ref[part : part + 1, :]).astype(
                jnp.bfloat16
            )
            if part == 0:
                q_ref[:, start : start + head_size] = head
            else:
                kv_ref[0, :, start : start + head_size] = head


def attend_kernel(turn, head_size, own_ref, other_ref, q_ref, kv_ref, stale_ref, fresh_ref, parts_ref, weights, sem):
    early = lax.rem(lax.axis_index("pipe"), 2) == 0
    mine = lax.rem(lax.axis_index("pipe"), 2) == turn

    @pl.when(mine)
    def _():
        pltpu.make_async_copy(own_ref, weights, sem).start()

    @pl.when(jnp.logical_not(mine))
    def _():
        pltpu.make_async_copy(other_ref, weights, sem).start()

    factor = 1.0 / math.sqrt(head_size)
    tokens, channels = q_ref.shape
    heads = []
    across = (((1,), (1,)), ((), ()))

    def far_of(kind, cut):
        stale = stale_ref[:, kind, :, cut].astype(jnp.float32).reshape(tokens, head_size)
        return jnp.where(early, stale, fresh_ref[kind, :, cut].astype(jnp.float32)).astype(
            jnp.bfloat16
        )

    for start in range(0, channels, head_size):
        cut = slice(start, start + head_size)
        query = q_ref[:, cut]
        near = lax.dot_general(query, kv_ref[0, :, cut], across, preferred_element_type=jnp.float32)
        far = lax.dot_general(query, far_of(0, cut), across, preferred_element_type=jnp.float32)
        near = jnp.exp(near * factor)
        far = jnp.exp(far * factor)
        total = jnp.sum(near, axis=-1, keepdims=True) + jnp.sum(far, axis=-1, keepdims=True)
        near = (near / total).astype(jnp.bfloat16)
        far = (far / total).astype(jnp.bfloat16)
        mixed = jnp.dot(near, kv_ref[1, :, cut], preferred_element_type=jnp.float32)
        mixed = mixed + jnp.dot(far, far_of(1, cut), preferred_element_type=jnp.float32)
        heads.append(mixed.astype(jnp.bfloat16))
    attended = jnp.concatenate(heads, axis=1)
    pltpu.make_async_copy(own_ref, weights, sem).wait()
    update = jnp.dot(attended, weights[...], preferred_element_type=jnp.float32)
    parts_ref[...] = update.reshape(parts_ref.shape).astype(jnp.bfloat16)


def params_of(limit):
    return pltpu.CompilerParams(vmem_limit_bytes=limit << 20)


def body(hidden, mod_shift, mod_scale, mod_gate, norm_gain, input_proj, output_proj, stale_cache):
    sections = lax.axis_size("pipe")
    seq = lax.axis_size("seq")
    pipe = lax.axis_index("pipe")
    core = lax.rem(pipe, 2)
    plane = pipe // 2
    rows, width = hidden.shape[1:]
    head_size = norm_gain.shape[2]
    channels = input_proj.shape[3]
    tokens = rows * seq

    place = lambda row, position: row * seq + position
    swap = [(place(row, s), place(row ^ 1, s)) for row in range(sections) for s in range(seq)]

    def across(blocks):
        return lax.all_to_all(blocks, "seq", split_axis=0, concat_axis=0, tiled=True)

    def upward(value, level):
        pairs = [
            (place(row, s), place(row + 2, s))
            for row in (2 * level, 2 * level + 1)
            for s in range(seq)
        ]
        return lax.ppermute(value, AXES, pairs)

    gains = jnp.pad(norm_gain[0].reshape(1, -1), ((0, 0), (0, width - 2 * head_size)))
    own_params = jnp.concatenate([mod_shift, mod_scale, mod_gate, gains], axis=0)
    own_in = jnp.transpose(input_proj[0], (1, 0, 2))
    own_out = output_proj[0]
    other_params = lax.ppermute(own_params, AXES, swap)
    own_in, own_out, other_params = lax.optimization_barrier((own_in, own_out, other_params))
    other_in = lax.ppermute(own_in, AXES, swap)
    other_out = lax.ppermute(own_out, AXES, swap)
    params = [jnp.where(core == turn, own_params, other_params) for turn in range(2)]
    gain_rows = [p[3, : 2 * head_size].reshape(2, head_size) for p in params]

    stale = pl.pallas_call(
        split_kernel,
        out_shape=jax.ShapeDtypeStruct((seq, 2, rows, channels), jnp.bfloat16),
        in_specs=[VMEM], out_specs=VMEM, compiler_params=params_of(16),
    )(stale_cache[0, 1])
    stale, hidden = lax.optimization_barrier((stale, hidden))
    stale = across(stale)
    stale_pair = [stale, lax.ppermute(stale, AXES, swap)]

    block_shape = jax.ShapeDtypeStruct((rows, width), jnp.bfloat16)

    def norm(x, turn):
        return pl.pallas_call(
            norm_kernel, out_shape=block_shape, in_specs=[VMEM] * 2, out_specs=VMEM,
            compiler_params=params_of(16),
        )(params[turn], x)

    def load(turn):
        return pl.pallas_call(
            functools.partial(load_kernel, turn),
            out_shape=jax.ShapeDtypeStruct(own_in.shape, jnp.bfloat16),
            in_specs=[ANY, ANY], out_specs=VMEM,
            scratch_shapes=[pltpu.SemaphoreType.DMA],
            compiler_params=params_of(16),
        )(own_in, other_in)

    def project(blocks, weights, turn):
        return pl.pallas_call(
            functools.partial(project_kernel, head_size),
            out_shape=(
                jax.ShapeDtypeStruct((tokens, channels), jnp.bfloat16),
                jax.ShapeDtypeStruct((2, tokens, channels), jnp.bfloat16),
            ),
            in_specs=[VMEM] * 3,
            out_specs=(VMEM, VMEM),
            compiler_params=params_of(32),
        )(gain_rows[turn], weights, blocks)

    def attend(queries, pair, fresh, turn):
        return pl.pallas_call(
            functools.partial(attend_kernel, turn, head_size),
            out_shape=jax.ShapeDtypeStruct((seq, rows, width), jnp.bfloat16),
            in_specs=[ANY, ANY] + [VMEM] * 4,
            out_specs=VMEM,
            scratch_shapes=[pltpu.VMEM(own_out.shape, jnp.bfloat16), pltpu.SemaphoreType.DMA],
            compiler_params=params_of(32),
        )(own_out, other_out, queries, pair, stale_pair[turn], fresh)

    def finish(x, parts, turn):
        return pl.pallas_call(
            finish_kernel, out_shape=(block_shape,) * 2, in_specs=[VMEM] * 4, out_specs=(VMEM,) * 2,
            compiler_params=params_of(16),
        )(params[turn], params[1 - turn], x, parts)

    outputs = [None, None]
    pairs = [None, None]
    freshes = [None, None]
    x = lax.dynamic_index_in_dim(hidden, core, 0, keepdims=False)
    for level in range(sections // 2):
        if level:
            x = upward(x, level - 1)
        normed = norm(x, 0)
        for turn in range(2):
            blocks = across(jnp.broadcast_to(normed, (seq,) + normed.shape))
            queries, pair = project(blocks, load(turn), turn)
            fresh = lax.ppermute(pair, AXES, swap)
            parts = attend(queries, pair, fresh, turn)
            x, normed = finish(x, across(parts), turn)
            here = plane == level
            keep = lambda new, old: new if old is None else jnp.where(here, new, old)
            outputs[turn] = keep(x, outputs[turn])
            pairs[turn] = keep(pair, pairs[turn])
            freshes[turn] = keep(fresh, freshes[turn])

    mine = jnp.where(core == 0, outputs[0], outputs[1])
    theirs = lax.ppermute(jnp.where(core == 0, outputs[1], outputs[0]), AXES, swap)
    block_output = jnp.stack(
        [jnp.where(core == 0, mine, theirs), jnp.where(core == 0, theirs, mine)]
    )
    cache = jnp.stack(
        [jnp.where(core == 0, pairs[0], freshes[1]), jnp.where(core == 0, freshes[0], pairs[1])]
    )
    cache = cache.reshape(2, 2, seq, rows, channels)
    cache = lax.all_to_all(cache, "seq", split_axis=2, concat_axis=4, tiled=True)
    cache = jnp.transpose(cache[:, :, 0], (0, 2, 1, 3))
    return block_output[None], cache[None]


def solution(mesh):
    in_specs = (
        P(None, "seq", None),
        P("pipe", None),
        P("pipe", None),
        P("pipe", None),
        P("pipe", None, None),
        P("pipe", None, None, "seq"),
        P("pipe", "seq", None),
        P("pipe", None, "seq", None, None),
    )
    out_specs = (P("pipe", None, "seq", None), P("pipe", None, "seq", None, None))
    return jax.shard_map(body, mesh=mesh, in_specs=in_specs, out_specs=out_specs, check_vma=False)
```

```python
import functools
import math

import jax
import jax.numpy as jnp
from jax import lax
from jax.experimental import pallas as pl
from jax.experimental.pallas import tpu as pltpu
from jax.sharding import PartitionSpec as P

AXES = ("pipe", "seq")
VMEM = pl.BlockSpec(memory_space=pltpu.VMEM)
ANY = pl.BlockSpec(memory_space=pl.ANY)


def ring_order(count):
    fast = 1
    while fast * fast * 4 <= count and count % (fast * 2) == 0:
        fast *= 2
    slow = count // fast
    if fast == 1 or slow % 2:
        return list(range(count))
    cells = [(0, 0)]
    for row in range(slow):
        columns = range(1, fast) if row % 2 == 0 else range(fast - 1, 0, -1)
        cells += [(row, column) for column in columns]
    cells += [(row, 0) for row in range(slow - 1, 0, -1)]
    return [row * fast + column for row, column in cells]


def pack_kernel(x_ref, cache_ref, out_ref):
    count, _, total = out_ref.shape
    width = x_ref.shape[1]
    channels = (total - width) // 2
    block = x_ref[...]
    sides = [cache_ref[:, kind, :] for kind in range(2)]
    for shard in range(count):
        out_ref[shard, :, :width] = block
        for kind in range(2):
            begin = width + kind * channels
            out_ref[shard, :, begin : begin + channels] = sides[kind][
                :, shard * channels : (shard + 1) * channels
            ]


def start_copies(turn, own_ref, other_ref, buffer, sems):
    mine = lax.rem(lax.axis_index("pipe"), 2) == turn
    parts = buffer.shape[0]

    @pl.when(mine)
    def _():
        for part in range(parts):
            pltpu.make_async_copy(own_ref.at[part], buffer.at[part], sems.at[part]).start()

    @pl.when(jnp.logical_not(mine))
    def _():
        for part in range(parts):
            pltpu.make_async_copy(other_ref.at[part], buffer.at[part], sems.at[part]).start()


def project_kernel(turn, head_size, params_ref, gain_ref, own_ref, other_ref, blocks_ref, q_ref, kv_ref, weights, sems):
    start_copies(turn, own_ref, other_ref, weights, sems)
    count, rows, _ = blocks_ref.shape
    width = params_ref.shape[1]
    values = blocks_ref[:, :, :width].astype(jnp.float32).reshape(count * rows, width)
    centered = values - jnp.mean(values, axis=-1, keepdims=True)
    spread = jnp.mean(centered * centered, axis=-1, keepdims=True)
    tokens = (
        centered * lax.rsqrt(spread + 1e-06) * (1.0 + params_ref[1:2, :]) + params_ref[0:1, :]
    ).astype(jnp.bfloat16)
    channels = weights.shape[2]
    for part in (0, 1, 2):
        pltpu.make_async_copy(own_ref.at[part], weights.at[part], sems.at[part]).wait()
        projected = jnp.dot(tokens, weights[part], preferred_element_type=jnp.float32)
        if part == 2:
            kv_ref[1] = projected.astype(jnp.bfloat16)
            continue
        for start in range(0, channels, head_size):
            head = projected[:, start : start + head_size]
            square = jnp.mean(head * head, axis=-1, keepdims=True)
            head = (head * lax.rsqrt(square + 1e-06) * gain_ref[part : part + 1, :]).astype(
                jnp.bfloat16
            )
            if part == 0:
                q_ref[:, start : start + head_size] = head
            else:
                kv_ref[0, :, start : start + head_size] = head


def attention(head_size, q_ref, kv_ref, stale_ref, fresh_ref):
    early = lax.rem(lax.axis_index("pipe"), 2) == 0
    factor = 1.0 / math.sqrt(head_size)
    tokens, channels = q_ref.shape
    heads = []
    across = (((1,), (1,)), ((), ()))

    def far_of(kind, start):
        begin = kind * channels + start
        stale = stale_ref[:, :, begin : begin + head_size].astype(jnp.float32)
        fresh = fresh_ref[kind, :, start : start + head_size].astype(jnp.float32)
        return jnp.where(early, stale.reshape(tokens, head_size), fresh).astype(jnp.bfloat16)

    for start in range(0, channels, head_size):
        cut = slice(start, start + head_size)
        query = q_ref[:, cut]
        near = lax.dot_general(query, kv_ref[0, :, cut], across, preferred_element_type=jnp.float32)
        far = lax.dot_general(query, far_of(0, start), across, preferred_element_type=jnp.float32)
        near = jnp.exp(near * factor)
        far = jnp.exp(far * factor)
        total = jnp.sum(near, axis=-1, keepdims=True) + jnp.sum(far, axis=-1, keepdims=True)
        near = (near / total).astype(jnp.bfloat16)
        far = (far / total).astype(jnp.bfloat16)
        mixed = jnp.dot(near, kv_ref[1, :, cut], preferred_element_type=jnp.float32)
        mixed = mixed + jnp.dot(far, far_of(1, start), preferred_element_type=jnp.float32)
        heads.append(mixed.astype(jnp.bfloat16))
    return jnp.concatenate(heads, axis=1)


def attend_kernel(head_size, q_ref, kv_ref, stale_ref, fresh_ref, out_ref):
    out_ref[...] = attention(head_size, q_ref, kv_ref, stale_ref, fresh_ref)


def partial_kernel(turn, head_size, own_ref, other_ref, q_ref, kv_ref, stale_ref, fresh_ref, *refs):
    extra, (parts_ref, weights, sems) = refs[:-3], refs[-3:]
    start_copies(turn, own_ref, other_ref, weights, sems)
    count, rows, _ = parts_ref.shape
    width = weights.shape[2]
    channels = q_ref.shape[1]
    for patch, cache in enumerate(extra):
        for kind in range(2):
            begin = width + (2 * patch + kind) * channels
            parts_ref[:, :, begin : begin + channels] = (
                cache[kind].astype(jnp.float32).reshape(count, rows, channels).astype(jnp.bfloat16)
            )
    attended = attention(head_size, q_ref, kv_ref, stale_ref, fresh_ref)
    pltpu.make_async_copy(own_ref.at[0], weights.at[0], sems.at[0]).wait()
    update = jnp.dot(attended, weights[0], preferred_element_type=jnp.float32)
    parts_ref[:, :, :width] = update.reshape(count, rows, width).astype(jnp.bfloat16)


def finish_kernel(params_ref, x_ref, parts_ref, out_ref):
    width = x_ref.shape[1]
    update = jnp.sum(parts_ref[:, :, :width].astype(jnp.float32), axis=0)
    out_ref[...] = (x_ref[...].astype(jnp.float32) + params_ref[2:3, :] * update).astype(
        jnp.bfloat16
    )


def whole_kernel(core_ref, order_ref, params_ref, att_ref, own_ref, other_ref, x_ref, out_ref, joined):
    step = pl.program_id(0)
    count, rows, tile = x_ref.shape
    channels = att_ref.shape[2]

    @pl.when(step == 0)
    def _():
        for shard in range(count):
            joined[:, shard * channels : (shard + 1) * channels] = att_ref[order_ref[shard]]

    def run(weights):
        update = jnp.dot(joined[...], weights, preferred_element_type=jnp.float32)
        x = x_ref[...].astype(jnp.float32).reshape(count * rows, tile)
        result = (x + params_ref[2:3, :] * update).reshape(count, rows, tile)
        out_ref[...] = result.astype(jnp.bfloat16)

    first = step < pl.num_programs(0) // 2

    @pl.when(first)
    def _():
        run(own_ref[...])

    @pl.when(jnp.logical_not(first))
    def _():
        run(other_ref[...])


def blank_kernel(*refs):
    pass


def params_of(limit):
    return pltpu.CompilerParams(vmem_limit_bytes=limit << 20)


def body(hidden, mod_shift, mod_scale, mod_gate, norm_gain, input_proj, output_proj, stale_cache):
    sections = lax.axis_size("pipe")
    planes = sections // 2
    seq = lax.axis_size("seq")
    pipe = lax.axis_index("pipe")
    me = lax.axis_index("seq")
    core = lax.rem(pipe, 2)
    plane = pipe // 2
    rows, width = hidden.shape[1:]
    head_size = norm_gain.shape[2]
    channels = input_proj.shape[3]
    tokens = rows * seq
    bf16 = lambda *shape: jax.ShapeDtypeStruct(shape, jnp.bfloat16)

    lowest, others = range(2), range(2, sections)
    place = lambda row, position: row * seq + position

    def swap(value, rows_of=range(sections)):
        pairs = [(place(row, s), place(row ^ 1, s)) for row in rows_of for s in range(seq)]
        return lax.ppermute(value, AXES, pairs)

    def upward(value, by=1):
        pairs = [
            (place(row, s), place((row + 2 * by) % sections, s))
            for row in range(sections)
            for s in range(seq)
        ]
        return lax.ppermute(value, AXES, pairs)

    ring = ring_order(seq)

    def around(value, step):
        pairs = [
            (place(row, ring[i]), place(row, ring[(i + step) % seq]))
            for row in others
            for i in range(seq)
        ]
        return lax.ppermute(value, AXES, pairs)

    spot = jnp.array([ring.index(s) for s in range(seq)], jnp.int32)
    moves = [-hop for hop in range(seq // 2 + 1)] + list(range(1, seq // 2))
    order = jnp.array(ring, jnp.int32)[
        jnp.remainder(spot[me] + jnp.array(moves, jnp.int32), seq)
    ]

    def across(blocks):
        return lax.all_to_all(blocks, "seq", split_axis=0, concat_axis=0, tiled=True)

    def spread(value):
        return across(jnp.broadcast_to(value, (seq,) + value.shape))

    def blank(*shapes):
        return pl.pallas_call(blank_kernel, out_shape=shapes, out_specs=(ANY,) * len(shapes))()

    gains = jnp.pad(norm_gain[0].reshape(1, -1), ((0, 0), (0, width - 2 * head_size)))
    own_params = jnp.concatenate([mod_shift, mod_scale, mod_gate, gains], axis=0)
    own_in = jnp.transpose(input_proj[0], (1, 0, 2))
    own_out = output_proj
    x = lax.dynamic_index_in_dim(hidden, core, 0, keepdims=False)
    packed = pl.pallas_call(
        pack_kernel, out_shape=bf16(seq, rows, width + 2 * channels),
        in_specs=[VMEM] * 2, out_specs=VMEM, compiler_params=params_of(16),
    )(x, stale_cache[0, 1])

    other_params = swap(own_params)
    own_in, own_out, other_params, packed = lax.optimization_barrier(
        (own_in, own_out, other_params, packed)
    )
    raised = upward(own_out)
    other_in = swap(own_in)
    other_out = swap(own_out)
    params = [jnp.where(core == turn, own_params, other_params) for turn in range(2)]
    gain_rows = [p[3, : 2 * head_size].reshape(2, head_size) for p in params]
    below = upward(params[1])

    def project(blocks, turn):
        return pl.pallas_call(
            functools.partial(project_kernel, turn, head_size),
            out_shape=(bf16(tokens, channels), bf16(2, tokens, channels)),
            in_specs=[VMEM, VMEM, ANY, ANY, VMEM],
            out_specs=(VMEM, VMEM),
            scratch_shapes=[
                pltpu.VMEM(own_in.shape, jnp.bfloat16), pltpu.SemaphoreType.DMA((3,)),
            ],
            compiler_params=params_of(56),
        )(params[turn], gain_rows[turn], own_in, other_in, blocks)

    def attend(queries, pair, stale, fresh):
        return pl.pallas_call(
            functools.partial(attend_kernel, head_size),
            out_shape=bf16(tokens, channels),
            in_specs=[VMEM] * 4, out_specs=VMEM,
            compiler_params=params_of(32),
        )(queries, pair, stale, fresh)

    def partial(queries, pair, stale, fresh, turn, extra=()):
        return pl.pallas_call(
            functools.partial(partial_kernel, turn, head_size),
            out_shape=bf16(seq, rows, width + 2 * channels * len(extra)),
            in_specs=[ANY, ANY] + [VMEM] * (4 + len(extra)),
            out_specs=VMEM,
            scratch_shapes=[
                pltpu.VMEM(own_out.shape, jnp.bfloat16), pltpu.SemaphoreType.DMA((1,)),
            ],
            compiler_params=params_of(32),
        )(own_out, other_out, queries, pair, stale, fresh, *extra)

    def finish(x, parts, turn):
        return pl.pallas_call(
            finish_kernel, out_shape=bf16(rows, width), in_specs=[VMEM] * 3, out_specs=VMEM,
            compiler_params=params_of(16),
        )(params[turn], x, parts)

    tile = next(t for t in (512, 384, 256, 128) if (width // 2) % t == 0)
    tiles = width // 2 // tile

    def whole(attended, own, other, x, gate_params):
        side = lambda step, core_ref: jnp.where(step < tiles, core_ref[0], 1 - core_ref[0])
        column = lambda step, core_ref: side(step, core_ref) * tiles + lax.rem(step, tiles)
        return pl.pallas_call(
            whole_kernel,
            grid_spec=pltpu.PrefetchScalarGridSpec(
                num_scalar_prefetch=2,
                grid=(2 * tiles,),
                in_specs=[
                    pl.BlockSpec((4, tile), lambda i, c, o: (0, column(i, c))),
                    pl.BlockSpec((seq, tokens, channels), lambda i, c, o: (0, 0, 0)),
                    pl.BlockSpec((seq * channels, tile), lambda i, c, o: (0, jnp.minimum(i, tiles - 1))),
                    pl.BlockSpec((seq * channels, tile), lambda i, c, o: (0, jnp.maximum(i - tiles, 0))),
                    pl.BlockSpec((seq, rows, tile), lambda i, c, o: (0, 0, column(i, c))),
                ],
                out_specs=pl.BlockSpec((seq, rows, tile), lambda i, c, o: (0, 0, column(i, c))),
                scratch_shapes=[pltpu.VMEM((tokens, seq * channels), jnp.bfloat16)],
            ),
            out_shape=bf16(seq, rows, width),
            compiler_params=params_of(40),
        )(core.astype(jnp.int32).reshape(1), order, gate_params, attended, own, other, x)

    blocks_shape = bf16(seq, rows, width)
    stale_shape = bf16(seq, rows, 2 * channels)
    pair_shape = bf16(2, tokens, channels)
    half_shape = bf16(seq * channels, width // 2)
    received = lax.cond(
        plane == 0, across, lambda value: blank(bf16(*packed.shape))[0], packed
    )

    def first_plane(received, raised):
        stale = received[:, :, width:]
        queries, pair0 = project(received, 0)
        fresh0 = swap(pair0, lowest)
        parts = across(partial(queries, pair0, stale, fresh0, 0))
        x1 = finish(x, parts, 0)
        blocks = spread(x1)
        stale = swap(stale, lowest)
        queries, pair1 = project(blocks, 1)
        fresh1 = swap(pair1, lowest)
        attended = attend(queries, pair1, stale, fresh1)
        nothing = blank(stale_shape, half_shape)
        return (x1, blocks, attended, pair0, fresh0, pair1, fresh1) + tuple(nothing)

    def other_planes(received, raised):
        stale = across(packed[:, :, width:])
        lent = swap(raised, others)
        below_out = jnp.where(core == 1, raised, lent)[0]
        mine = lax.dynamic_slice_in_dim(below_out, core * (width // 2), width // 2, 1)
        right, left = [mine], [mine]
        for hop in range(1, seq // 2 + 1):
            right.append(around(right[-1], 1))
            if hop < seq // 2:
                left.append(around(left[-1], -1))
        gathered = jnp.concatenate(right + left[1:], axis=0)
        nothing = blank(
            bf16(rows, width), blocks_shape, bf16(tokens, channels),
            pair_shape, pair_shape, pair_shape, pair_shape,
        )
        return tuple(nothing) + (stale, gathered)

    x1, blocks, attended, pair0, fresh0, pair1, fresh1, stale, gathered = lax.cond(
        plane == 0, first_plane, other_planes, received, raised
    )
    gathered_other = swap(gathered)
    stale_pair = [stale, swap(stale)]
    outputs = [x1, None]
    saved = [
        jnp.where(core == 0, pair0, fresh1), jnp.where(core == 0, fresh0, pair1)
    ]
    for level in range(1, planes):
        attended = upward(attended)
        blocks = upward(blocks)
        blocks = whole(spread(attended), gathered, gathered_other, blocks, below)
        x = lax.dynamic_index_in_dim(blocks, me, 0, keepdims=False)
        down = upward(x, -1)
        outputs[1] = down if outputs[1] is None else jnp.where(plane == level - 1, down, outputs[1])
        queries, pair0 = project(blocks, 0)
        fresh0 = swap(pair0)
        parts = across(partial(queries, pair0, stale_pair[0], fresh0, 0))
        x = finish(x, parts, 0)
        here = plane == level
        outputs[0] = jnp.where(here, x, outputs[0])
        blocks = spread(x)
        queries, pair1 = project(blocks, 1)
        fresh1 = swap(pair1)
        now = [jnp.where(core == 0, pair0, fresh1), jnp.where(core == 0, fresh0, pair1)]
        saved = [jnp.where(here, new, old) for new, old in zip(now, saved)]
        if level < planes - 1:
            attended = attend(queries, pair1, stale_pair[1], fresh1)
    parts = across(partial(queries, pair1, stale_pair[1], fresh1, 1, saved))
    x = finish(x, parts, 1)
    outputs[1] = jnp.where(plane == planes - 1, x, outputs[1])

    mine = jnp.where(core == 0, outputs[0], outputs[1])
    theirs = swap(jnp.where(core == 0, outputs[1], outputs[0]))
    block_output = jnp.stack(
        [jnp.where(core == 0, mine, theirs), jnp.where(core == 0, theirs, mine)]
    )
    cache = parts[:, :, width:].reshape(seq, rows, 2, 2, channels)
    cache = jnp.transpose(cache, (2, 1, 3, 0, 4)).reshape(2, rows, 2, seq * channels)
    return block_output[None], cache[None]


def solution(mesh):
    in_specs = (
        P(None, "seq", None),
        P("pipe", None),
        P("pipe", None),
        P("pipe", None),
        P("pipe", None, None),
        P("pipe", None, None, "seq"),
        P("pipe", "seq", None),
        P("pipe", None, "seq", None, None),
    )
    out_specs = (P("pipe", None, "seq", None), P("pipe", None, "seq", None, None))
    return jax.shard_map(body, mesh=mesh, in_specs=in_specs, out_specs=out_specs, check_vma=False)
```

```python
import functools
import math

import jax
import jax.numpy as jnp
from jax import lax
from jax.experimental import pallas as pl
from jax.experimental.pallas import tpu as pltpu
from jax.sharding import PartitionSpec as P

AXES = ("pipe", "seq")
VMEM = pl.BlockSpec(memory_space=pltpu.VMEM)
ANY = pl.BlockSpec(memory_space=pl.ANY)


def normalise(values, params_ref):
    centered = values - jnp.mean(values, axis=-1, keepdims=True)
    spread = jnp.mean(centered * centered, axis=-1, keepdims=True)
    return (
        centered * lax.rsqrt(spread + 1e-06) * (1.0 + params_ref[1:2, :]) + params_ref[0:1, :]
    ).astype(jnp.bfloat16)


def norm_kernel(params_ref, x_ref, out_ref):
    block = normalise(x_ref[...].astype(jnp.float32), params_ref)
    for shard in range(out_ref.shape[0]):
        out_ref[shard] = block


def pack_kernel(params_ref, x_ref, cache_ref, out_ref):
    count, _, total = out_ref.shape
    width = x_ref.shape[1]
    channels = (total - width) // 2
    block = normalise(x_ref[...].astype(jnp.float32), params_ref)
    sides = [cache_ref[:, kind, :] for kind in range(2)]
    for shard in range(count):
        out_ref[shard, :, :width] = block
        for kind in range(2):
            begin = width + kind * channels
            out_ref[shard, :, begin : begin + channels] = sides[kind][
                :, shard * channels : (shard + 1) * channels
            ]


def start_copies(turn, own_ref, other_ref, buffer, sems):
    mine = lax.rem(lax.axis_index("pipe"), 2) == turn
    parts = buffer.shape[0]

    @pl.when(mine)
    def _():
        for part in range(parts):
            pltpu.make_async_copy(own_ref.at[part], buffer.at[part], sems.at[part]).start()

    @pl.when(jnp.logical_not(mine))
    def _():
        for part in range(parts):
            pltpu.make_async_copy(other_ref.at[part], buffer.at[part], sems.at[part]).start()


def project_kernel(turn, head_size, gain_ref, own_ref, other_ref, blocks_ref, q_ref, kv_ref, weights, sems):
    start_copies(turn, own_ref, other_ref, weights, sems)
    count, rows, _ = blocks_ref.shape
    width = weights.shape[1]
    tokens = (
        blocks_ref[:, :, :width].astype(jnp.float32).reshape(count * rows, width).astype(jnp.bfloat16)
    )
    channels = weights.shape[2]
    for part in (0, 1, 2):
        pltpu.make_async_copy(own_ref.at[part], weights.at[part], sems.at[part]).wait()
        projected = jnp.dot(tokens, weights[part], preferred_element_type=jnp.float32)
        if part == 2:
            kv_ref[1] = projected.astype(jnp.bfloat16)
            continue
        for start in range(0, channels, head_size):
            head = projected[:, start : start + head_size]
            square = jnp.mean(head * head, axis=-1, keepdims=True)
            head = (head * lax.rsqrt(square + 1e-06) * gain_ref[part : part + 1, :]).astype(
                jnp.bfloat16
            )
            if part == 0:
                q_ref[:, start : start + head_size] = head
            else:
                kv_ref[0, :, start : start + head_size] = head


def attention(head_size, q_ref, kv_ref, far_ref):
    factor = 1.0 / math.sqrt(head_size)
    tokens, channels = q_ref.shape
    heads = []
    across = (((1,), (1,)), ((), ()))

    def far_of(kind, start):
        if far_ref.shape[2] == channels:
            return far_ref[kind, :, start : start + head_size]
        begin = kind * channels + start
        blocks = far_ref[:, :, begin : begin + head_size].astype(jnp.float32)
        return blocks.reshape(tokens, head_size).astype(jnp.bfloat16)

    for start in range(0, channels, head_size):
        cut = slice(start, start + head_size)
        query = q_ref[:, cut]
        near = lax.dot_general(query, kv_ref[0, :, cut], across, preferred_element_type=jnp.float32)
        far = lax.dot_general(query, far_of(0, start), across, preferred_element_type=jnp.float32)
        near = jnp.exp(near * factor)
        far = jnp.exp(far * factor)
        total = jnp.sum(near, axis=-1, keepdims=True) + jnp.sum(far, axis=-1, keepdims=True)
        near = (near / total).astype(jnp.bfloat16)
        far = (far / total).astype(jnp.bfloat16)
        mixed = jnp.dot(near, kv_ref[1, :, cut], preferred_element_type=jnp.float32)
        mixed = mixed + jnp.dot(far, far_of(1, start), preferred_element_type=jnp.float32)
        heads.append(mixed.astype(jnp.bfloat16))
    return jnp.concatenate(heads, axis=1)


def put_cache(caches, out_ref, offset):
    count, rows, _ = out_ref.shape
    channels = caches[0].shape[2] if caches else 0
    for patch, cache in enumerate(caches):
        for kind in range(2):
            begin = offset + (2 * patch + kind) * channels
            out_ref[:, :, begin : begin + channels] = (
                cache[kind].astype(jnp.float32).reshape(count, rows, channels).astype(jnp.bfloat16)
            )


def cache_kernel(*refs):
    put_cache(refs[:-1], refs[-1], 0)


def partial_kernel(turn, head_size, own_ref, other_ref, q_ref, kv_ref, far_ref, *refs):
    extra, (parts_ref, weights, sems) = refs[:-3], refs[-3:]
    start_copies(turn, own_ref, other_ref, weights, sems)
    count, rows, _ = parts_ref.shape
    width = weights.shape[2]
    put_cache(extra, parts_ref, width)
    attended = attention(head_size, q_ref, kv_ref, far_ref)
    pltpu.make_async_copy(own_ref.at[0], weights.at[0], sems.at[0]).wait()
    update = jnp.dot(attended, weights[0], preferred_element_type=jnp.float32)
    parts_ref[:, :, :width] = update.reshape(count, rows, width).astype(jnp.bfloat16)


def finish_kernel(params_ref, next_ref, x_ref, parts_ref, out_ref, *normed):
    width = x_ref.shape[1]
    update = jnp.sum(parts_ref[:, :, :width].astype(jnp.float32), axis=0)
    result = (x_ref[...].astype(jnp.float32) + params_ref[2:3, :] * update).astype(jnp.bfloat16)
    out_ref[...] = result
    for blocks_ref in normed:
        block = normalise(result.astype(jnp.float32), next_ref)
        for shard in range(blocks_ref.shape[0]):
            blocks_ref[shard] = block


def blank_kernel(*refs):
    pass


def params_of(limit):
    return pltpu.CompilerParams(vmem_limit_bytes=limit << 20)


def body(hidden, mod_shift, mod_scale, mod_gate, norm_gain, input_proj, output_proj, stale_cache):
    sections = lax.axis_size("pipe")
    planes = sections // 2
    seq = lax.axis_size("seq")
    pipe = lax.axis_index("pipe")
    core = lax.rem(pipe, 2)
    plane = pipe // 2
    rows, width = hidden.shape[1:]
    head_size = norm_gain.shape[2]
    channels = input_proj.shape[3]
    tokens = rows * seq
    bf16 = lambda *shape: jax.ShapeDtypeStruct(shape, jnp.bfloat16)

    place = lambda row, position: row * seq + position

    def swap(value):
        pairs = [(place(row, s), place(row ^ 1, s)) for row in range(sections) for s in range(seq)]
        return lax.ppermute(value, AXES, pairs)

    def upward(value, level, side):
        row = 2 * level + side
        return lax.ppermute(value, AXES, [(place(row, s), place(row + 2, s)) for s in range(seq)])

    def across(blocks):
        return lax.all_to_all(blocks, "seq", split_axis=0, concat_axis=0, tiled=True)

    def blank(*shapes):
        return pl.pallas_call(blank_kernel, out_shape=shapes, out_specs=(ANY,) * len(shapes))()

    gains = jnp.pad(norm_gain[0].reshape(1, -1), ((0, 0), (0, width - 2 * head_size)))
    own_params = jnp.concatenate([mod_shift, mod_scale, mod_gate, gains], axis=0)
    own_in = jnp.transpose(input_proj[0], (1, 0, 2))
    own_out = output_proj
    x = lax.dynamic_index_in_dim(hidden, core, 0, keepdims=False)
    packed = pl.pallas_call(
        pack_kernel, out_shape=bf16(seq, rows, width + 2 * channels),
        in_specs=[VMEM] * 3, out_specs=VMEM, compiler_params=params_of(16),
    )(own_params, x, stale_cache[0, 1])

    other_params = swap(own_params)
    own_in, own_out, other_params, packed = lax.optimization_barrier(
        (own_in, own_out, other_params, packed)
    )
    other_in = swap(own_in)
    other_out = swap(own_out)
    params = [jnp.where(core == turn, own_params, other_params) for turn in range(2)]
    gain_rows = [p[3, : 2 * head_size].reshape(2, head_size) for p in params]
    blocks_shape = bf16(seq, rows, width)

    def norm(x, turn):
        return pl.pallas_call(
            norm_kernel, out_shape=blocks_shape, in_specs=[VMEM] * 2, out_specs=VMEM,
            compiler_params=params_of(16),
        )(params[turn], x)

    def project(blocks, turn):
        return pl.pallas_call(
            functools.partial(project_kernel, turn, head_size),
            out_shape=(bf16(tokens, channels), bf16(2, tokens, channels)),
            in_specs=[VMEM, ANY, ANY, VMEM],
            out_specs=(VMEM, VMEM),
            scratch_shapes=[
                pltpu.VMEM(own_in.shape, jnp.bfloat16), pltpu.SemaphoreType.DMA((3,)),
            ],
            compiler_params=params_of(56),
        )(gain_rows[turn], own_in, other_in, blocks)

    def partial(blocks, far, turn, extra=lambda pair: ()):
        queries, pair = project(blocks, turn)
        caches = extra(pair)
        parts = pl.pallas_call(
            functools.partial(partial_kernel, turn, head_size),
            out_shape=bf16(seq, rows, width + 2 * channels * len(caches)),
            in_specs=[ANY, ANY] + [VMEM] * (3 + len(caches)),
            out_specs=VMEM,
            scratch_shapes=[
                pltpu.VMEM(own_out.shape, jnp.bfloat16), pltpu.SemaphoreType.DMA((1,)),
            ],
            compiler_params=params_of(32),
        )(own_out, other_out, queries, pair, far, *caches)
        return parts, pair

    def finish(x, parts, turn, onward):
        shapes = (bf16(rows, width),) + (blocks_shape,) * onward
        return pl.pallas_call(
            finish_kernel, out_shape=shapes, in_specs=[VMEM] * 4, out_specs=(VMEM,) * len(shapes),
            compiler_params=params_of(16),
        )(params[turn], params[1 - turn], x, parts)

    early = core == 0
    either = lambda on_early, on_late: lax.cond(early, on_early, on_late)

    def first_early():
        value = across(packed)
        return value, value[:, :, width:]

    def first_late():
        return blank(bf16(*packed.shape))[0], across(packed[:, :, width:])

    received, stale = either(first_early, first_late)
    stale_pair = [stale, swap(stale)]
    pair = None
    blocks_out, sources = {}, {}
    for layer in range(sections):
        turn, level = layer % 2, layer // 2
        crossing = layer > 0 and turn == 0

        def early_scatter():
            parts, fresh = partial(received, stale_pair[turn], turn)
            return parts, fresh, x

        def late_gather():
            old = blank(bf16(2, tokens, channels))[0] if pair is None else pair
            if layer == 0 or crossing:
                return norm(x, turn), old, x
            result, normed = finish(x, received, 1 - turn, 1)
            return normed, old, result

        if crossing:
            x = either(lambda: x, lambda: finish(x, received, 1 - turn, 0)[0])
            blocks_out[layer - 1, 1] = x
            x = jnp.where(early, x, upward(x, level - 1, 1))
        payload, pair, x = either(early_scatter, late_gather)
        if layer > 0 and not crossing:
            blocks_out[layer - 1, 1] = x
        sources[layer, 0] = pair
        got = swap(pair)
        sources[layer, 2] = got
        received = across(payload)
        if layer == sections - 1:
            break

        crossing = turn == 1

        def early_gather():
            if crossing:
                return norm(x, 1 - turn), pair, x
            result, normed = finish(x, received, turn, 1)
            return normed, pair, result

        def late_scatter():
            parts, fresh = partial(received, got, turn)
            return parts, fresh, x

        if crossing:
            x = either(lambda: finish(x, received, turn, 0)[0], lambda: x)
            blocks_out[layer, 0] = x
            x = jnp.where(early, upward(x, level, 0), x)
        payload, pair, x = either(early_gather, late_scatter)
        if not crossing:
            blocks_out[layer, 0] = x
        sources[layer, 1] = pair
        if crossing:
            active = pipe == jnp.where(early, 2 * level + 2, 2 * level + 1)
            received = lax.cond(active, across, lambda _: blank(blocks_shape)[0], payload)
        else:
            received = across(payload)

    def by_plane(values):
        chosen = values[0]
        for level in range(1, planes):
            chosen = jnp.where(plane == level, values[level], chosen)
        return chosen

    last = sections - 1
    first_cache = by_plane(
        [jnp.where(early, sources[2 * m, 0], sources[2 * m + 1, 2]) for m in range(planes)]
    )
    second_cache = by_plane(
        [
            jnp.where(early, sources[2 * m + 1, 2], sources[2 * m + 1, int(m < planes - 1)])
            for m in range(planes)
        ]
    )

    def last_early():
        result = finish(x, received, last % 2, 0)[0]
        packed = pl.pallas_call(
            cache_kernel, out_shape=bf16(seq, rows, 4 * channels),
            in_specs=[VMEM] * 2, out_specs=VMEM, compiler_params=params_of(16),
        )(first_cache, second_cache)
        return result, across(packed)

    def last_late():
        extra = lambda fresh: (first_cache, jnp.where(plane == planes - 1, fresh, second_cache))
        parts, _ = partial(received, got, last % 2, extra)
        parts = across(parts)
        return finish(x, parts, last % 2, 0)[0], parts[:, :, width:]

    x, cache = either(last_early, last_late)
    blocks_out[last, 0] = blocks_out[last, 1] = x
    mine = by_plane(
        [jnp.where(early, blocks_out[2 * m, 0], blocks_out[2 * m + 1, 1]) for m in range(planes)]
    )
    theirs = swap(
        by_plane(
            [jnp.where(early, blocks_out[2 * m + 1, 0], blocks_out[2 * m, 1]) for m in range(planes)]
        )
    )
    block_output = jnp.stack([jnp.where(early, mine, theirs), jnp.where(early, theirs, mine)])
    cache = cache.reshape(seq, rows, 2, 2, channels)
    cache = jnp.transpose(cache, (2, 1, 3, 0, 4)).reshape(2, rows, 2, seq * channels)
    return block_output[None], cache[None]


def solution(mesh):
    in_specs = (
        P(None, "seq", None),
        P("pipe", None),
        P("pipe", None),
        P("pipe", None),
        P("pipe", None, None),
        P("pipe", None, None, "seq"),
        P("pipe", "seq", None),
        P("pipe", None, "seq", None, None),
    )
    out_specs = (P("pipe", None, "seq", None), P("pipe", None, "seq", None, None))
    return jax.shard_map(body, mesh=mesh, in_specs=in_specs, out_specs=out_specs, check_vma=False)
```

```python
import functools
import math

import jax
import jax.numpy as jnp
from jax import lax
from jax.experimental import pallas as pl
from jax.experimental.pallas import tpu as pltpu
from jax.sharding import PartitionSpec as P

AXES = ("pipe", "seq")
VMEM = pl.BlockSpec(memory_space=pltpu.VMEM)
ANY = pl.BlockSpec(memory_space=pl.ANY)
HBM = pl.BlockSpec(memory_space=pltpu.HBM)


def normalise(values, params_ref):
    centered = values - jnp.mean(values, axis=-1, keepdims=True)
    spread = jnp.mean(centered * centered, axis=-1, keepdims=True)
    return (
        centered * lax.rsqrt(spread + 1e-06) * (1.0 + params_ref[1:2, :]) + params_ref[0:1, :]
    ).astype(jnp.bfloat16)


def spread_block(block, buffer, out_ref, sems):
    width = buffer.shape[1]
    buffer[...] = block
    copies = [
        pltpu.make_async_copy(buffer, out_ref.at[shard, :, :width], sems.at[shard])
        for shard in range(out_ref.shape[0])
    ]
    for copy in copies:
        copy.start()
    return copies


def norm_kernel(params_ref, x_ref, out_ref, buffer, sems):
    block = normalise(x_ref[...].astype(jnp.float32), params_ref)
    for copy in spread_block(block, buffer, out_ref, sems):
        copy.wait()


def pack_kernel(params_ref, x_ref, cache_ref, out_ref, buffer, sems, sides, sem):
    count, _, total = sides.shape
    width = x_ref.shape[1]
    channels = total // 2
    block = normalise(x_ref[...].astype(jnp.float32), params_ref)
    copies = spread_block(block, buffer, out_ref, sems)
    for kind in range(2):
        rows = cache_ref[:, kind, :]
        for shard in range(count):
            sides[shard, :, kind * channels : (kind + 1) * channels] = rows[
                :, shard * channels : (shard + 1) * channels
            ]
    copies.append(pltpu.make_async_copy(sides, out_ref.at[:, :, width:], sem))
    copies[-1].start()
    for copy in copies:
        copy.wait()


def attention(head_size, q_ref, kv_ref, far_ref):
    factor = 1.0 / math.sqrt(head_size)
    tokens, channels = q_ref.shape
    heads = []
    across = (((1,), (1,)), ((), ()))

    def far_of(kind, start):
        if far_ref.shape[2] == channels:
            return far_ref[kind, :, start : start + head_size]
        begin = kind * channels + start
        blocks = far_ref[:, :, begin : begin + head_size].astype(jnp.float32)
        return blocks.reshape(tokens, head_size).astype(jnp.bfloat16)

    for start in range(0, channels, head_size):
        cut = slice(start, start + head_size)
        query = q_ref[:, cut]
        near = lax.dot_general(query, kv_ref[0, :, cut], across, preferred_element_type=jnp.float32)
        far = lax.dot_general(query, far_of(0, start), across, preferred_element_type=jnp.float32)
        near = jnp.exp(near * factor)
        far = jnp.exp(far * factor)
        total = jnp.sum(near, axis=-1, keepdims=True) + jnp.sum(far, axis=-1, keepdims=True)
        near = (near / total).astype(jnp.bfloat16)
        far = (far / total).astype(jnp.bfloat16)
        mixed = jnp.dot(near, kv_ref[1, :, cut], preferred_element_type=jnp.float32)
        mixed = mixed + jnp.dot(far, far_of(1, start), preferred_element_type=jnp.float32)
        heads.append(mixed.astype(jnp.bfloat16))
    return jnp.concatenate(heads, axis=1)


def put_cache(caches, out_ref, offset):
    count, rows, _ = out_ref.shape
    channels = caches[0].shape[2]
    for patch, cache in enumerate(caches):
        for kind in range(2):
            begin = offset + (2 * patch + kind) * channels
            out_ref[:, :, begin : begin + channels] = (
                cache[kind].astype(jnp.float32).reshape(count, rows, channels).astype(jnp.bfloat16)
            )


def cache_kernel(*refs):
    put_cache(refs[:-1], refs[-1], 0)


def block_kernel(
    turn, head_size, planes, gain_ref, own_in, other_in, own_out, other_out, blocks_ref, far_ref, *refs
):
    caches, refs = refs[:-10], refs[-10:]
    parts_ref, kv_ref, blocks, w_in, w_out, parts, q_ref, in_sems, sems, part_sems = refs
    count, rows, width = blocks.shape
    channels = w_out.shape[0]
    pieces = in_sems.shape[1]
    depth = width // pieces
    mine = lax.rem(lax.axis_index("pipe"), 2) == turn

    def weight_copies(source_in, source_out):
        for part in (1, 2, 0):
            for piece in range(pieces):
                cut = pl.ds(piece * depth, depth)
                pltpu.make_async_copy(
                    source_in.at[part, cut], w_in.at[part, cut], in_sems.at[part, piece]
                ).start()
        pltpu.make_async_copy(source_out.at[0], w_out, sems.at[1]).start()

    fetch = pltpu.make_async_copy(blocks_ref.at[:, :, :width], blocks, sems.at[0])
    fetch.start()

    @pl.when(mine)
    def _():
        weight_copies(own_in, own_out)

    @pl.when(jnp.logical_not(mine))
    def _():
        weight_copies(other_in, other_out)

    fetch.wait()
    tokens = blocks[...].astype(jnp.float32).reshape(count * rows, width).astype(jnp.bfloat16)
    for part in (1, 2, 0):
        for piece in range(pieces):
            cut = pl.ds(piece * depth, depth)
            pltpu.make_async_copy(
                own_in.at[part, cut], w_in.at[part, cut], in_sems.at[part, piece]
            ).wait()
        projected = jnp.dot(tokens, w_in[part], preferred_element_type=jnp.float32)
        if part == 2:
            kv_ref[1] = projected.astype(jnp.bfloat16)
            continue
        for start in range(0, channels, head_size):
            head = projected[:, start : start + head_size]
            square = jnp.mean(head * head, axis=-1, keepdims=True)
            head = (head * lax.rsqrt(square + 1e-06) * gain_ref[part : part + 1, :]).astype(
                jnp.bfloat16
            )
            if part == 0:
                q_ref[:, start : start + head_size] = head
            else:
                kv_ref[0, :, start : start + head_size] = head

    sent = []

    def send(begin, size, sem):
        cut = pl.ds(begin, size)
        sent.append(
            pltpu.make_async_copy(parts.at[:, :, cut], parts_ref.at[:, :, cut], part_sems.at[sem])
        )
        sent[-1].start()

    steps = part_sems.shape[0] - 1
    if caches:
        last = lax.axis_index("pipe") // 2 == planes - 1
        first, second = caches
        put_cache((first, jnp.where(last, kv_ref[...], second[...])), parts, width)
        send(width, 4 * channels, steps)
    attended = attention(head_size, q_ref, kv_ref, far_ref)
    pltpu.make_async_copy(own_out.at[0], w_out, sems.at[1]).wait()
    tile = width // steps
    for step in range(steps):
        cut = slice(step * tile, (step + 1) * tile)
        update = jnp.dot(attended, w_out[:, cut], preferred_element_type=jnp.float32)
        parts[:, :, cut] = update.reshape(count, rows, tile).astype(jnp.bfloat16)
        send(step * tile, tile, step)
    for copy in sent:
        copy.wait()


def finish_kernel(params_ref, next_ref, x_ref, parts_ref, out_ref, *rest):
    width = x_ref.shape[1]
    update = jnp.sum(parts_ref[:, :, :width].astype(jnp.float32), axis=0)
    result = (x_ref[...].astype(jnp.float32) + params_ref[2:3, :] * update).astype(jnp.bfloat16)
    out_ref[...] = result
    if rest:
        blocks_ref, buffer, sems = rest
        block = normalise(result.astype(jnp.float32), next_ref)
        for copy in spread_block(block, buffer, blocks_ref, sems):
            copy.wait()


def blank_kernel(*refs):
    pass


def params_of(limit):
    return pltpu.CompilerParams(vmem_limit_bytes=limit << 20)


def body(hidden, mod_shift, mod_scale, mod_gate, norm_gain, input_proj, output_proj, stale_cache):
    sections = lax.axis_size("pipe")
    planes = sections // 2
    seq = lax.axis_size("seq")
    pipe = lax.axis_index("pipe")
    core = lax.rem(pipe, 2)
    plane = pipe // 2
    rows, width = hidden.shape[1:]
    head_size = norm_gain.shape[2]
    channels = input_proj.shape[3]
    tokens = rows * seq
    bf16 = lambda *shape: jax.ShapeDtypeStruct(shape, jnp.bfloat16)

    place = lambda row, position: row * seq + position

    def swap(value):
        pairs = [(place(row, s), place(row ^ 1, s)) for row in range(sections) for s in range(seq)]
        return lax.ppermute(value, AXES, pairs)

    def upward(value, level, side):
        row = 2 * level + side
        return lax.ppermute(value, AXES, [(place(row, s), place(row + 2, s)) for s in range(seq)])

    def across(blocks):
        return lax.all_to_all(blocks, "seq", split_axis=0, concat_axis=0, tiled=True)

    def blank(*shapes):
        return pl.pallas_call(blank_kernel, out_shape=shapes, out_specs=(ANY,) * len(shapes))()

    gains = jnp.pad(norm_gain[0].reshape(1, -1), ((0, 0), (0, width - 2 * head_size)))
    own_params = jnp.concatenate([mod_shift, mod_scale, mod_gate, gains], axis=0)
    own_in = jnp.transpose(input_proj[0], (1, 0, 2))
    own_out = output_proj
    x = lax.dynamic_index_in_dim(hidden, core, 0, keepdims=False)
    spreading = [pltpu.VMEM((rows, width), jnp.bfloat16), pltpu.SemaphoreType.DMA((seq,))]
    packed = pl.pallas_call(
        pack_kernel, out_shape=bf16(seq, rows, width + 2 * channels),
        in_specs=[VMEM] * 3, out_specs=HBM,
        scratch_shapes=spreading + [
            pltpu.VMEM((seq, rows, 2 * channels), jnp.bfloat16), pltpu.SemaphoreType.DMA,
        ],
        compiler_params=params_of(16),
    )(own_params, x, stale_cache[0, 1])

    other_params = swap(own_params)
    own_in, own_out, other_params, packed = lax.optimization_barrier(
        (own_in, own_out, other_params, packed)
    )
    other_in = swap(own_in)
    other_out = swap(own_out)
    params = [jnp.where(core == turn, own_params, other_params) for turn in range(2)]
    gain_rows = [p[3, : 2 * head_size].reshape(2, head_size) for p in params]
    blocks_shape = bf16(seq, rows, width)

    def norm(x, turn):
        return pl.pallas_call(
            norm_kernel, out_shape=blocks_shape, in_specs=[VMEM] * 2, out_specs=HBM,
            scratch_shapes=spreading, compiler_params=params_of(16),
        )(params[turn], x)

    def block(blocks, far, turn, caches=()):
        total = width + 2 * channels * len(caches)
        return pl.pallas_call(
            functools.partial(block_kernel, turn, head_size, planes),
            out_shape=(bf16(seq, rows, total), bf16(2, tokens, channels)),
            in_specs=[VMEM] + [HBM] * 4 + [ANY] + [VMEM] * (1 + len(caches)),
            out_specs=(HBM, VMEM),
            scratch_shapes=[
                pltpu.VMEM((seq, rows, width), jnp.bfloat16),
                pltpu.VMEM(own_in.shape, jnp.bfloat16),
                pltpu.VMEM(own_out.shape[1:], jnp.bfloat16),
                pltpu.VMEM((seq, rows, total), jnp.bfloat16),
                pltpu.VMEM((tokens, channels), jnp.bfloat16),
                pltpu.SemaphoreType.DMA((3, 2)),
                pltpu.SemaphoreType.DMA((2,)),
                pltpu.SemaphoreType.DMA((5,)),
            ],
            compiler_params=params_of(32),
        )(gain_rows[turn], own_in, other_in, own_out, other_out, blocks, far, *caches)

    def finish(x, parts, turn, onward):
        shapes = (bf16(rows, width),) + (blocks_shape,) * onward
        return pl.pallas_call(
            finish_kernel, out_shape=shapes, in_specs=[VMEM] * 4,
            out_specs=(VMEM,) + (HBM,) * onward,
            scratch_shapes=spreading * onward, compiler_params=params_of(16),
        )(params[turn], params[1 - turn], x, parts)

    early = core == 0
    either = lambda on_early, on_late: lax.cond(early, on_early, on_late)

    def first_early():
        value = across(packed)
        return value, value[:, :, width:]

    def first_late():
        return blank(bf16(*packed.shape))[0], across(packed[:, :, width:])

    received, stale = either(first_early, first_late)
    stale_pair = [stale, swap(stale)]
    pair_shape, block_shape = bf16(2, tokens, channels), bf16(rows, width)
    late_pair = None
    early_x, late_x = x, x
    blocks_out, sources = {}, {}
    for layer in range(sections):
        turn, level = layer % 2, layer // 2
        crossing = layer > 0 and turn == 0

        def early_scatter():
            parts, fresh = block(received, stale_pair[turn], turn)
            return parts, fresh, blank(block_shape)[0]

        def late_gather():
            old = late_pair if turn else blank(pair_shape)[0]
            if turn == 0:
                return norm(late_x, turn), old, blank(block_shape)[0]
            result, normed = finish(late_x, received, 1 - turn, 1)
            return normed, old, result

        if crossing:
            late_x = either(
                lambda: blank(block_shape)[0], lambda: finish(late_x, received, 1 - turn, 0)[0]
            )
            blocks_out[layer - 1, 1] = late_x
            late_x = upward(late_x, level - 1, 1)
        payload, pair, result = either(early_scatter, late_gather)
        if turn:
            late_x = blocks_out[layer - 1, 1] = result
        sources[layer, 0] = pair
        got = swap(pair)
        sources[layer, 2] = got
        received = across(payload)
        if layer == sections - 1:
            break

        crossing = turn == 1

        def early_gather():
            if crossing:
                return norm(early_x, 1 - turn), blank(pair_shape)[0], blank(block_shape)[0]
            result, normed = finish(early_x, received, turn, 1)
            return normed, blank(pair_shape)[0], result

        def late_scatter():
            parts, fresh = block(received, got, turn)
            return parts, fresh, blank(block_shape)[0]

        if crossing:
            early_x = either(
                lambda: finish(early_x, received, turn, 0)[0], lambda: blank(block_shape)[0]
            )
            blocks_out[layer, 0] = early_x
            early_x = upward(early_x, level, 0)
        payload, late_pair, result = either(early_gather, late_scatter)
        if not crossing:
            early_x = blocks_out[layer, 0] = result
        sources[layer, 1] = late_pair
        if crossing:
            active = pipe == jnp.where(early, 2 * level + 2, 2 * level + 1)
            received = lax.cond(active, across, lambda _: blank(blocks_shape)[0], payload)
        else:
            received = across(payload)

    def by_plane(values):
        chosen = values[0]
        for level in range(1, planes):
            chosen = jnp.where(plane == level, values[level], chosen)
        return chosen

    last = sections - 1
    first_cache = by_plane(
        [jnp.where(early, sources[2 * m, 0], sources[2 * m + 1, 2]) for m in range(planes)]
    )
    second_cache = by_plane(
        [
            jnp.where(early, sources[2 * m + 1, 2], sources[2 * m + 1, int(m < planes - 1)])
            for m in range(planes)
        ]
    )

    def last_early():
        result = finish(early_x, received, last % 2, 0)[0]
        packed = pl.pallas_call(
            cache_kernel, out_shape=bf16(seq, rows, 4 * channels),
            in_specs=[VMEM] * 2, out_specs=VMEM, compiler_params=params_of(16),
        )(first_cache, second_cache)
        return result, across(packed)

    def last_late():
        parts, _ = block(received, got, last % 2, (first_cache, second_cache))
        parts = across(parts)
        return finish(late_x, parts, last % 2, 0)[0], parts[:, :, width:]

    x, cache = either(last_early, last_late)
    blocks_out[last, 0] = blocks_out[last, 1] = x
    mine = by_plane(
        [jnp.where(early, blocks_out[2 * m, 0], blocks_out[2 * m + 1, 1]) for m in range(planes)]
    )
    theirs = swap(
        by_plane(
            [jnp.where(early, blocks_out[2 * m + 1, 0], blocks_out[2 * m, 1]) for m in range(planes)]
        )
    )
    block_output = jnp.stack([jnp.where(early, mine, theirs), jnp.where(early, theirs, mine)])
    cache = cache.reshape(seq, rows, 2, 2, channels)
    cache = jnp.transpose(cache, (2, 1, 3, 0, 4)).reshape(2, rows, 2, seq * channels)
    return block_output[None], cache[None]


def solution(mesh):
    in_specs = (
        P(None, "seq", None),
        P("pipe", None),
        P("pipe", None),
        P("pipe", None),
        P("pipe", None, None),
        P("pipe", None, None, "seq"),
        P("pipe", "seq", None),
        P("pipe", None, "seq", None, None),
    )
    out_specs = (P("pipe", None, "seq", None), P("pipe", None, "seq", None, None))
    return jax.shard_map(body, mesh=mesh, in_specs=in_specs, out_specs=out_specs, check_vma=False)
```

```python
import functools
import math

import jax
import jax.numpy as jnp
from jax import lax
from jax.experimental import pallas as pl
from jax.experimental.pallas import tpu as pltpu
from jax.sharding import PartitionSpec as P

AXES = ("pipe", "seq")
VMEM = pl.BlockSpec(memory_space=pltpu.VMEM)
ANY = pl.BlockSpec(memory_space=pl.ANY)
HBM = pl.BlockSpec(memory_space=pltpu.HBM)


def ring_order(count):
    fast = 1
    while fast * fast * 4 <= count and count % (fast * 2) == 0:
        fast *= 2
    slow = count // fast
    if fast == 1 or slow % 2:
        return list(range(count))
    cells = [(0, 0)]
    for row in range(slow):
        columns = range(1, fast) if row % 2 == 0 else range(fast - 1, 0, -1)
        cells += [(row, column) for column in columns]
    cells += [(row, 0) for row in range(slow - 1, 0, -1)]
    return [row * fast + column for row, column in cells]


def normalise(values, params_ref):
    centered = values - jnp.mean(values, axis=-1, keepdims=True)
    spread = jnp.mean(centered * centered, axis=-1, keepdims=True)
    return (
        centered * lax.rsqrt(spread + 1e-06) * (1.0 + params_ref[1:2, :]) + params_ref[0:1, :]
    ).astype(jnp.bfloat16)


def spread_block(block, buffer, out_ref, sems):
    width = buffer.shape[1]
    buffer[...] = block
    copies = [
        pltpu.make_async_copy(buffer, out_ref.at[shard, :, :width], sems.at[shard])
        for shard in range(out_ref.shape[0])
    ]
    for copy in copies:
        copy.start()
    return copies


def pack_kernel(x_ref, cache_ref, out_ref, buffer, sems, sides, sem):
    count, _, total = sides.shape
    width = x_ref.shape[1]
    channels = total // 2
    copies = spread_block(x_ref[...], buffer, out_ref, sems)
    for kind in range(2):
        rows = cache_ref[:, kind, :]
        for shard in range(count):
            sides[shard, :, kind * channels : (kind + 1) * channels] = rows[
                :, shard * channels : (shard + 1) * channels
            ]
    copies.append(pltpu.make_async_copy(sides, out_ref.at[:, :, width:], sem))
    copies[-1].start()
    for copy in copies:
        copy.wait()


def attention(head_size, q_ref, kv_ref, far_ref):
    factor = 1.0 / math.sqrt(head_size)
    channels = q_ref.shape[1]
    heads = []
    across = (((1,), (1,)), ((), ()))

    def far_of(kind, start):
        if len(far_ref.shape) == 3:
            return far_ref[kind, :, start : start + head_size]
        return far_ref[:, kind * channels + start : kind * channels + start + head_size]

    for start in range(0, channels, head_size):
        cut = slice(start, start + head_size)
        query = q_ref[:, cut]
        near = lax.dot_general(query, kv_ref[0, :, cut], across, preferred_element_type=jnp.float32)
        far = lax.dot_general(query, far_of(0, start), across, preferred_element_type=jnp.float32)
        near = jnp.exp(near * factor)
        far = jnp.exp(far * factor)
        total = jnp.sum(near, axis=-1, keepdims=True) + jnp.sum(far, axis=-1, keepdims=True)
        near = (near / total).astype(jnp.bfloat16)
        far = (far / total).astype(jnp.bfloat16)
        mixed = jnp.dot(near, kv_ref[1, :, cut], preferred_element_type=jnp.float32)
        mixed = mixed + jnp.dot(far, far_of(1, start), preferred_element_type=jnp.float32)
        heads.append(mixed.astype(jnp.bfloat16))
    return jnp.concatenate(heads, axis=1)


def put_cache(caches, out_ref, offset):
    channels = caches[0].shape[2]
    for patch, cache in enumerate(caches):
        for kind in range(2):
            begin = offset + (2 * patch + kind) * channels
            out_ref[:, begin : begin + channels] = cache[kind]


def cache_kernel(*refs):
    put_cache(refs[:-1], refs[-1], 0)


def block_kernel(
    turn, head_size, planes, normed, whole, params_ref, gain_ref, own_in, other_in, own_out, other_out,
    blocks_ref, far_ref, *refs
):
    caches, refs = refs[:-11], refs[-11:]
    out_ref, kv_ref, blocks, far, w_in, w_out, parts, q_ref, in_sems, sems, part_sems = refs
    width = blocks.shape[1]
    channels = w_out.shape[0]
    pieces = in_sems.shape[1]
    depth = width // pieces
    mine = lax.rem(lax.axis_index("pipe"), 2) == turn

    def weight_copies(source_in, source_out):
        for part in (1, 2, 0):
            for piece in range(pieces):
                cut = pl.ds(piece * depth, depth)
                pltpu.make_async_copy(
                    source_in.at[part, cut], w_in.at[part, cut], in_sems.at[part, piece]
                ).start()
        if not whole:
            pltpu.make_async_copy(source_out.at[0], w_out, sems.at[1]).start()

    fetch = pltpu.make_async_copy(blocks_ref.at[:, :width], blocks, sems.at[0])
    fetch.start()
    if len(far.shape) == 3:
        fetch_far = pltpu.make_async_copy(far_ref, far, sems.at[2])
    else:
        begin = far_ref.shape[1] - far.shape[1]
        fetch_far = pltpu.make_async_copy(far_ref.at[:, begin:], far, sems.at[2])
    fetch_far.start()

    @pl.when(mine)
    def _():
        weight_copies(own_in, own_out)

    @pl.when(jnp.logical_not(mine))
    def _():
        weight_copies(other_in, other_out)

    fetch.wait()
    if normed:
        tokens = blocks[...]
    else:
        tokens = normalise(blocks[...].astype(jnp.float32), params_ref)
    for part in (1, 2, 0):
        for piece in range(pieces):
            cut = pl.ds(piece * depth, depth)
            pltpu.make_async_copy(
                own_in.at[part, cut], w_in.at[part, cut], in_sems.at[part, piece]
            ).wait()
        projected = jnp.dot(tokens, w_in[part], preferred_element_type=jnp.float32)
        if part == 2:
            kv_ref[1] = projected.astype(jnp.bfloat16)
            continue
        for start in range(0, channels, head_size):
            head = projected[:, start : start + head_size]
            square = jnp.mean(head * head, axis=-1, keepdims=True)
            head = (head * lax.rsqrt(square + 1e-06) * gain_ref[part : part + 1, :]).astype(
                jnp.bfloat16
            )
            if part == 0:
                q_ref[:, start : start + head_size] = head
            else:
                kv_ref[0, :, start : start + head_size] = head

    fetch_far.wait()
    if whole:
        out_ref[...] = attention(head_size, q_ref, kv_ref, far)
        return
    sent = []

    def send(begin, size, sem):
        cut = pl.ds(begin, size)
        sent.append(
            pltpu.make_async_copy(parts.at[:, cut], out_ref.at[:, cut], part_sems.at[sem])
        )
        sent[-1].start()

    steps = part_sems.shape[0] - 1
    if caches:
        last = lax.axis_index("pipe") // 2 == planes - 1
        first, second = caches
        put_cache((first, jnp.where(last, kv_ref[...], second[...])), parts, width)
        send(width, 4 * channels, steps)
    attended = attention(head_size, q_ref, kv_ref, far)
    pltpu.make_async_copy(own_out.at[0], w_out, sems.at[1]).wait()
    tile = width // steps
    for step in range(steps):
        cut = slice(step * tile, (step + 1) * tile)
        update = jnp.dot(attended, w_out[:, cut], preferred_element_type=jnp.float32)
        parts[:, cut] = update.astype(jnp.bfloat16)
        send(step * tile, tile, step)
    for copy in sent:
        copy.wait()


def finish_kernel(normed, params_ref, next_ref, x_ref, parts_ref, out_ref, *rest):
    width = x_ref.shape[1]
    update = jnp.sum(parts_ref[:, :, :width].astype(jnp.float32), axis=0)
    result = (x_ref[...].astype(jnp.float32) + params_ref[2:3, :] * update).astype(jnp.bfloat16)
    out_ref[...] = result
    if rest:
        blocks_ref, buffer, sems = rest
        block = normalise(result.astype(jnp.float32), next_ref) if normed else result
        for copy in spread_block(block, buffer, blocks_ref, sems):
            copy.wait()


def whole_kernel(core_ref, order_ref, params_ref, att_ref, own_ref, other_ref, x_ref, out_ref, joined):
    step = pl.program_id(0)
    channels = att_ref.shape[2]

    @pl.when(step == 0)
    def _():
        for shard in range(att_ref.shape[0]):
            joined[:, shard * channels : (shard + 1) * channels] = att_ref[order_ref[shard]]

    def run(weights):
        update = jnp.dot(joined[...], weights, preferred_element_type=jnp.float32)
        out_ref[...] = (x_ref[...].astype(jnp.float32) + params_ref[2:3, :] * update).astype(
            jnp.bfloat16
        )

    first = step < pl.num_programs(0) // 2

    @pl.when(first)
    def _():
        run(own_ref[...])

    @pl.when(jnp.logical_not(first))
    def _():
        run(other_ref[...])


def blank_kernel(*refs):
    pass


def params_of(limit):
    return pltpu.CompilerParams(vmem_limit_bytes=limit << 20)


def body(hidden, mod_shift, mod_scale, mod_gate, norm_gain, input_proj, output_proj, stale_cache):
    sections = lax.axis_size("pipe")
    planes = sections // 2
    seq = lax.axis_size("seq")
    pipe = lax.axis_index("pipe")
    core = lax.rem(pipe, 2)
    plane = pipe // 2
    rows, width = hidden.shape[1:]
    head_size = norm_gain.shape[2]
    channels = input_proj.shape[3]
    tokens = rows * seq
    bf16 = lambda *shape: jax.ShapeDtypeStruct(shape, jnp.bfloat16)

    me = lax.axis_index("seq")
    early = core == 0
    place = lambda row, position: row * seq + position
    lowest, others = range(2), range(2, sections)
    either = lambda on_early, on_late: lax.cond(early, on_early, on_late)

    def swap(value, rows_of=range(sections)):
        pairs = [(place(row, s), place(row ^ 1, s)) for row in rows_of for s in range(seq)]
        return lax.ppermute(value, AXES, pairs)

    def upward(value, by=2, rows_of=range(sections)):
        pairs = [
            (place(row, s), place((row + by * (row in rows_of)) % sections, s))
            for row in range(sections)
            for s in range(seq)
        ]
        return lax.ppermute(value, AXES, pairs)

    ring = ring_order(seq)

    def around(value, step):
        pairs = [
            (place(row, ring[i]), place(row, ring[(i + step) % seq]))
            for row in others
            for i in range(seq)
        ]
        return lax.ppermute(value, AXES, pairs)

    spot = jnp.array([ring.index(s) for s in range(seq)], jnp.int32)
    moves = [-hop for hop in range(seq // 2 + 1)] + list(range(1, seq // 2))
    order = jnp.array(ring, jnp.int32)[
        jnp.remainder(spot[me] + jnp.array(moves, jnp.int32), seq)
    ]

    def across(blocks):
        return lax.all_to_all(blocks, "seq", split_axis=0, concat_axis=0, tiled=True)

    def blank(*shapes):
        return pl.pallas_call(blank_kernel, out_shape=shapes, out_specs=(ANY,) * len(shapes))()

    one_block, all_blocks = bf16(rows, width), bf16(seq, rows, width)
    wide_blocks = bf16(seq, rows, width + 2 * channels)
    pair_shape, side_shape = bf16(2, tokens, channels), bf16(tokens, 2 * channels)
    attended_shape = bf16(tokens, channels)
    spreading = [pltpu.VMEM((rows, width), jnp.bfloat16), pltpu.SemaphoreType.DMA((seq,))]
    flat = lambda blocks: blocks.reshape(tokens, blocks.shape[2])
    apart = lambda values: values.reshape(seq, rows, values.shape[1])

    gains = jnp.pad(norm_gain[0].reshape(1, -1), ((0, 0), (0, width - 2 * head_size)))
    own_params = jnp.concatenate([mod_shift, mod_scale, mod_gate, gains], axis=0)
    own_in = jnp.transpose(input_proj[0], (1, 0, 2))
    own_out = output_proj
    x = lax.dynamic_index_in_dim(hidden, core, 0, keepdims=False)
    packed = pl.pallas_call(
        pack_kernel, out_shape=wide_blocks,
        in_specs=[VMEM] * 2, out_specs=HBM,
        scratch_shapes=spreading + [
            pltpu.VMEM((seq, rows, 2 * channels), jnp.bfloat16), pltpu.SemaphoreType.DMA,
        ],
        compiler_params=params_of(16),
    )(x, stale_cache[0, 1])

    other_params = swap(own_params)
    own_in, own_out, other_params, packed = lax.optimization_barrier(
        (own_in, own_out, other_params, packed)
    )
    raised = upward(own_out, rows_of=range(1, sections, 2))
    other_in = swap(own_in)
    other_out = swap(own_out)
    params = [jnp.where(early == (turn == 0), own_params, other_params) for turn in range(2)]
    gain_rows = [p[3, : 2 * head_size].reshape(2, head_size) for p in params]
    below = upward(params[1])

    def block(blocks, far, turn, normed=False, whole=False, caches=()):
        total = width + 2 * channels * len(caches)
        out, pair = pl.pallas_call(
            functools.partial(block_kernel, turn, head_size, planes, normed, whole),
            out_shape=(attended_shape if whole else bf16(tokens, total), pair_shape),
            in_specs=[VMEM] * 2 + [HBM] * 4 + [ANY] * 2 + [VMEM] * len(caches),
            out_specs=(VMEM if whole else HBM, VMEM),
            scratch_shapes=[
                pltpu.VMEM((tokens, width), jnp.bfloat16),
                pltpu.VMEM((2, tokens, channels) if far.ndim == 3 else side_shape.shape, jnp.bfloat16),
                pltpu.VMEM(own_in.shape, jnp.bfloat16),
                pltpu.VMEM(own_out.shape[1:], jnp.bfloat16),
                pltpu.VMEM((tokens, total), jnp.bfloat16),
                pltpu.VMEM((tokens, channels), jnp.bfloat16),
                pltpu.SemaphoreType.DMA((3, 2)),
                pltpu.SemaphoreType.DMA((3,)),
                pltpu.SemaphoreType.DMA((5,)),
            ],
            compiler_params=params_of(32),
        )(
            params[turn], gain_rows[turn], own_in, other_in, own_out, other_out,
            flat(blocks), far, *caches
        )
        return (out if whole else apart(out)), pair

    def finish(x, parts, turn, onward=False, normed=False):
        shapes = (one_block,) + (all_blocks,) * onward
        out = pl.pallas_call(
            functools.partial(finish_kernel, normed),
            out_shape=shapes, in_specs=[VMEM] * 4, out_specs=(VMEM,) + (HBM,) * onward,
            scratch_shapes=spreading * onward, compiler_params=params_of(16),
        )(params[turn], params[1 - turn], x, parts)
        return (out[0], across(out[1])) if onward else out[0]

    tile = next(t for t in (512, 384, 256, 128) if (width // 2) % t == 0)
    tiles = width // 2 // tile

    def whole(attended, own, other, x):
        side = lambda step, core_ref: jnp.where(step < tiles, core_ref[0], 1 - core_ref[0])
        column = lambda step, core_ref: side(step, core_ref) * tiles + lax.rem(step, tiles)
        result = pl.pallas_call(
            whole_kernel,
            grid_spec=pltpu.PrefetchScalarGridSpec(
                num_scalar_prefetch=2,
                grid=(2 * tiles,),
                in_specs=[
                    pl.BlockSpec((4, tile), lambda i, c, o: (0, column(i, c))),
                    pl.BlockSpec((seq, tokens, channels), lambda i, c, o: (0, 0, 0)),
                    pl.BlockSpec((seq * channels, tile), lambda i, c, o: (0, jnp.minimum(i, tiles - 1))),
                    pl.BlockSpec((seq * channels, tile), lambda i, c, o: (0, jnp.maximum(i - tiles, 0))),
                    pl.BlockSpec((tokens, tile), lambda i, c, o: (0, column(i, c))),
                ],
                out_specs=pl.BlockSpec((tokens, tile), lambda i, c, o: (0, column(i, c))),
                scratch_shapes=[pltpu.VMEM((tokens, seq * channels), jnp.bfloat16)],
            ),
            out_shape=bf16(tokens, width),
            compiler_params=params_of(32),
        )(core.astype(jnp.int32).reshape(1), order, below, attended, own, other, flat(x))
        return apart(result)

    def first_level(raised):
        def early_start():
            received = across(packed)
            parts, pair = block(received, flat(received), 0)
            return parts, pair, blank(wide_blocks)[0], blank(side_shape)[0]

        def late_start():
            received = across(packed)
            return (
                blank(all_blocks)[0], blank(pair_shape)[0], received, flat(received[:, :, width:])
            )

        parts, pair, received, lent = either(early_start, late_start)
        fresh = swap(pair, lowest)
        lent = swap(lent, lowest)
        state = rest_of_level(0, x, parts, received, pair, fresh, lent, lowest)
        return state + tuple(blank(side_shape, side_shape, bf16(seq * channels, width // 2)))

    def other_levels(raised):
        lent = swap(raised, others)
        below_out = jnp.where(early, lent, raised)[0]
        mine = lax.dynamic_slice_in_dim(below_out, core * (width // 2), width // 2, 1)
        right, left = [mine], [mine]
        for hop in range(1, seq // 2 + 1):
            right.append(around(right[-1], 1))
            if hop < seq // 2:
                left.append(around(left[-1], -1))
        gathered = jnp.concatenate(right + left[1:], axis=0)
        side = flat(across(packed[:, :, width:]))
        nothing = blank(one_block, all_blocks, attended_shape, pair_shape, pair_shape, pair_shape)
        return tuple(nothing) + (side, swap(side, others), gathered)

    def rest_of_level(level, x, parts, blocks, pair0, fresh, stale, rows_of):
        normed = level == planes - 1

        def early_middle():
            result, gathered = finish(x, across(parts), 0, True, normed)
            out, pair = block(gathered, stale, 1, normed, not normed)
            return (result, gathered, out, pair) if not normed else (result, out, pair)

        def late_middle():
            parts, pair = block(blocks, fresh, 0)
            result, gathered = finish(x, across(parts), 0, True, normed)
            if normed:
                return result, gathered, pair
            return result, gathered, blank(attended_shape)[0], pair

        if normed:
            result, values, pair = either(early_middle, late_middle)
            return result, values, pair0, pair, swap(pair, rows_of)
        result, gathered, attended, pair = either(early_middle, late_middle)
        got = swap(pair, rows_of)

        def late_end():
            return block(gathered, got, 1, False, True)

        attended, pair1 = either(lambda: (attended, pair), late_end)
        first = pair0, got, pair1
        return (result, gathered, attended) + first

    x1, blocks, attended, pair0, got, pair1, stale, stale_other, gathered = lax.cond(
        plane == 0, first_level, other_levels, raised
    )
    gathered_other = swap(gathered)
    outputs = [x1, None]
    saved = [jnp.where(early, pair0, got), jnp.where(early, got, pair1)]
    for level in range(1, planes):
        here, last = plane == level, level == planes - 1
        attended = upward(attended)
        blocks = upward(blocks)

        def output_below():
            spread = jnp.broadcast_to(attended, (seq,) + attended.shape)
            result = whole(across(spread), gathered, gathered_other, blocks)
            return lax.dynamic_index_in_dim(result, me, 0, keepdims=False), result

        def early_start():
            own, result = output_below()
            parts, pair = block(result, stale, 0)
            return own, parts, pair

        def late_start():
            own, result = output_below()
            return own, result, blank(pair_shape)[0]

        x, values, pair0 = either(early_start, late_start)
        fresh = swap(pair0)
        down = upward(x, -2)
        outputs[1] = down if outputs[1] is None else jnp.where(plane == level - 1, down, outputs[1])
        state = rest_of_level(level, x, values, values, pair0, fresh, stale_other, range(sections))
        if not last:
            result, blocks, attended, pair0, got, pair1 = state
            now = [jnp.where(early, pair0, got), jnp.where(early, got, pair1)]
        else:
            result, values, pair0, pair, got = state
            now = [jnp.where(early, pair0, got), got]
        outputs[0] = jnp.where(here, result, outputs[0])
        saved = [jnp.where(here, new, old) for new, old in zip(now, saved)]

    def last_early():
        out = finish(result, across(values), 1)
        packed = pl.pallas_call(
            cache_kernel, out_shape=bf16(tokens, 4 * channels),
            in_specs=[VMEM] * 2, out_specs=VMEM, compiler_params=params_of(16),
        )(*saved)
        return out, across(apart(packed))

    def last_late():
        parts, _ = block(values, got, 1, True, False, tuple(saved))
        parts = across(parts)
        return finish(result, parts, 1), parts[:, :, width:]

    x, cache = either(last_early, last_late)
    outputs[1] = jnp.where(plane == planes - 1, x, outputs[1])
    mine = jnp.where(early, outputs[0], outputs[1])
    theirs = swap(jnp.where(early, outputs[1], outputs[0]))
    block_output = jnp.stack([jnp.where(early, mine, theirs), jnp.where(early, theirs, mine)])
    cache = cache.reshape(seq, rows, 2, 2, channels)
    cache = jnp.transpose(cache, (2, 1, 3, 0, 4)).reshape(2, rows, 2, seq * channels)
    return block_output[None], cache[None]


def solution(mesh):
    in_specs = (
        P(None, "seq", None),
        P("pipe", None),
        P("pipe", None),
        P("pipe", None),
        P("pipe", None, None),
        P("pipe", None, None, "seq"),
        P("pipe", "seq", None),
        P("pipe", None, "seq", None, None),
    )
    out_specs = (P("pipe", None, "seq", None), P("pipe", None, "seq", None, None))
    return jax.shard_map(body, mesh=mesh, in_specs=in_specs, out_specs=out_specs, check_vma=False)
```

```python
import functools
import math

import jax
import jax.numpy as jnp
from jax import lax
from jax.experimental import pallas as pl
from jax.experimental.pallas import tpu as pltpu
from jax.sharding import PartitionSpec as P

AXES = ("pipe", "seq")
VMEM = pl.BlockSpec(memory_space=pltpu.VMEM)
ANY = pl.BlockSpec(memory_space=pl.ANY)
HBM = pl.BlockSpec(memory_space=pltpu.HBM)


def normalise(values, params_ref):
    centered = values - jnp.mean(values, axis=-1, keepdims=True)
    spread = jnp.mean(centered * centered, axis=-1, keepdims=True)
    return (
        centered * lax.rsqrt(spread + 1e-06) * (1.0 + params_ref[1:2, :]) + params_ref[0:1, :]
    ).astype(jnp.bfloat16)


def spread_block(block, buffer, out_ref, sems):
    width = buffer.shape[1]
    buffer[...] = block
    copies = [
        pltpu.make_async_copy(buffer, out_ref.at[shard, :, :width], sems.at[shard])
        for shard in range(out_ref.shape[0])
    ]
    for copy in copies:
        copy.start()
    return copies


def norm_kernel(params_ref, x_ref, out_ref, buffer, sems):
    block = normalise(x_ref[...].astype(jnp.float32), params_ref)
    for copy in spread_block(block, buffer, out_ref, sems):
        copy.wait()


def pack_kernel(params_ref, x_ref, cache_ref, out_ref, buffer, sems, sides, sem):
    count, _, total = sides.shape
    width = x_ref.shape[1]
    channels = total // 2
    block = normalise(x_ref[...].astype(jnp.float32), params_ref)
    copies = spread_block(block, buffer, out_ref, sems)
    for kind in range(2):
        rows = cache_ref[:, kind, :]
        for shard in range(count):
            sides[shard, :, kind * channels : (kind + 1) * channels] = rows[
                :, shard * channels : (shard + 1) * channels
            ]
    copies.append(pltpu.make_async_copy(sides, out_ref.at[:, :, width:], sem))
    copies[-1].start()
    for copy in copies:
        copy.wait()


def attention(head_size, q_ref, kv_ref, far_ref):
    factor = 1.0 / math.sqrt(head_size)
    channels = q_ref.shape[1]
    heads = []
    across = (((1,), (1,)), ((), ()))

    def far_of(kind, start):
        if len(far_ref.shape) == 3:
            return far_ref[kind, :, start : start + head_size]
        return far_ref[:, kind * channels + start : kind * channels + start + head_size]

    for start in range(0, channels, head_size):
        cut = slice(start, start + head_size)
        query = q_ref[:, cut]
        near = lax.dot_general(query, kv_ref[0, :, cut], across, preferred_element_type=jnp.float32)
        far = lax.dot_general(query, far_of(0, start), across, preferred_element_type=jnp.float32)
        near = jnp.exp(near * factor)
        far = jnp.exp(far * factor)
        total = jnp.sum(near, axis=-1, keepdims=True) + jnp.sum(far, axis=-1, keepdims=True)
        near = (near / total).astype(jnp.bfloat16)
        far = (far / total).astype(jnp.bfloat16)
        mixed = jnp.dot(near, kv_ref[1, :, cut], preferred_element_type=jnp.float32)
        mixed = mixed + jnp.dot(far, far_of(1, start), preferred_element_type=jnp.float32)
        heads.append(mixed.astype(jnp.bfloat16))
    return jnp.concatenate(heads, axis=1)


def put_cache(caches, out_ref, offset):
    channels = caches[0].shape[2]
    for patch, cache in enumerate(caches):
        for kind in range(2):
            begin = offset + (2 * patch + kind) * channels
            out_ref[:, begin : begin + channels] = cache[kind]


def cache_kernel(*refs):
    put_cache(refs[:-1], refs[-1], 0)


def block_kernel(
    turn, head_size, planes, gain_ref, own_in, other_in, own_out, other_out, blocks_ref, far_ref, *refs
):
    caches, refs = refs[:-11], refs[-11:]
    out_ref, kv_ref, blocks, far, w_in, w_out, parts, q_ref, in_sems, sems, part_sems = refs
    width = blocks.shape[1]
    channels = w_out.shape[0]
    pieces = in_sems.shape[1]
    depth = width // pieces
    mine = lax.rem(lax.axis_index("pipe"), 2) == turn

    def weight_copies(source_in, source_out):
        for part in (1, 2, 0):
            for piece in range(pieces):
                cut = pl.ds(piece * depth, depth)
                pltpu.make_async_copy(
                    source_in.at[part, cut], w_in.at[part, cut], in_sems.at[part, piece]
                ).start()
        pltpu.make_async_copy(source_out.at[0], w_out, sems.at[1]).start()

    fetch = pltpu.make_async_copy(blocks_ref.at[:, :width], blocks, sems.at[0])
    fetch.start()
    if len(far.shape) == 3:
        fetch_far = pltpu.make_async_copy(far_ref, far, sems.at[2])
    else:
        begin = far_ref.shape[1] - far.shape[1]
        fetch_far = pltpu.make_async_copy(far_ref.at[:, begin:], far, sems.at[2])
    fetch_far.start()

    @pl.when(mine)
    def _():
        weight_copies(own_in, own_out)

    @pl.when(jnp.logical_not(mine))
    def _():
        weight_copies(other_in, other_out)

    fetch.wait()
    tokens = blocks[...]
    for part in (1, 2, 0):
        for piece in range(pieces):
            cut = pl.ds(piece * depth, depth)
            pltpu.make_async_copy(
                own_in.at[part, cut], w_in.at[part, cut], in_sems.at[part, piece]
            ).wait()
        projected = jnp.dot(tokens, w_in[part], preferred_element_type=jnp.float32)
        if part == 2:
            kv_ref[1] = projected.astype(jnp.bfloat16)
            continue
        for start in range(0, channels, head_size):
            head = projected[:, start : start + head_size]
            square = jnp.mean(head * head, axis=-1, keepdims=True)
            head = (head * lax.rsqrt(square + 1e-06) * gain_ref[part : part + 1, :]).astype(
                jnp.bfloat16
            )
            if part == 0:
                q_ref[:, start : start + head_size] = head
            else:
                kv_ref[0, :, start : start + head_size] = head

    fetch_far.wait()
    sent = []

    def send(begin, size, sem):
        cut = pl.ds(begin, size)
        sent.append(
            pltpu.make_async_copy(parts.at[:, cut], out_ref.at[:, cut], part_sems.at[sem])
        )
        sent[-1].start()

    steps = part_sems.shape[0] - 1
    if caches:
        last = lax.axis_index("pipe") // 2 == planes - 1
        first, second = caches
        put_cache((first, jnp.where(last, kv_ref[...], second[...])), parts, width)
        send(width, 4 * channels, steps)
    attended = attention(head_size, q_ref, kv_ref, far)
    pltpu.make_async_copy(own_out.at[0], w_out, sems.at[1]).wait()
    tile = width // steps
    for step in range(steps):
        cut = slice(step * tile, (step + 1) * tile)
        update = jnp.dot(attended, w_out[:, cut], preferred_element_type=jnp.float32)
        parts[:, cut] = update.astype(jnp.bfloat16)
        send(step * tile, tile, step)
    for copy in sent:
        copy.wait()


def finish_kernel(params_ref, next_ref, x_ref, parts_ref, out_ref, *rest):
    width = x_ref.shape[1]
    update = jnp.sum(parts_ref[:, :, :width].astype(jnp.float32), axis=0)
    result = (x_ref[...].astype(jnp.float32) + params_ref[2:3, :] * update).astype(jnp.bfloat16)
    out_ref[...] = result
    if rest:
        blocks_ref, buffer, sems = rest
        block = normalise(result.astype(jnp.float32), next_ref)
        for copy in spread_block(block, buffer, blocks_ref, sems):
            copy.wait()


def blank_kernel(*refs):
    pass


def params_of(limit):
    return pltpu.CompilerParams(vmem_limit_bytes=limit << 20)


def body(hidden, mod_shift, mod_scale, mod_gate, norm_gain, input_proj, output_proj, stale_cache):
    sections = lax.axis_size("pipe")
    planes = sections // 2
    seq = lax.axis_size("seq")
    pipe = lax.axis_index("pipe")
    core = lax.rem(pipe, 2)
    plane = pipe // 2
    rows, width = hidden.shape[1:]
    head_size = norm_gain.shape[2]
    channels = input_proj.shape[3]
    tokens = rows * seq
    bf16 = lambda *shape: jax.ShapeDtypeStruct(shape, jnp.bfloat16)

    place = lambda row, position: row * seq + position

    def swap(value):
        pairs = [(place(row, s), place(row ^ 1, s)) for row in range(sections) for s in range(seq)]
        return lax.ppermute(value, AXES, pairs)

    def upward(value, level, side):
        row = 2 * level + side
        return lax.ppermute(value, AXES, [(place(row, s), place(row + 2, s)) for s in range(seq)])

    def across(blocks):
        return lax.all_to_all(blocks, "seq", split_axis=0, concat_axis=0, tiled=True)

    def blank(*shapes):
        return pl.pallas_call(blank_kernel, out_shape=shapes, out_specs=(ANY,) * len(shapes))()

    gains = jnp.pad(norm_gain[0].reshape(1, -1), ((0, 0), (0, width - 2 * head_size)))
    own_params = jnp.concatenate([mod_shift, mod_scale, mod_gate, gains], axis=0)
    own_in = jnp.transpose(input_proj[0], (1, 0, 2))
    own_out = output_proj
    x = lax.dynamic_index_in_dim(hidden, core, 0, keepdims=False)
    spreading = [pltpu.VMEM((rows, width), jnp.bfloat16), pltpu.SemaphoreType.DMA((seq,))]
    packed = pl.pallas_call(
        pack_kernel, out_shape=bf16(seq, rows, width + 2 * channels),
        in_specs=[VMEM] * 3, out_specs=HBM,
        scratch_shapes=spreading + [
            pltpu.VMEM((seq, rows, 2 * channels), jnp.bfloat16), pltpu.SemaphoreType.DMA,
        ],
        compiler_params=params_of(16),
    )(own_params, x, stale_cache[0, 1])

    other_params = swap(own_params)
    own_in, own_out, other_params, packed = lax.optimization_barrier(
        (own_in, own_out, other_params, packed)
    )
    other_in = swap(own_in)
    other_out = swap(own_out)
    params = [jnp.where(core == turn, own_params, other_params) for turn in range(2)]
    gain_rows = [p[3, : 2 * head_size].reshape(2, head_size) for p in params]
    blocks_shape = bf16(seq, rows, width)

    def norm(x, turn):
        return pl.pallas_call(
            norm_kernel, out_shape=blocks_shape, in_specs=[VMEM] * 2, out_specs=HBM,
            scratch_shapes=spreading, compiler_params=params_of(16),
        )(params[turn], x)

    flat = lambda blocks: blocks.reshape(tokens, blocks.shape[2])
    apart = lambda values: values.reshape(seq, rows, values.shape[1])

    def block(blocks, far, turn, caches=()):
        total = width + 2 * channels * len(caches)
        side = (2, tokens, channels) if far.ndim == 3 else (tokens, 2 * channels)
        out, pair = pl.pallas_call(
            functools.partial(block_kernel, turn, head_size, planes),
            out_shape=(bf16(tokens, total), bf16(2, tokens, channels)),
            in_specs=[VMEM] + [HBM] * 4 + [ANY] * 2 + [VMEM] * len(caches),
            out_specs=(HBM, VMEM),
            scratch_shapes=[
                pltpu.VMEM((tokens, width), jnp.bfloat16),
                pltpu.VMEM(side, jnp.bfloat16),
                pltpu.VMEM(own_in.shape, jnp.bfloat16),
                pltpu.VMEM(own_out.shape[1:], jnp.bfloat16),
                pltpu.VMEM((tokens, total), jnp.bfloat16),
                pltpu.VMEM((tokens, channels), jnp.bfloat16),
                pltpu.SemaphoreType.DMA((3, 2)),
                pltpu.SemaphoreType.DMA((3,)),
                pltpu.SemaphoreType.DMA((5,)),
            ],
            compiler_params=params_of(32),
        )(
            gain_rows[turn], own_in, other_in, own_out, other_out, flat(blocks), far, *caches
        )
        return apart(out), pair

    def finish(x, parts, turn, onward):
        shapes = (bf16(rows, width),) + (blocks_shape,) * onward
        return pl.pallas_call(
            finish_kernel, out_shape=shapes, in_specs=[VMEM] * 4,
            out_specs=(VMEM,) + (HBM,) * onward,
            scratch_shapes=spreading * onward, compiler_params=params_of(16),
        )(params[turn], params[1 - turn], x, parts)

    early = core == 0
    either = lambda on_early, on_late: lax.cond(early, on_early, on_late)

    def first_early():
        return across(packed), blank(bf16(tokens, 2 * channels))[0]

    def first_late():
        return blank(bf16(*packed.shape))[0], flat(across(packed[:, :, width:]))

    received, stale = either(first_early, first_late)
    stales = [flat(received), swap(stale)]
    pair_shape, block_shape = bf16(2, tokens, channels), bf16(rows, width)
    late_pair = None
    early_x, late_x = x, x
    blocks_out, sources = {}, {}
    for layer in range(sections):
        turn, level = layer % 2, layer // 2
        crossing = layer > 0 and turn == 0

        def early_scatter():
            parts, fresh = block(received, stales[turn], turn)
            return parts, fresh, blank(block_shape)[0]

        def late_gather():
            old = late_pair if turn else blank(pair_shape)[0]
            if turn == 0:
                return norm(late_x, turn), old, blank(block_shape)[0]
            result, normed = finish(late_x, received, 1 - turn, 1)
            return normed, old, result

        if crossing:
            late_x = either(
                lambda: blank(block_shape)[0], lambda: finish(late_x, received, 1 - turn, 0)[0]
            )
            blocks_out[layer - 1, 1] = late_x
            late_x = upward(late_x, level - 1, 1)
        payload, pair, result = either(early_scatter, late_gather)
        if turn:
            late_x = blocks_out[layer - 1, 1] = result
        sources[layer, 0] = pair
        got = swap(pair)
        sources[layer, 2] = got
        received = across(payload)
        if layer == sections - 1:
            break

        crossing = turn == 1

        def early_gather():
            if crossing:
                return norm(early_x, 1 - turn), blank(pair_shape)[0], blank(block_shape)[0]
            result, normed = finish(early_x, received, turn, 1)
            return normed, blank(pair_shape)[0], result

        def late_scatter():
            parts, fresh = block(received, got, turn)
            return parts, fresh, blank(block_shape)[0]

        if crossing:
            early_x = either(
                lambda: finish(early_x, received, turn, 0)[0], lambda: blank(block_shape)[0]
            )
            blocks_out[layer, 0] = early_x
            early_x = upward(early_x, level, 0)
        payload, late_pair, result = either(early_gather, late_scatter)
        if not crossing:
            early_x = blocks_out[layer, 0] = result
        sources[layer, 1] = late_pair
        if crossing:
            active = pipe == jnp.where(early, 2 * level + 2, 2 * level + 1)
            received = lax.cond(active, across, lambda _: blank(blocks_shape)[0], payload)
        else:
            received = across(payload)

    def by_plane(values):
        chosen = values[0]
        for level in range(1, planes):
            chosen = jnp.where(plane == level, values[level], chosen)
        return chosen

    last = sections - 1
    first_cache = by_plane(
        [jnp.where(early, sources[2 * m, 0], sources[2 * m + 1, 2]) for m in range(planes)]
    )
    second_cache = by_plane(
        [
            jnp.where(early, sources[2 * m + 1, 2], sources[2 * m + 1, int(m < planes - 1)])
            for m in range(planes)
        ]
    )

    def last_early():
        result = finish(early_x, received, last % 2, 0)[0]
        packed = pl.pallas_call(
            cache_kernel, out_shape=bf16(tokens, 4 * channels),
            in_specs=[VMEM] * 2, out_specs=VMEM, compiler_params=params_of(16),
        )(first_cache, second_cache)
        return result, across(apart(packed))

    def last_late():
        parts, _ = block(received, got, last % 2, (first_cache, second_cache))
        parts = across(parts)
        return finish(late_x, parts, last % 2, 0)[0], parts[:, :, width:]

    x, cache = either(last_early, last_late)
    blocks_out[last, 0] = blocks_out[last, 1] = x
    mine = by_plane(
        [jnp.where(early, blocks_out[2 * m, 0], blocks_out[2 * m + 1, 1]) for m in range(planes)]
    )
    theirs = swap(
        by_plane(
            [jnp.where(early, blocks_out[2 * m + 1, 0], blocks_out[2 * m, 1]) for m in range(planes)]
        )
    )
    block_output = jnp.stack([jnp.where(early, mine, theirs), jnp.where(early, theirs, mine)])
    cache = cache.reshape(seq, rows, 2, 2, channels)
    cache = jnp.transpose(cache, (2, 1, 3, 0, 4)).reshape(2, rows, 2, seq * channels)
    return block_output[None], cache[None]


def solution(mesh):
    in_specs = (
        P(None, "seq", None),
        P("pipe", None),
        P("pipe", None),
        P("pipe", None),
        P("pipe", None, None),
        P("pipe", None, None, "seq"),
        P("pipe", "seq", None),
        P("pipe", None, "seq", None, None),
    )
    out_specs = (P("pipe", None, "seq", None), P("pipe", None, "seq", None, None))
    return jax.shard_map(body, mesh=mesh, in_specs=in_specs, out_specs=out_specs, check_vma=False)
```

```python
import functools
import math

import jax
import jax.numpy as jnp
from jax import lax
from jax.experimental import pallas as pl
from jax.experimental.pallas import tpu as pltpu
from jax.sharding import PartitionSpec as P

AXES = ("pipe", "seq")
VMEM = pl.BlockSpec(memory_space=pltpu.VMEM)
ANY = pl.BlockSpec(memory_space=pl.ANY)
HBM = pl.BlockSpec(memory_space=pltpu.HBM)


def ring_order(count):
    fast = 1
    while fast * fast * 4 <= count and count % (fast * 2) == 0:
        fast *= 2
    slow = count // fast
    if fast == 1 or slow % 2:
        return list(range(count))
    cells = [(0, 0)]
    for row in range(slow):
        columns = range(1, fast) if row % 2 == 0 else range(fast - 1, 0, -1)
        cells += [(row, column) for column in columns]
    cells += [(row, 0) for row in range(slow - 1, 0, -1)]
    return [row * fast + column for row, column in cells]


def normalise(values, params_ref):
    centered = values - jnp.mean(values, axis=-1, keepdims=True)
    spread = jnp.mean(centered * centered, axis=-1, keepdims=True)
    return (
        centered * lax.rsqrt(spread + 1e-06) * (1.0 + params_ref[1:2, :]) + params_ref[0:1, :]
    ).astype(jnp.bfloat16)


def spread_block(block, buffer, out_ref, sems):
    width = buffer.shape[1]
    buffer[...] = block
    copies = [
        pltpu.make_async_copy(buffer, out_ref.at[shard, :, :width], sems.at[shard])
        for shard in range(out_ref.shape[0])
    ]
    for copy in copies:
        copy.start()
    return copies


def norm_kernel(params_ref, x_ref, out_ref, buffer, sems):
    block = normalise(x_ref[...].astype(jnp.float32), params_ref)
    for copy in spread_block(block, buffer, out_ref, sems):
        copy.wait()


def pack_kernel(params_ref, x_ref, cache_ref, out_ref, buffer, sems, sides, sem):
    count, _, total = sides.shape
    width = x_ref.shape[1]
    channels = total // 2
    block = normalise(x_ref[...].astype(jnp.float32), params_ref)
    copies = spread_block(block, buffer, out_ref, sems)
    for kind in range(2):
        rows = cache_ref[:, kind, :]
        for shard in range(count):
            sides[shard, :, kind * channels : (kind + 1) * channels] = rows[
                :, shard * channels : (shard + 1) * channels
            ]
    copies.append(pltpu.make_async_copy(sides, out_ref.at[:, :, width:], sem))
    copies[-1].start()
    for copy in copies:
        copy.wait()


def attention(head_size, q_ref, kv_ref, far_ref):
    factor = 1.0 / math.sqrt(head_size)
    channels = q_ref.shape[1]
    heads = []
    across = (((1,), (1,)), ((), ()))

    def far_of(kind, start):
        if len(far_ref.shape) == 3:
            return far_ref[kind, :, start : start + head_size]
        return far_ref[:, kind * channels + start : kind * channels + start + head_size]

    for start in range(0, channels, head_size):
        cut = slice(start, start + head_size)
        query = q_ref[:, cut]
        near = lax.dot_general(query, kv_ref[0, :, cut], across, preferred_element_type=jnp.float32)
        far = lax.dot_general(query, far_of(0, start), across, preferred_element_type=jnp.float32)
        near = jnp.exp(near * factor)
        far = jnp.exp(far * factor)
        total = jnp.sum(near, axis=-1, keepdims=True) + jnp.sum(far, axis=-1, keepdims=True)
        near = (near / total).astype(jnp.bfloat16)
        far = (far / total).astype(jnp.bfloat16)
        mixed = jnp.dot(near, kv_ref[1, :, cut], preferred_element_type=jnp.float32)
        mixed = mixed + jnp.dot(far, far_of(1, start), preferred_element_type=jnp.float32)
        heads.append(mixed.astype(jnp.bfloat16))
    return jnp.concatenate(heads, axis=1)


def block_kernel(
    turn, head_size, only, gain_ref, own_in, other_in, own_out, other_out, blocks_ref, far_ref, *refs
):
    caches, refs = refs[:-11], refs[-11:]
    out_ref, kv_ref, blocks, far, w_in, w_out, parts, q_ref, in_sems, sems, part_sems = refs
    width = blocks.shape[1]
    channels = w_out.shape[0]
    pieces = in_sems.shape[1]
    depth = width // pieces
    mine = lax.rem(lax.axis_index("pipe"), 2) == turn

    def weight_copies(source_in, source_out):
        for part in (1, 2, 0):
            for piece in range(pieces):
                cut = pl.ds(piece * depth, depth)
                pltpu.make_async_copy(
                    source_in.at[part, cut], w_in.at[part, cut], in_sems.at[part, piece]
                ).start()
        if not only:
            pltpu.make_async_copy(source_out.at[0], w_out, sems.at[1]).start()

    fetch = pltpu.make_async_copy(blocks_ref.at[:, :width], blocks, sems.at[0])
    fetch.start()
    if len(far.shape) == 3:
        fetch_far = pltpu.make_async_copy(far_ref, far, sems.at[2])
    else:
        begin = far_ref.shape[1] - far.shape[1]
        fetch_far = pltpu.make_async_copy(far_ref.at[:, begin:], far, sems.at[2])
    fetch_far.start()

    @pl.when(mine)
    def _():
        weight_copies(own_in, own_out)

    @pl.when(jnp.logical_not(mine))
    def _():
        weight_copies(other_in, other_out)

    fetch.wait()
    tokens = blocks[...]
    for part in (1, 2, 0):
        for piece in range(pieces):
            cut = pl.ds(piece * depth, depth)
            pltpu.make_async_copy(
                own_in.at[part, cut], w_in.at[part, cut], in_sems.at[part, piece]
            ).wait()
        projected = jnp.dot(tokens, w_in[part], preferred_element_type=jnp.float32)
        if part == 2:
            kv_ref[1] = projected.astype(jnp.bfloat16)
            continue
        for start in range(0, channels, head_size):
            head = projected[:, start : start + head_size]
            square = jnp.mean(head * head, axis=-1, keepdims=True)
            head = (head * lax.rsqrt(square + 1e-06) * gain_ref[part : part + 1, :]).astype(
                jnp.bfloat16
            )
            if part == 0:
                q_ref[:, start : start + head_size] = head
            else:
                kv_ref[0, :, start : start + head_size] = head

    fetch_far.wait()
    if only:
        out_ref[:, :channels] = attention(head_size, q_ref, kv_ref, far)
        for patch, cache in enumerate(caches):
            for kind in range(2):
                begin = (1 + 2 * patch + kind) * channels
                out_ref[:, begin : begin + channels] = cache[kind]
        return
    sent = []

    def send(begin, size, sem):
        cut = pl.ds(begin, size)
        sent.append(
            pltpu.make_async_copy(parts.at[:, cut], out_ref.at[:, cut], part_sems.at[sem])
        )
        sent[-1].start()

    steps = part_sems.shape[0]
    attended = attention(head_size, q_ref, kv_ref, far)
    pltpu.make_async_copy(own_out.at[0], w_out, sems.at[1]).wait()
    tile = width // steps
    for step in range(steps):
        cut = slice(step * tile, (step + 1) * tile)
        update = jnp.dot(attended, w_out[:, cut], preferred_element_type=jnp.float32)
        parts[:, cut] = update.astype(jnp.bfloat16)
        send(step * tile, tile, step)
    for copy in sent:
        copy.wait()


def finish_kernel(params_ref, next_ref, x_ref, parts_ref, out_ref, *rest):
    width = x_ref.shape[1]
    update = jnp.sum(parts_ref[:, :, :width].astype(jnp.float32), axis=0)
    result = (x_ref[...].astype(jnp.float32) + params_ref[2:3, :] * update).astype(jnp.bfloat16)
    out_ref[...] = result
    if rest:
        blocks_ref, buffer, sems = rest
        block = normalise(result.astype(jnp.float32), next_ref)
        for copy in spread_block(block, buffer, blocks_ref, sems):
            copy.wait()


def output_kernel(
    order_ref, params_ref, next_ref, x_ref, att_ref, weights_ref, out_ref, blocks_ref, joined, total, buffer, sems
):
    step, steps = pl.program_id(0), pl.num_programs(0)
    channels = joined.shape[1] // att_ref.shape[0]
    tile = weights_ref.shape[1]

    @pl.when(step == 0)
    def _():
        for shard in range(att_ref.shape[0]):
            joined[:, shard * channels : (shard + 1) * channels] = att_ref[
                order_ref[shard], :, :channels
            ]

    total[step] = jnp.dot(joined[...], weights_ref[...], preferred_element_type=jnp.float32)

    @pl.when(step == steps - 1)
    def _():
        for part in range(total.shape[0]):
            cut = slice(part * tile, (part + 1) * tile)
            out_ref[:, cut] = (
                x_ref[:, cut].astype(jnp.float32) + params_ref[2:3, cut] * total[part]
            ).astype(jnp.bfloat16)
        block = normalise(out_ref[...].astype(jnp.float32), next_ref)
        for copy in spread_block(block, buffer, blocks_ref, sems):
            copy.wait()


def blank_kernel(*refs):
    pass


def params_of(limit):
    return pltpu.CompilerParams(vmem_limit_bytes=limit << 20)


def body(hidden, mod_shift, mod_scale, mod_gate, norm_gain, input_proj, output_proj, stale_cache):
    sections = lax.axis_size("pipe")
    planes = sections // 2
    seq = lax.axis_size("seq")
    pipe = lax.axis_index("pipe")
    core = lax.rem(pipe, 2)
    plane = pipe // 2
    rows, width = hidden.shape[1:]
    head_size = norm_gain.shape[2]
    channels = input_proj.shape[3]
    tokens = rows * seq
    bf16 = lambda *shape: jax.ShapeDtypeStruct(shape, jnp.bfloat16)

    place = lambda row, position: row * seq + position

    lowest, others = range(2), range(2, sections)

    def swap(value, rows_of=range(sections)):
        pairs = [(place(row, s), place(row ^ 1, s)) for row in rows_of for s in range(seq)]
        return lax.ppermute(value, AXES, pairs)

    def upward(value):
        pairs = [
            (place(row, s), place((row + 2) % sections, s))
            for row in range(sections)
            for s in range(seq)
        ]
        return lax.ppermute(value, AXES, pairs)

    ring = ring_order(seq)

    def around(value, step):
        pairs = [
            (place(row, ring[i]), place(row, ring[(i + step) % seq]))
            for row in others
            for i in range(seq)
        ]
        return lax.ppermute(value, AXES, pairs)

    spot = jnp.array([ring.index(s) for s in range(seq)], jnp.int32)
    half = seq // 2
    moves = [-hop for hop in range(half)] + list(range(1, half)) + [half]
    order = jnp.array(ring, jnp.int32)[
        jnp.remainder(spot[lax.axis_index("seq")] + jnp.array(moves, jnp.int32), seq)
    ]

    def across(blocks):
        return lax.all_to_all(blocks, "seq", split_axis=0, concat_axis=0, tiled=True)

    def blank(*shapes):
        return pl.pallas_call(blank_kernel, out_shape=shapes, out_specs=(ANY,) * len(shapes))()

    gains = jnp.pad(norm_gain[0].reshape(1, -1), ((0, 0), (0, width - 2 * head_size)))
    own_params = jnp.concatenate([mod_shift, mod_scale, mod_gate, gains], axis=0)
    own_in = jnp.transpose(input_proj[0], (1, 0, 2))
    own_out = output_proj
    x = lax.dynamic_index_in_dim(hidden, core, 0, keepdims=False)
    spreading = [pltpu.VMEM((rows, width), jnp.bfloat16), pltpu.SemaphoreType.DMA((seq,))]
    packed = pl.pallas_call(
        pack_kernel, out_shape=bf16(seq, rows, width + 2 * channels),
        in_specs=[VMEM] * 3, out_specs=HBM,
        scratch_shapes=spreading + [
            pltpu.VMEM((seq, rows, 2 * channels), jnp.bfloat16), pltpu.SemaphoreType.DMA,
        ],
        compiler_params=params_of(16),
    )(own_params, x, stale_cache[0, 1])

    other_params = swap(own_params)
    own_in, own_out, other_params, packed = lax.optimization_barrier(
        (own_in, own_out, other_params, packed)
    )
    other_in = swap(own_in)
    other_out = swap(own_out)
    params = [jnp.where(core == turn, own_params, other_params) for turn in range(2)]
    gain_rows = [p[3, : 2 * head_size].reshape(2, head_size) for p in params]
    blocks_shape = bf16(seq, rows, width)

    def norm(x, turn):
        return pl.pallas_call(
            norm_kernel, out_shape=blocks_shape, in_specs=[VMEM] * 2, out_specs=HBM,
            scratch_shapes=spreading, compiler_params=params_of(16),
        )(params[turn], x)

    flat = lambda blocks: blocks.reshape(tokens, blocks.shape[2])
    apart = lambda values: values.reshape(seq, rows, values.shape[1])

    def block(blocks, far, turn, only=False, caches=()):
        total = channels * (1 + 2 * len(caches)) if only else width
        side = (2, tokens, channels) if far.ndim == 3 else (tokens, 2 * channels)
        out, pair = pl.pallas_call(
            functools.partial(block_kernel, turn, head_size, only),
            out_shape=(bf16(tokens, total), pair_shape),
            in_specs=[VMEM] + [HBM] * 4 + [ANY] * 2 + [VMEM] * len(caches),
            out_specs=(VMEM if only else HBM, VMEM),
            scratch_shapes=[
                pltpu.VMEM((tokens, width), jnp.bfloat16),
                pltpu.VMEM(side, jnp.bfloat16),
                pltpu.VMEM(own_in.shape, jnp.bfloat16),
                pltpu.VMEM(own_out.shape[1:], jnp.bfloat16),
                pltpu.VMEM((tokens, width), jnp.bfloat16),
                pltpu.VMEM((tokens, channels), jnp.bfloat16),
                pltpu.SemaphoreType.DMA((3, 2)),
                pltpu.SemaphoreType.DMA((3,)),
                pltpu.SemaphoreType.DMA((4,)),
            ],
            compiler_params=params_of(32),
        )(
            gain_rows[turn], own_in, other_in, own_out, other_out, flat(blocks), far, *caches
        )
        return apart(out), pair

    tile = next(t for t in (512, 384, 256, 128) if width % t == 0)

    def output(x, attended, weights, turn):
        return pl.pallas_call(
            output_kernel,
            grid_spec=pltpu.PrefetchScalarGridSpec(
                num_scalar_prefetch=1,
                grid=(width // tile,),
                in_specs=[
                    pl.BlockSpec((4, width), lambda i, o: (0, 0)),
                    pl.BlockSpec((4, width), lambda i, o: (0, 0)),
                    pl.BlockSpec((rows, width), lambda i, o: (0, 0)),
                    pl.BlockSpec(attended.shape, lambda i, o: (0, 0, 0)),
                    pl.BlockSpec((seq * channels, tile), lambda i, o: (0, i)),
                ],
                out_specs=(pl.BlockSpec((rows, width), lambda i, o: (0, 0)), HBM),
                scratch_shapes=[
                    pltpu.VMEM((rows, seq * channels), jnp.bfloat16),
                    pltpu.VMEM((width // tile, rows, tile), jnp.float32),
                ] + spreading,
            ),
            out_shape=(bf16(rows, width), blocks_shape),
            compiler_params=params_of(32),
        )(order, params[turn], params[1 - turn], x, attended, weights)

    def finish(x, parts, turn, onward):
        shapes = (bf16(rows, width),) + (blocks_shape,) * onward
        return pl.pallas_call(
            finish_kernel, out_shape=shapes, in_specs=[VMEM] * 4,
            out_specs=(VMEM,) + (HBM,) * onward,
            scratch_shapes=spreading * onward, compiler_params=params_of(16),
        )(params[turn], params[1 - turn], x, parts)

    early = core == 0
    either = lambda on_early, on_late: lax.cond(early, on_early, on_late)

    pair_shape, block_shape = bf16(2, tokens, channels), bf16(rows, width)
    side_shape = bf16(tokens, 2 * channels)
    att_shape = bf16(seq, rows, channels)
    nothing = lambda shape: blank(shape)[0]

    def first_plane():
        def start_early():
            received = across(packed)
            parts, fresh = block(received, flat(received), 0)
            return parts, fresh, nothing(side_shape)

        def start_late():
            side = flat(across(packed[:, :, width:]))
            return norm(x, 0), nothing(pair_shape), side

        payload, pair0, side = either(start_early, start_late)
        fresh = swap(pair0, lowest)
        received = across(payload)
        side = swap(side, lowest)

        def gather_early():
            result, normed = finish(x, received, 0, 1)
            return normed, nothing(pair_shape), result

        def scatter_late():
            parts, own = block(received, fresh, 0)
            return parts, own, nothing(block_shape)

        payload, late_pair, early_x = either(gather_early, scatter_late)
        received = across(payload)

        def scatter_early():
            parts, fresh = block(received, side, 1)
            return parts, fresh, nothing(block_shape)

        def gather_late():
            result, normed = finish(x, received, 0, 1)
            return normed, late_pair, result

        payload, pair, late_x = either(scatter_early, gather_late)
        got = swap(pair, lowest)
        received = across(payload)

        def end_early():
            return finish(early_x, received, 1, 0)[0], nothing(pair_shape)

        def end_late():
            parts, own = block(received, got, 1)
            return finish(late_x, across(parts), 1, 0)[0], own

        moved, pair1 = either(end_early, end_late)
        return (
            jnp.where(early, early_x, late_x), moved, pair0, got, pair1,
            nothing(side_shape), nothing(side_shape), nothing(bf16(seq * channels, width)),
        )

    def other_planes():
        mine = own_out[0]
        right, left = [mine], [mine]
        for hop in range(1, half):
            right.append(around(right[-1], 1))
            left.append(around(left[-1], -1))
        cut = mine.shape[0] // 2
        far_side = [around(right[-1][:cut], 1), around(left[-1][cut:], -1)]
        gathered = jnp.concatenate(right + left[1:] + far_side, axis=0)
        side = flat(across(packed[:, :, width:]))
        return (
            nothing(block_shape), nothing(block_shape), nothing(pair_shape), nothing(pair_shape),
            nothing(pair_shape), side, swap(side, others), gathered,
        )

    first_out, moved, pair0, got, pair1, side, other_side, gathered = lax.cond(
        plane == 0, first_plane, other_planes
    )
    gathered_other = swap(gathered)
    first_outs, second_outs = [first_out], [moved]
    firsts = [jnp.where(early, pair0, got)]
    seconds = [jnp.where(early, got, pair1)]
    for level in range(1, planes):
        final = level == planes - 1
        x = upward(moved)
        received = either(lambda: across(norm(x, 0)), lambda: nothing(blocks_shape))

        def attend_early():
            attended, fresh = block(received, side, 0, True)
            return across(attended), nothing(blocks_shape), fresh

        def gather_late():
            return nothing(att_shape), across(norm(x, 0)), nothing(pair_shape)

        attended, received, pair0 = either(attend_early, gather_late)
        fresh = swap(pair0)

        def next_early():
            result, normed = output(x, attended, gathered, 0)
            return nothing(att_shape), across(normed), nothing(pair_shape), result

        def attend_late():
            attended, own = block(received, fresh, 0, True)
            return across(attended), nothing(blocks_shape), own, nothing(block_shape)

        attended, received, late_pair, early_x = either(next_early, attend_late)

        def attend_again():
            attended, fresh = block(received, other_side, 1, True)
            return across(attended), nothing(blocks_shape), fresh, nothing(block_shape)

        def next_late():
            result, normed = output(x, attended, gathered_other, 0)
            return nothing(att_shape), across(normed), late_pair, result

        attended, received, pair, late_x = either(attend_again, next_late)
        got = swap(pair)
        first_outs.append(jnp.where(early, early_x, late_x))
        firsts.append(jnp.where(early, pair0, got))

        def by_plane(values):
            chosen = values[0]
            for at in range(1, level + 1):
                chosen = jnp.where(plane == at, values[at], chosen)
            return chosen

        if final:
            first_cache, second_cache = by_plane(firsts), by_plane(seconds + [got])

        def end_early():
            result, _ = output(early_x, attended, gathered_other, 1)
            if not final:
                return result, nothing(pair_shape)
            caches = jnp.concatenate([*first_cache, *second_cache], axis=1)
            return result, across(apart(caches))

        def end_late():
            if not final:
                attended, own = block(received, got, 1, True)
                return output(late_x, across(attended), gathered, 1)[0], own
            attended, own = block(received, got, 1, True, (first_cache,))
            own = jnp.where(plane == level, own, second_cache)
            both = jnp.concatenate([flat(attended), *own], axis=1)
            both = across(apart(both))
            return output(late_x, both, gathered, 1)[0], both[:, :, channels:]

        moved, pair1 = either(end_early, end_late)
        second_outs.append(moved)
        seconds.append(jnp.where(early, got, pair1) if not final else None)

    cache = pair1
    mine = by_plane([jnp.where(early, a, b) for a, b in zip(first_outs, second_outs)])
    theirs = swap(by_plane([jnp.where(early, b, a) for a, b in zip(first_outs, second_outs)]))
    block_output = jnp.stack([jnp.where(early, mine, theirs), jnp.where(early, theirs, mine)])
    cache = cache.reshape(seq, rows, 2, 2, channels)
    cache = jnp.transpose(cache, (2, 1, 3, 0, 4)).reshape(2, rows, 2, seq * channels)
    return block_output[None], cache[None]


def solution(mesh):
    in_specs = (
        P(None, "seq", None),
        P("pipe", None),
        P("pipe", None),
        P("pipe", None),
        P("pipe", None, None),
        P("pipe", None, None, "seq"),
        P("pipe", "seq", None),
        P("pipe", None, "seq", None, None),
    )
    out_specs = (P("pipe", None, "seq", None), P("pipe", None, "seq", None, None))
    return jax.shard_map(body, mesh=mesh, in_specs=in_specs, out_specs=out_specs, check_vma=False)
```

```python
import functools
import math

import jax
import jax.numpy as jnp
from jax import lax
from jax.experimental import pallas as pl
from jax.experimental.pallas import tpu as pltpu
from jax.sharding import PartitionSpec as P

AXES = ("pipe", "seq")
VMEM = pl.BlockSpec(memory_space=pltpu.VMEM)
ANY = pl.BlockSpec(memory_space=pl.ANY)
HBM = pl.BlockSpec(memory_space=pltpu.HBM)


def ring_order(count):
    fast = 1
    while fast * fast * 4 <= count and count % (fast * 2) == 0:
        fast *= 2
    slow = count // fast
    if fast == 1 or slow % 2:
        return list(range(count))
    cells = [(0, 0)]
    for row in range(slow):
        columns = range(1, fast) if row % 2 == 0 else range(fast - 1, 0, -1)
        cells += [(row, column) for column in columns]
    cells += [(row, 0) for row in range(slow - 1, 0, -1)]
    return [row * fast + column for row, column in cells]


def normalise(values, params_ref):
    centered = values - jnp.mean(values, axis=-1, keepdims=True)
    spread = jnp.mean(centered * centered, axis=-1, keepdims=True)
    return (
        centered * lax.rsqrt(spread + 1e-06) * (1.0 + params_ref[1:2, :]) + params_ref[0:1, :]
    ).astype(jnp.bfloat16)


def spread_block(block, buffer, out_ref, sems):
    width = buffer.shape[1]
    buffer[...] = block
    copies = [
        pltpu.make_async_copy(buffer, out_ref.at[shard, :, :width], sems.at[shard])
        for shard in range(out_ref.shape[0])
    ]
    for copy in copies:
        copy.start()
    return copies


def norm_kernel(params_ref, x_ref, out_ref, buffer, sems):
    block = normalise(x_ref[...].astype(jnp.float32), params_ref)
    for copy in spread_block(block, buffer, out_ref, sems):
        copy.wait()


def pack_kernel(params_ref, x_ref, cache_ref, out_ref, buffer, sems, sides, sem):
    count, _, total = sides.shape
    width = x_ref.shape[1]
    channels = total // 2
    block = normalise(x_ref[...].astype(jnp.float32), params_ref)
    copies = spread_block(block, buffer, out_ref, sems)
    for kind in range(2):
        rows = cache_ref[:, kind, :]
        for shard in range(count):
            sides[shard, :, kind * channels : (kind + 1) * channels] = rows[
                :, shard * channels : (shard + 1) * channels
            ]
    copies.append(pltpu.make_async_copy(sides, out_ref.at[:, :, width:], sem))
    copies[-1].start()
    for copy in copies:
        copy.wait()


def attention(head_size, q_ref, kv_ref, far_ref):
    factor = 1.0 / math.sqrt(head_size)
    channels = q_ref.shape[1]
    heads = []
    across = (((1,), (1,)), ((), ()))

    def far_of(kind, start):
        if len(far_ref.shape) == 3:
            return far_ref[kind, :, start : start + head_size]
        return far_ref[:, kind * channels + start : kind * channels + start + head_size]

    for start in range(0, channels, head_size):
        cut = slice(start, start + head_size)
        query = q_ref[:, cut]
        near = lax.dot_general(query, kv_ref[0, :, cut], across, preferred_element_type=jnp.float32)
        far = lax.dot_general(query, far_of(0, start), across, preferred_element_type=jnp.float32)
        near = jnp.exp(near * factor)
        far = jnp.exp(far * factor)
        total = jnp.sum(near, axis=-1, keepdims=True) + jnp.sum(far, axis=-1, keepdims=True)
        near = (near / total).astype(jnp.bfloat16)
        far = (far / total).astype(jnp.bfloat16)
        mixed = jnp.dot(near, kv_ref[1, :, cut], preferred_element_type=jnp.float32)
        mixed = mixed + jnp.dot(far, far_of(1, start), preferred_element_type=jnp.float32)
        heads.append(mixed.astype(jnp.bfloat16))
    return jnp.concatenate(heads, axis=1)


def block_kernel(
    head_size, only, gain_ref, in_ref, out_weights_ref, blocks_ref, far_ref, *refs
):
    caches, refs = refs[:-11], refs[-11:]
    out_ref, kv_ref, blocks, far, w_in, w_out, parts, q_ref, in_sems, sems, part_sems = refs
    width = blocks.shape[1]
    channels = w_out.shape[0]
    pieces = in_sems.shape[1]
    depth = width // pieces
    fetch = pltpu.make_async_copy(blocks_ref.at[:, :width], blocks, sems.at[0])
    fetch.start()
    if len(far.shape) == 3:
        fetch_far = pltpu.make_async_copy(far_ref, far, sems.at[2])
    else:
        begin = far_ref.shape[1] - far.shape[1]
        fetch_far = pltpu.make_async_copy(far_ref.at[:, begin:], far, sems.at[2])
    fetch_far.start()

    for part in (1, 2, 0):
        for piece in range(pieces):
            cut = pl.ds(piece * depth, depth)
            pltpu.make_async_copy(
                in_ref.at[part, cut], w_in.at[part, cut], in_sems.at[part, piece]
            ).start()
    if not only:
        pltpu.make_async_copy(out_weights_ref.at[0], w_out, sems.at[1]).start()
    fetch.wait()
    tokens = blocks[...]
    for part in (1, 2, 0):
        for piece in range(pieces):
            cut = pl.ds(piece * depth, depth)
            pltpu.make_async_copy(
                in_ref.at[part, cut], w_in.at[part, cut], in_sems.at[part, piece]
            ).wait()
        projected = jnp.dot(tokens, w_in[part], preferred_element_type=jnp.float32)
        if part == 2:
            kv_ref[1] = projected.astype(jnp.bfloat16)
            continue
        for start in range(0, channels, head_size):
            head = projected[:, start : start + head_size]
            square = jnp.mean(head * head, axis=-1, keepdims=True)
            head = (head * lax.rsqrt(square + 1e-06) * gain_ref[part : part + 1, :]).astype(
                jnp.bfloat16
            )
            if part == 0:
                q_ref[:, start : start + head_size] = head
            else:
                kv_ref[0, :, start : start + head_size] = head

    fetch_far.wait()
    if only:
        out_ref[:, :channels] = attention(head_size, q_ref, kv_ref, far)
        for patch, cache in enumerate(caches):
            for kind in range(2):
                begin = (1 + 2 * patch + kind) * channels
                out_ref[:, begin : begin + channels] = cache[kind]
        return
    sent = []

    def send(begin, size, sem):
        cut = pl.ds(begin, size)
        sent.append(
            pltpu.make_async_copy(parts.at[:, cut], out_ref.at[:, cut], part_sems.at[sem])
        )
        sent[-1].start()

    steps = part_sems.shape[0]
    attended = attention(head_size, q_ref, kv_ref, far)
    pltpu.make_async_copy(out_weights_ref.at[0], w_out, sems.at[1]).wait()
    tile = width // steps
    for step in range(steps):
        cut = slice(step * tile, (step + 1) * tile)
        update = jnp.dot(attended, w_out[:, cut], preferred_element_type=jnp.float32)
        parts[:, cut] = update.astype(jnp.bfloat16)
        send(step * tile, tile, step)
    for copy in sent:
        copy.wait()


def finish_kernel(params_ref, next_ref, x_ref, parts_ref, out_ref, *rest):
    width = x_ref.shape[1]
    update = jnp.sum(parts_ref[:, :, :width].astype(jnp.float32), axis=0)
    result = (x_ref[...].astype(jnp.float32) + params_ref[2:3, :] * update).astype(jnp.bfloat16)
    out_ref[...] = result
    if rest:
        blocks_ref, buffer, sems = rest
        block = normalise(result.astype(jnp.float32), next_ref)
        for copy in spread_block(block, buffer, blocks_ref, sems):
            copy.wait()


def output_kernel(
    order_ref, params_ref, next_ref, x_ref, att_ref, weights_ref, out_ref, blocks_ref, total, buffer, sems
):
    step = pl.program_id(0)
    channels = weights_ref.shape[0]
    update = jnp.dot(
        att_ref[order_ref[step], :, :channels], weights_ref[...], preferred_element_type=jnp.float32
    )

    @pl.when(step == 0)
    def _():
        total[...] = update

    @pl.when(step > 0)
    def _():
        total[...] += update

    @pl.when(step == pl.num_programs(0) - 1)
    def _():
        result = (x_ref[...].astype(jnp.float32) + params_ref[2:3, :] * total[...]).astype(
            jnp.bfloat16
        )
        out_ref[...] = result
        block = normalise(result.astype(jnp.float32), next_ref)
        for copy in spread_block(block, buffer, blocks_ref, sems):
            copy.wait()


def blank_kernel(*refs):
    pass


def params_of(limit):
    return pltpu.CompilerParams(vmem_limit_bytes=limit << 20)


def body(hidden, mod_shift, mod_scale, mod_gate, norm_gain, input_proj, output_proj, stale_cache):
    sections = lax.axis_size("pipe")
    planes = sections // 2
    seq = lax.axis_size("seq")
    pipe = lax.axis_index("pipe")
    core = lax.rem(pipe, 2)
    plane = pipe // 2
    rows, width = hidden.shape[1:]
    head_size = norm_gain.shape[2]
    channels = input_proj.shape[3]
    tokens = rows * seq
    bf16 = lambda *shape: jax.ShapeDtypeStruct(shape, jnp.bfloat16)

    place = lambda row, position: row * seq + position

    lowest, others = range(2), range(2, sections)

    def swap(value, rows_of=range(sections)):
        pairs = [(place(row, s), place(row ^ 1, s)) for row in rows_of for s in range(seq)]
        return lax.ppermute(value, AXES, pairs)

    def upward(value):
        pairs = [
            (place(row, s), place((row + 2) % sections, s))
            for row in range(sections)
            for s in range(seq)
        ]
        return lax.ppermute(value, AXES, pairs)

    ring = ring_order(seq)

    def around(value, step):
        pairs = [
            (place(row, ring[i]), place(row, ring[(i + step) % seq]))
            for row in others
            for i in range(seq)
        ]
        return lax.ppermute(value, AXES, pairs)

    spot = jnp.array([ring.index(s) for s in range(seq)], jnp.int32)
    half = seq // 2
    moves = [-hop for hop in range(half)] + list(range(1, half)) + [half]
    order = jnp.array(ring, jnp.int32)[
        jnp.remainder(spot[lax.axis_index("seq")] + jnp.array(moves, jnp.int32), seq)
    ]

    def across(blocks):
        return lax.all_to_all(blocks, "seq", split_axis=0, concat_axis=0, tiled=True)

    def blank(*shapes):
        return pl.pallas_call(blank_kernel, out_shape=shapes, out_specs=(ANY,) * len(shapes))()

    gains = jnp.pad(norm_gain[0].reshape(1, -1), ((0, 0), (0, width - 2 * head_size)))
    own_params = jnp.concatenate([mod_shift, mod_scale, mod_gate, gains], axis=0)
    own_in = jnp.transpose(input_proj[0], (1, 0, 2))
    own_out = output_proj
    x = lax.dynamic_index_in_dim(hidden, core, 0, keepdims=False)
    spreading = [pltpu.VMEM((rows, width), jnp.bfloat16), pltpu.SemaphoreType.DMA((seq,))]
    packed = pl.pallas_call(
        pack_kernel, out_shape=bf16(seq, rows, width + 2 * channels),
        in_specs=[VMEM] * 3, out_specs=HBM,
        scratch_shapes=spreading + [
            pltpu.VMEM((seq, rows, 2 * channels), jnp.bfloat16), pltpu.SemaphoreType.DMA,
        ],
        compiler_params=params_of(16),
    )(own_params, x, stale_cache[0, 1])

    other_params = swap(own_params)
    own_in, own_out, other_params, packed = lax.optimization_barrier(
        (own_in, own_out, other_params, packed)
    )
    own = own_in, own_out
    params = [jnp.where(core == turn, own_params, other_params) for turn in range(2)]
    gain_rows = [p[3, : 2 * head_size].reshape(2, head_size) for p in params]
    blocks_shape = bf16(seq, rows, width)

    def norm(x, turn):
        return pl.pallas_call(
            norm_kernel, out_shape=blocks_shape, in_specs=[VMEM] * 2, out_specs=HBM,
            scratch_shapes=spreading, compiler_params=params_of(16),
        )(params[turn], x)

    flat = lambda blocks: blocks.reshape(tokens, blocks.shape[2])
    apart = lambda values: values.reshape(seq, rows, values.shape[1])

    def block(blocks, far, turn, weights, only=False, caches=()):
        total = channels * (1 + 2 * len(caches)) if only else width
        side = (2, tokens, channels) if far.ndim == 3 else (tokens, 2 * channels)
        out, pair = pl.pallas_call(
            functools.partial(block_kernel, head_size, only),
            out_shape=(bf16(tokens, total), pair_shape),
            in_specs=[VMEM] + [HBM] * 2 + [ANY] * 2 + [VMEM] * len(caches),
            out_specs=(VMEM if only else HBM, VMEM),
            scratch_shapes=[
                pltpu.VMEM((tokens, width), jnp.bfloat16),
                pltpu.VMEM(side, jnp.bfloat16),
                pltpu.VMEM(own_in.shape, jnp.bfloat16),
                pltpu.VMEM(own_out.shape[1:], jnp.bfloat16),
                pltpu.VMEM((tokens, width), jnp.bfloat16),
                pltpu.VMEM((tokens, channels), jnp.bfloat16),
                pltpu.SemaphoreType.DMA((3, 2)),
                pltpu.SemaphoreType.DMA((3,)),
                pltpu.SemaphoreType.DMA((4,)),
            ],
            compiler_params=params_of(32),
        )(
            gain_rows[turn], *weights, flat(blocks), far, *caches
        )
        return apart(out), pair

    def output(x, attended, weights, turn):
        return pl.pallas_call(
            output_kernel,
            grid_spec=pltpu.PrefetchScalarGridSpec(
                num_scalar_prefetch=1,
                grid=(seq,),
                in_specs=[
                    pl.BlockSpec((4, width), lambda i, o: (0, 0)),
                    pl.BlockSpec((4, width), lambda i, o: (0, 0)),
                    pl.BlockSpec((rows, width), lambda i, o: (0, 0)),
                    pl.BlockSpec(attended.shape, lambda i, o: (0, 0, 0)),
                    pl.BlockSpec((channels, width), lambda i, o: (i, 0)),
                ],
                out_specs=(pl.BlockSpec((rows, width), lambda i, o: (0, 0)), HBM),
                scratch_shapes=[
                    pltpu.VMEM((rows, width), jnp.float32),
                ] + spreading,
            ),
            out_shape=(bf16(rows, width), blocks_shape),
            compiler_params=params_of(32),
        )(order, params[turn], params[1 - turn], x, attended, weights)

    def finish(x, parts, turn, onward):
        shapes = (bf16(rows, width),) + (blocks_shape,) * onward
        return pl.pallas_call(
            finish_kernel, out_shape=shapes, in_specs=[VMEM] * 4,
            out_specs=(VMEM,) + (HBM,) * onward,
            scratch_shapes=spreading * onward, compiler_params=params_of(16),
        )(params[turn], params[1 - turn], x, parts)

    early = core == 0
    either = lambda on_early, on_late: lax.cond(early, on_early, on_late)

    pair_shape, block_shape = bf16(2, tokens, channels), bf16(rows, width)
    side_shape = bf16(tokens, 2 * channels)
    att_shape = bf16(seq, rows, channels)
    nothing = lambda shape: blank(shape)[0]

    def first_plane():
        other = swap(own_in, lowest), swap(own_out, lowest)

        def start_early():
            received = across(packed)
            parts, fresh = block(received, flat(received), 0, own)
            return parts, fresh, nothing(side_shape)

        def start_late():
            side = flat(across(packed[:, :, width:]))
            return norm(x, 0), nothing(pair_shape), side

        payload, pair0, side = either(start_early, start_late)
        fresh = swap(pair0, lowest)
        received = across(payload)
        side = swap(side, lowest)

        def gather_early():
            result, normed = finish(x, received, 0, 1)
            return normed, nothing(pair_shape), result

        def scatter_late():
            parts, late = block(received, fresh, 0, other)
            return parts, late, nothing(block_shape)

        payload, late_pair, early_x = either(gather_early, scatter_late)
        received = across(payload)

        def scatter_early():
            parts, fresh = block(received, side, 1, other)
            return parts, fresh, nothing(block_shape)

        def gather_late():
            result, normed = finish(x, received, 0, 1)
            return normed, late_pair, result

        payload, pair, late_x = either(scatter_early, gather_late)
        got = swap(pair, lowest)
        received = across(payload)

        def end_early():
            return finish(early_x, received, 1, 0)[0], nothing(pair_shape)

        def end_late():
            parts, late = block(received, got, 1, own)
            return finish(late_x, across(parts), 1, 0)[0], late

        moved, pair1 = either(end_early, end_late)
        return (
            jnp.where(early, early_x, late_x), moved, pair0, got, pair1,
            nothing(side_shape), nothing(side_shape), nothing(bf16(seq * channels, width)), nothing(bf16(*own_in.shape)),
        )

    def other_planes():
        side, mine = lax.optimization_barrier(
            (flat(across(packed[:, :, width:])), own_out[0])
        )
        cut = mine.shape[0] // 2
        streams = [[mine[:cut]], [mine[cut:]], [mine[:cut]], [mine[cut:]]]
        for hop in range(half):
            for stream, step, hops in zip(streams, (1, 1, -1, -1), (half, half - 1, half - 1, half)):
                if hop < hops:
                    stream.append(around(stream[-1], step))
        first, second, third, fourth = streams
        pieces = [piece for pair in zip(first[:half], second) for piece in pair]
        pieces += [piece for pair in zip(third[1:], fourth[1:half]) for piece in pair]
        gathered = jnp.concatenate(pieces + [first[half], fourth[half]], axis=0)
        return (
            nothing(block_shape), nothing(block_shape), nothing(pair_shape), nothing(pair_shape),
            nothing(pair_shape), side, swap(side, others), gathered, swap(own_in, others),
        )

    first_out, moved, pair0, got, pair1, side, other_side, gathered, other_in = lax.cond(
        plane == 0, first_plane, other_planes
    )
    gathered_other = swap(gathered)
    other = other_in, own_out
    first_outs, second_outs = [first_out], [moved]
    firsts = [jnp.where(early, pair0, got)]
    seconds = [jnp.where(early, got, pair1)]
    for level in range(1, planes):
        final = level == planes - 1
        x = upward(moved)
        received = either(lambda: across(norm(x, 0)), lambda: nothing(blocks_shape))

        def attend_early():
            attended, fresh = block(received, side, 0, own, True)
            return across(attended), nothing(blocks_shape), fresh

        def gather_late():
            return nothing(att_shape), across(norm(x, 0)), nothing(pair_shape)

        attended, received, pair0 = either(attend_early, gather_late)
        fresh = swap(pair0)

        def next_early():
            result, normed = output(x, attended, gathered, 0)
            return nothing(att_shape), across(normed), nothing(pair_shape), result

        def attend_late():
            attended, late = block(received, fresh, 0, other, True)
            return across(attended), nothing(blocks_shape), late, nothing(block_shape)

        attended, received, late_pair, early_x = either(next_early, attend_late)

        def attend_again():
            attended, fresh = block(received, other_side, 1, other, True)
            return across(attended), nothing(blocks_shape), fresh, nothing(block_shape)

        def next_late():
            result, normed = output(x, attended, gathered_other, 0)
            return nothing(att_shape), across(normed), late_pair, result

        attended, received, pair, late_x = either(attend_again, next_late)
        got = swap(pair)
        first_outs.append(jnp.where(early, early_x, late_x))
        firsts.append(jnp.where(early, pair0, got))

        def by_plane(values):
            chosen = values[0]
            for at in range(1, level + 1):
                chosen = jnp.where(plane == at, values[at], chosen)
            return chosen

        if final:
            first_cache, second_cache = by_plane(firsts), by_plane(seconds + [got])

        def end_early():
            result, _ = output(early_x, attended, gathered_other, 1)
            if not final:
                return result, nothing(pair_shape)
            caches = jnp.concatenate([*first_cache, *second_cache], axis=1)
            return result, across(apart(caches))

        def end_late():
            if not final:
                attended, late = block(received, got, 1, own, True)
                return output(late_x, across(attended), gathered, 1)[0], late
            attended, late = block(received, got, 1, own, True, (first_cache,))
            late = jnp.where(plane == level, late, second_cache)
            both = jnp.concatenate([flat(attended), *late], axis=1)
            both = across(apart(both))
            return output(late_x, both, gathered, 1)[0], both[:, :, channels:]

        moved, pair1 = either(end_early, end_late)
        second_outs.append(moved)
        seconds.append(jnp.where(early, got, pair1) if not final else None)

    cache = pair1
    mine = by_plane([jnp.where(early, a, b) for a, b in zip(first_outs, second_outs)])
    theirs = swap(by_plane([jnp.where(early, b, a) for a, b in zip(first_outs, second_outs)]))
    block_output = jnp.stack([jnp.where(early, mine, theirs), jnp.where(early, theirs, mine)])
    cache = cache.reshape(seq, rows, 2, 2, channels)
    cache = jnp.transpose(cache, (2, 1, 3, 0, 4)).reshape(2, rows, 2, seq * channels)
    return block_output[None], cache[None]


def solution(mesh):
    in_specs = (
        P(None, "seq", None),
        P("pipe", None),
        P("pipe", None),
        P("pipe", None),
        P("pipe", None, None),
        P("pipe", None, None, "seq"),
        P("pipe", "seq", None),
        P("pipe", None, "seq", None, None),
    )
    out_specs = (P("pipe", None, "seq", None), P("pipe", None, "seq", None, None))
    return jax.shard_map(body, mesh=mesh, in_specs=in_specs, out_specs=out_specs, check_vma=False)
```

```python
import functools
import math

import jax
import jax.numpy as jnp
from jax import lax
from jax.experimental import pallas as pl
from jax.experimental.pallas import tpu as pltpu
from jax.sharding import PartitionSpec as P

AXES = ("pipe", "seq")
VMEM = pl.BlockSpec(memory_space=pltpu.VMEM)
ANY = pl.BlockSpec(memory_space=pl.ANY)
HBM = pl.BlockSpec(memory_space=pltpu.HBM)


def ring_order(count):
    fast = 1
    while fast * fast * 4 <= count and count % (fast * 2) == 0:
        fast *= 2
    slow = count // fast
    if fast == 1 or slow % 2:
        return list(range(count))
    cells = [(0, 0)]
    for row in range(slow):
        columns = range(1, fast) if row % 2 == 0 else range(fast - 1, 0, -1)
        cells += [(row, column) for column in columns]
    cells += [(row, 0) for row in range(slow - 1, 0, -1)]
    return [row * fast + column for row, column in cells]


def normalise(values, params_ref):
    centered = values - jnp.mean(values, axis=-1, keepdims=True)
    spread = jnp.mean(centered * centered, axis=-1, keepdims=True)
    return (
        centered * lax.rsqrt(spread + 1e-06) * (1.0 + params_ref[1:2, :]) + params_ref[0:1, :]
    ).astype(jnp.bfloat16)


def spread_block(block, buffer, out_ref, sems):
    width = buffer.shape[1]
    buffer[...] = block
    copies = [
        pltpu.make_async_copy(buffer, out_ref.at[shard, :, :width], sems.at[shard])
        for shard in range(out_ref.shape[0])
    ]
    for copy in copies:
        copy.start()
    return copies


def norm_kernel(params_ref, x_ref, out_ref, buffer, sems):
    block = normalise(x_ref[...].astype(jnp.float32), params_ref)
    for copy in spread_block(block, buffer, out_ref, sems):
        copy.wait()


def pack_kernel(params_ref, x_ref, cache_ref, out_ref, buffer, sems, sides, sem):
    count, _, total = sides.shape
    width = x_ref.shape[1]
    channels = total // 2
    block = normalise(x_ref[...].astype(jnp.float32), params_ref)
    copies = spread_block(block, buffer, out_ref, sems)
    for kind in range(2):
        rows = cache_ref[:, kind, :]
        for shard in range(count):
            sides[shard, :, kind * channels : (kind + 1) * channels] = rows[
                :, shard * channels : (shard + 1) * channels
            ]
    copies.append(pltpu.make_async_copy(sides, out_ref.at[:, :, width:], sem))
    copies[-1].start()
    for copy in copies:
        copy.wait()


def attention(head_size, q_ref, kv_ref, far_ref):
    factor = 1.0 / math.sqrt(head_size)
    channels = q_ref.shape[1]
    heads = []
    across = (((1,), (1,)), ((), ()))

    def far_of(kind, start):
        if len(far_ref.shape) == 3:
            return far_ref[kind, :, start : start + head_size]
        return far_ref[:, kind * channels + start : kind * channels + start + head_size]

    for start in range(0, channels, head_size):
        cut = slice(start, start + head_size)
        query = q_ref[:, cut]
        near = lax.dot_general(query, kv_ref[0, :, cut], across, preferred_element_type=jnp.float32)
        far = lax.dot_general(query, far_of(0, start), across, preferred_element_type=jnp.float32)
        near = jnp.exp(near * factor)
        far = jnp.exp(far * factor)
        total = jnp.sum(near, axis=-1, keepdims=True) + jnp.sum(far, axis=-1, keepdims=True)
        near = (near / total).astype(jnp.bfloat16)
        far = (far / total).astype(jnp.bfloat16)
        mixed = jnp.dot(near, kv_ref[1, :, cut], preferred_element_type=jnp.float32)
        mixed = mixed + jnp.dot(far, far_of(1, start), preferred_element_type=jnp.float32)
        heads.append(mixed.astype(jnp.bfloat16))
    return jnp.concatenate(heads, axis=1)


def block_kernel(
    head_size, only, gain_ref, in_ref, out_weights_ref, blocks_ref, far_ref, *refs
):
    caches, refs = refs[:-11], refs[-11:]
    out_ref, kv_ref, blocks, far, w_in, w_out, parts, q_ref, in_sems, sems, part_sems = refs
    width = blocks.shape[1]
    channels = w_out.shape[0]
    pieces = in_sems.shape[1]
    depth = width // pieces
    fetch = pltpu.make_async_copy(blocks_ref.at[:, :width], blocks, sems.at[0])
    fetch.start()
    if len(far.shape) == 3:
        fetch_far = pltpu.make_async_copy(far_ref, far, sems.at[2])
    else:
        begin = far_ref.shape[1] - far.shape[1]
        fetch_far = pltpu.make_async_copy(far_ref.at[:, begin:], far, sems.at[2])
    fetch_far.start()

    for part in (1, 2, 0):
        for piece in range(pieces):
            cut = pl.ds(piece * depth, depth)
            pltpu.make_async_copy(
                in_ref.at[part, cut], w_in.at[part, cut], in_sems.at[part, piece]
            ).start()
    if not only:
        pltpu.make_async_copy(out_weights_ref.at[0], w_out, sems.at[1]).start()
    fetch.wait()
    tokens = blocks[...]
    for part in (1, 2, 0):
        for piece in range(pieces):
            cut = pl.ds(piece * depth, depth)
            pltpu.make_async_copy(
                in_ref.at[part, cut], w_in.at[part, cut], in_sems.at[part, piece]
            ).wait()
        projected = jnp.dot(tokens, w_in[part], preferred_element_type=jnp.float32)
        if part == 2:
            kv_ref[1] = projected.astype(jnp.bfloat16)
            continue
        for start in range(0, channels, head_size):
            head = projected[:, start : start + head_size]
            square = jnp.mean(head * head, axis=-1, keepdims=True)
            head = (head * lax.rsqrt(square + 1e-06) * gain_ref[part : part + 1, :]).astype(
                jnp.bfloat16
            )
            if part == 0:
                q_ref[:, start : start + head_size] = head
            else:
                kv_ref[0, :, start : start + head_size] = head

    fetch_far.wait()
    if only:
        out_ref[:, :channels] = attention(head_size, q_ref, kv_ref, far)
        for patch, cache in enumerate(caches):
            for kind in range(2):
                begin = (1 + 2 * patch + kind) * channels
                out_ref[:, begin : begin + channels] = cache[kind]
        return
    sent = []

    def send(begin, size, sem):
        cut = pl.ds(begin, size)
        sent.append(
            pltpu.make_async_copy(parts.at[:, cut], out_ref.at[:, cut], part_sems.at[sem])
        )
        sent[-1].start()

    steps = part_sems.shape[0]
    attended = attention(head_size, q_ref, kv_ref, far)
    pltpu.make_async_copy(out_weights_ref.at[0], w_out, sems.at[1]).wait()
    tile = width // steps
    for step in range(steps):
        cut = slice(step * tile, (step + 1) * tile)
        update = jnp.dot(attended, w_out[:, cut], preferred_element_type=jnp.float32)
        parts[:, cut] = update.astype(jnp.bfloat16)
        send(step * tile, tile, step)
    for copy in sent:
        copy.wait()


def finish_kernel(params_ref, next_ref, x_ref, parts_ref, out_ref, *rest):
    width = x_ref.shape[1]
    update = jnp.sum(parts_ref[:, :, :width].astype(jnp.float32), axis=0)
    result = (x_ref[...].astype(jnp.float32) + params_ref[2:3, :] * update).astype(jnp.bfloat16)
    out_ref[...] = result
    if rest:
        blocks_ref, buffer, sems = rest
        block = normalise(result.astype(jnp.float32), next_ref)
        for copy in spread_block(block, buffer, blocks_ref, sems):
            copy.wait()


def output_kernel(
    order_ref, params_ref, next_ref, x_ref, att_ref, weights_ref, out_ref, *rest
):
    total, rest = rest[-1], rest[:-1]
    step = pl.program_id(0)
    channels = weights_ref.shape[0]
    update = jnp.dot(
        att_ref[order_ref[step], :, :channels], weights_ref[...], preferred_element_type=jnp.float32
    )

    @pl.when(step == 0)
    def _():
        total[...] = update

    @pl.when(step > 0)
    def _():
        total[...] += update

    @pl.when(step == pl.num_programs(0) - 1)
    def _():
        result = (x_ref[...].astype(jnp.float32) + params_ref[2:3, :] * total[...]).astype(
            jnp.bfloat16
        )
        out_ref[...] = result
        if rest:
            blocks_ref, buffer, sems = rest
            block = normalise(result.astype(jnp.float32), next_ref)
            for copy in spread_block(block, buffer, blocks_ref, sems):
                copy.wait()


def blank_kernel(*refs):
    pass


def params_of(limit):
    return pltpu.CompilerParams(vmem_limit_bytes=limit << 20)


def body(hidden, mod_shift, mod_scale, mod_gate, norm_gain, input_proj, output_proj, stale_cache):
    sections = lax.axis_size("pipe")
    planes = sections // 2
    seq = lax.axis_size("seq")
    pipe = lax.axis_index("pipe")
    core = lax.rem(pipe, 2)
    plane = pipe // 2
    rows, width = hidden.shape[1:]
    head_size = norm_gain.shape[2]
    channels = input_proj.shape[3]
    tokens = rows * seq
    bf16 = lambda *shape: jax.ShapeDtypeStruct(shape, jnp.bfloat16)

    place = lambda row, position: row * seq + position

    lowest, others = range(2), range(2, sections)

    def swap(value, rows_of=range(sections)):
        pairs = [(place(row, s), place(row ^ 1, s)) for row in rows_of for s in range(seq)]
        return lax.ppermute(value, AXES, pairs)

    def upward(value):
        pairs = [
            (place(row, s), place((row + 2) % sections, s))
            for row in range(sections)
            for s in range(seq)
        ]
        return lax.ppermute(value, AXES, pairs)

    ring = ring_order(seq)

    def around(value, step):
        pairs = [
            (place(row, ring[i]), place(row, ring[(i + step) % seq]))
            for row in others
            for i in range(seq)
        ]
        return lax.ppermute(value, AXES, pairs)

    spot = jnp.array([ring.index(s) for s in range(seq)], jnp.int32)
    half = seq // 2
    moves = [-hop for hop in range(half)] + list(range(1, half)) + [half]
    order = jnp.array(ring, jnp.int32)[
        jnp.remainder(spot[lax.axis_index("seq")] + jnp.array(moves, jnp.int32), seq)
    ]

    def across(blocks):
        return lax.all_to_all(blocks, "seq", split_axis=0, concat_axis=0, tiled=True)

    def blank(*shapes):
        return pl.pallas_call(blank_kernel, out_shape=shapes, out_specs=(ANY,) * len(shapes))()

    gains = jnp.pad(norm_gain[0].reshape(1, -1), ((0, 0), (0, width - 2 * head_size)))
    own_params = jnp.concatenate([mod_shift, mod_scale, mod_gate, gains], axis=0)
    own_in = jnp.transpose(input_proj[0], (1, 0, 2))
    own_out = output_proj
    x = lax.dynamic_index_in_dim(hidden, core, 0, keepdims=False)
    spreading = [pltpu.VMEM((rows, width), jnp.bfloat16), pltpu.SemaphoreType.DMA((seq,))]
    packed = pl.pallas_call(
        pack_kernel, out_shape=bf16(seq, rows, width + 2 * channels),
        in_specs=[VMEM] * 3, out_specs=HBM,
        scratch_shapes=spreading + [
            pltpu.VMEM((seq, rows, 2 * channels), jnp.bfloat16), pltpu.SemaphoreType.DMA,
        ],
        compiler_params=params_of(16),
    )(own_params, x, stale_cache[0, 1])

    other_params = swap(own_params)
    own_in, own_out, other_params, packed = lax.optimization_barrier(
        (own_in, own_out, other_params, packed)
    )
    own = own_in, own_out
    params = [jnp.where(core == turn, own_params, other_params) for turn in range(2)]
    gain_rows = [p[3, : 2 * head_size].reshape(2, head_size) for p in params]
    blocks_shape = bf16(seq, rows, width)

    def norm(x, turn):
        return pl.pallas_call(
            norm_kernel, out_shape=blocks_shape, in_specs=[VMEM] * 2, out_specs=HBM,
            scratch_shapes=spreading, compiler_params=params_of(16),
        )(params[turn], x)

    flat = lambda blocks: blocks.reshape(tokens, blocks.shape[2])
    apart = lambda values: values.reshape(seq, rows, values.shape[1])

    def block(blocks, far, turn, weights, only=False, caches=()):
        total = channels * (1 + 2 * len(caches)) if only else width
        side = (2, tokens, channels) if far.ndim == 3 else (tokens, 2 * channels)
        out, pair = pl.pallas_call(
            functools.partial(block_kernel, head_size, only),
            out_shape=(bf16(tokens, total), pair_shape),
            in_specs=[VMEM] + [HBM] * 2 + [ANY] * 2 + [VMEM] * len(caches),
            out_specs=(VMEM if only else HBM, VMEM),
            scratch_shapes=[
                pltpu.VMEM((tokens, width), jnp.bfloat16),
                pltpu.VMEM(side, jnp.bfloat16),
                pltpu.VMEM(own_in.shape, jnp.bfloat16),
                pltpu.VMEM(own_out.shape[1:], jnp.bfloat16),
                pltpu.VMEM((tokens, width), jnp.bfloat16),
                pltpu.VMEM((tokens, channels), jnp.bfloat16),
                pltpu.SemaphoreType.DMA((3, 2)),
                pltpu.SemaphoreType.DMA((3,)),
                pltpu.SemaphoreType.DMA((4,)),
            ],
            compiler_params=params_of(32),
        )(
            gain_rows[turn], *weights, flat(blocks), far, *caches
        )
        return apart(out), pair

    def output(x, attended, weights, turn, onward=False):
        return pl.pallas_call(
            output_kernel,
            grid_spec=pltpu.PrefetchScalarGridSpec(
                num_scalar_prefetch=1,
                grid=(seq,),
                in_specs=[
                    pl.BlockSpec((4, width), lambda i, o: (0, 0)),
                    pl.BlockSpec((4, width), lambda i, o: (0, 0)),
                    pl.BlockSpec((rows, width), lambda i, o: (0, 0)),
                    pl.BlockSpec(attended.shape, lambda i, o: (0, 0, 0)),
                    pl.BlockSpec((channels, width), lambda i, o: (i, 0)),
                ],
                out_specs=(pl.BlockSpec((rows, width), lambda i, o: (0, 0)),) + (HBM,) * onward,
                scratch_shapes=spreading * onward + [pltpu.VMEM((rows, width), jnp.float32)],
            ),
            out_shape=(bf16(rows, width),) + (blocks_shape,) * onward,
            compiler_params=params_of(32),
        )(order, params[turn], params[1 - turn], x, attended, weights)

    def finish(x, parts, turn, onward):
        shapes = (bf16(rows, width),) + (blocks_shape,) * onward
        return pl.pallas_call(
            finish_kernel, out_shape=shapes, in_specs=[VMEM] * 4,
            out_specs=(VMEM,) + (HBM,) * onward,
            scratch_shapes=spreading * onward, compiler_params=params_of(16),
        )(params[turn], params[1 - turn], x, parts)

    early = core == 0
    either = lambda on_early, on_late: lax.cond(early, on_early, on_late)

    pair_shape, block_shape = bf16(2, tokens, channels), bf16(rows, width)
    side_shape = bf16(tokens, 2 * channels)
    att_shape = bf16(seq, rows, channels)
    nothing = lambda shape: blank(shape)[0]

    def first_plane():
        other = swap(own_in, lowest), swap(own_out, lowest)

        def start_early():
            received = across(packed)
            parts, fresh = block(received, flat(received), 0, own)
            return parts, fresh, nothing(side_shape)

        def start_late():
            side = flat(across(packed[:, :, width:]))
            return norm(x, 0), nothing(pair_shape), side

        payload, pair0, side = either(start_early, start_late)
        fresh = swap(pair0, lowest)
        fresh, side = lax.optimization_barrier((fresh, side))
        received = across(payload)
        side = swap(side, lowest)

        def gather_early():
            result, normed = finish(x, received, 0, 1)
            return normed, nothing(pair_shape), result

        def scatter_late():
            parts, late = block(received, fresh, 0, other)
            return parts, late, nothing(block_shape)

        payload, late_pair, early_x = either(gather_early, scatter_late)
        received = across(payload)

        def scatter_early():
            parts, fresh = block(received, side, 1, other)
            return parts, fresh, nothing(block_shape)

        def gather_late():
            result, normed = finish(x, received, 0, 1)
            return normed, late_pair, result

        payload, pair, late_x = either(scatter_early, gather_late)
        got = swap(pair, lowest)
        received = across(payload)

        def end_early():
            return finish(early_x, received, 1, 0)[0], nothing(pair_shape)

        def end_late():
            parts, late = block(received, got, 1, own)
            return finish(late_x, across(parts), 1, 0)[0], late

        moved, pair1 = either(end_early, end_late)
        return (
            jnp.where(early, early_x, late_x), moved, pair0, got, pair1,
            nothing(side_shape), nothing(side_shape), nothing(bf16(seq * channels, width)), nothing(bf16(*own_in.shape)),
        )

    def other_planes():
        side, mine = lax.optimization_barrier(
            (flat(across(packed[:, :, width:])), own_out[0])
        )
        cut = mine.shape[0] // 2
        streams = [[mine[:cut]], [mine[cut:]], [mine[:cut]], [mine[cut:]]]
        def advance(one, two):
            ahead, behind = lax.optimization_barrier((streams[one][-1], streams[two][-1]))
            streams[one].append(around(ahead, 1))
            streams[two].append(around(behind, -1))

        for hop in range(half):
            advance(0, 3)
            if hop < half - 1:
                advance(1, 2)
        first, second, third, fourth = streams
        pieces = [piece for pair in zip(first[:half], second) for piece in pair]
        pieces += [piece for pair in zip(third[1:], fourth[1:half]) for piece in pair]
        gathered = jnp.concatenate(pieces + [first[half], fourth[half]], axis=0)
        return (
            nothing(block_shape), nothing(block_shape), nothing(pair_shape), nothing(pair_shape),
            nothing(pair_shape), side, swap(side, others), gathered, swap(own_in, others),
        )

    first_out, moved, pair0, got, pair1, side, other_side, gathered, other_in = lax.cond(
        plane == 0, first_plane, other_planes
    )
    gathered_other = swap(gathered)
    other = other_in, own_out
    first_outs, second_outs = [first_out], [moved]
    firsts = [jnp.where(early, pair0, got)]
    seconds = [jnp.where(early, got, pair1)]
    for level in range(1, planes):
        final = level == planes - 1
        x = upward(moved)
        received = either(lambda: across(norm(x, 0)), lambda: nothing(blocks_shape))

        def attend_early():
            attended, fresh = block(received, side, 0, own, True)
            return across(attended), nothing(blocks_shape), fresh

        def gather_late():
            return nothing(att_shape), across(norm(x, 0)), nothing(pair_shape)

        attended, received, pair0 = either(attend_early, gather_late)
        fresh = swap(pair0)

        def next_early():
            result, normed = output(x, attended, gathered, 0, True)
            return nothing(att_shape), across(normed), nothing(pair_shape), result

        def attend_late():
            attended, late = block(received, fresh, 0, other, True)
            return across(attended), nothing(blocks_shape), late, nothing(block_shape)

        attended, received, late_pair, early_x = either(next_early, attend_late)

        def attend_again():
            attended, fresh = block(received, other_side, 1, other, True)
            return across(attended), nothing(blocks_shape), fresh, nothing(block_shape)

        def next_late():
            result, normed = output(x, attended, gathered_other, 0, True)
            return nothing(att_shape), across(normed), late_pair, result

        attended, received, pair, late_x = either(attend_again, next_late)
        got = swap(pair)
        first_outs.append(jnp.where(early, early_x, late_x))
        firsts.append(jnp.where(early, pair0, got))

        def by_plane(values):
            chosen = values[0]
            for at in range(1, level + 1):
                chosen = jnp.where(plane == at, values[at], chosen)
            return chosen

        if final:
            first_cache, second_cache = by_plane(firsts), by_plane(seconds + [got])

        def end_early():
            result = output(early_x, attended, gathered_other, 1)[0]
            if not final:
                return result, nothing(pair_shape)
            caches = jnp.concatenate([*first_cache, *second_cache], axis=1)
            return result, across(apart(caches))

        def end_late():
            if not final:
                attended, late = block(received, got, 1, own, True)
                return output(late_x, across(attended), gathered, 1)[0], late
            attended, late = block(received, got, 1, own, True, (first_cache,))
            late = jnp.where(plane == level, late, second_cache)
            both = jnp.concatenate([flat(attended), *late], axis=1)
            both = across(apart(both))
            return output(late_x, both, gathered, 1)[0], both[:, :, channels:]

        moved, pair1 = either(end_early, end_late)
        second_outs.append(moved)
        seconds.append(jnp.where(early, got, pair1) if not final else None)

    cache = pair1
    mine = by_plane([jnp.where(early, a, b) for a, b in zip(first_outs, second_outs)])
    theirs = swap(by_plane([jnp.where(early, b, a) for a, b in zip(first_outs, second_outs)]))
    block_output = jnp.stack([jnp.where(early, mine, theirs), jnp.where(early, theirs, mine)])
    cache = cache.reshape(seq, rows, 2, 2, channels)
    cache = jnp.transpose(cache, (2, 1, 3, 0, 4)).reshape(2, rows, 2, seq * channels)
    return block_output[None], cache[None]


def solution(mesh):
    in_specs = (
        P(None, "seq", None),
        P("pipe", None),
        P("pipe", None),
        P("pipe", None),
        P("pipe", None, None),
        P("pipe", None, None, "seq"),
        P("pipe", "seq", None),
        P("pipe", None, "seq", None, None),
    )
    out_specs = (P("pipe", None, "seq", None), P("pipe", None, "seq", None, None))
    return jax.shard_map(body, mesh=mesh, in_specs=in_specs, out_specs=out_specs, check_vma=False)
```

```python
import functools
import math

import jax
import jax.numpy as jnp
from jax import lax
from jax.experimental import pallas as pl
from jax.experimental.pallas import tpu as pltpu
from jax.sharding import PartitionSpec as P

AXES = ("pipe", "seq")
VMEM = pl.BlockSpec(memory_space=pltpu.VMEM)
ANY = pl.BlockSpec(memory_space=pl.ANY)
HBM = pl.BlockSpec(memory_space=pltpu.HBM)


def normalise(values, params_ref):
    centered = values - jnp.mean(values, axis=-1, keepdims=True)
    spread = jnp.mean(centered * centered, axis=-1, keepdims=True)
    return (
        centered * lax.rsqrt(spread + 1e-06) * (1.0 + params_ref[1:2, :]) + params_ref[0:1, :]
    ).astype(jnp.bfloat16)


def spread_block(block, buffer, out_ref, sems):
    width = buffer.shape[1]
    buffer[...] = block
    copies = [
        pltpu.make_async_copy(buffer, out_ref.at[shard, :, :width], sems.at[shard])
        for shard in range(out_ref.shape[0])
    ]
    for copy in copies:
        copy.start()
    return copies


def norm_kernel(params_ref, x_ref, out_ref, buffer, sems):
    block = normalise(x_ref[...].astype(jnp.float32), params_ref)
    for copy in spread_block(block, buffer, out_ref, sems):
        copy.wait()


def pack_kernel(params_ref, x_ref, cache_ref, out_ref, buffer, sems, sides, sem):
    count, _, total = sides.shape
    width = x_ref.shape[1]
    channels = total // 2
    block = normalise(x_ref[...].astype(jnp.float32), params_ref)
    copies = spread_block(block, buffer, out_ref, sems)
    for kind in range(2):
        rows = cache_ref[:, kind, :]
        for shard in range(count):
            sides[shard, :, kind * channels : (kind + 1) * channels] = rows[
                :, shard * channels : (shard + 1) * channels
            ]
    copies.append(pltpu.make_async_copy(sides, out_ref.at[:, :, width:], sem))
    copies[-1].start()
    for copy in copies:
        copy.wait()


def attention(head_size, q_ref, kv_ref, far_ref):
    factor = 1.0 / math.sqrt(head_size)
    channels = q_ref.shape[1]
    heads = []
    across = (((1,), (1,)), ((), ()))

    def far_of(kind, start):
        if len(far_ref.shape) == 3:
            return far_ref[kind, :, start : start + head_size]
        return far_ref[:, kind * channels + start : kind * channels + start + head_size]

    for start in range(0, channels, head_size):
        cut = slice(start, start + head_size)
        query = q_ref[:, cut]
        near = lax.dot_general(query, kv_ref[0, :, cut], across, preferred_element_type=jnp.float32)
        far = lax.dot_general(query, far_of(0, start), across, preferred_element_type=jnp.float32)
        near = jnp.exp(near * factor)
        far = jnp.exp(far * factor)
        total = jnp.sum(near, axis=-1, keepdims=True) + jnp.sum(far, axis=-1, keepdims=True)
        near = (near / total).astype(jnp.bfloat16)
        far = (far / total).astype(jnp.bfloat16)
        mixed = jnp.dot(near, kv_ref[1, :, cut], preferred_element_type=jnp.float32)
        mixed = mixed + jnp.dot(far, far_of(1, start), preferred_element_type=jnp.float32)
        heads.append(mixed.astype(jnp.bfloat16))
    return jnp.concatenate(heads, axis=1)


def put_cache(caches, out_ref, offset):
    channels = caches[0].shape[2]
    for patch, cache in enumerate(caches):
        for kind in range(2):
            begin = offset + (2 * patch + kind) * channels
            out_ref[:, begin : begin + channels] = cache[kind]


def cache_kernel(*refs):
    put_cache(refs[:-1], refs[-1], 0)


def block_kernel(
    head_size, planes, gain_ref, in_ref, out_weights_ref, blocks_ref, far_ref, *refs
):
    caches, refs = refs[:-11], refs[-11:]
    out_ref, kv_ref, blocks, far, w_in, w_out, parts, q_ref, in_sems, sems, part_sems = refs
    width = blocks.shape[1]
    channels = w_out.shape[0]
    pieces = in_sems.shape[1]
    depth = width // pieces
    fetch = pltpu.make_async_copy(blocks_ref.at[:, :width], blocks, sems.at[0])
    fetch.start()
    if len(far.shape) == 3:
        fetch_far = pltpu.make_async_copy(far_ref, far, sems.at[2])
    else:
        begin = far_ref.shape[1] - far.shape[1]
        fetch_far = pltpu.make_async_copy(far_ref.at[:, begin:], far, sems.at[2])
    fetch_far.start()

    for part in (1, 2, 0):
        for piece in range(pieces):
            cut = pl.ds(piece * depth, depth)
            pltpu.make_async_copy(
                in_ref.at[part, cut], w_in.at[part, cut], in_sems.at[part, piece]
            ).start()
    pltpu.make_async_copy(out_weights_ref.at[0], w_out, sems.at[1]).start()
    fetch.wait()
    tokens = blocks[...]
    for part in (1, 2, 0):
        for piece in range(pieces):
            cut = pl.ds(piece * depth, depth)
            pltpu.make_async_copy(
                in_ref.at[part, cut], w_in.at[part, cut], in_sems.at[part, piece]
            ).wait()
        projected = jnp.dot(tokens, w_in[part], preferred_element_type=jnp.float32)
        if part == 2:
            kv_ref[1] = projected.astype(jnp.bfloat16)
            continue
        for start in range(0, channels, head_size):
            head = projected[:, start : start + head_size]
            square = jnp.mean(head * head, axis=-1, keepdims=True)
            head = (head * lax.rsqrt(square + 1e-06) * gain_ref[part : part + 1, :]).astype(
                jnp.bfloat16
            )
            if part == 0:
                q_ref[:, start : start + head_size] = head
            else:
                kv_ref[0, :, start : start + head_size] = head

    fetch_far.wait()
    sent = []

    def send(begin, size, sem):
        cut = pl.ds(begin, size)
        sent.append(
            pltpu.make_async_copy(parts.at[:, cut], out_ref.at[:, cut], part_sems.at[sem])
        )
        sent[-1].start()

    steps = part_sems.shape[0] - 1
    if caches:
        last = lax.axis_index("pipe") // 2 == planes - 1
        first, second = caches
        put_cache((first, jnp.where(last, kv_ref[...], second[...])), parts, width)
        send(width, 4 * channels, steps)
    attended = attention(head_size, q_ref, kv_ref, far)
    pltpu.make_async_copy(out_weights_ref.at[0], w_out, sems.at[1]).wait()
    tile = width // steps
    for step in range(steps):
        cut = slice(step * tile, (step + 1) * tile)
        update = jnp.dot(attended, w_out[:, cut], preferred_element_type=jnp.float32)
        parts[:, cut] = update.astype(jnp.bfloat16)
        send(step * tile, tile, step)
    for copy in sent:
        copy.wait()


def finish_kernel(shards, cached, params_ref, next_ref, x_ref, parts_ref, out_ref, *refs):
    parts, part_sems, refs = refs[-2], refs[-1], refs[:-2]
    width = x_ref.shape[1]
    fetches = [
        pltpu.make_async_copy(parts_ref.at[shard, :, :width], parts.at[shard], part_sems.at[shard])
        for shard in range(shards)
    ]
    for fetch in fetches:
        fetch.start()
    if cached:
        cache_ref, caches, cache_sem = refs
        fetch = pltpu.make_async_copy(parts_ref.at[:, :, width:], caches, cache_sem)
        fetch.start()
    update = jnp.zeros(x_ref.shape, jnp.float32)
    for shard in range(shards):
        fetches[shard].wait()
        update = update + parts[shard].astype(jnp.float32)
    result = (x_ref[...].astype(jnp.float32) + params_ref[2:3, :] * update).astype(jnp.bfloat16)
    out_ref[...] = result
    if cached:
        fetch.wait()
        place_cache(caches, cache_ref)
    elif refs:
        blocks_ref, buffer, sems = refs
        block = normalise(result.astype(jnp.float32), next_ref)
        for copy in spread_block(block, buffer, blocks_ref, sems):
            copy.wait()


def place_cache(caches, out_ref):
    channels = caches.shape[2] // 4
    for patch in range(2):
        for shard in range(caches.shape[0]):
            begin = 2 * patch * channels
            sides = [
                caches[shard, :, begin + kind * channels : begin + (kind + 1) * channels].astype(
                    jnp.float32
                )
                for kind in range(2)
            ]
            out_ref[patch, :, :, shard * channels : (shard + 1) * channels] = jnp.stack(
                sides, axis=1
            ).astype(jnp.bfloat16)


def place_kernel(caches_ref, out_ref):
    place_cache(caches_ref, out_ref)


def blank_kernel(*refs):
    pass


def params_of(limit):
    return pltpu.CompilerParams(vmem_limit_bytes=limit << 20)


def body(hidden, mod_shift, mod_scale, mod_gate, norm_gain, input_proj, output_proj, stale_cache):
    sections = lax.axis_size("pipe")
    planes = sections // 2
    seq = lax.axis_size("seq")
    pipe = lax.axis_index("pipe")
    core = lax.rem(pipe, 2)
    plane = pipe // 2
    rows, width = hidden.shape[1:]
    head_size = norm_gain.shape[2]
    channels = input_proj.shape[3]
    tokens = rows * seq
    bf16 = lambda *shape: jax.ShapeDtypeStruct(shape, jnp.bfloat16)

    place = lambda row, position: row * seq + position

    def swap(value):
        pairs = [(place(row, s), place(row ^ 1, s)) for row in range(sections) for s in range(seq)]
        return lax.ppermute(value, AXES, pairs)

    def upward(value, level, side):
        row = 2 * level + side
        return lax.ppermute(value, AXES, [(place(row, s), place(row + 2, s)) for s in range(seq)])

    def across(blocks):
        return lax.all_to_all(blocks, "seq", split_axis=0, concat_axis=0, tiled=True)

    def blank(*shapes):
        return pl.pallas_call(blank_kernel, out_shape=shapes, out_specs=(ANY,) * len(shapes))()

    gains = jnp.pad(norm_gain[0].reshape(1, -1), ((0, 0), (0, width - 2 * head_size)))
    own_params = jnp.concatenate([mod_shift, mod_scale, mod_gate, gains], axis=0)
    own_in = jnp.transpose(input_proj[0], (1, 0, 2))
    own_out = output_proj
    x = lax.dynamic_index_in_dim(hidden, core, 0, keepdims=False)
    spreading = [pltpu.VMEM((rows, width), jnp.bfloat16), pltpu.SemaphoreType.DMA((seq,))]
    packed = pl.pallas_call(
        pack_kernel, out_shape=bf16(seq, rows, width + 2 * channels),
        in_specs=[VMEM] * 3, out_specs=HBM,
        scratch_shapes=spreading + [
            pltpu.VMEM((seq, rows, 2 * channels), jnp.bfloat16), pltpu.SemaphoreType.DMA,
        ],
        compiler_params=params_of(16),
    )(own_params, x, stale_cache[0, 1])

    other_params = swap(own_params)
    own_in, own_out, other_params, packed = lax.optimization_barrier(
        (own_in, own_out, other_params, packed)
    )
    other_in = swap(own_in)
    other_out = swap(own_out)
    own, other = (own_in, own_out), (other_in, other_out)
    params = [jnp.where(core == turn, own_params, other_params) for turn in range(2)]
    gain_rows = [p[3, : 2 * head_size].reshape(2, head_size) for p in params]
    blocks_shape = bf16(seq, rows, width)

    def norm(x, turn):
        return pl.pallas_call(
            norm_kernel, out_shape=blocks_shape, in_specs=[VMEM] * 2, out_specs=HBM,
            scratch_shapes=spreading, compiler_params=params_of(16),
        )(params[turn], x)

    flat = lambda blocks: blocks.reshape(tokens, blocks.shape[2])
    apart = lambda values: values.reshape(seq, rows, values.shape[1])

    def block(blocks, far, turn, weights, caches=()):
        total = width + 2 * channels * len(caches)
        side = (2, tokens, channels) if far.ndim == 3 else (tokens, 2 * channels)
        out, pair = pl.pallas_call(
            functools.partial(block_kernel, head_size, planes),
            out_shape=(bf16(tokens, total), bf16(2, tokens, channels)),
            in_specs=[VMEM] + [HBM] * 2 + [ANY] * 2 + [VMEM] * len(caches),
            out_specs=(HBM, VMEM),
            scratch_shapes=[
                pltpu.VMEM((tokens, width), jnp.bfloat16),
                pltpu.VMEM(side, jnp.bfloat16),
                pltpu.VMEM(own_in.shape, jnp.bfloat16),
                pltpu.VMEM(own_out.shape[1:], jnp.bfloat16),
                pltpu.VMEM((tokens, total), jnp.bfloat16),
                pltpu.VMEM((tokens, channels), jnp.bfloat16),
                pltpu.SemaphoreType.DMA((3, 2)),
                pltpu.SemaphoreType.DMA((3,)),
                pltpu.SemaphoreType.DMA((5,)),
            ],
            compiler_params=params_of(32),
        )(
            gain_rows[turn], *weights, flat(blocks), far, *caches
        )
        return apart(out), pair

    cache_shape = bf16(2, rows, 2, seq * channels)

    def finish(x, parts, turn, onward, cached=False):
        shapes = (bf16(rows, width),) + (blocks_shape,) * onward + (cache_shape,) * cached
        scratch = spreading * onward
        if cached:
            scratch = [
                pltpu.VMEM((seq, rows, 4 * channels), jnp.bfloat16), pltpu.SemaphoreType.DMA,
            ]
        return pl.pallas_call(
            functools.partial(finish_kernel, seq, cached),
            out_shape=shapes, in_specs=[VMEM] * 3 + [ANY],
            out_specs=(VMEM,) + (HBM,) * onward + (VMEM,) * cached,
            scratch_shapes=scratch + [
                pltpu.VMEM((seq, rows, width), jnp.bfloat16), pltpu.SemaphoreType.DMA((seq,)),
            ],
            compiler_params=params_of(16),
        )(params[turn], params[1 - turn], x, parts)

    early = core == 0
    either = lambda on_early, on_late: lax.cond(early, on_early, on_late)

    pair_shape, block_shape = bf16(2, tokens, channels), bf16(rows, width)
    side_shape = bf16(tokens, 2 * channels)

    def first_early():
        received = across(packed)
        side = flat(received)
        parts, fresh = block(received, side, 0, own)
        kept = lax.cond(
            plane == 0, lambda: blank(side_shape)[0], lambda: side[:, width:]
        )
        return parts, fresh, kept

    def first_late():
        side = flat(across(packed[:, :, width:]))
        return norm(x, 0), blank(pair_shape)[0], side

    late_pair = None
    early_x, late_x = x, x
    blocks_out, sources = {}, {}
    for layer in range(sections):
        turn, level = layer % 2, layer // 2
        crossing = layer > 0 and turn == 0

        def early_scatter():
            parts, fresh = block(received, stales[turn], turn, other if turn else own)
            return parts, fresh, blank(block_shape)[0]

        def late_gather():
            old = late_pair if turn else blank(pair_shape)[0]
            if turn == 0:
                return norm(late_x, turn), old, blank(block_shape)[0]
            result, normed = finish(late_x, received, 1 - turn, 1)
            return normed, old, result

        if crossing:
            late_x = either(
                lambda: blank(block_shape)[0], lambda: finish(late_x, received, 1 - turn, 0)[0]
            )
            blocks_out[layer - 1, 1] = late_x
            late_x = upward(late_x, level - 1, 1)
        if layer == 0:
            payload, pair, side = either(first_early, first_late)
            stales = [side, swap(side)]
        else:
            payload, pair, result = either(early_scatter, late_gather)
        if turn:
            late_x = blocks_out[layer - 1, 1] = result
        sources[layer, 0] = pair
        got = swap(pair)
        sources[layer, 2] = got
        received = across(payload)
        if layer == sections - 1:
            break

        crossing = turn == 1

        def early_gather():
            if crossing:
                return norm(early_x, 1 - turn), blank(pair_shape)[0], blank(block_shape)[0]
            result, normed = finish(early_x, received, turn, 1)
            return normed, blank(pair_shape)[0], result

        def late_scatter():
            parts, fresh = block(received, got, turn, own if turn else other)
            return parts, fresh, blank(block_shape)[0]

        if crossing:
            early_x = either(
                lambda: finish(early_x, received, turn, 0)[0], lambda: blank(block_shape)[0]
            )
            blocks_out[layer, 0] = early_x
            early_x = upward(early_x, level, 0)
        payload, late_pair, result = either(early_gather, late_scatter)
        if not crossing:
            early_x = blocks_out[layer, 0] = result
        sources[layer, 1] = late_pair
        if crossing:
            active = pipe == jnp.where(early, 2 * level + 2, 2 * level + 1)
            received = lax.cond(active, across, lambda _: blank(blocks_shape)[0], payload)
        else:
            received = across(payload)

    def by_plane(values):
        chosen = values[0]
        for level in range(1, planes):
            chosen = jnp.where(plane == level, values[level], chosen)
        return chosen

    last = sections - 1
    first_cache = by_plane(
        [jnp.where(early, sources[2 * m, 0], sources[2 * m + 1, 2]) for m in range(planes)]
    )
    second_cache = by_plane(
        [
            jnp.where(early, sources[2 * m + 1, 2], sources[2 * m + 1, int(m < planes - 1)])
            for m in range(planes)
        ]
    )

    def last_early():
        result = finish(early_x, received, last % 2, 0)[0]
        packed = pl.pallas_call(
            cache_kernel, out_shape=bf16(tokens, 4 * channels),
            in_specs=[VMEM] * 2, out_specs=VMEM, compiler_params=params_of(16),
        )(first_cache, second_cache)
        cache = pl.pallas_call(
            place_kernel, out_shape=cache_shape, in_specs=[VMEM], out_specs=VMEM,
            compiler_params=params_of(16),
        )(across(apart(packed)))
        return result, cache

    def last_late():
        parts, _ = block(received, got, last % 2, own if last % 2 else other, (first_cache, second_cache))
        return finish(late_x, across(parts), last % 2, 0, True)

    x, cache = either(last_early, last_late)
    blocks_out[last, 0] = blocks_out[last, 1] = x
    mine = by_plane(
        [jnp.where(early, blocks_out[2 * m, 0], blocks_out[2 * m + 1, 1]) for m in range(planes)]
    )
    theirs = swap(
        by_plane(
            [jnp.where(early, blocks_out[2 * m + 1, 0], blocks_out[2 * m, 1]) for m in range(planes)]
        )
    )
    block_output = jnp.stack([jnp.where(early, mine, theirs), jnp.where(early, theirs, mine)])
    return block_output[None], cache[None]


def solution(mesh):
    in_specs = (
        P(None, "seq", None),
        P("pipe", None),
        P("pipe", None),
        P("pipe", None),
        P("pipe", None, None),
        P("pipe", None, None, "seq"),
        P("pipe", "seq", None),
        P("pipe", None, "seq", None, None),
    )
    out_specs = (P("pipe", None, "seq", None), P("pipe", None, "seq", None, None))
    return jax.shard_map(body, mesh=mesh, in_specs=in_specs, out_specs=out_specs, check_vma=False)
```

```python
import functools
import math

import jax
import jax.numpy as jnp
from jax import lax
from jax.experimental import pallas as pl
from jax.experimental.pallas import tpu as pltpu
from jax.sharding import PartitionSpec as P

AXES = ("pipe", "seq")
VMEM = pl.BlockSpec(memory_space=pltpu.VMEM)
ANY = pl.BlockSpec(memory_space=pl.ANY)
HBM = pl.BlockSpec(memory_space=pltpu.HBM)


def normalise(values, params_ref):
    centered = values - jnp.mean(values, axis=-1, keepdims=True)
    spread = jnp.mean(centered * centered, axis=-1, keepdims=True)
    return (
        centered * lax.rsqrt(spread + 1e-06) * (1.0 + params_ref[1:2, :]) + params_ref[0:1, :]
    ).astype(jnp.bfloat16)


def spread_block(block, buffer, out_ref, sems):
    width = buffer.shape[1]
    buffer[...] = block
    copies = [
        pltpu.make_async_copy(buffer, out_ref.at[shard, :, :width], sems.at[shard])
        for shard in range(out_ref.shape[0])
    ]
    for copy in copies:
        copy.start()
    return copies


def norm_kernel(params_ref, x_ref, out_ref, buffer, sems):
    block = normalise(x_ref[...].astype(jnp.float32), params_ref)
    for copy in spread_block(block, buffer, out_ref, sems):
        copy.wait()


def pack_kernel(params_ref, x_ref, cache_ref, out_ref, buffer, sems, sides, sem):
    count, _, total = sides.shape
    width = x_ref.shape[1]
    channels = total // 2
    block = normalise(x_ref[...].astype(jnp.float32), params_ref)
    copies = spread_block(block, buffer, out_ref, sems)
    for kind in range(2):
        rows = cache_ref[:, kind, :]
        for shard in range(count):
            sides[shard, :, kind * channels : (kind + 1) * channels] = rows[
                :, shard * channels : (shard + 1) * channels
            ]
    copies.append(pltpu.make_async_copy(sides, out_ref.at[:, :, width:], sem))
    copies[-1].start()
    for copy in copies:
        copy.wait()


def attention(head_size, q_ref, kv_ref, far_ref):
    factor = 1.0 / math.sqrt(head_size)
    channels = q_ref.shape[1]
    heads = []
    across = (((1,), (1,)), ((), ()))

    def far_of(kind, start):
        if len(far_ref.shape) == 3:
            return far_ref[kind, :, start : start + head_size]
        return far_ref[:, kind * channels + start : kind * channels + start + head_size]

    for start in range(0, channels, head_size):
        cut = slice(start, start + head_size)
        query = q_ref[:, cut]
        near = lax.dot_general(query, kv_ref[0, :, cut], across, preferred_element_type=jnp.float32)
        far = lax.dot_general(query, far_of(0, start), across, preferred_element_type=jnp.float32)
        near = jnp.exp(near * factor)
        far = jnp.exp(far * factor)
        total = jnp.sum(near, axis=-1, keepdims=True) + jnp.sum(far, axis=-1, keepdims=True)
        near = (near / total).astype(jnp.bfloat16)
        far = (far / total).astype(jnp.bfloat16)
        mixed = jnp.dot(near, kv_ref[1, :, cut], preferred_element_type=jnp.float32)
        mixed = mixed + jnp.dot(far, far_of(1, start), preferred_element_type=jnp.float32)
        heads.append(mixed.astype(jnp.bfloat16))
    return jnp.concatenate(heads, axis=1)


def put_cache(caches, out_ref, offset):
    channels = caches[0].shape[2]
    for patch, cache in enumerate(caches):
        for kind in range(2):
            begin = offset + (2 * patch + kind) * channels
            out_ref[:, begin : begin + channels] = cache[kind]


def cache_kernel(*refs):
    put_cache(refs[:-1], refs[-1], 0)


def block_kernel(
    turn, head_size, planes, gain_ref, own_in, other_in, own_out, other_out, blocks_ref, far_ref, *refs
):
    caches, refs = refs[:-11], refs[-11:]
    out_ref, kv_ref, blocks, far, w_in, w_out, parts, q_ref, in_sems, sems, part_sems = refs
    width = blocks.shape[1]
    channels = w_out.shape[0]
    pieces = in_sems.shape[1]
    depth = width // pieces
    mine = lax.rem(lax.axis_index("pipe"), 2) == turn

    def weight_copies(source_in, source_out):
        for part in (1, 2, 0):
            for piece in range(pieces):
                cut = pl.ds(piece * depth, depth)
                pltpu.make_async_copy(
                    source_in.at[part, cut], w_in.at[part, cut], in_sems.at[part, piece]
                ).start()
        pltpu.make_async_copy(source_out.at[0], w_out, sems.at[1]).start()

    fetch = pltpu.make_async_copy(blocks_ref.at[:, :width], blocks, sems.at[0])
    fetch.start()
    if len(far.shape) == 3:
        fetch_far = pltpu.make_async_copy(far_ref, far, sems.at[2])
    else:
        begin = far_ref.shape[1] - far.shape[1]
        fetch_far = pltpu.make_async_copy(far_ref.at[:, begin:], far, sems.at[2])
    fetch_far.start()

    @pl.when(mine)
    def _():
        weight_copies(own_in, own_out)

    @pl.when(jnp.logical_not(mine))
    def _():
        weight_copies(other_in, other_out)

    fetch.wait()
    tokens = blocks[...]
    for part in (1, 2, 0):
        for piece in range(pieces):
            cut = pl.ds(piece * depth, depth)
            pltpu.make_async_copy(
                own_in.at[part, cut], w_in.at[part, cut], in_sems.at[part, piece]
            ).wait()
        projected = jnp.dot(tokens, w_in[part], preferred_element_type=jnp.float32)
        if part == 2:
            kv_ref[1] = projected.astype(jnp.bfloat16)
            continue
        for start in range(0, channels, head_size):
            head = projected[:, start : start + head_size]
            square = jnp.mean(head * head, axis=-1, keepdims=True)
            head = (head * lax.rsqrt(square + 1e-06) * gain_ref[part : part + 1, :]).astype(
                jnp.bfloat16
            )
            if part == 0:
                q_ref[:, start : start + head_size] = head
            else:
                kv_ref[0, :, start : start + head_size] = head

    fetch_far.wait()
    sent = []

    def send(begin, size, sem):
        cut = pl.ds(begin, size)
        sent.append(
            pltpu.make_async_copy(parts.at[:, cut], out_ref.at[:, cut], part_sems.at[sem])
        )
        sent[-1].start()

    steps = part_sems.shape[0] - 1
    if caches:
        last = lax.axis_index("pipe") // 2 == planes - 1
        first, second = caches
        put_cache((first, jnp.where(last, kv_ref[...], second[...])), parts, width)
        send(width, 4 * channels, steps)
    attended = attention(head_size, q_ref, kv_ref, far)
    pltpu.make_async_copy(own_out.at[0], w_out, sems.at[1]).wait()
    tile = width // steps
    for step in range(steps):
        cut = slice(step * tile, (step + 1) * tile)
        update = jnp.dot(attended, w_out[:, cut], preferred_element_type=jnp.float32)
        parts[:, cut] = update.astype(jnp.bfloat16)
        send(step * tile, tile, step)
    for copy in sent:
        copy.wait()


def finish_kernel(params_ref, next_ref, x_ref, parts_ref, out_ref, *rest):
    width = x_ref.shape[1]
    update = jnp.sum(parts_ref[:, :, :width].astype(jnp.float32), axis=0)
    result = (x_ref[...].astype(jnp.float32) + params_ref[2:3, :] * update).astype(jnp.bfloat16)
    out_ref[...] = result
    if rest:
        blocks_ref, buffer, sems = rest
        block = normalise(result.astype(jnp.float32), next_ref)
        for copy in spread_block(block, buffer, blocks_ref, sems):
            copy.wait()


def blank_kernel(*refs):
    pass


def params_of(limit):
    return pltpu.CompilerParams(vmem_limit_bytes=limit << 20)


def body(hidden, mod_shift, mod_scale, mod_gate, norm_gain, input_proj, output_proj, stale_cache):
    sections = lax.axis_size("pipe")
    planes = sections // 2
    seq = lax.axis_size("seq")
    pipe = lax.axis_index("pipe")
    core = lax.rem(pipe, 2)
    plane = pipe // 2
    rows, width = hidden.shape[1:]
    head_size = norm_gain.shape[2]
    channels = input_proj.shape[3]
    tokens = rows * seq
    bf16 = lambda *shape: jax.ShapeDtypeStruct(shape, jnp.bfloat16)

    place = lambda row, position: row * seq + position

    def swap(value):
        pairs = [(place(row, s), place(row ^ 1, s)) for row in range(sections) for s in range(seq)]
        return lax.ppermute(value, AXES, pairs)

    def upward(value, level, side):
        row = 2 * level + side
        return lax.ppermute(value, AXES, [(place(row, s), place(row + 2, s)) for s in range(seq)])

    def across(blocks):
        return lax.all_to_all(blocks, "seq", split_axis=0, concat_axis=0, tiled=True)

    fast = 1
    while fast * fast * 4 <= seq and seq % (fast * 2) == 0:
        fast *= 2
    columns = [list(range(start, seq, fast)) for start in range(fast)]
    stepwise = fast == 2

    def gather_stepwise(copies):
        ours = lax.all_to_all(
            copies, "seq", split_axis=0, concat_axis=0, tiled=True, axis_index_groups=columns
        )
        pairs = [(place(row, s), place(row, s ^ 1)) for row in range(0, sections, 2) for s in range(seq)]
        theirs = lax.ppermute(ours, AXES, pairs)
        lower = lax.rem(lax.axis_index("seq"), 2) == 0
        both = [jnp.where(lower, ours, theirs), jnp.where(lower, theirs, ours)]
        return jnp.stack(both, axis=1).reshape(seq, rows, width)

    def blank(*shapes):
        return pl.pallas_call(blank_kernel, out_shape=shapes, out_specs=(ANY,) * len(shapes))()

    gains = jnp.pad(norm_gain[0].reshape(1, -1), ((0, 0), (0, width - 2 * head_size)))
    own_params = jnp.concatenate([mod_shift, mod_scale, mod_gate, gains], axis=0)
    own_in = jnp.transpose(input_proj[0], (1, 0, 2))
    own_out = output_proj
    x = lax.dynamic_index_in_dim(hidden, core, 0, keepdims=False)
    spreading = [pltpu.VMEM((rows, width), jnp.bfloat16), pltpu.SemaphoreType.DMA((seq,))]
    packed = pl.pallas_call(
        pack_kernel, out_shape=bf16(seq, rows, width + 2 * channels),
        in_specs=[VMEM] * 3, out_specs=HBM,
        scratch_shapes=spreading + [
            pltpu.VMEM((seq, rows, 2 * channels), jnp.bfloat16), pltpu.SemaphoreType.DMA,
        ],
        compiler_params=params_of(16),
    )(own_params, x, stale_cache[0, 1])

    other_params = swap(own_params)
    own_in, own_out, other_params, packed = lax.optimization_barrier(
        (own_in, own_out, other_params, packed)
    )
    other_in = swap(own_in)
    other_out = swap(own_out)
    params = [jnp.where(core == turn, own_params, other_params) for turn in range(2)]
    gain_rows = [p[3, : 2 * head_size].reshape(2, head_size) for p in params]
    blocks_shape = bf16(seq, rows, width)

    def norm(x, turn):
        return pl.pallas_call(
            norm_kernel, out_shape=blocks_shape, in_specs=[VMEM] * 2, out_specs=HBM,
            scratch_shapes=spreading, compiler_params=params_of(16),
        )(params[turn], x)

    flat = lambda blocks: blocks.reshape(tokens, blocks.shape[2])
    apart = lambda values: values.reshape(seq, rows, values.shape[1])

    def block(blocks, far, turn, caches=()):
        total = width + 2 * channels * len(caches)
        side = (2, tokens, channels) if far.ndim == 3 else (tokens, 2 * channels)
        out, pair = pl.pallas_call(
            functools.partial(block_kernel, turn, head_size, planes),
            out_shape=(bf16(tokens, total), bf16(2, tokens, channels)),
            in_specs=[VMEM] + [HBM] * 4 + [ANY] * 2 + [VMEM] * len(caches),
            out_specs=(HBM, VMEM),
            scratch_shapes=[
                pltpu.VMEM((tokens, width), jnp.bfloat16),
                pltpu.VMEM(side, jnp.bfloat16),
                pltpu.VMEM(own_in.shape, jnp.bfloat16),
                pltpu.VMEM(own_out.shape[1:], jnp.bfloat16),
                pltpu.VMEM((tokens, total), jnp.bfloat16),
                pltpu.VMEM((tokens, channels), jnp.bfloat16),
                pltpu.SemaphoreType.DMA((3, 2)),
                pltpu.SemaphoreType.DMA((3,)),
                pltpu.SemaphoreType.DMA((5,)),
            ],
            compiler_params=params_of(32),
        )(
            gain_rows[turn], own_in, other_in, own_out, other_out, flat(blocks), far, *caches
        )
        return apart(out), pair

    def finish(x, parts, turn, onward, copies=seq):
        shapes = (bf16(rows, width),) + (bf16(copies, rows, width),) * onward
        return pl.pallas_call(
            finish_kernel, out_shape=shapes, in_specs=[VMEM] * 4,
            out_specs=(VMEM,) + (HBM,) * onward,
            scratch_shapes=spreading * onward, compiler_params=params_of(16),
        )(params[turn], params[1 - turn], x, parts)

    early = core == 0
    either = lambda on_early, on_late: lax.cond(early, on_early, on_late)

    def first_early():
        return across(packed), blank(bf16(tokens, 2 * channels))[0]

    def first_late():
        return blank(bf16(*packed.shape))[0], flat(across(packed[:, :, width:]))

    received, stale = either(first_early, first_late)
    stales = [flat(received), swap(stale)]
    pair_shape, block_shape = bf16(2, tokens, channels), bf16(rows, width)
    late_pair = None
    early_x, late_x = x, x
    blocks_out, sources = {}, {}
    for layer in range(sections):
        turn, level = layer % 2, layer // 2
        crossing = layer > 0 and turn == 0

        def early_scatter():
            parts, fresh = block(received, stales[turn], turn)
            return parts, fresh, blank(block_shape)[0]

        def late_gather():
            old = late_pair if turn else blank(pair_shape)[0]
            if turn == 0:
                return norm(late_x, turn), old, blank(block_shape)[0]
            result, normed = finish(late_x, received, 1 - turn, 1)
            return normed, old, result

        if crossing:
            late_x = either(
                lambda: blank(block_shape)[0], lambda: finish(late_x, received, 1 - turn, 0)[0]
            )
            blocks_out[layer - 1, 1] = late_x
            late_x = upward(late_x, level - 1, 1)
        payload, pair, result = either(early_scatter, late_gather)
        if turn:
            late_x = blocks_out[layer - 1, 1] = result
        sources[layer, 0] = pair
        got = swap(pair)
        sources[layer, 2] = got
        received = across(payload)
        if layer == sections - 1:
            break

        crossing = turn == 1

        def early_gather():
            if crossing:
                return norm(early_x, 1 - turn), blank(pair_shape)[0], blank(block_shape)[0]
            if stepwise:
                result, normed = finish(early_x, received, turn, 1, seq // fast)
                return gather_stepwise(normed), blank(pair_shape)[0], result
            result, normed = finish(early_x, received, turn, 1)
            return across(normed), blank(pair_shape)[0], result

        def late_scatter():
            parts, fresh = block(received, got, turn)
            return (parts if crossing else across(parts)), fresh, blank(block_shape)[0]

        if crossing:
            early_x = either(
                lambda: finish(early_x, received, turn, 0)[0], lambda: blank(block_shape)[0]
            )
            blocks_out[layer, 0] = early_x
            early_x = upward(early_x, level, 0)
        payload, late_pair, result = either(early_gather, late_scatter)
        if not crossing:
            early_x = blocks_out[layer, 0] = result
        sources[layer, 1] = late_pair
        if crossing:
            active = pipe == jnp.where(early, 2 * level + 2, 2 * level + 1)
            received = lax.cond(active, across, lambda _: blank(blocks_shape)[0], payload)
        else:
            received = payload

    def by_plane(values):
        chosen = values[0]
        for level in range(1, planes):
            chosen = jnp.where(plane == level, values[level], chosen)
        return chosen

    last = sections - 1
    first_cache = by_plane(
        [jnp.where(early, sources[2 * m, 0], sources[2 * m + 1, 2]) for m in range(planes)]
    )
    second_cache = by_plane(
        [
            jnp.where(early, sources[2 * m + 1, 2], sources[2 * m + 1, int(m < planes - 1)])
            for m in range(planes)
        ]
    )

    def last_early():
        result = finish(early_x, received, last % 2, 0)[0]
        packed = pl.pallas_call(
            cache_kernel, out_shape=bf16(tokens, 4 * channels),
            in_specs=[VMEM] * 2, out_specs=VMEM, compiler_params=params_of(16),
        )(first_cache, second_cache)
        return result, across(apart(packed))

    def last_late():
        parts, _ = block(received, got, last % 2, (first_cache, second_cache))
        parts = across(parts)
        return finish(late_x, parts, last % 2, 0)[0], parts[:, :, width:]

    x, cache = either(last_early, last_late)
    blocks_out[last, 0] = blocks_out[last, 1] = x
    mine = by_plane(
        [jnp.where(early, blocks_out[2 * m, 0], blocks_out[2 * m + 1, 1]) for m in range(planes)]
    )
    theirs = swap(
        by_plane(
            [jnp.where(early, blocks_out[2 * m + 1, 0], blocks_out[2 * m, 1]) for m in range(planes)]
        )
    )
    block_output = jnp.stack([jnp.where(early, mine, theirs), jnp.where(early, theirs, mine)])
    cache = cache.reshape(seq, rows, 2, 2, channels)
    cache = jnp.transpose(cache, (2, 1, 3, 0, 4)).reshape(2, rows, 2, seq * channels)
    return block_output[None], cache[None]


def solution(mesh):
    in_specs = (
        P(None, "seq", None),
        P("pipe", None),
        P("pipe", None),
        P("pipe", None),
        P("pipe", None, None),
        P("pipe", None, None, "seq"),
        P("pipe", "seq", None),
        P("pipe", None, "seq", None, None),
    )
    out_specs = (P("pipe", None, "seq", None), P("pipe", None, "seq", None, None))
    return jax.shard_map(body, mesh=mesh, in_specs=in_specs, out_specs=out_specs, check_vma=False)
```

```python
import functools
import math

import jax
import jax.numpy as jnp
from jax import lax
from jax.experimental import pallas as pl
from jax.experimental.pallas import tpu as pltpu
from jax.sharding import PartitionSpec as P

AXES = ("pipe", "seq")
VMEM = pl.BlockSpec(memory_space=pltpu.VMEM)
ANY = pl.BlockSpec(memory_space=pl.ANY)
HBM = pl.BlockSpec(memory_space=pltpu.HBM)


def normalise(values, params_ref):
    centered = values - jnp.mean(values, axis=-1, keepdims=True)
    spread = jnp.mean(centered * centered, axis=-1, keepdims=True)
    return (
        centered * lax.rsqrt(spread + 1e-06) * (1.0 + params_ref[1:2, :]) + params_ref[0:1, :]
    ).astype(jnp.bfloat16)


def spread_block(block, buffer, out_ref, sems):
    width = buffer.shape[1]
    buffer[...] = block
    copies = [
        pltpu.make_async_copy(buffer, out_ref.at[shard, :, :width], sems.at[shard])
        for shard in range(out_ref.shape[0])
    ]
    for copy in copies:
        copy.start()
    return copies


def norm_kernel(params_ref, x_ref, out_ref, buffer, sems):
    block = normalise(x_ref[...].astype(jnp.float32), params_ref)
    for copy in spread_block(block, buffer, out_ref, sems):
        copy.wait()


def pack_kernel(params_ref, x_ref, cache_ref, out_ref, buffer, sems, sides, sem):
    count, _, total = sides.shape
    width = x_ref.shape[1]
    channels = total // 2
    block = normalise(x_ref[...].astype(jnp.float32), params_ref)
    copies = spread_block(block, buffer, out_ref, sems)
    for kind in range(2):
        rows = cache_ref[:, kind, :]
        for shard in range(count):
            sides[shard, :, kind * channels : (kind + 1) * channels] = rows[
                :, shard * channels : (shard + 1) * channels
            ]
    copies.append(pltpu.make_async_copy(sides, out_ref.at[:, :, width:], sem))
    copies[-1].start()
    for copy in copies:
        copy.wait()


def attention(head_size, q_ref, kv_ref, far_ref):
    factor = 1.0 / math.sqrt(head_size)
    channels = q_ref.shape[1]
    heads = []
    across = (((1,), (1,)), ((), ()))

    def far_of(kind, start):
        if len(far_ref.shape) == 3:
            return far_ref[kind, :, start : start + head_size]
        return far_ref[:, kind * channels + start : kind * channels + start + head_size]

    for start in range(0, channels, head_size):
        cut = slice(start, start + head_size)
        query = q_ref[:, cut]
        near = lax.dot_general(query, kv_ref[0, :, cut], across, preferred_element_type=jnp.float32)
        far = lax.dot_general(query, far_of(0, start), across, preferred_element_type=jnp.float32)
        near = jnp.exp(near * factor)
        far = jnp.exp(far * factor)
        total = jnp.sum(near, axis=-1, keepdims=True) + jnp.sum(far, axis=-1, keepdims=True)
        near = (near / total).astype(jnp.bfloat16)
        far = (far / total).astype(jnp.bfloat16)
        mixed = jnp.dot(near, kv_ref[1, :, cut], preferred_element_type=jnp.float32)
        mixed = mixed + jnp.dot(far, far_of(1, start), preferred_element_type=jnp.float32)
        heads.append(mixed.astype(jnp.bfloat16))
    return jnp.concatenate(heads, axis=1)


def put_cache(caches, out_ref, offset):
    channels = caches[0].shape[2]
    for patch, cache in enumerate(caches):
        for kind in range(2):
            begin = offset + (2 * patch + kind) * channels
            out_ref[:, begin : begin + channels] = cache[kind]


def cache_kernel(*refs):
    put_cache(refs[:-1], refs[-1], 0)


def block_kernel(
    head_size, planes, gain_ref, in_ref, out_weights_ref, blocks_ref, far_ref, *refs
):
    caches, refs = refs[:-11], refs[-11:]
    out_ref, kv_ref, blocks, far, w_in, w_out, parts, q_ref, in_sems, sems, part_sems = refs
    width = blocks.shape[1]
    channels = w_out.shape[0]
    pieces = in_sems.shape[1]
    depth = width // pieces
    fetch = pltpu.make_async_copy(blocks_ref.at[:, :width], blocks, sems.at[0])
    fetch.start()
    if len(far.shape) == 3:
        fetch_far = pltpu.make_async_copy(far_ref, far, sems.at[2])
    else:
        begin = far_ref.shape[1] - far.shape[1]
        fetch_far = pltpu.make_async_copy(far_ref.at[:, begin:], far, sems.at[2])
    fetch_far.start()

    for part in (1, 2, 0):
        for piece in range(pieces):
            cut = pl.ds(piece * depth, depth)
            pltpu.make_async_copy(
                in_ref.at[part, cut], w_in.at[part, cut], in_sems.at[part, piece]
            ).start()
    pltpu.make_async_copy(out_weights_ref.at[0], w_out, sems.at[1]).start()
    fetch.wait()
    tokens = blocks[...]
    for part in (1, 2, 0):
        for piece in range(pieces):
            cut = pl.ds(piece * depth, depth)
            pltpu.make_async_copy(
                in_ref.at[part, cut], w_in.at[part, cut], in_sems.at[part, piece]
            ).wait()
        projected = jnp.dot(tokens, w_in[part], preferred_element_type=jnp.float32)
        if part == 2:
            kv_ref[1] = projected.astype(jnp.bfloat16)
            continue
        for start in range(0, channels, head_size):
            head = projected[:, start : start + head_size]
            square = jnp.mean(head * head, axis=-1, keepdims=True)
            head = (head * lax.rsqrt(square + 1e-06) * gain_ref[part : part + 1, :]).astype(
                jnp.bfloat16
            )
            if part == 0:
                q_ref[:, start : start + head_size] = head
            else:
                kv_ref[0, :, start : start + head_size] = head

    fetch_far.wait()
    sent = []

    def send(begin, size, sem):
        cut = pl.ds(begin, size)
        sent.append(
            pltpu.make_async_copy(parts.at[:, cut], out_ref.at[:, cut], part_sems.at[sem])
        )
        sent[-1].start()

    steps = part_sems.shape[0] - 1
    if caches:
        last = lax.axis_index("pipe") // 2 == planes - 1
        first, second = caches
        put_cache((first, jnp.where(last, kv_ref[...], second[...])), parts, width)
        send(width, 4 * channels, steps)
    attended = attention(head_size, q_ref, kv_ref, far)
    pltpu.make_async_copy(out_weights_ref.at[0], w_out, sems.at[1]).wait()
    tile = width // steps
    for step in range(steps):
        cut = slice(step * tile, (step + 1) * tile)
        update = jnp.dot(attended, w_out[:, cut], preferred_element_type=jnp.float32)
        parts[:, cut] = update.astype(jnp.bfloat16)
        send(step * tile, tile, step)
    for copy in sent:
        copy.wait()


def finish_kernel(params_ref, next_ref, x_ref, parts_ref, out_ref, *rest):
    width = x_ref.shape[1]
    update = jnp.sum(parts_ref[:, :, :width].astype(jnp.float32), axis=0)
    result = (x_ref[...].astype(jnp.float32) + params_ref[2:3, :] * update).astype(jnp.bfloat16)
    out_ref[...] = result
    if rest:
        blocks_ref, buffer, sems = rest
        block = normalise(result.astype(jnp.float32), next_ref)
        for copy in spread_block(block, buffer, blocks_ref, sems):
            copy.wait()


def blank_kernel(*refs):
    pass


def params_of(limit):
    return pltpu.CompilerParams(vmem_limit_bytes=limit << 20)


def body(hidden, mod_shift, mod_scale, mod_gate, norm_gain, input_proj, output_proj, stale_cache):
    sections = lax.axis_size("pipe")
    planes = sections // 2
    seq = lax.axis_size("seq")
    pipe = lax.axis_index("pipe")
    core = lax.rem(pipe, 2)
    plane = pipe // 2
    rows, width = hidden.shape[1:]
    head_size = norm_gain.shape[2]
    channels = input_proj.shape[3]
    tokens = rows * seq
    bf16 = lambda *shape: jax.ShapeDtypeStruct(shape, jnp.bfloat16)

    place = lambda row, position: row * seq + position

    def swap(value):
        pairs = [(place(row, s), place(row ^ 1, s)) for row in range(sections) for s in range(seq)]
        return lax.ppermute(value, AXES, pairs)

    def upward(value, level, side):
        row = 2 * level + side
        return lax.ppermute(value, AXES, [(place(row, s), place(row + 2, s)) for s in range(seq)])

    def across(blocks):
        return lax.all_to_all(blocks, "seq", split_axis=0, concat_axis=0, tiled=True)

    def blank(*shapes):
        return pl.pallas_call(blank_kernel, out_shape=shapes, out_specs=(ANY,) * len(shapes))()

    gains = jnp.pad(norm_gain[0].reshape(1, -1), ((0, 0), (0, width - 2 * head_size)))
    own_params = jnp.concatenate([mod_shift, mod_scale, mod_gate, gains], axis=0)
    own_in = jnp.transpose(input_proj[0], (1, 0, 2))
    own_out = output_proj
    x = lax.dynamic_index_in_dim(hidden, core, 0, keepdims=False)
    spreading = [pltpu.VMEM((rows, width), jnp.bfloat16), pltpu.SemaphoreType.DMA((seq,))]
    packed = pl.pallas_call(
        pack_kernel, out_shape=bf16(seq, rows, width + 2 * channels),
        in_specs=[VMEM] * 3, out_specs=HBM,
        scratch_shapes=spreading + [
            pltpu.VMEM((seq, rows, 2 * channels), jnp.bfloat16), pltpu.SemaphoreType.DMA,
        ],
        compiler_params=params_of(16),
    )(own_params, x, stale_cache[0, 1])

    other_params = swap(own_params)
    own_in, own_out, other_params, packed = lax.optimization_barrier(
        (own_in, own_out, other_params, packed)
    )
    other_in = swap(own_in)
    other_out = swap(own_out)
    own, other = (own_in, own_out), (other_in, other_out)
    params = [jnp.where(core == turn, own_params, other_params) for turn in range(2)]
    gain_rows = [p[3, : 2 * head_size].reshape(2, head_size) for p in params]
    blocks_shape = bf16(seq, rows, width)

    def norm(x, turn):
        return pl.pallas_call(
            norm_kernel, out_shape=blocks_shape, in_specs=[VMEM] * 2, out_specs=HBM,
            scratch_shapes=spreading, compiler_params=params_of(16),
        )(params[turn], x)

    flat = lambda blocks: blocks.reshape(tokens, blocks.shape[2])
    apart = lambda values: values.reshape(seq, rows, values.shape[1])

    def block(blocks, far, turn, weights, caches=()):
        total = width + 2 * channels * len(caches)
        side = (2, tokens, channels) if far.ndim == 3 else (tokens, 2 * channels)
        out, pair = pl.pallas_call(
            functools.partial(block_kernel, head_size, planes),
            out_shape=(bf16(tokens, total), bf16(2, tokens, channels)),
            in_specs=[VMEM] + [HBM] * 2 + [ANY] * 2 + [VMEM] * len(caches),
            out_specs=(HBM, VMEM),
            scratch_shapes=[
                pltpu.VMEM((tokens, width), jnp.bfloat16),
                pltpu.VMEM(side, jnp.bfloat16),
                pltpu.VMEM(own_in.shape, jnp.bfloat16),
                pltpu.VMEM(own_out.shape[1:], jnp.bfloat16),
                pltpu.VMEM((tokens, total), jnp.bfloat16),
                pltpu.VMEM((tokens, channels), jnp.bfloat16),
                pltpu.SemaphoreType.DMA((3, 2)),
                pltpu.SemaphoreType.DMA((3,)),
                pltpu.SemaphoreType.DMA((5,)),
            ],
            compiler_params=params_of(32),
        )(
            gain_rows[turn], *weights, flat(blocks), far, *caches
        )
        return apart(out), pair

    def finish(x, parts, turn, onward):
        shapes = (bf16(rows, width),) + (blocks_shape,) * onward
        return pl.pallas_call(
            finish_kernel, out_shape=shapes, in_specs=[VMEM] * 4,
            out_specs=(VMEM,) + (HBM,) * onward,
            scratch_shapes=spreading * onward, compiler_params=params_of(16),
        )(params[turn], params[1 - turn], x, parts)

    early = core == 0
    either = lambda on_early, on_late: lax.cond(early, on_early, on_late)

    pair_shape, block_shape = bf16(2, tokens, channels), bf16(rows, width)
    side_shape = bf16(tokens, 2 * channels)

    def first_early():
        received = across(packed)
        side = flat(received)
        parts, fresh = block(received, side, 0, own)
        kept = lax.cond(plane == 0, lambda: blank(side_shape)[0], lambda: side[:, width:])
        return parts, fresh, kept

    def first_late():
        side = flat(across(packed[:, :, width:]))
        blocks, side = lax.optimization_barrier((norm(x, 0), side))
        return across(blocks), blank(pair_shape)[0], side

    gathered, pair, side = either(first_early, first_late)
    late_pair = None
    early_x, late_x = x, x
    blocks_out, sources = {}, {}
    for layer in range(sections):
        turn, level = layer % 2, layer // 2
        crossing = layer > 0 and turn == 0

        def early_scatter():
            parts, fresh = block(received, stales[turn], turn, other if turn else own)
            return parts, fresh, blank(block_shape)[0]

        def late_gather():
            old = late_pair if turn else blank(pair_shape)[0]
            if turn == 0:
                return norm(late_x, turn), old, blank(block_shape)[0]
            result, normed = finish(late_x, received, 1 - turn, 1)
            return normed, old, result

        if crossing:
            late_x = either(
                lambda: blank(block_shape)[0], lambda: finish(late_x, received, 1 - turn, 0)[0]
            )
            blocks_out[layer - 1, 1] = late_x
            late_x = upward(late_x, level - 1, 1)
        if layer:
            payload, pair, result = either(early_scatter, late_gather)
        if turn:
            late_x = blocks_out[layer - 1, 1] = result
        sources[layer, 0] = pair
        got = swap(pair)
        sources[layer, 2] = got
        if layer:
            received = across(payload)
        else:
            gathered, got, side = lax.optimization_barrier((gathered, got, side))
            stales = [side, swap(side)]
            received = either(lambda: across(gathered), lambda: blank(blocks_shape)[0])
        if layer == sections - 1:
            break

        crossing = turn == 1

        def early_gather():
            if crossing:
                return norm(early_x, 1 - turn), blank(pair_shape)[0], blank(block_shape)[0]
            result, normed = finish(early_x, received, turn, 1)
            return normed, blank(pair_shape)[0], result

        def late_scatter():
            parts, fresh = block(gathered if layer == 0 else received, got, turn, own if turn else other)
            return parts, fresh, blank(block_shape)[0]

        if crossing:
            early_x = either(
                lambda: finish(early_x, received, turn, 0)[0], lambda: blank(block_shape)[0]
            )
            blocks_out[layer, 0] = early_x
            early_x = upward(early_x, level, 0)
        payload, late_pair, result = either(early_gather, late_scatter)
        if not crossing:
            early_x = blocks_out[layer, 0] = result
        sources[layer, 1] = late_pair
        if crossing:
            active = pipe == jnp.where(early, 2 * level + 2, 2 * level + 1)
            received = lax.cond(active, across, lambda _: blank(blocks_shape)[0], payload)
        else:
            received = across(payload)

    def by_plane(values):
        chosen = values[0]
        for level in range(1, planes):
            chosen = jnp.where(plane == level, values[level], chosen)
        return chosen

    last = sections - 1
    first_cache = by_plane(
        [jnp.where(early, sources[2 * m, 0], sources[2 * m + 1, 2]) for m in range(planes)]
    )
    second_cache = by_plane(
        [
            jnp.where(early, sources[2 * m + 1, 2], sources[2 * m + 1, int(m < planes - 1)])
            for m in range(planes)
        ]
    )

    def last_early():
        result = finish(early_x, received, last % 2, 0)[0]
        packed = pl.pallas_call(
            cache_kernel, out_shape=bf16(tokens, 4 * channels),
            in_specs=[VMEM] * 2, out_specs=VMEM, compiler_params=params_of(16),
        )(first_cache, second_cache)
        return result, across(apart(packed))

    def last_late():
        parts, _ = block(received, got, last % 2, own if last % 2 else other, (first_cache, second_cache))
        parts = across(parts)
        return finish(late_x, parts, last % 2, 0)[0], parts[:, :, width:]

    x, cache = either(last_early, last_late)
    blocks_out[last, 0] = blocks_out[last, 1] = x
    mine = by_plane(
        [jnp.where(early, blocks_out[2 * m, 0], blocks_out[2 * m + 1, 1]) for m in range(planes)]
    )
    theirs = swap(
        by_plane(
            [jnp.where(early, blocks_out[2 * m + 1, 0], blocks_out[2 * m, 1]) for m in range(planes)]
        )
    )
    block_output = jnp.stack([jnp.where(early, mine, theirs), jnp.where(early, theirs, mine)])
    cache = cache.reshape(seq, rows, 2, 2, channels)
    cache = jnp.transpose(cache, (2, 1, 3, 0, 4)).reshape(2, rows, 2, seq * channels)
    return block_output[None], cache[None]


def solution(mesh):
    in_specs = (
        P(None, "seq", None),
        P("pipe", None),
        P("pipe", None),
        P("pipe", None),
        P("pipe", None, None),
        P("pipe", None, None, "seq"),
        P("pipe", "seq", None),
        P("pipe", None, "seq", None, None),
    )
    out_specs = (P("pipe", None, "seq", None), P("pipe", None, "seq", None, None))
    return jax.shard_map(body, mesh=mesh, in_specs=in_specs, out_specs=out_specs, check_vma=False)
```

```python
import functools
import math

import jax
import jax.numpy as jnp
from jax import lax
from jax.experimental import pallas as pl
from jax.experimental.pallas import tpu as pltpu
from jax.sharding import PartitionSpec as P

AXES = ("pipe", "seq")
VMEM = pl.BlockSpec(memory_space=pltpu.VMEM)
ANY = pl.BlockSpec(memory_space=pl.ANY)
HBM = pl.BlockSpec(memory_space=pltpu.HBM)


def normalise(values, params_ref):
    return normalise_by(values, params_ref[0:1, :], params_ref[1:2, :])


def normalise_by(values, shift_row, scale_row):
    centered = values - jnp.mean(values, axis=-1, keepdims=True)
    spread = jnp.mean(centered * centered, axis=-1, keepdims=True)
    return (centered * lax.rsqrt(spread + 1e-06) * (1.0 + scale_row) + shift_row).astype(
        jnp.bfloat16
    )


def spread_block(block, buffer, out_ref, sems):
    width = buffer.shape[1]
    buffer[...] = block
    copies = [
        pltpu.make_async_copy(buffer, out_ref.at[shard, :, :width], sems.at[shard])
        for shard in range(out_ref.shape[0])
    ]
    for copy in copies:
        copy.start()
    return copies


def norm_kernel(params_ref, x_ref, out_ref, buffer, sems):
    block = normalise(x_ref[...].astype(jnp.float32), params_ref)
    for copy in spread_block(block, buffer, out_ref, sems):
        copy.wait()


def pack_kernel(shift_ref, scale_ref, hidden_ref, stale_ref, out_ref, buffer, sems, sides, sem, cache, cache_sem):
    fetch = pltpu.make_async_copy(stale_ref.at[0, 1], cache, cache_sem)
    fetch.start()
    count, _, total = sides.shape
    width = hidden_ref.shape[2]
    channels = total // 2
    early = lax.rem(lax.axis_index("pipe"), 2) == 0
    x = jnp.where(
        early, hidden_ref[0].astype(jnp.float32), hidden_ref[1].astype(jnp.float32)
    )
    block = normalise_by(x, shift_ref[...], scale_ref[...])
    copies = spread_block(block, buffer, out_ref, sems)
    fetch.wait()
    for kind in range(2):
        rows = cache[:, kind, :]
        for shard in range(count):
            sides[shard, :, kind * channels : (kind + 1) * channels] = rows[
                :, shard * channels : (shard + 1) * channels
            ]
    copies.append(pltpu.make_async_copy(sides, out_ref.at[:, :, width:], sem))
    copies[-1].start()
    for copy in copies:
        copy.wait()


def attention(head_size, q_ref, kv_ref, far_ref):
    factor = 1.0 / math.sqrt(head_size)
    channels = q_ref.shape[1]
    heads = []
    across = (((1,), (1,)), ((), ()))

    def far_of(kind, start):
        if len(far_ref.shape) == 3:
            return far_ref[kind, :, start : start + head_size]
        return far_ref[:, kind * channels + start : kind * channels + start + head_size]

    for start in range(0, channels, head_size):
        cut = slice(start, start + head_size)
        query = q_ref[:, cut]
        near = lax.dot_general(query, kv_ref[0, :, cut], across, preferred_element_type=jnp.float32)
        far = lax.dot_general(query, far_of(0, start), across, preferred_element_type=jnp.float32)
        near = jnp.exp(near * factor)
        far = jnp.exp(far * factor)
        total = jnp.sum(near, axis=-1, keepdims=True) + jnp.sum(far, axis=-1, keepdims=True)
        near = (near / total).astype(jnp.bfloat16)
        far = (far / total).astype(jnp.bfloat16)
        mixed = jnp.dot(near, kv_ref[1, :, cut], preferred_element_type=jnp.float32)
        mixed = mixed + jnp.dot(far, far_of(1, start), preferred_element_type=jnp.float32)
        heads.append(mixed.astype(jnp.bfloat16))
    return jnp.concatenate(heads, axis=1)


def put_cache(caches, out_ref, offset):
    channels = caches[0].shape[2]
    for patch, cache in enumerate(caches):
        for kind in range(2):
            begin = offset + (2 * patch + kind) * channels
            out_ref[:, begin : begin + channels] = cache[kind]


def cache_kernel(*refs):
    put_cache(refs[:-1], refs[-1], 0)


def block_kernel(
    turn, head_size, planes, gain_ref, own_in, other_in, own_out, other_out, blocks_ref, far_ref, *refs
):
    caches, refs = refs[:-11], refs[-11:]
    out_ref, kv_ref, blocks, far, w_in, w_out, parts, q_ref, in_sems, sems, part_sems = refs
    width = blocks.shape[1]
    channels = w_out.shape[0]
    pieces = in_sems.shape[1]
    depth = width // pieces
    mine = lax.rem(lax.axis_index("pipe"), 2) == turn

    def weight_copies(source_in, source_out):
        for part in (1, 2, 0):
            for piece in range(pieces):
                cut = pl.ds(piece * depth, depth)
                pltpu.make_async_copy(
                    source_in.at[part, cut], w_in.at[part, cut], in_sems.at[part, piece]
                ).start()
        pltpu.make_async_copy(source_out.at[0], w_out, sems.at[1]).start()

    fetch = pltpu.make_async_copy(blocks_ref.at[:, :width], blocks, sems.at[0])
    fetch.start()
    if len(far.shape) == 3:
        fetch_far = pltpu.make_async_copy(far_ref, far, sems.at[2])
    else:
        begin = far_ref.shape[1] - far.shape[1]
        fetch_far = pltpu.make_async_copy(far_ref.at[:, begin:], far, sems.at[2])
    fetch_far.start()

    @pl.when(mine)
    def _():
        weight_copies(own_in, own_out)

    @pl.when(jnp.logical_not(mine))
    def _():
        weight_copies(other_in, other_out)

    fetch.wait()
    tokens = blocks[...]
    for part in (1, 2, 0):
        for piece in range(pieces):
            cut = pl.ds(piece * depth, depth)
            pltpu.make_async_copy(
                own_in.at[part, cut], w_in.at[part, cut], in_sems.at[part, piece]
            ).wait()
        projected = jnp.dot(tokens, w_in[part], preferred_element_type=jnp.float32)
        if part == 2:
            kv_ref[1] = projected.astype(jnp.bfloat16)
            continue
        for start in range(0, channels, head_size):
            head = projected[:, start : start + head_size]
            square = jnp.mean(head * head, axis=-1, keepdims=True)
            head = (head * lax.rsqrt(square + 1e-06) * gain_ref[part : part + 1, :]).astype(
                jnp.bfloat16
            )
            if part == 0:
                q_ref[:, start : start + head_size] = head
            else:
                kv_ref[0, :, start : start + head_size] = head

    fetch_far.wait()
    sent = []

    def send(begin, size, sem):
        cut = pl.ds(begin, size)
        sent.append(
            pltpu.make_async_copy(parts.at[:, cut], out_ref.at[:, cut], part_sems.at[sem])
        )
        sent[-1].start()

    steps = part_sems.shape[0] - 1
    if caches:
        last = lax.axis_index("pipe") // 2 == planes - 1
        first, second = caches
        put_cache((first, jnp.where(last, kv_ref[...], second[...])), parts, width)
        send(width, 4 * channels, steps)
    attended = attention(head_size, q_ref, kv_ref, far)
    pltpu.make_async_copy(own_out.at[0], w_out, sems.at[1]).wait()
    tile = width // steps
    for step in range(steps):
        cut = slice(step * tile, (step + 1) * tile)
        update = jnp.dot(attended, w_out[:, cut], preferred_element_type=jnp.float32)
        parts[:, cut] = update.astype(jnp.bfloat16)
        send(step * tile, tile, step)
    for copy in sent:
        copy.wait()


def place_cache(caches, out_ref, offset):
    channels = (caches.shape[2] - offset) // 4
    for patch in range(2):
        for shard in range(caches.shape[0]):
            begin = offset + 2 * patch * channels
            sides = [
                caches[shard, :, begin + kind * channels : begin + (kind + 1) * channels].astype(
                    jnp.float32
                )
                for kind in range(2)
            ]
            out_ref[patch, :, :, shard * channels : (shard + 1) * channels] = jnp.stack(
                sides, axis=1
            ).astype(jnp.bfloat16)


def place_kernel(caches_ref, out_ref):
    place_cache(caches_ref, out_ref, 0)


def last_kernel(params_ref, x_ref, parts_ref, out_ref, cache_ref):
    width = x_ref.shape[1]
    update = jnp.sum(parts_ref[:, :, :width].astype(jnp.float32), axis=0)
    out_ref[...] = (x_ref[...].astype(jnp.float32) + params_ref[2:3, :] * update).astype(
        jnp.bfloat16
    )
    place_cache(parts_ref, cache_ref, width)


def pair_kernel(mine_ref, theirs_ref, out_ref):
    mine, theirs = mine_ref[...], theirs_ref[...]
    early = lax.rem(lax.axis_index("pipe"), 2) == 0
    out_ref[0] = jnp.where(early, mine, theirs)
    out_ref[1] = jnp.where(early, theirs, mine)


def finish_kernel(params_ref, next_ref, x_ref, parts_ref, out_ref, *rest):
    width = x_ref.shape[1]
    update = jnp.sum(parts_ref[:, :, :width].astype(jnp.float32), axis=0)
    result = (x_ref[...].astype(jnp.float32) + params_ref[2:3, :] * update).astype(jnp.bfloat16)
    out_ref[...] = result
    if rest:
        blocks_ref, buffer, sems = rest
        block = normalise(result.astype(jnp.float32), next_ref)
        for copy in spread_block(block, buffer, blocks_ref, sems):
            copy.wait()


def blank_kernel(*refs):
    pass


def params_of(limit):
    return pltpu.CompilerParams(vmem_limit_bytes=limit << 20)


def body(hidden, mod_shift, mod_scale, mod_gate, norm_gain, input_proj, output_proj, stale_cache):
    sections = lax.axis_size("pipe")
    planes = sections // 2
    seq = lax.axis_size("seq")
    pipe = lax.axis_index("pipe")
    core = lax.rem(pipe, 2)
    plane = pipe // 2
    rows, width = hidden.shape[1:]
    head_size = norm_gain.shape[2]
    channels = input_proj.shape[3]
    tokens = rows * seq
    bf16 = lambda *shape: jax.ShapeDtypeStruct(shape, jnp.bfloat16)

    place = lambda row, position: row * seq + position

    def swap(value):
        pairs = [(place(row, s), place(row ^ 1, s)) for row in range(sections) for s in range(seq)]
        return lax.ppermute(value, AXES, pairs)

    def upward(value, level, side):
        row = 2 * level + side
        return lax.ppermute(value, AXES, [(place(row, s), place(row + 2, s)) for s in range(seq)])

    def across(blocks):
        return lax.all_to_all(blocks, "seq", split_axis=0, concat_axis=0, tiled=True)

    def blank(*shapes):
        return pl.pallas_call(blank_kernel, out_shape=shapes, out_specs=(ANY,) * len(shapes))()

    gains = jnp.pad(norm_gain[0].reshape(1, -1), ((0, 0), (0, width - 2 * head_size)))
    own_params = jnp.concatenate([mod_shift, mod_scale, mod_gate, gains], axis=0)
    own_in = jnp.transpose(input_proj[0], (1, 0, 2))
    own_out = output_proj
    x = lax.dynamic_index_in_dim(hidden, core, 0, keepdims=False)
    spreading = [pltpu.VMEM((rows, width), jnp.bfloat16), pltpu.SemaphoreType.DMA((seq,))]
    packed = pl.pallas_call(
        pack_kernel, out_shape=bf16(seq, rows, width + 2 * channels),
        in_specs=[VMEM] * 3 + [ANY], out_specs=HBM,
        scratch_shapes=spreading + [
            pltpu.VMEM((seq, rows, 2 * channels), jnp.bfloat16), pltpu.SemaphoreType.DMA,
            pltpu.VMEM(stale_cache.shape[2:], jnp.bfloat16), pltpu.SemaphoreType.DMA,
        ],
        compiler_params=params_of(16),
    )(mod_shift, mod_scale, hidden, stale_cache)

    other_params = swap(own_params)
    own_in, own_out, other_params, packed = lax.optimization_barrier(
        (own_in, own_out, other_params, packed)
    )
    other_in = swap(own_in)
    other_out = swap(own_out)
    params = [jnp.where(core == turn, own_params, other_params) for turn in range(2)]
    gain_rows = [p[3, : 2 * head_size].reshape(2, head_size) for p in params]
    blocks_shape = bf16(seq, rows, width)

    def norm(x, turn):
        return pl.pallas_call(
            norm_kernel, out_shape=blocks_shape, in_specs=[VMEM] * 2, out_specs=HBM,
            scratch_shapes=spreading, compiler_params=params_of(16),
        )(params[turn], x)

    flat = lambda blocks: blocks.reshape(tokens, blocks.shape[2])
    apart = lambda values: values.reshape(seq, rows, values.shape[1])

    def block(blocks, far, turn, caches=()):
        total = width + 2 * channels * len(caches)
        side = (2, tokens, channels) if far.ndim == 3 else (tokens, 2 * channels)
        out, pair = pl.pallas_call(
            functools.partial(block_kernel, turn, head_size, planes),
            out_shape=(bf16(tokens, total), bf16(2, tokens, channels)),
            in_specs=[VMEM] + [HBM] * 4 + [ANY] * 2 + [VMEM] * len(caches),
            out_specs=(HBM, VMEM),
            scratch_shapes=[
                pltpu.VMEM((tokens, width), jnp.bfloat16),
                pltpu.VMEM(side, jnp.bfloat16),
                pltpu.VMEM(own_in.shape, jnp.bfloat16),
                pltpu.VMEM(own_out.shape[1:], jnp.bfloat16),
                pltpu.VMEM((tokens, total), jnp.bfloat16),
                pltpu.VMEM((tokens, channels), jnp.bfloat16),
                pltpu.SemaphoreType.DMA((3, 2)),
                pltpu.SemaphoreType.DMA((3,)),
                pltpu.SemaphoreType.DMA((5,)),
            ],
            compiler_params=params_of(32),
        )(
            gain_rows[turn], own_in, other_in, own_out, other_out, flat(blocks), far, *caches
        )
        return apart(out), pair

    def finish(x, parts, turn, onward):
        shapes = (bf16(rows, width),) + (blocks_shape,) * onward
        return pl.pallas_call(
            finish_kernel, out_shape=shapes, in_specs=[VMEM] * 4,
            out_specs=(VMEM,) + (HBM,) * onward,
            scratch_shapes=spreading * onward, compiler_params=params_of(16),
        )(params[turn], params[1 - turn], x, parts)

    early = core == 0
    either = lambda on_early, on_late: lax.cond(early, on_early, on_late)

    def first_early():
        return across(packed), blank(bf16(tokens, 2 * channels))[0]

    def first_late():
        return blank(bf16(*packed.shape))[0], flat(across(packed[:, :, width:]))

    received, stale = either(first_early, first_late)
    stales = [flat(received), swap(stale)]
    pair_shape, block_shape = bf16(2, tokens, channels), bf16(rows, width)
    late_pair = None
    early_x, late_x = x, x
    blocks_out, sources = {}, {}
    for layer in range(sections):
        turn, level = layer % 2, layer // 2
        crossing = layer > 0 and turn == 0

        def early_scatter():
            parts, fresh = block(received, stales[turn], turn)
            return parts, fresh, blank(block_shape)[0]

        def late_gather():
            old = late_pair if turn else blank(pair_shape)[0]
            if turn == 0:
                return norm(late_x, turn), old, blank(block_shape)[0]
            result, normed = finish(late_x, received, 1 - turn, 1)
            return normed, old, result

        if crossing:
            late_x = either(
                lambda: blank(block_shape)[0], lambda: finish(late_x, received, 1 - turn, 0)[0]
            )
            blocks_out[layer - 1, 1] = late_x
            late_x = upward(late_x, level - 1, 1)
        payload, pair, result = either(early_scatter, late_gather)
        if turn:
            late_x = blocks_out[layer - 1, 1] = result
        sources[layer, 0] = pair
        got = swap(pair)
        sources[layer, 2] = got
        received = across(payload)
        if layer == sections - 1:
            break

        crossing = turn == 1

        def early_gather():
            if crossing:
                return norm(early_x, 1 - turn), blank(pair_shape)[0], blank(block_shape)[0]
            result, normed = finish(early_x, received, turn, 1)
            return normed, blank(pair_shape)[0], result

        def late_scatter():
            parts, fresh = block(received, got, turn)
            return parts, fresh, blank(block_shape)[0]

        if crossing:
            early_x = either(
                lambda: finish(early_x, received, turn, 0)[0], lambda: blank(block_shape)[0]
            )
            blocks_out[layer, 0] = early_x
            early_x = upward(early_x, level, 0)
        payload, late_pair, result = either(early_gather, late_scatter)
        if not crossing:
            early_x = blocks_out[layer, 0] = result
        sources[layer, 1] = late_pair
        if crossing:
            active = pipe == jnp.where(early, 2 * level + 2, 2 * level + 1)
            received = lax.cond(active, across, lambda _: blank(blocks_shape)[0], payload)
        else:
            received = across(payload)

    def by_plane(values):
        chosen = values[0]
        for level in range(1, planes):
            chosen = jnp.where(plane == level, values[level], chosen)
        return chosen

    last = sections - 1
    first_cache = by_plane(
        [jnp.where(early, sources[2 * m, 0], sources[2 * m + 1, 2]) for m in range(planes)]
    )
    second_cache = by_plane(
        [
            jnp.where(early, sources[2 * m + 1, 2], sources[2 * m + 1, int(m < planes - 1)])
            for m in range(planes)
        ]
    )

    cache_shape = bf16(2, rows, 2, seq * channels)

    def last_early():
        result = finish(early_x, received, last % 2, 0)[0]
        packed = pl.pallas_call(
            cache_kernel, out_shape=bf16(tokens, 4 * channels),
            in_specs=[VMEM] * 2, out_specs=VMEM, compiler_params=params_of(16),
        )(first_cache, second_cache)
        cache = pl.pallas_call(
            place_kernel, out_shape=cache_shape, in_specs=[VMEM], out_specs=VMEM,
            compiler_params=params_of(16),
        )(across(apart(packed)))
        return result, cache

    def last_late():
        parts, _ = block(received, got, last % 2, (first_cache, second_cache))
        return tuple(
            pl.pallas_call(
                last_kernel, out_shape=(block_shape, cache_shape),
                in_specs=[VMEM] * 3, out_specs=(VMEM,) * 2, compiler_params=params_of(16),
            )(params[last % 2], late_x, across(parts))
        )

    x, cache = either(last_early, last_late)
    blocks_out[last, 0] = blocks_out[last, 1] = x
    mine = by_plane(
        [jnp.where(early, blocks_out[2 * m, 0], blocks_out[2 * m + 1, 1]) for m in range(planes)]
    )
    theirs = swap(
        by_plane(
            [jnp.where(early, blocks_out[2 * m + 1, 0], blocks_out[2 * m, 1]) for m in range(planes)]
        )
    )
    block_output = pl.pallas_call(
        pair_kernel, out_shape=bf16(2, rows, width), in_specs=[VMEM] * 2, out_specs=VMEM,
        compiler_params=params_of(16),
    )(mine, theirs)
    return block_output[None], cache[None]


def solution(mesh):
    in_specs = (
        P(None, "seq", None),
        P("pipe", None),
        P("pipe", None),
        P("pipe", None),
        P("pipe", None, None),
        P("pipe", None, None, "seq"),
        P("pipe", "seq", None),
        P("pipe", None, "seq", None, None),
    )
    out_specs = (P("pipe", None, "seq", None), P("pipe", None, "seq", None, None))
    return jax.shard_map(body, mesh=mesh, in_specs=in_specs, out_specs=out_specs, check_vma=False)
```

```python
import functools
import math

import jax
import jax.numpy as jnp
from jax import lax
from jax.experimental import pallas as pl
from jax.experimental.pallas import tpu as pltpu
from jax.sharding import PartitionSpec as P

AXES = ("pipe", "seq")
VMEM = pl.BlockSpec(memory_space=pltpu.VMEM)
ANY = pl.BlockSpec(memory_space=pl.ANY)
HBM = pl.BlockSpec(memory_space=pltpu.HBM)


def normalise(values, params_ref):
    centered = values - jnp.mean(values, axis=-1, keepdims=True)
    spread = jnp.mean(centered * centered, axis=-1, keepdims=True)
    return (
        centered * lax.rsqrt(spread + 1e-06) * (1.0 + params_ref[1:2, :]) + params_ref[0:1, :]
    ).astype(jnp.bfloat16)


def spread_block(block, buffer, out_ref, sems):
    width = buffer.shape[1]
    buffer[...] = block
    copies = [
        pltpu.make_async_copy(buffer, out_ref.at[shard, :, :width], sems.at[shard])
        for shard in range(out_ref.shape[0])
    ]
    for copy in copies:
        copy.start()
    return copies


def norm_kernel(params_ref, x_ref, out_ref, buffer, sems):
    block = normalise(x_ref[...].astype(jnp.float32), params_ref)
    for copy in spread_block(block, buffer, out_ref, sems):
        copy.wait()


def pack_kernel(params_ref, x_ref, cache_ref, out_ref, buffer, sems, sides, sem):
    count, _, total = sides.shape
    width = x_ref.shape[1]
    channels = total // 2
    block = normalise(x_ref[...].astype(jnp.float32), params_ref)
    copies = spread_block(block, buffer, out_ref, sems)
    for kind in range(2):
        rows = cache_ref[:, kind, :]
        for shard in range(count):
            sides[shard, :, kind * channels : (kind + 1) * channels] = rows[
                :, shard * channels : (shard + 1) * channels
            ]
    copies.append(pltpu.make_async_copy(sides, out_ref.at[:, :, width:], sem))
    copies[-1].start()
    for copy in copies:
        copy.wait()


def attention(head_size, q_ref, kv_ref, far_ref):
    factor = 1.0 / math.sqrt(head_size)
    channels = q_ref.shape[1]
    heads = []
    across = (((1,), (1,)), ((), ()))

    def far_of(kind, start):
        if len(far_ref.shape) == 3:
            return far_ref[kind, :, start : start + head_size]
        return far_ref[:, kind * channels + start : kind * channels + start + head_size]

    for start in range(0, channels, head_size):
        cut = slice(start, start + head_size)
        query = q_ref[:, cut]
        near = lax.dot_general(query, kv_ref[0, :, cut], across, preferred_element_type=jnp.float32)
        far = lax.dot_general(query, far_of(0, start), across, preferred_element_type=jnp.float32)
        near = jnp.exp(near * factor)
        far = jnp.exp(far * factor)
        total = jnp.sum(near, axis=-1, keepdims=True) + jnp.sum(far, axis=-1, keepdims=True)
        near = (near / total).astype(jnp.bfloat16)
        far = (far / total).astype(jnp.bfloat16)
        mixed = jnp.dot(near, kv_ref[1, :, cut], preferred_element_type=jnp.float32)
        mixed = mixed + jnp.dot(far, far_of(1, start), preferred_element_type=jnp.float32)
        heads.append(mixed.astype(jnp.bfloat16))
    return jnp.concatenate(heads, axis=1)


def put_cache(caches, out_ref, offset):
    channels = caches[0].shape[2]
    for patch, cache in enumerate(caches):
        for kind in range(2):
            begin = offset + (2 * patch + kind) * channels
            out_ref[:, begin : begin + channels] = cache[kind]


def cache_kernel(*refs):
    put_cache(refs[:-1], refs[-1], 0)


def block_kernel(
    turn, head_size, planes, gain_ref, own_in, other_in, own_out, other_out, blocks_ref, far_ref, *refs
):
    caches, refs = refs[:-11], refs[-11:]
    out_ref, kv_ref, blocks, far, w_in, w_out, parts, q_ref, in_sems, sems, part_sems = refs
    width = blocks.shape[1]
    channels = w_out.shape[0]
    pieces = in_sems.shape[1]
    depth = width // pieces
    mine = lax.rem(lax.axis_index("pipe"), 2) == turn

    def weight_copies(source_in, source_out):
        for part in (1, 2, 0):
            for piece in range(pieces):
                cut = pl.ds(piece * depth, depth)
                pltpu.make_async_copy(
                    source_in.at[part, cut], w_in.at[part, cut], in_sems.at[part, piece]
                ).start()
        pltpu.make_async_copy(source_out.at[0], w_out, sems.at[1]).start()

    fetch = pltpu.make_async_copy(blocks_ref.at[:, :width], blocks, sems.at[0])
    fetch.start()
    if len(far.shape) == 3:
        fetch_far = pltpu.make_async_copy(far_ref, far, sems.at[2])
    else:
        begin = far_ref.shape[1] - far.shape[1]
        fetch_far = pltpu.make_async_copy(far_ref.at[:, begin:], far, sems.at[2])
    fetch_far.start()

    @pl.when(mine)
    def _():
        weight_copies(own_in, own_out)

    @pl.when(jnp.logical_not(mine))
    def _():
        weight_copies(other_in, other_out)

    fetch.wait()
    tokens = blocks[...]
    for part in (1, 2, 0):
        for piece in range(pieces):
            cut = pl.ds(piece * depth, depth)
            pltpu.make_async_copy(
                own_in.at[part, cut], w_in.at[part, cut], in_sems.at[part, piece]
            ).wait()
        projected = jnp.dot(tokens, w_in[part], preferred_element_type=jnp.float32)
        if part == 2:
            kv_ref[1] = projected.astype(jnp.bfloat16)
            continue
        for start in range(0, channels, head_size):
            head = projected[:, start : start + head_size]
            square = jnp.mean(head * head, axis=-1, keepdims=True)
            head = (head * lax.rsqrt(square + 1e-06) * gain_ref[part : part + 1, :]).astype(
                jnp.bfloat16
            )
            if part == 0:
                q_ref[:, start : start + head_size] = head
            else:
                kv_ref[0, :, start : start + head_size] = head

    fetch_far.wait()
    sent = []

    def send(begin, size, sem):
        cut = pl.ds(begin, size)
        sent.append(
            pltpu.make_async_copy(parts.at[:, cut], out_ref.at[:, cut], part_sems.at[sem])
        )
        sent[-1].start()

    steps = part_sems.shape[0] - 1
    if caches:
        last = lax.axis_index("pipe") // 2 == planes - 1
        first, second = caches
        put_cache((first, jnp.where(last, kv_ref[...], second[...])), parts, width)
        send(width, 4 * channels, steps)
    attended = attention(head_size, q_ref, kv_ref, far)
    pltpu.make_async_copy(own_out.at[0], w_out, sems.at[1]).wait()
    tile = width // steps
    for step in range(steps):
        cut = slice(step * tile, (step + 1) * tile)
        update = jnp.dot(attended, w_out[:, cut], preferred_element_type=jnp.float32)
        parts[:, cut] = update.astype(jnp.bfloat16)
        send(step * tile, tile, step)
    for copy in sent:
        copy.wait()


def place_cache(caches, out_ref, offset):
    channels = (caches.shape[2] - offset) // 4
    for patch in range(2):
        for shard in range(caches.shape[0]):
            begin = offset + 2 * patch * channels
            sides = [
                caches[shard, :, begin + kind * channels : begin + (kind + 1) * channels].astype(
                    jnp.float32
                )
                for kind in range(2)
            ]
            out_ref[patch, :, :, shard * channels : (shard + 1) * channels] = jnp.stack(
                sides, axis=1
            ).astype(jnp.bfloat16)


def place_kernel(caches_ref, out_ref):
    place_cache(caches_ref, out_ref, 0)


def last_kernel(params_ref, x_ref, parts_ref, out_ref, cache_ref):
    width = x_ref.shape[1]
    update = jnp.sum(parts_ref[:, :, :width].astype(jnp.float32), axis=0)
    out_ref[...] = (x_ref[...].astype(jnp.float32) + params_ref[2:3, :] * update).astype(
        jnp.bfloat16
    )
    place_cache(parts_ref, cache_ref, width)


def pair_kernel(mine_ref, theirs_ref, out_ref):
    mine, theirs = mine_ref[...], theirs_ref[...]
    early = lax.rem(lax.axis_index("pipe"), 2) == 0
    out_ref[0] = jnp.where(early, mine, theirs)
    out_ref[1] = jnp.where(early, theirs, mine)


def finish_kernel(params_ref, next_ref, x_ref, parts_ref, out_ref, *rest):
    width = x_ref.shape[1]
    update = jnp.sum(parts_ref[:, :, :width].astype(jnp.float32), axis=0)
    result = (x_ref[...].astype(jnp.float32) + params_ref[2:3, :] * update).astype(jnp.bfloat16)
    out_ref[...] = result
    if rest:
        blocks_ref, buffer, sems = rest
        block = normalise(result.astype(jnp.float32), next_ref)
        for copy in spread_block(block, buffer, blocks_ref, sems):
            copy.wait()


def blank_kernel(*refs):
    pass


def params_of(limit):
    return pltpu.CompilerParams(vmem_limit_bytes=limit << 20)


def body(hidden, mod_shift, mod_scale, mod_gate, norm_gain, input_proj, output_proj, stale_cache):
    sections = lax.axis_size("pipe")
    planes = sections // 2
    seq = lax.axis_size("seq")
    pipe = lax.axis_index("pipe")
    core = lax.rem(pipe, 2)
    plane = pipe // 2
    rows, width = hidden.shape[1:]
    head_size = norm_gain.shape[2]
    channels = input_proj.shape[3]
    tokens = rows * seq
    bf16 = lambda *shape: jax.ShapeDtypeStruct(shape, jnp.bfloat16)

    place = lambda row, position: row * seq + position

    def swap(value):
        pairs = [(place(row, s), place(row ^ 1, s)) for row in range(sections) for s in range(seq)]
        return lax.ppermute(value, AXES, pairs)

    def upward(value, level, side):
        row = 2 * level + side
        return lax.ppermute(value, AXES, [(place(row, s), place(row + 2, s)) for s in range(seq)])

    def across(blocks):
        return lax.all_to_all(blocks, "seq", split_axis=0, concat_axis=0, tiled=True)

    def blank(*shapes):
        return pl.pallas_call(blank_kernel, out_shape=shapes, out_specs=(ANY,) * len(shapes))()

    gains = jnp.pad(norm_gain[0].reshape(1, -1), ((0, 0), (0, width - 2 * head_size)))
    own_params = jnp.concatenate([mod_shift, mod_scale, mod_gate, gains], axis=0)
    own_in = jnp.transpose(input_proj[0], (1, 0, 2))
    own_out = output_proj
    x = lax.dynamic_index_in_dim(hidden, core, 0, keepdims=False)
    spreading = [pltpu.VMEM((rows, width), jnp.bfloat16), pltpu.SemaphoreType.DMA((seq,))]
    packed = pl.pallas_call(
        pack_kernel, out_shape=bf16(seq, rows, width + 2 * channels),
        in_specs=[VMEM] * 3, out_specs=HBM,
        scratch_shapes=spreading + [
            pltpu.VMEM((seq, rows, 2 * channels), jnp.bfloat16), pltpu.SemaphoreType.DMA,
        ],
        compiler_params=params_of(16),
    )(own_params, x, stale_cache[0, 1])

    other_params = swap(own_params)
    own_in, own_out, other_params, packed = lax.optimization_barrier(
        (own_in, own_out, other_params, packed)
    )
    other_in = swap(own_in)
    other_out = swap(own_out)
    params = [jnp.where(core == turn, own_params, other_params) for turn in range(2)]
    gain_rows = [p[3, : 2 * head_size].reshape(2, head_size) for p in params]
    blocks_shape = bf16(seq, rows, width)

    def norm(x, turn):
        return pl.pallas_call(
            norm_kernel, out_shape=blocks_shape, in_specs=[VMEM] * 2, out_specs=HBM,
            scratch_shapes=spreading, compiler_params=params_of(16),
        )(params[turn], x)

    flat = lambda blocks: blocks.reshape(tokens, blocks.shape[2])
    apart = lambda values: values.reshape(seq, rows, values.shape[1])

    def block(blocks, far, turn, caches=()):
        total = width + 2 * channels * len(caches)
        side = (2, tokens, channels) if far.ndim == 3 else (tokens, 2 * channels)
        out, pair = pl.pallas_call(
            functools.partial(block_kernel, turn, head_size, planes),
            out_shape=(bf16(tokens, total), bf16(2, tokens, channels)),
            in_specs=[VMEM] + [HBM] * 4 + [ANY] * 2 + [VMEM] * len(caches),
            out_specs=(HBM, VMEM),
            scratch_shapes=[
                pltpu.VMEM((tokens, width), jnp.bfloat16),
                pltpu.VMEM(side, jnp.bfloat16),
                pltpu.VMEM(own_in.shape, jnp.bfloat16),
                pltpu.VMEM(own_out.shape[1:], jnp.bfloat16),
                pltpu.VMEM((tokens, total), jnp.bfloat16),
                pltpu.VMEM((tokens, channels), jnp.bfloat16),
                pltpu.SemaphoreType.DMA((3, 2)),
                pltpu.SemaphoreType.DMA((3,)),
                pltpu.SemaphoreType.DMA((5,)),
            ],
            compiler_params=params_of(32),
        )(
            gain_rows[turn], own_in, other_in, own_out, other_out, flat(blocks), far, *caches
        )
        return apart(out), pair

    def finish(x, parts, turn, onward):
        shapes = (bf16(rows, width),) + (blocks_shape,) * onward
        return pl.pallas_call(
            finish_kernel, out_shape=shapes, in_specs=[VMEM] * 4,
            out_specs=(VMEM,) + (HBM,) * onward,
            scratch_shapes=spreading * onward, compiler_params=params_of(16),
        )(params[turn], params[1 - turn], x, parts)

    early = core == 0
    either = lambda on_early, on_late: lax.cond(early, on_early, on_late)

    def first_early():
        return across(packed), blank(bf16(tokens, 2 * channels))[0]

    def first_late():
        return blank(bf16(*packed.shape))[0], flat(across(packed[:, :, width:]))

    received, stale = either(first_early, first_late)
    stales = [flat(received), swap(stale)]
    pair_shape, block_shape = bf16(2, tokens, channels), bf16(rows, width)
    late_pair = None
    early_x, late_x = x, x
    blocks_out, sources = {}, {}
    for layer in range(sections):
        turn, level = layer % 2, layer // 2
        crossing = layer > 0 and turn == 0

        def early_scatter():
            parts, fresh = block(received, stales[turn], turn)
            return parts, fresh, blank(block_shape)[0]

        def late_gather():
            old = late_pair if turn else blank(pair_shape)[0]
            if turn == 0:
                return norm(late_x, turn), old, blank(block_shape)[0]
            result, normed = finish(late_x, received, 1 - turn, 1)
            return normed, old, result

        if crossing:
            late_x = either(
                lambda: blank(block_shape)[0], lambda: finish(late_x, received, 1 - turn, 0)[0]
            )
            blocks_out[layer - 1, 1] = late_x
            late_x = upward(late_x, level - 1, 1)
        payload, pair, result = either(early_scatter, late_gather)
        if turn:
            late_x = blocks_out[layer - 1, 1] = result
        sources[layer, 0] = pair
        got = swap(pair)
        sources[layer, 2] = got
        received = across(payload)
        if layer == sections - 1:
            break

        crossing = turn == 1

        def early_gather():
            if crossing:
                return norm(early_x, 1 - turn), blank(pair_shape)[0], blank(block_shape)[0]
            result, normed = finish(early_x, received, turn, 1)
            kept = sources[layer, 0] if layer == sections - 2 else blank(pair_shape)[0]
            return normed, kept, result

        def late_scatter():
            parts, fresh = block(received, got, turn)
            return parts, fresh, blank(block_shape)[0]

        if crossing:
            early_x = either(
                lambda: finish(early_x, received, turn, 0)[0], lambda: blank(block_shape)[0]
            )
            blocks_out[layer, 0] = early_x
            early_x = upward(early_x, level, 0)
        payload, late_pair, result = either(early_gather, late_scatter)
        if not crossing:
            early_x = blocks_out[layer, 0] = result
        sources[layer, 1] = late_pair
        if layer == sections - 2:
            lowered = lax.ppermute(
                late_pair,
                AXES,
                [(place(r, s), place((r - 2) % sections, s)) for r in range(sections) for s in range(seq)],
            )
            lowered = lax.cond(
                plane == planes - 2,
                lambda: across(apart(jnp.concatenate([lowered[0], lowered[1]], axis=1))),
                lambda: blank(bf16(seq, rows, 2 * channels))[0],
            )
        if crossing:
            active = pipe == jnp.where(early, 2 * level + 2, 2 * level + 1)
            received = lax.cond(active, across, lambda _: blank(blocks_shape)[0], payload)
        else:
            received = across(payload)

    def by_plane(values):
        chosen = values[0]
        for level in range(1, planes):
            chosen = jnp.where(plane == level, values[level], chosen)
        return chosen

    last = sections - 1
    lowered, received = lax.optimization_barrier((lowered, received))
    crossed = lax.ppermute(
        lowered,
        AXES,
        [
            (place(r, s), place(r ^ (r // 2 == planes - 2), s))
            for r in range(sections)
            for s in range(seq)
        ],
    )
    partner = {2 * planes - 4: 2 * planes - 2, 2 * planes - 2: 2 * planes - 4}
    returned = lax.ppermute(
        jnp.concatenate([lowered, crossed], axis=2),
        AXES,
        [(place(r, s), place(partner.get(r, r), s)) for r in range(sections) for s in range(seq)],
    )
    first_cache = by_plane(
        [jnp.where(early, sources[2 * m, 0], sources[2 * m + 1, 2]) for m in range(planes)]
    )
    second_cache = by_plane(
        [
            jnp.where(early, sources[2 * m + 1, 2], sources[2 * m + 1, int(m < planes - 1)])
            for m in range(planes)
        ]
    )

    cache_shape = bf16(2, rows, 2, seq * channels)

    def laid_out(caches):
        return pl.pallas_call(
            place_kernel, out_shape=cache_shape, in_specs=[VMEM], out_specs=VMEM,
            compiler_params=params_of(16),
        )(caches)

    def packed_cache():
        packed = pl.pallas_call(
            cache_kernel, out_shape=bf16(tokens, 4 * channels),
            in_specs=[VMEM] * 2, out_specs=VMEM, compiler_params=params_of(16),
        )(first_cache, second_cache)
        return laid_out(across(apart(packed)))

    def last_early():
        result = finish(early_x, received, last % 2, 0)[0]
        return result, lax.cond(plane == planes - 1, lambda: laid_out(returned), packed_cache)

    def last_late():
        return tuple(
            pl.pallas_call(
                last_kernel, out_shape=(block_shape, cache_shape),
                in_specs=[VMEM] * 3, out_specs=(VMEM,) * 2, compiler_params=params_of(16),
            )(
                params[last % 2],
                late_x,
                across(
                    block(received, got, last % 2, (first_cache, second_cache))[0]
                ),
            )
        )

    x, cache = either(last_early, last_late)
    blocks_out[last, 0] = blocks_out[last, 1] = x
    mine = by_plane(
        [jnp.where(early, blocks_out[2 * m, 0], blocks_out[2 * m + 1, 1]) for m in range(planes)]
    )
    theirs = swap(
        by_plane(
            [jnp.where(early, blocks_out[2 * m + 1, 0], blocks_out[2 * m, 1]) for m in range(planes)]
        )
    )
    block_output = pl.pallas_call(
        pair_kernel, out_shape=bf16(2, rows, width), in_specs=[VMEM] * 2, out_specs=VMEM,
        compiler_params=params_of(16),
    )(mine, theirs)
    return block_output[None], cache[None]


def solution(mesh):
    in_specs = (
        P(None, "seq", None),
        P("pipe", None),
        P("pipe", None),
        P("pipe", None),
        P("pipe", None, None),
        P("pipe", None, None, "seq"),
        P("pipe", "seq", None),
        P("pipe", None, "seq", None, None),
    )
    out_specs = (P("pipe", None, "seq", None), P("pipe", None, "seq", None, None))
    return jax.shard_map(body, mesh=mesh, in_specs=in_specs, out_specs=out_specs, check_vma=False)
```

```python
import functools
import math

import jax
import jax.numpy as jnp
from jax import lax
from jax.experimental import pallas as pl
from jax.experimental.pallas import tpu as pltpu
from jax.sharding import PartitionSpec as P

AXES = ("pipe", "seq")
VMEM = pl.BlockSpec(memory_space=pltpu.VMEM)
ANY = pl.BlockSpec(memory_space=pl.ANY)
HBM = pl.BlockSpec(memory_space=pltpu.HBM)


def normalise(values, params_ref):
    centered = values - jnp.mean(values, axis=-1, keepdims=True)
    spread = jnp.mean(centered * centered, axis=-1, keepdims=True)
    return (
        centered * lax.rsqrt(spread + 1e-06) * (1.0 + params_ref[1:2, :]) + params_ref[0:1, :]
    ).astype(jnp.bfloat16)


def spread_block(block, buffer, out_ref, sems):
    width = buffer.shape[1]
    buffer[...] = block
    copies = [
        pltpu.make_async_copy(buffer, out_ref.at[shard, :, :width], sems.at[shard])
        for shard in range(out_ref.shape[0])
    ]
    for copy in copies:
        copy.start()
    return copies


def norm_kernel(params_ref, x_ref, out_ref, buffer, sems):
    block = normalise(x_ref[...].astype(jnp.float32), params_ref)
    for copy in spread_block(block, buffer, out_ref, sems):
        copy.wait()


def pack_kernel(params_ref, x_ref, cache_ref, out_ref, buffer, sems, sides, sem):
    count, _, total = sides.shape
    width = x_ref.shape[1]
    channels = total // 2
    block = normalise(x_ref[...].astype(jnp.float32), params_ref)
    copies = spread_block(block, buffer, out_ref, sems)
    for kind in range(2):
        rows = cache_ref[:, kind, :]
        for shard in range(count):
            sides[shard, :, kind * channels : (kind + 1) * channels] = rows[
                :, shard * channels : (shard + 1) * channels
            ]
    copies.append(pltpu.make_async_copy(sides, out_ref.at[:, :, width:], sem))
    copies[-1].start()
    for copy in copies:
        copy.wait()


def attention(head_size, q_ref, kv_ref, far_ref):
    factor = 1.0 / math.sqrt(head_size)
    channels = q_ref.shape[1]
    heads = []
    across = (((1,), (1,)), ((), ()))

    def far_of(kind, start):
        if len(far_ref.shape) == 3:
            return far_ref[kind, :, start : start + head_size]
        return far_ref[:, kind * channels + start : kind * channels + start + head_size]

    for start in range(0, channels, head_size):
        cut = slice(start, start + head_size)
        query = q_ref[:, cut]
        near = lax.dot_general(query, kv_ref[0, :, cut], across, preferred_element_type=jnp.float32)
        far = lax.dot_general(query, far_of(0, start), across, preferred_element_type=jnp.float32)
        near = jnp.exp(near * factor)
        far = jnp.exp(far * factor)
        total = jnp.sum(near, axis=-1, keepdims=True) + jnp.sum(far, axis=-1, keepdims=True)
        near = (near / total).astype(jnp.bfloat16)
        far = (far / total).astype(jnp.bfloat16)
        mixed = jnp.dot(near, kv_ref[1, :, cut], preferred_element_type=jnp.float32)
        mixed = mixed + jnp.dot(far, far_of(1, start), preferred_element_type=jnp.float32)
        heads.append(mixed.astype(jnp.bfloat16))
    return jnp.concatenate(heads, axis=1)


def put_cache(caches, out_ref, offset):
    channels = caches[0].shape[2]
    for patch, cache in enumerate(caches):
        for kind in range(2):
            begin = offset + (2 * patch + kind) * channels
            out_ref[:, begin : begin + channels] = cache[kind]


def cache_kernel(*refs):
    put_cache(refs[:-1], refs[-1], 0)


def block_kernel(
    turn, head_size, planes, gain_ref, own_in, other_in, own_out, other_out, blocks_ref, far_ref, *refs
):
    caches, refs = refs[:-11], refs[-11:]
    out_ref, kv_ref, blocks, far, w_in, w_out, parts, q_ref, in_sems, sems, part_sems = refs
    width = blocks.shape[1]
    channels = w_out.shape[0]
    pieces = in_sems.shape[1]
    depth = width // pieces
    mine = lax.rem(lax.axis_index("pipe"), 2) == turn

    def weight_copies(source_in, source_out):
        for part in (1, 2, 0):
            for piece in range(pieces):
                cut = pl.ds(piece * depth, depth)
                pltpu.make_async_copy(
                    source_in.at[part, cut], w_in.at[part, cut], in_sems.at[part, piece]
                ).start()
        pltpu.make_async_copy(source_out.at[0], w_out, sems.at[1]).start()

    fetch = pltpu.make_async_copy(blocks_ref.at[:, :width], blocks, sems.at[0])
    fetch.start()
    if len(far.shape) == 3:
        fetch_far = pltpu.make_async_copy(far_ref, far, sems.at[2])
    else:
        begin = far_ref.shape[1] - far.shape[1]
        fetch_far = pltpu.make_async_copy(far_ref.at[:, begin:], far, sems.at[2])
    fetch_far.start()

    @pl.when(mine)
    def _():
        weight_copies(own_in, own_out)

    @pl.when(jnp.logical_not(mine))
    def _():
        weight_copies(other_in, other_out)

    fetch.wait()
    tokens = blocks[...]
    for part in (1, 2, 0):
        for piece in range(pieces):
            cut = pl.ds(piece * depth, depth)
            pltpu.make_async_copy(
                own_in.at[part, cut], w_in.at[part, cut], in_sems.at[part, piece]
            ).wait()
        projected = jnp.dot(tokens, w_in[part], preferred_element_type=jnp.float32)
        if part == 2:
            kv_ref[1] = projected.astype(jnp.bfloat16)
            continue
        for start in range(0, channels, head_size):
            head = projected[:, start : start + head_size]
            square = jnp.mean(head * head, axis=-1, keepdims=True)
            head = (head * lax.rsqrt(square + 1e-06) * gain_ref[part : part + 1, :]).astype(
                jnp.bfloat16
            )
            if part == 0:
                q_ref[:, start : start + head_size] = head
            else:
                kv_ref[0, :, start : start + head_size] = head

    fetch_far.wait()
    sent = []

    def send(begin, size, sem):
        cut = pl.ds(begin, size)
        sent.append(
            pltpu.make_async_copy(parts.at[:, cut], out_ref.at[:, cut], part_sems.at[sem])
        )
        sent[-1].start()

    steps = part_sems.shape[0] - 1
    if caches:
        last = lax.axis_index("pipe") // 2 == planes - 1
        first, second = caches
        put_cache((first, jnp.where(last, kv_ref[...], second[...])), parts, width)
        send(width, 4 * channels, steps)
    attended = attention(head_size, q_ref, kv_ref, far)
    pltpu.make_async_copy(own_out.at[0], w_out, sems.at[1]).wait()
    tile = width // steps
    for step in range(steps):
        cut = slice(step * tile, (step + 1) * tile)
        update = jnp.dot(attended, w_out[:, cut], preferred_element_type=jnp.float32)
        parts[:, cut] = update.astype(jnp.bfloat16)
        send(step * tile, tile, step)
    for copy in sent:
        copy.wait()


def place_cache(caches, out_ref, offset):
    channels = (caches.shape[2] - offset) // 4
    for patch in range(2):
        for shard in range(caches.shape[0]):
            begin = offset + 2 * patch * channels
            sides = [
                caches[shard, :, begin + kind * channels : begin + (kind + 1) * channels].astype(
                    jnp.float32
                )
                for kind in range(2)
            ]
            out_ref[patch, :, :, shard * channels : (shard + 1) * channels] = jnp.stack(
                sides, axis=1
            ).astype(jnp.bfloat16)


def place_kernel(caches_ref, out_ref):
    place_cache(caches_ref, out_ref, 0)


def last_kernel(params_ref, x_ref, parts_ref, out_ref, cache_ref):
    width = x_ref.shape[1]
    update = jnp.sum(parts_ref[:, :, :width].astype(jnp.float32), axis=0)
    out_ref[...] = (x_ref[...].astype(jnp.float32) + params_ref[2:3, :] * update).astype(
        jnp.bfloat16
    )
    place_cache(parts_ref, cache_ref, width)


def pair_kernel(mine_ref, theirs_ref, out_ref):
    mine, theirs = mine_ref[...], theirs_ref[...]
    early = lax.rem(lax.axis_index("pipe"), 2) == 0
    out_ref[0] = jnp.where(early, mine, theirs)
    out_ref[1] = jnp.where(early, theirs, mine)


def finish_kernel(params_ref, next_ref, x_ref, parts_ref, out_ref, *rest):
    width = x_ref.shape[1]
    update = jnp.sum(parts_ref[:, :, :width].astype(jnp.float32), axis=0)
    result = (x_ref[...].astype(jnp.float32) + params_ref[2:3, :] * update).astype(jnp.bfloat16)
    out_ref[...] = result
    if rest:
        blocks_ref, buffer, sems = rest
        block = normalise(result.astype(jnp.float32), next_ref)
        for copy in spread_block(block, buffer, blocks_ref, sems):
            copy.wait()


def blank_kernel(*refs):
    pass


def params_of(limit):
    return pltpu.CompilerParams(vmem_limit_bytes=limit << 20)


def body(hidden, mod_shift, mod_scale, mod_gate, norm_gain, input_proj, output_proj, stale_cache):
    sections = lax.axis_size("pipe")
    planes = sections // 2
    seq = lax.axis_size("seq")
    pipe = lax.axis_index("pipe")
    core = lax.rem(pipe, 2)
    plane = pipe // 2
    rows, width = hidden.shape[1:]
    head_size = norm_gain.shape[2]
    channels = input_proj.shape[3]
    tokens = rows * seq
    bf16 = lambda *shape: jax.ShapeDtypeStruct(shape, jnp.bfloat16)

    place = lambda row, position: row * seq + position

    def swap(value):
        pairs = [(place(row, s), place(row ^ 1, s)) for row in range(sections) for s in range(seq)]
        return lax.ppermute(value, AXES, pairs)

    def upward(value, level, side):
        row = 2 * level + side
        return lax.ppermute(value, AXES, [(place(row, s), place(row + 2, s)) for s in range(seq)])

    def across(blocks):
        return lax.all_to_all(blocks, "seq", split_axis=0, concat_axis=0, tiled=True)

    def blank(*shapes):
        return pl.pallas_call(blank_kernel, out_shape=shapes, out_specs=(ANY,) * len(shapes))()

    gains = jnp.pad(norm_gain[0].reshape(1, -1), ((0, 0), (0, width - 2 * head_size)))
    own_params = jnp.concatenate([mod_shift, mod_scale, mod_gate, gains], axis=0)
    own_in = jnp.transpose(input_proj[0], (1, 0, 2))
    own_out = output_proj
    x = lax.dynamic_index_in_dim(hidden, core, 0, keepdims=False)
    spreading = [pltpu.VMEM((rows, width), jnp.bfloat16), pltpu.SemaphoreType.DMA((seq,))]
    packed = pl.pallas_call(
        pack_kernel, out_shape=bf16(seq, rows, width + 2 * channels),
        in_specs=[VMEM] * 3, out_specs=HBM,
        scratch_shapes=spreading + [
            pltpu.VMEM((seq, rows, 2 * channels), jnp.bfloat16), pltpu.SemaphoreType.DMA,
        ],
        compiler_params=params_of(16),
    )(own_params, x, stale_cache[0, 1])

    other_params = swap(own_params)
    own_in, own_out, other_params, packed = lax.optimization_barrier(
        (own_in, own_out, other_params, packed)
    )
    other_in = swap(own_in)
    other_out = swap(own_out)
    params = [jnp.where(core == turn, own_params, other_params) for turn in range(2)]
    gain_rows = [p[3, : 2 * head_size].reshape(2, head_size) for p in params]
    blocks_shape = bf16(seq, rows, width)

    def norm(x, turn):
        return pl.pallas_call(
            norm_kernel, out_shape=blocks_shape, in_specs=[VMEM] * 2, out_specs=HBM,
            scratch_shapes=spreading, compiler_params=params_of(16),
        )(params[turn], x)

    flat = lambda blocks: blocks.reshape(tokens, blocks.shape[2])
    apart = lambda values: values.reshape(seq, rows, values.shape[1])

    def block(blocks, far, turn, caches=()):
        total = width + 2 * channels * len(caches)
        side = (2, tokens, channels) if far.ndim == 3 else (tokens, 2 * channels)
        out, pair = pl.pallas_call(
            functools.partial(block_kernel, turn, head_size, planes),
            out_shape=(bf16(tokens, total), bf16(2, tokens, channels)),
            in_specs=[VMEM] + [HBM] * 4 + [ANY] * 2 + [VMEM] * len(caches),
            out_specs=(HBM, VMEM),
            scratch_shapes=[
                pltpu.VMEM((tokens, width), jnp.bfloat16),
                pltpu.VMEM(side, jnp.bfloat16),
                pltpu.VMEM(own_in.shape, jnp.bfloat16),
                pltpu.VMEM(own_out.shape[1:], jnp.bfloat16),
                pltpu.VMEM((tokens, total), jnp.bfloat16),
                pltpu.VMEM((tokens, channels), jnp.bfloat16),
                pltpu.SemaphoreType.DMA((3, 2)),
                pltpu.SemaphoreType.DMA((3,)),
                pltpu.SemaphoreType.DMA((5,)),
            ],
            compiler_params=params_of(32),
        )(
            gain_rows[turn], own_in, other_in, own_out, other_out, flat(blocks), far, *caches
        )
        return apart(out), pair

    def finish(x, parts, turn, onward):
        shapes = (bf16(rows, width),) + (blocks_shape,) * onward
        return pl.pallas_call(
            finish_kernel, out_shape=shapes, in_specs=[VMEM] * 4,
            out_specs=(VMEM,) + (HBM,) * onward,
            scratch_shapes=spreading * onward, compiler_params=params_of(16),
        )(params[turn], params[1 - turn], x, parts)

    early = core == 0
    either = lambda on_early, on_late: lax.cond(early, on_early, on_late)

    def first_early():
        return across(packed), blank(bf16(tokens, 2 * channels))[0]

    def first_late():
        return blank(bf16(*packed.shape))[0], flat(across(packed[:, :, width:]))

    received, stale = either(first_early, first_late)
    stales = [flat(received), swap(stale)]
    pair_shape, block_shape = bf16(2, tokens, channels), bf16(rows, width)
    late_pair = None
    early_x, late_x = x, x
    blocks_out, sources = {}, {}
    for layer in range(sections):
        turn, level = layer % 2, layer // 2
        crossing = layer > 0 and turn == 0

        def early_scatter():
            parts, fresh = block(received, stales[turn], turn)
            return parts, fresh, blank(block_shape)[0]

        def late_gather():
            old = late_pair if turn else blank(pair_shape)[0]
            if turn == 0:
                return norm(late_x, turn), old, blank(block_shape)[0]
            result, normed = finish(late_x, received, 1 - turn, 1)
            return normed, old, result

        if crossing:
            late_x = either(
                lambda: blank(block_shape)[0], lambda: finish(late_x, received, 1 - turn, 0)[0]
            )
            blocks_out[layer - 1, 1] = late_x
            late_x = upward(late_x, level - 1, 1)
        payload, pair, result = either(early_scatter, late_gather)
        if turn:
            late_x = blocks_out[layer - 1, 1] = result
        sources[layer, 0] = pair
        got = swap(pair)
        sources[layer, 2] = got
        received = across(payload)
        if layer == sections - 1:
            break

        crossing = turn == 1

        def early_gather():
            if crossing:
                return norm(early_x, 1 - turn), blank(pair_shape)[0], blank(block_shape)[0]
            result, normed = finish(early_x, received, turn, 1)
            return normed, blank(pair_shape)[0], result

        def late_scatter():
            parts, fresh = block(received, got, turn)
            return parts, fresh, blank(block_shape)[0]

        if crossing:
            early_x = either(
                lambda: finish(early_x, received, turn, 0)[0], lambda: blank(block_shape)[0]
            )
            blocks_out[layer, 0] = early_x
            early_x = upward(early_x, level, 0)
        payload, late_pair, result = either(early_gather, late_scatter)
        if not crossing:
            early_x = blocks_out[layer, 0] = result
        sources[layer, 1] = late_pair
        if crossing:
            active = pipe == jnp.where(early, 2 * level + 2, 2 * level + 1)
            received = lax.cond(active, across, lambda _: blank(blocks_shape)[0], payload)
        else:
            received = across(payload)

    def by_plane(values):
        chosen = values[0]
        for level in range(1, planes):
            chosen = jnp.where(plane == level, values[level], chosen)
        return chosen

    last = sections - 1
    first_cache = by_plane(
        [jnp.where(early, sources[2 * m, 0], sources[2 * m + 1, 2]) for m in range(planes)]
    )
    second_cache = by_plane(
        [
            jnp.where(early, sources[2 * m + 1, 2], sources[2 * m + 1, int(m < planes - 1)])
            for m in range(planes)
        ]
    )

    cache_shape = bf16(2, rows, 2, seq * channels)

    def last_early():
        result = finish(early_x, received, last % 2, 0)[0]
        packed = pl.pallas_call(
            cache_kernel, out_shape=bf16(tokens, 4 * channels),
            in_specs=[VMEM] * 2, out_specs=VMEM, compiler_params=params_of(16),
        )(first_cache, second_cache)
        cache = pl.pallas_call(
            place_kernel, out_shape=cache_shape, in_specs=[VMEM], out_specs=VMEM,
            compiler_params=params_of(16),
        )(across(apart(packed)))
        return result, cache

    def last_late():
        parts, _ = block(received, got, last % 2, (first_cache, second_cache))
        return tuple(
            pl.pallas_call(
                last_kernel, out_shape=(block_shape, cache_shape),
                in_specs=[VMEM] * 3, out_specs=(VMEM,) * 2, compiler_params=params_of(16),
            )(params[last % 2], late_x, across(parts))
        )

    x, cache = either(last_early, last_late)
    blocks_out[last, 0] = blocks_out[last, 1] = x
    mine = by_plane(
        [jnp.where(early, blocks_out[2 * m, 0], blocks_out[2 * m + 1, 1]) for m in range(planes)]
    )
    theirs = swap(
        by_plane(
            [jnp.where(early, blocks_out[2 * m + 1, 0], blocks_out[2 * m, 1]) for m in range(planes)]
        )
    )
    block_output = pl.pallas_call(
        pair_kernel, out_shape=bf16(2, rows, width), in_specs=[VMEM] * 2, out_specs=VMEM,
        compiler_params=params_of(16),
    )(mine, theirs)
    return block_output[None], cache[None]


def solution(mesh):
    in_specs = (
        P(None, "seq", None),
        P("pipe", None),
        P("pipe", None),
        P("pipe", None),
        P("pipe", None, None),
        P("pipe", None, None, "seq"),
        P("pipe", "seq", None),
        P("pipe", None, "seq", None, None),
    )
    out_specs = (P("pipe", None, "seq", None), P("pipe", None, "seq", None, None))
    return jax.shard_map(body, mesh=mesh, in_specs=in_specs, out_specs=out_specs, check_vma=False)
```

```python
import functools
import math

import jax
import jax.numpy as jnp
from jax import lax
from jax.experimental import pallas as pl
from jax.experimental.pallas import tpu as pltpu
from jax.sharding import PartitionSpec as P

AXES = ("pipe", "seq")
VMEM = pl.BlockSpec(memory_space=pltpu.VMEM)
ANY = pl.BlockSpec(memory_space=pl.ANY)
HBM = pl.BlockSpec(memory_space=pltpu.HBM)


def normalise(values, params_ref):
    centered = values - jnp.mean(values, axis=-1, keepdims=True)
    spread = jnp.mean(centered * centered, axis=-1, keepdims=True)
    return (
        centered * lax.rsqrt(spread + 1e-06) * (1.0 + params_ref[1:2, :]) + params_ref[0:1, :]
    ).astype(jnp.bfloat16)


def spread_block(block, buffer, out_ref, sems):
    width = buffer.shape[1]
    buffer[...] = block
    copies = [
        pltpu.make_async_copy(buffer, out_ref.at[shard, :, :width], sems.at[shard])
        for shard in range(out_ref.shape[0])
    ]
    for copy in copies:
        copy.start()
    return copies


def norm_kernel(params_ref, x_ref, out_ref, buffer, sems):
    block = normalise(x_ref[...].astype(jnp.float32), params_ref)
    for copy in spread_block(block, buffer, out_ref, sems):
        copy.wait()


def pack_kernel(params_ref, x_ref, cache_ref, out_ref, buffer, sems, sides, sem):
    count, _, total = sides.shape
    width = x_ref.shape[1]
    channels = total // 2
    block = normalise(x_ref[...].astype(jnp.float32), params_ref)
    copies = spread_block(block, buffer, out_ref, sems)
    for kind in range(2):
        rows = cache_ref[:, kind, :]
        for shard in range(count):
            sides[shard, :, kind * channels : (kind + 1) * channels] = rows[
                :, shard * channels : (shard + 1) * channels
            ]
    copies.append(pltpu.make_async_copy(sides, out_ref.at[:, :, width:], sem))
    copies[-1].start()
    for copy in copies:
        copy.wait()


def attention(head_size, q_ref, kv_ref, far_ref):
    factor = 1.0 / math.sqrt(head_size)
    channels = q_ref.shape[1]
    heads = []
    across = (((1,), (1,)), ((), ()))

    def far_of(kind, start):
        if len(far_ref.shape) == 3:
            return far_ref[kind, :, start : start + head_size]
        return far_ref[:, kind * channels + start : kind * channels + start + head_size]

    for start in range(0, channels, head_size):
        cut = slice(start, start + head_size)
        query = q_ref[:, cut]
        near = lax.dot_general(query, kv_ref[0, :, cut], across, preferred_element_type=jnp.float32)
        far = lax.dot_general(query, far_of(0, start), across, preferred_element_type=jnp.float32)
        near = jnp.exp(near * factor)
        far = jnp.exp(far * factor)
        total = jnp.sum(near, axis=-1, keepdims=True) + jnp.sum(far, axis=-1, keepdims=True)
        near = (near / total).astype(jnp.bfloat16)
        far = (far / total).astype(jnp.bfloat16)
        mixed = jnp.dot(near, kv_ref[1, :, cut], preferred_element_type=jnp.float32)
        mixed = mixed + jnp.dot(far, far_of(1, start), preferred_element_type=jnp.float32)
        heads.append(mixed.astype(jnp.bfloat16))
    return jnp.concatenate(heads, axis=1)


def put_cache(caches, out_ref, offset):
    channels = caches[0].shape[2]
    for patch, cache in enumerate(caches):
        for kind in range(2):
            begin = offset + (2 * patch + kind) * channels
            out_ref[:, begin : begin + channels] = cache[kind]


def cache_kernel(*refs):
    put_cache(refs[:-1], refs[-1], 0)


def block_kernel(
    head_size, planes, gain_ref, in_ref, out_weights_ref, blocks_ref, far_ref, *refs
):
    caches, refs = refs[:-11], refs[-11:]
    out_ref, kv_ref, blocks, far, w_in, w_out, parts, q_ref, in_sems, sems, part_sems = refs
    width = blocks.shape[1]
    channels = w_out.shape[0]
    pieces = in_sems.shape[1]
    depth = width // pieces
    fetch = pltpu.make_async_copy(blocks_ref.at[:, :width], blocks, sems.at[0])
    fetch.start()
    if len(far.shape) == 3:
        fetch_far = pltpu.make_async_copy(far_ref, far, sems.at[2])
    else:
        begin = far_ref.shape[1] - far.shape[1]
        fetch_far = pltpu.make_async_copy(far_ref.at[:, begin:], far, sems.at[2])
    fetch_far.start()

    for part in (1, 2, 0):
        for piece in range(pieces):
            cut = pl.ds(piece * depth, depth)
            pltpu.make_async_copy(
                in_ref.at[part, cut], w_in.at[part, cut], in_sems.at[part, piece]
            ).start()
    pltpu.make_async_copy(out_weights_ref.at[0], w_out, sems.at[1]).start()
    fetch.wait()
    tokens = blocks[...]
    for part in (1, 2, 0):
        for piece in range(pieces):
            cut = pl.ds(piece * depth, depth)
            pltpu.make_async_copy(
                in_ref.at[part, cut], w_in.at[part, cut], in_sems.at[part, piece]
            ).wait()
        projected = jnp.dot(tokens, w_in[part], preferred_element_type=jnp.float32)
        if part == 2:
            kv_ref[1] = projected.astype(jnp.bfloat16)
            continue
        for start in range(0, channels, head_size):
            head = projected[:, start : start + head_size]
            square = jnp.mean(head * head, axis=-1, keepdims=True)
            head = (head * lax.rsqrt(square + 1e-06) * gain_ref[part : part + 1, :]).astype(
                jnp.bfloat16
            )
            if part == 0:
                q_ref[:, start : start + head_size] = head
            else:
                kv_ref[0, :, start : start + head_size] = head

    fetch_far.wait()
    sent = []

    def send(begin, size, sem):
        cut = pl.ds(begin, size)
        sent.append(
            pltpu.make_async_copy(parts.at[:, cut], out_ref.at[:, cut], part_sems.at[sem])
        )
        sent[-1].start()

    steps = part_sems.shape[0] - 1
    if caches:
        last = lax.axis_index("pipe") // 2 == planes - 1
        first, second = caches
        put_cache((first, jnp.where(last, kv_ref[...], second[...])), parts, width)
        send(width, 4 * channels, steps)
    attended = attention(head_size, q_ref, kv_ref, far)
    pltpu.make_async_copy(out_weights_ref.at[0], w_out, sems.at[1]).wait()
    tile = width // steps
    for step in range(steps):
        cut = slice(step * tile, (step + 1) * tile)
        update = jnp.dot(attended, w_out[:, cut], preferred_element_type=jnp.float32)
        parts[:, cut] = update.astype(jnp.bfloat16)
        send(step * tile, tile, step)
    for copy in sent:
        copy.wait()


def place_cache(caches, out_ref, offset):
    channels = (caches.shape[2] - offset) // 4
    for patch in range(2):
        for shard in range(caches.shape[0]):
            begin = offset + 2 * patch * channels
            sides = [
                caches[shard, :, begin + kind * channels : begin + (kind + 1) * channels].astype(
                    jnp.float32
                )
                for kind in range(2)
            ]
            out_ref[patch, :, :, shard * channels : (shard + 1) * channels] = jnp.stack(
                sides, axis=1
            ).astype(jnp.bfloat16)


def place_kernel(caches_ref, out_ref):
    place_cache(caches_ref, out_ref, 0)


def last_kernel(params_ref, x_ref, parts_ref, out_ref, cache_ref):
    width = x_ref.shape[1]
    update = jnp.sum(parts_ref[:, :, :width].astype(jnp.float32), axis=0)
    out_ref[...] = (x_ref[...].astype(jnp.float32) + params_ref[2:3, :] * update).astype(
        jnp.bfloat16
    )
    place_cache(parts_ref, cache_ref, width)


def pair_kernel(mine_ref, theirs_ref, out_ref):
    mine, theirs = mine_ref[...], theirs_ref[...]
    early = lax.rem(lax.axis_index("pipe"), 2) == 0
    out_ref[0] = jnp.where(early, mine, theirs)
    out_ref[1] = jnp.where(early, theirs, mine)


def finish_kernel(params_ref, next_ref, x_ref, parts_ref, out_ref, *rest):
    width = x_ref.shape[1]
    update = jnp.sum(parts_ref[:, :, :width].astype(jnp.float32), axis=0)
    result = (x_ref[...].astype(jnp.float32) + params_ref[2:3, :] * update).astype(jnp.bfloat16)
    out_ref[...] = result
    if rest:
        blocks_ref, buffer, sems = rest
        block = normalise(result.astype(jnp.float32), next_ref)
        for copy in spread_block(block, buffer, blocks_ref, sems):
            copy.wait()


def blank_kernel(*refs):
    pass


def params_of(limit):
    return pltpu.CompilerParams(vmem_limit_bytes=limit << 20)


def body(hidden, mod_shift, mod_scale, mod_gate, norm_gain, input_proj, output_proj, stale_cache):
    sections = lax.axis_size("pipe")
    planes = sections // 2
    seq = lax.axis_size("seq")
    pipe = lax.axis_index("pipe")
    core = lax.rem(pipe, 2)
    plane = pipe // 2
    rows, width = hidden.shape[1:]
    head_size = norm_gain.shape[2]
    channels = input_proj.shape[3]
    tokens = rows * seq
    bf16 = lambda *shape: jax.ShapeDtypeStruct(shape, jnp.bfloat16)

    place = lambda row, position: row * seq + position

    def swap(value):
        pairs = [(place(row, s), place(row ^ 1, s)) for row in range(sections) for s in range(seq)]
        return lax.ppermute(value, AXES, pairs)

    def upward(value, level, side):
        row = 2 * level + side
        return lax.ppermute(value, AXES, [(place(row, s), place(row + 2, s)) for s in range(seq)])

    def across(blocks):
        return lax.all_to_all(blocks, "seq", split_axis=0, concat_axis=0, tiled=True)

    def blank(*shapes):
        return pl.pallas_call(blank_kernel, out_shape=shapes, out_specs=(ANY,) * len(shapes))()

    gains = jnp.pad(norm_gain[0].reshape(1, -1), ((0, 0), (0, width - 2 * head_size)))
    own_params = jnp.concatenate([mod_shift, mod_scale, mod_gate, gains], axis=0)
    own_in = jnp.transpose(input_proj[0], (1, 0, 2))
    own_out = output_proj
    x = lax.dynamic_index_in_dim(hidden, core, 0, keepdims=False)
    spreading = [pltpu.VMEM((rows, width), jnp.bfloat16), pltpu.SemaphoreType.DMA((seq,))]
    packed = pl.pallas_call(
        pack_kernel, out_shape=bf16(seq, rows, width + 2 * channels),
        in_specs=[VMEM] * 3, out_specs=HBM,
        scratch_shapes=spreading + [
            pltpu.VMEM((seq, rows, 2 * channels), jnp.bfloat16), pltpu.SemaphoreType.DMA,
        ],
        compiler_params=params_of(16),
    )(own_params, x, stale_cache[0, 1])

    other_params = swap(own_params)
    own_in, own_out, other_params, packed = lax.optimization_barrier(
        (own_in, own_out, other_params, packed)
    )
    other_in = swap(own_in)
    other_out = swap(own_out)
    own, other = (own_in, own_out), (other_in, other_out)
    params = [jnp.where(core == turn, own_params, other_params) for turn in range(2)]
    gain_rows = [p[3, : 2 * head_size].reshape(2, head_size) for p in params]
    blocks_shape = bf16(seq, rows, width)

    def norm(x, turn):
        return pl.pallas_call(
            norm_kernel, out_shape=blocks_shape, in_specs=[VMEM] * 2, out_specs=HBM,
            scratch_shapes=spreading, compiler_params=params_of(16),
        )(params[turn], x)

    flat = lambda blocks: blocks.reshape(tokens, blocks.shape[2])
    apart = lambda values: values.reshape(seq, rows, values.shape[1])

    def block(blocks, far, turn, weights, caches=()):
        total = width + 2 * channels * len(caches)
        side = (2, tokens, channels) if far.ndim == 3 else (tokens, 2 * channels)
        out, pair = pl.pallas_call(
            functools.partial(block_kernel, head_size, planes),
            out_shape=(bf16(tokens, total), bf16(2, tokens, channels)),
            in_specs=[VMEM] + [HBM] * 2 + [ANY] * 2 + [VMEM] * len(caches),
            out_specs=(HBM, VMEM),
            scratch_shapes=[
                pltpu.VMEM((tokens, width), jnp.bfloat16),
                pltpu.VMEM(side, jnp.bfloat16),
                pltpu.VMEM(own_in.shape, jnp.bfloat16),
                pltpu.VMEM(own_out.shape[1:], jnp.bfloat16),
                pltpu.VMEM((tokens, total), jnp.bfloat16),
                pltpu.VMEM((tokens, channels), jnp.bfloat16),
                pltpu.SemaphoreType.DMA((3, 2)),
                pltpu.SemaphoreType.DMA((3,)),
                pltpu.SemaphoreType.DMA((5,)),
            ],
            compiler_params=params_of(32),
        )(
            gain_rows[turn], *weights, flat(blocks), far, *caches
        )
        return apart(out), pair

    def finish(x, parts, turn, onward):
        shapes = (bf16(rows, width),) + (blocks_shape,) * onward
        return pl.pallas_call(
            finish_kernel, out_shape=shapes, in_specs=[VMEM] * 4,
            out_specs=(VMEM,) + (HBM,) * onward,
            scratch_shapes=spreading * onward, compiler_params=params_of(16),
        )(params[turn], params[1 - turn], x, parts)

    early = core == 0
    either = lambda on_early, on_late: lax.cond(early, on_early, on_late)

    pair_shape, block_shape = bf16(2, tokens, channels), bf16(rows, width)
    side_shape = bf16(tokens, 2 * channels)

    def first_early():
        received = across(packed)
        side = flat(received)
        parts, fresh = block(received, side, 0, own)
        kept = lax.cond(plane == 0, lambda: blank(side_shape)[0], lambda: side[:, width:])
        return parts, fresh, kept

    def first_late():
        side = flat(across(packed[:, :, width:]))
        later, side = lax.optimization_barrier((x, side))
        return norm(later, 0), blank(pair_shape)[0], side

    late_pair = None
    early_x, late_x = x, x
    blocks_out, sources = {}, {}
    for layer in range(sections):
        turn, level = layer % 2, layer // 2
        crossing = layer > 0 and turn == 0

        def early_scatter():
            parts, fresh = block(received, stales[turn], turn, other if turn else own)
            return parts, fresh, blank(block_shape)[0]

        def late_gather():
            old = late_pair if turn else blank(pair_shape)[0]
            if turn == 0:
                return norm(late_x, turn), old, blank(block_shape)[0]
            result, normed = finish(late_x, received, 1 - turn, 1)
            return normed, old, result

        if crossing:
            late_x = either(
                lambda: blank(block_shape)[0], lambda: finish(late_x, received, 1 - turn, 0)[0]
            )
            blocks_out[layer - 1, 1] = late_x
            late_x = upward(late_x, level - 1, 1)
        if layer == 0:
            payload, pair, side = either(first_early, first_late)
            stales = [side, swap(side)]
        else:
            payload, pair, result = either(early_scatter, late_gather)
        if turn:
            late_x = blocks_out[layer - 1, 1] = result
        sources[layer, 0] = pair
        got = swap(pair)
        sources[layer, 2] = got
        received = across(payload)
        if layer == sections - 1:
            break

        crossing = turn == 1

        def early_gather():
            if crossing:
                return norm(early_x, 1 - turn), blank(pair_shape)[0], blank(block_shape)[0]
            result, normed = finish(early_x, received, turn, 1)
            return normed, blank(pair_shape)[0], result

        def late_scatter():
            parts, fresh = block(received, got, turn, own if turn else other)
            return parts, fresh, blank(block_shape)[0]

        if crossing:
            early_x = either(
                lambda: finish(early_x, received, turn, 0)[0], lambda: blank(block_shape)[0]
            )
            blocks_out[layer, 0] = early_x
            early_x = upward(early_x, level, 0)
        payload, late_pair, result = either(early_gather, late_scatter)
        if not crossing:
            early_x = blocks_out[layer, 0] = result
        sources[layer, 1] = late_pair
        if crossing:
            active = pipe == jnp.where(early, 2 * level + 2, 2 * level + 1)
            received = lax.cond(active, across, lambda _: blank(blocks_shape)[0], payload)
        else:
            received = across(payload)

    def by_plane(values):
        chosen = values[0]
        for level in range(1, planes):
            chosen = jnp.where(plane == level, values[level], chosen)
        return chosen

    last = sections - 1
    first_cache = by_plane(
        [jnp.where(early, sources[2 * m, 0], sources[2 * m + 1, 2]) for m in range(planes)]
    )
    second_cache = by_plane(
        [
            jnp.where(early, sources[2 * m + 1, 2], sources[2 * m + 1, int(m < planes - 1)])
            for m in range(planes)
        ]
    )

    cache_shape = bf16(2, rows, 2, seq * channels)

    def last_early():
        result = finish(early_x, received, last % 2, 0)[0]
        packed = pl.pallas_call(
            cache_kernel, out_shape=bf16(tokens, 4 * channels),
            in_specs=[VMEM] * 2, out_specs=VMEM, compiler_params=params_of(16),
        )(first_cache, second_cache)
        cache = pl.pallas_call(
            place_kernel, out_shape=cache_shape, in_specs=[VMEM], out_specs=VMEM,
            compiler_params=params_of(16),
        )(across(apart(packed)))
        return result, cache

    def last_late():
        parts, _ = block(received, got, last % 2, own if last % 2 else other, (first_cache, second_cache))
        return tuple(
            pl.pallas_call(
                last_kernel, out_shape=(block_shape, cache_shape),
                in_specs=[VMEM] * 3, out_specs=(VMEM,) * 2, compiler_params=params_of(16),
            )(params[last % 2], late_x, across(parts))
        )

    x, cache = either(last_early, last_late)
    blocks_out[last, 0] = blocks_out[last, 1] = x
    mine = by_plane(
        [jnp.where(early, blocks_out[2 * m, 0], blocks_out[2 * m + 1, 1]) for m in range(planes)]
    )
    theirs = swap(
        by_plane(
            [jnp.where(early, blocks_out[2 * m + 1, 0], blocks_out[2 * m, 1]) for m in range(planes)]
        )
    )
    block_output = pl.pallas_call(
        pair_kernel, out_shape=bf16(2, rows, width), in_specs=[VMEM] * 2, out_specs=VMEM,
        compiler_params=params_of(16),
    )(mine, theirs)
    return block_output[None], cache[None]


def solution(mesh):
    in_specs = (
        P(None, "seq", None),
        P("pipe", None),
        P("pipe", None),
        P("pipe", None),
        P("pipe", None, None),
        P("pipe", None, None, "seq"),
        P("pipe", "seq", None),
        P("pipe", None, "seq", None, None),
    )
    out_specs = (P("pipe", None, "seq", None), P("pipe", None, "seq", None, None))
    return jax.shard_map(body, mesh=mesh, in_specs=in_specs, out_specs=out_specs, check_vma=False)
```

```python
import functools
import math

import jax
import jax.numpy as jnp
from jax import lax
from jax.experimental import pallas as pl
from jax.experimental.pallas import tpu as pltpu
from jax.sharding import PartitionSpec as P

AXES = ("pipe", "seq")
VMEM = pl.BlockSpec(memory_space=pltpu.VMEM)
ANY = pl.BlockSpec(memory_space=pl.ANY)
HBM = pl.BlockSpec(memory_space=pltpu.HBM)


def normalise(values, params_ref):
    centered = values - jnp.mean(values, axis=-1, keepdims=True)
    spread = jnp.mean(centered * centered, axis=-1, keepdims=True)
    return (
        centered * lax.rsqrt(spread + 1e-06) * (1.0 + params_ref[1:2, :]) + params_ref[0:1, :]
    ).astype(jnp.bfloat16)


def spread_block(block, buffer, out_ref, sems):
    width = buffer.shape[1]
    buffer[...] = block
    copies = [
        pltpu.make_async_copy(buffer, out_ref.at[shard, :, :width], sems.at[shard])
        for shard in range(out_ref.shape[0])
    ]
    for copy in copies:
        copy.start()
    return copies


def norm_kernel(params_ref, x_ref, out_ref, buffer, sems):
    block = normalise(x_ref[...].astype(jnp.float32), params_ref)
    for copy in spread_block(block, buffer, out_ref, sems):
        copy.wait()


def pack_kernel(params_ref, x_ref, cache_ref, out_ref, buffer, sems, sides, sem):
    count, _, total = sides.shape
    width = x_ref.shape[1]
    channels = total // 2
    block = normalise(x_ref[...].astype(jnp.float32), params_ref)
    copies = spread_block(block, buffer, out_ref, sems)
    for kind in range(2):
        rows = cache_ref[:, kind, :]
        for shard in range(count):
            sides[shard, :, kind * channels : (kind + 1) * channels] = rows[
                :, shard * channels : (shard + 1) * channels
            ]
    copies.append(pltpu.make_async_copy(sides, out_ref.at[:, :, width:], sem))
    copies[-1].start()
    for copy in copies:
        copy.wait()


def attention(head_size, q_ref, kv_ref, far_ref):
    factor = 1.0 / math.sqrt(head_size)
    channels = q_ref.shape[1]
    heads = []
    across = (((1,), (1,)), ((), ()))

    def far_of(kind, start):
        if len(far_ref.shape) == 3:
            return far_ref[kind, :, start : start + head_size]
        return far_ref[:, kind * channels + start : kind * channels + start + head_size]

    for start in range(0, channels, head_size):
        cut = slice(start, start + head_size)
        query = q_ref[:, cut]
        near = lax.dot_general(query, kv_ref[0, :, cut], across, preferred_element_type=jnp.float32)
        far = lax.dot_general(query, far_of(0, start), across, preferred_element_type=jnp.float32)
        near = jnp.exp(near * factor)
        far = jnp.exp(far * factor)
        total = jnp.sum(near, axis=-1, keepdims=True) + jnp.sum(far, axis=-1, keepdims=True)
        near = (near / total).astype(jnp.bfloat16)
        far = (far / total).astype(jnp.bfloat16)
        mixed = jnp.dot(near, kv_ref[1, :, cut], preferred_element_type=jnp.float32)
        mixed = mixed + jnp.dot(far, far_of(1, start), preferred_element_type=jnp.float32)
        heads.append(mixed.astype(jnp.bfloat16))
    return jnp.concatenate(heads, axis=1)


def put_cache(caches, out_ref, offset):
    channels = caches[0].shape[2]
    for patch, cache in enumerate(caches):
        for kind in range(2):
            begin = offset + (2 * patch + kind) * channels
            out_ref[:, begin : begin + channels] = cache[kind]


def cache_kernel(*refs):
    put_cache(refs[:-1], refs[-1], 0)


def block_kernel(
    turn, head_size, planes, gain_ref, own_in, other_in, own_out, other_out, blocks_ref, far_ref, *refs
):
    caches, refs = refs[:-11], refs[-11:]
    out_ref, kv_ref, blocks, far, w_in, w_out, parts, q_ref, in_sems, sems, part_sems = refs
    width = blocks.shape[1]
    channels = w_out.shape[0]
    pieces = in_sems.shape[1]
    depth = width // pieces
    mine = lax.rem(lax.axis_index("pipe"), 2) == turn

    def weight_copies(source_in, source_out):
        for part in (1, 2, 0):
            for piece in range(pieces):
                cut = pl.ds(piece * depth, depth)
                pltpu.make_async_copy(
                    source_in.at[part, cut], w_in.at[part, cut], in_sems.at[part, piece]
                ).start()
        pltpu.make_async_copy(source_out.at[0], w_out, sems.at[1]).start()

    fetch = pltpu.make_async_copy(blocks_ref.at[:, :width], blocks, sems.at[0])
    fetch.start()
    if len(far.shape) == 3:
        fetch_far = pltpu.make_async_copy(far_ref, far, sems.at[2])
    else:
        begin = far_ref.shape[1] - far.shape[1]
        fetch_far = pltpu.make_async_copy(far_ref.at[:, begin:], far, sems.at[2])
    fetch_far.start()

    @pl.when(mine)
    def _():
        weight_copies(own_in, own_out)

    @pl.when(jnp.logical_not(mine))
    def _():
        weight_copies(other_in, other_out)

    fetch.wait()
    tokens = blocks[...]
    for part in (1, 2, 0):
        for piece in range(pieces):
            cut = pl.ds(piece * depth, depth)
            pltpu.make_async_copy(
                own_in.at[part, cut], w_in.at[part, cut], in_sems.at[part, piece]
            ).wait()
        projected = jnp.dot(tokens, w_in[part], preferred_element_type=jnp.float32)
        if part == 2:
            kv_ref[1] = projected.astype(jnp.bfloat16)
            continue
        for start in range(0, channels, head_size):
            head = projected[:, start : start + head_size]
            square = jnp.mean(head * head, axis=-1, keepdims=True)
            head = (head * lax.rsqrt(square + 1e-06) * gain_ref[part : part + 1, :]).astype(
                jnp.bfloat16
            )
            if part == 0:
                q_ref[:, start : start + head_size] = head
            else:
                kv_ref[0, :, start : start + head_size] = head

    fetch_far.wait()
    sent = []

    def send(begin, size, sem):
        cut = pl.ds(begin, size)
        sent.append(
            pltpu.make_async_copy(parts.at[:, cut], out_ref.at[:, cut], part_sems.at[sem])
        )
        sent[-1].start()

    steps = part_sems.shape[0] - 1
    if caches:
        last = lax.axis_index("pipe") // 2 == planes - 1
        first, second = caches
        put_cache((first, jnp.where(last, kv_ref[...], second[...])), parts, width)
        send(width, 4 * channels, steps)
    attended = attention(head_size, q_ref, kv_ref, far)
    pltpu.make_async_copy(own_out.at[0], w_out, sems.at[1]).wait()
    tile = width // steps
    for step in range(steps):
        cut = slice(step * tile, (step + 1) * tile)
        update = jnp.dot(attended, w_out[:, cut], preferred_element_type=jnp.float32)
        parts[:, cut] = update.astype(jnp.bfloat16)
        send(step * tile, tile, step)
    for copy in sent:
        copy.wait()


def place_cache(caches, out_ref, offset):
    channels = (caches.shape[2] - offset) // 4
    for patch in range(2):
        for shard in range(caches.shape[0]):
            begin = offset + 2 * patch * channels
            sides = [
                caches[shard, :, begin + kind * channels : begin + (kind + 1) * channels].astype(
                    jnp.float32
                )
                for kind in range(2)
            ]
            out_ref[patch, :, :, shard * channels : (shard + 1) * channels] = jnp.stack(
                sides, axis=1
            ).astype(jnp.bfloat16)


def place_kernel(caches_ref, out_ref):
    place_cache(caches_ref, out_ref, 0)


def last_kernel(params_ref, x_ref, parts_ref, out_ref, cache_ref):
    width = x_ref.shape[1]
    update = jnp.sum(parts_ref[:, :, :width].astype(jnp.float32), axis=0)
    out_ref[...] = (x_ref[...].astype(jnp.float32) + params_ref[2:3, :] * update).astype(
        jnp.bfloat16
    )
    place_cache(parts_ref, cache_ref, width)


def pair_kernel(mine_ref, theirs_ref, out_ref):
    mine, theirs = mine_ref[...], theirs_ref[...]
    early = lax.rem(lax.axis_index("pipe"), 2) == 0
    out_ref[0] = jnp.where(early, mine, theirs)
    out_ref[1] = jnp.where(early, theirs, mine)


def finish_kernel(params_ref, next_ref, x_ref, parts_ref, out_ref, *rest):
    width = x_ref.shape[1]
    update = jnp.sum(parts_ref[:, :, :width].astype(jnp.float32), axis=0)
    result = (x_ref[...].astype(jnp.float32) + params_ref[2:3, :] * update).astype(jnp.bfloat16)
    out_ref[...] = result
    if rest:
        blocks_ref, buffer, sems = rest
        block = normalise(result.astype(jnp.float32), next_ref)
        for copy in spread_block(block, buffer, blocks_ref, sems):
            copy.wait()


def blank_kernel(*refs):
    pass


def params_of(limit):
    return pltpu.CompilerParams(vmem_limit_bytes=limit << 20)


def body(hidden, mod_shift, mod_scale, mod_gate, norm_gain, input_proj, output_proj, stale_cache):
    sections = lax.axis_size("pipe")
    planes = sections // 2
    seq = lax.axis_size("seq")
    pipe = lax.axis_index("pipe")
    core = lax.rem(pipe, 2)
    plane = pipe // 2
    rows, width = hidden.shape[1:]
    head_size = norm_gain.shape[2]
    channels = input_proj.shape[3]
    tokens = rows * seq
    bf16 = lambda *shape: jax.ShapeDtypeStruct(shape, jnp.bfloat16)

    place = lambda row, position: row * seq + position

    def swap(value):
        pairs = [(place(row, s), place(row ^ 1, s)) for row in range(sections) for s in range(seq)]
        return lax.ppermute(value, AXES, pairs)

    def upward(value, level, side):
        row = 2 * level + side
        return lax.ppermute(value, AXES, [(place(row, s), place(row + 2, s)) for s in range(seq)])

    def across(blocks):
        return lax.all_to_all(blocks, "seq", split_axis=0, concat_axis=0, tiled=True)

    def blank(*shapes):
        return pl.pallas_call(blank_kernel, out_shape=shapes, out_specs=(ANY,) * len(shapes))()

    gains = jnp.pad(norm_gain[0].reshape(1, -1), ((0, 0), (0, width - 2 * head_size)))
    own_params = jnp.concatenate([mod_shift, mod_scale, mod_gate, gains], axis=0)
    own_in = jnp.transpose(input_proj[0], (1, 0, 2))
    own_out = output_proj
    x = lax.dynamic_index_in_dim(hidden, core, 0, keepdims=False)
    spreading = [pltpu.VMEM((rows, width), jnp.bfloat16), pltpu.SemaphoreType.DMA((seq,))]
    packed = pl.pallas_call(
        pack_kernel, out_shape=bf16(seq, rows, width + 2 * channels),
        in_specs=[VMEM] * 3, out_specs=HBM,
        scratch_shapes=spreading + [
            pltpu.VMEM((seq, rows, 2 * channels), jnp.bfloat16), pltpu.SemaphoreType.DMA,
        ],
        compiler_params=params_of(16),
    )(own_params, x, stale_cache[0, 1])

    other_params = swap(own_params)
    own_in, own_out, other_params, packed = lax.optimization_barrier(
        (own_in, own_out, other_params, packed)
    )
    other_in = swap(own_in)
    other_out = swap(own_out)
    params = [jnp.where(core == turn, own_params, other_params) for turn in range(2)]
    gain_rows = [p[3, : 2 * head_size].reshape(2, head_size) for p in params]
    blocks_shape = bf16(seq, rows, width)

    def norm(x, turn):
        return pl.pallas_call(
            norm_kernel, out_shape=blocks_shape, in_specs=[VMEM] * 2, out_specs=HBM,
            scratch_shapes=spreading, compiler_params=params_of(16),
        )(params[turn], x)

    flat = lambda blocks: blocks.reshape(tokens, blocks.shape[2])
    apart = lambda values: values.reshape(seq, rows, values.shape[1])

    def block(blocks, far, turn, caches=()):
        total = width + 2 * channels * len(caches)
        side = (2, tokens, channels) if far.ndim == 3 else (tokens, 2 * channels)
        out, pair = pl.pallas_call(
            functools.partial(block_kernel, turn, head_size, planes),
            out_shape=(bf16(tokens, total), bf16(2, tokens, channels)),
            in_specs=[VMEM] + [HBM] * 4 + [ANY] * 2 + [VMEM] * len(caches),
            out_specs=(HBM, VMEM),
            scratch_shapes=[
                pltpu.VMEM((tokens, width), jnp.bfloat16),
                pltpu.VMEM(side, jnp.bfloat16),
                pltpu.VMEM(own_in.shape, jnp.bfloat16),
                pltpu.VMEM(own_out.shape[1:], jnp.bfloat16),
                pltpu.VMEM((tokens, total), jnp.bfloat16),
                pltpu.VMEM((tokens, channels), jnp.bfloat16),
                pltpu.SemaphoreType.DMA((3, 2)),
                pltpu.SemaphoreType.DMA((3,)),
                pltpu.SemaphoreType.DMA((5,)),
            ],
            compiler_params=params_of(32),
        )(
            gain_rows[turn], own_in, other_in, own_out, other_out, flat(blocks), far, *caches
        )
        return apart(out), pair

    def finish(x, parts, turn, onward):
        shapes = (bf16(rows, width),) + (blocks_shape,) * onward
        return pl.pallas_call(
            finish_kernel, out_shape=shapes, in_specs=[VMEM] * 4,
            out_specs=(VMEM,) + (HBM,) * onward,
            scratch_shapes=spreading * onward, compiler_params=params_of(16),
        )(params[turn], params[1 - turn], x, parts)

    early = core == 0
    either = lambda on_early, on_late: lax.cond(early, on_early, on_late)

    def first_early():
        return across(packed), blank(bf16(tokens, 2 * channels))[0]

    def first_late():
        return blank(bf16(*packed.shape))[0], flat(across(packed[:, :, width:]))

    received, stale = either(first_early, first_late)
    stales = [flat(received), swap(stale)]
    pair_shape, block_shape = bf16(2, tokens, channels), bf16(rows, width)
    late_pair = None
    early_x, late_x = x, x
    blocks_out, sources = {}, {}
    for layer in range(sections):
        turn, level = layer % 2, layer // 2
        crossing = layer > 0 and turn == 0

        def early_scatter():
            parts, fresh = block(received, stales[turn], turn)
            return parts, fresh, blank(block_shape)[0]

        def late_gather():
            old = late_pair if turn else blank(pair_shape)[0]
            if turn == 0:
                return norm(late_x, turn), old, blank(block_shape)[0]
            result, normed = finish(late_x, received, 1 - turn, 1)
            return normed, old, result

        if crossing:
            late_x = either(
                lambda: blank(block_shape)[0], lambda: finish(late_x, received, 1 - turn, 0)[0]
            )
            blocks_out[layer - 1, 1] = late_x
            late_x = upward(late_x, level - 1, 1)
        payload, pair, result = either(early_scatter, late_gather)
        if turn:
            late_x = blocks_out[layer - 1, 1] = result
        sources[layer, 0] = pair
        got = swap(pair)
        sources[layer, 2] = got
        received = across(payload)
        if layer == sections - 1:
            break

        crossing = turn == 1

        def early_gather():
            if crossing:
                return norm(early_x, 1 - turn), blank(pair_shape)[0], blank(block_shape)[0]
            result = finish(early_x, received, turn, 0)[0]
            return norm(result, 1 - turn), blank(pair_shape)[0], result

        def late_scatter():
            parts, fresh = block(received, got, turn)
            return parts, fresh, blank(block_shape)[0]

        if crossing:
            early_x = either(
                lambda: finish(early_x, received, turn, 0)[0], lambda: blank(block_shape)[0]
            )
            blocks_out[layer, 0] = early_x
            early_x = upward(early_x, level, 0)
        payload, late_pair, result = either(early_gather, late_scatter)
        if not crossing:
            early_x = blocks_out[layer, 0] = result
        sources[layer, 1] = late_pair
        if crossing:
            active = pipe == jnp.where(early, 2 * level + 2, 2 * level + 1)
            received = lax.cond(active, across, lambda _: blank(blocks_shape)[0], payload)
        else:
            received = across(payload)

    def by_plane(values):
        chosen = values[0]
        for level in range(1, planes):
            chosen = jnp.where(plane == level, values[level], chosen)
        return chosen

    last = sections - 1
    first_cache = by_plane(
        [jnp.where(early, sources[2 * m, 0], sources[2 * m + 1, 2]) for m in range(planes)]
    )
    second_cache = by_plane(
        [
            jnp.where(early, sources[2 * m + 1, 2], sources[2 * m + 1, int(m < planes - 1)])
            for m in range(planes)
        ]
    )

    cache_shape = bf16(2, rows, 2, seq * channels)

    def last_early():
        result = finish(early_x, received, last % 2, 0)[0]
        packed = pl.pallas_call(
            cache_kernel, out_shape=bf16(tokens, 4 * channels),
            in_specs=[VMEM] * 2, out_specs=VMEM, compiler_params=params_of(16),
        )(first_cache, second_cache)
        cache = pl.pallas_call(
            place_kernel, out_shape=cache_shape, in_specs=[VMEM], out_specs=VMEM,
            compiler_params=params_of(16),
        )(across(apart(packed)))
        return result, cache

    def last_late():
        parts, _ = block(received, got, last % 2, (first_cache, second_cache))
        return tuple(
            pl.pallas_call(
                last_kernel, out_shape=(block_shape, cache_shape),
                in_specs=[VMEM] * 3, out_specs=(VMEM,) * 2, compiler_params=params_of(16),
            )(params[last % 2], late_x, across(parts))
        )

    x, cache = either(last_early, last_late)
    blocks_out[last, 0] = blocks_out[last, 1] = x
    mine = by_plane(
        [jnp.where(early, blocks_out[2 * m, 0], blocks_out[2 * m + 1, 1]) for m in range(planes)]
    )
    theirs = swap(
        by_plane(
            [jnp.where(early, blocks_out[2 * m + 1, 0], blocks_out[2 * m, 1]) for m in range(planes)]
        )
    )
    block_output = pl.pallas_call(
        pair_kernel, out_shape=bf16(2, rows, width), in_specs=[VMEM] * 2, out_specs=VMEM,
        compiler_params=params_of(16),
    )(mine, theirs)
    return block_output[None], cache[None]


def solution(mesh):
    in_specs = (
        P(None, "seq", None),
        P("pipe", None),
        P("pipe", None),
        P("pipe", None),
        P("pipe", None, None),
        P("pipe", None, None, "seq"),
        P("pipe", "seq", None),
        P("pipe", None, "seq", None, None),
    )
    out_specs = (P("pipe", None, "seq", None), P("pipe", None, "seq", None, None))
    return jax.shard_map(body, mesh=mesh, in_specs=in_specs, out_specs=out_specs, check_vma=False)
```

```python
import functools
import math

import jax
import jax.numpy as jnp
from jax import lax
from jax.experimental import pallas as pl
from jax.experimental.pallas import tpu as pltpu
from jax.sharding import PartitionSpec as P

AXES = ("pipe", "seq")
VMEM = pl.BlockSpec(memory_space=pltpu.VMEM)
ANY = pl.BlockSpec(memory_space=pl.ANY)
HBM = pl.BlockSpec(memory_space=pltpu.HBM)


def normalise(values, params_ref):
    centered = values - jnp.mean(values, axis=-1, keepdims=True)
    spread = jnp.mean(centered * centered, axis=-1, keepdims=True)
    return (
        centered * lax.rsqrt(spread + 1e-06) * (1.0 + params_ref[1:2, :]) + params_ref[0:1, :]
    ).astype(jnp.bfloat16)


def spread_block(block, buffer, out_ref, sems):
    width = buffer.shape[1]
    buffer[...] = block
    copies = [
        pltpu.make_async_copy(buffer, out_ref.at[shard, :, :width], sems.at[shard])
        for shard in range(out_ref.shape[0])
    ]
    for copy in copies:
        copy.start()
    return copies


def norm_kernel(params_ref, x_ref, out_ref, buffer, sems):
    block = normalise(x_ref[...].astype(jnp.float32), params_ref)
    for copy in spread_block(block, buffer, out_ref, sems):
        copy.wait()


def pack_kernel(params_ref, x_ref, cache_ref, out_ref, buffer, sems, sides, sem):
    count, _, total = sides.shape
    width = x_ref.shape[1]
    channels = total // 2
    block = normalise(x_ref[...].astype(jnp.float32), params_ref)
    copies = spread_block(block, buffer, out_ref, sems)
    for kind in range(2):
        rows = cache_ref[:, kind, :]
        for shard in range(count):
            sides[shard, :, kind * channels : (kind + 1) * channels] = rows[
                :, shard * channels : (shard + 1) * channels
            ]
    copies.append(pltpu.make_async_copy(sides, out_ref.at[:, :, width:], sem))
    copies[-1].start()
    for copy in copies:
        copy.wait()


def attention(head_size, q_ref, kv_ref, far_ref):
    factor = 1.0 / math.sqrt(head_size)
    channels = q_ref.shape[1]
    heads = []
    across = (((1,), (1,)), ((), ()))

    def far_of(kind, start):
        if len(far_ref.shape) == 3:
            return far_ref[kind, :, start : start + head_size]
        return far_ref[:, kind * channels + start : kind * channels + start + head_size]

    for start in range(0, channels, head_size):
        cut = slice(start, start + head_size)
        query = q_ref[:, cut]
        near = lax.dot_general(query, kv_ref[0, :, cut], across, preferred_element_type=jnp.float32)
        far = lax.dot_general(query, far_of(0, start), across, preferred_element_type=jnp.float32)
        near = jnp.exp(near * factor)
        far = jnp.exp(far * factor)
        total = jnp.sum(near, axis=-1, keepdims=True) + jnp.sum(far, axis=-1, keepdims=True)
        near = (near / total).astype(jnp.bfloat16)
        far = (far / total).astype(jnp.bfloat16)
        mixed = jnp.dot(near, kv_ref[1, :, cut], preferred_element_type=jnp.float32)
        mixed = mixed + jnp.dot(far, far_of(1, start), preferred_element_type=jnp.float32)
        heads.append(mixed.astype(jnp.bfloat16))
    return jnp.concatenate(heads, axis=1)


def put_cache(caches, out_ref, offset):
    channels = caches[0].shape[2]
    for patch, cache in enumerate(caches):
        for kind in range(2):
            begin = offset + (2 * patch + kind) * channels
            out_ref[:, begin : begin + channels] = cache[kind]


def cache_kernel(*refs):
    put_cache(refs[:-1], refs[-1], 0)


def block_kernel(
    turn, head_size, planes, gain_ref, own_in, other_in, own_out, other_out, blocks_ref, far_ref, *refs
):
    caches, refs = refs[:-11], refs[-11:]
    out_ref, kv_ref, blocks, far, w_in, w_out, parts, q_ref, in_sems, sems, part_sems = refs
    width = blocks.shape[1]
    channels = w_out.shape[0]
    pieces = in_sems.shape[1]
    depth = width // pieces
    mine = lax.rem(lax.axis_index("pipe"), 2) == turn

    def weight_copies(source_in, source_out):
        for part in (1, 2, 0):
            for piece in range(pieces):
                cut = pl.ds(piece * depth, depth)
                pltpu.make_async_copy(
                    source_in.at[part, cut], w_in.at[part, cut], in_sems.at[part, piece]
                ).start()
        pltpu.make_async_copy(source_out.at[0], w_out, sems.at[1]).start()

    fetch = pltpu.make_async_copy(blocks_ref.at[:, :width], blocks, sems.at[0])
    fetch.start()
    if len(far.shape) == 3:
        fetch_far = pltpu.make_async_copy(far_ref, far, sems.at[2])
    else:
        begin = far_ref.shape[1] - far.shape[1]
        fetch_far = pltpu.make_async_copy(far_ref.at[:, begin:], far, sems.at[2])
    fetch_far.start()

    @pl.when(mine)
    def _():
        weight_copies(own_in, own_out)

    @pl.when(jnp.logical_not(mine))
    def _():
        weight_copies(other_in, other_out)

    fetch.wait()
    tokens = blocks[...]
    for part in (1, 2, 0):
        for piece in range(pieces):
            cut = pl.ds(piece * depth, depth)
            pltpu.make_async_copy(
                own_in.at[part, cut], w_in.at[part, cut], in_sems.at[part, piece]
            ).wait()
        projected = jnp.dot(tokens, w_in[part], preferred_element_type=jnp.float32)
        if part == 2:
            kv_ref[1] = projected.astype(jnp.bfloat16)
            continue
        for start in range(0, channels, head_size):
            head = projected[:, start : start + head_size]
            square = jnp.mean(head * head, axis=-1, keepdims=True)
            head = (head * lax.rsqrt(square + 1e-06) * gain_ref[part : part + 1, :]).astype(
                jnp.bfloat16
            )
            if part == 0:
                q_ref[:, start : start + head_size] = head
            else:
                kv_ref[0, :, start : start + head_size] = head

    fetch_far.wait()
    sent = []

    def send(begin, size, sem):
        cut = pl.ds(begin, size)
        sent.append(
            pltpu.make_async_copy(parts.at[:, cut], out_ref.at[:, cut], part_sems.at[sem])
        )
        sent[-1].start()

    steps = part_sems.shape[0] - 1
    if caches:
        last = lax.axis_index("pipe") // 2 == planes - 1
        first, second = caches
        put_cache((first, jnp.where(last, kv_ref[...], second[...])), parts, width)
        send(width, 4 * channels, steps)
    attended = attention(head_size, q_ref, kv_ref, far)
    pltpu.make_async_copy(own_out.at[0], w_out, sems.at[1]).wait()
    tile = width // steps
    for step in range(steps):
        cut = slice(step * tile, (step + 1) * tile)
        update = jnp.dot(attended, w_out[:, cut], preferred_element_type=jnp.float32)
        parts[:, cut] = update.astype(jnp.bfloat16)
        send(step * tile, tile, step)
    for copy in sent:
        copy.wait()


def place_cache(caches, out_ref, offset):
    channels = (caches.shape[2] - offset) // 4
    for patch in range(2):
        for shard in range(caches.shape[0]):
            begin = offset + 2 * patch * channels
            sides = [
                caches[shard, :, begin + kind * channels : begin + (kind + 1) * channels].astype(
                    jnp.float32
                )
                for kind in range(2)
            ]
            out_ref[patch, :, :, shard * channels : (shard + 1) * channels] = jnp.stack(
                sides, axis=1
            ).astype(jnp.bfloat16)


def place_kernel(caches_ref, out_ref):
    place_cache(caches_ref, out_ref, 0)


def last_kernel(params_ref, x_ref, parts_ref, out_ref, cache_ref):
    width = x_ref.shape[1]
    update = jnp.sum(parts_ref[:, :, :width].astype(jnp.float32), axis=0)
    out_ref[...] = (x_ref[...].astype(jnp.float32) + params_ref[2:3, :] * update).astype(
        jnp.bfloat16
    )
    place_cache(parts_ref, cache_ref, width)


def pair_kernel(mine_ref, theirs_ref, out_ref):
    mine, theirs = mine_ref[...], theirs_ref[...]
    early = lax.rem(lax.axis_index("pipe"), 2) == 0
    out_ref[0] = jnp.where(early, mine, theirs)
    out_ref[1] = jnp.where(early, theirs, mine)


def finish_kernel(params_ref, next_ref, x_ref, parts_ref, out_ref, *rest):
    width = x_ref.shape[1]
    update = jnp.sum(parts_ref[:, :, :width].astype(jnp.float32), axis=0)
    result = (x_ref[...].astype(jnp.float32) + params_ref[2:3, :] * update).astype(jnp.bfloat16)
    out_ref[...] = result
    if rest:
        blocks_ref, buffer, sems = rest
        block = normalise(result.astype(jnp.float32), next_ref)
        for copy in spread_block(block, buffer, blocks_ref, sems):
            copy.wait()


def blank_kernel(*refs):
    pass


def params_of(limit):
    return pltpu.CompilerParams(vmem_limit_bytes=limit << 20)


def body(hidden, mod_shift, mod_scale, mod_gate, norm_gain, input_proj, output_proj, stale_cache):
    sections = lax.axis_size("pipe")
    planes = sections // 2
    seq = lax.axis_size("seq")
    pipe = lax.axis_index("pipe")
    core = lax.rem(pipe, 2)
    plane = pipe // 2
    rows, width = hidden.shape[1:]
    head_size = norm_gain.shape[2]
    channels = input_proj.shape[3]
    tokens = rows * seq
    bf16 = lambda *shape: jax.ShapeDtypeStruct(shape, jnp.bfloat16)

    place = lambda row, position: row * seq + position

    def swap(value):
        pairs = [(place(row, s), place(row ^ 1, s)) for row in range(sections) for s in range(seq)]
        return lax.ppermute(value, AXES, pairs)

    def upward(value, level, side):
        row = 2 * level + side
        return lax.ppermute(value, AXES, [(place(row, s), place(row + 2, s)) for s in range(seq)])

    def across(blocks):
        return lax.all_to_all(blocks, "seq", split_axis=0, concat_axis=0, tiled=True)

    def blank(*shapes):
        return pl.pallas_call(blank_kernel, out_shape=shapes, out_specs=(ANY,) * len(shapes))()

    gains = jnp.pad(norm_gain[0].reshape(1, -1), ((0, 0), (0, width - 2 * head_size)))
    own_params = jnp.concatenate([mod_shift, mod_scale, mod_gate, gains], axis=0)
    own_in = jnp.transpose(input_proj[0], (1, 0, 2))
    own_out = output_proj
    x = lax.dynamic_index_in_dim(hidden, core, 0, keepdims=False)
    spreading = [pltpu.VMEM((rows, width), jnp.bfloat16), pltpu.SemaphoreType.DMA((seq,))]
    packed = pl.pallas_call(
        pack_kernel, out_shape=bf16(seq, rows, width + 2 * channels),
        in_specs=[VMEM] * 3, out_specs=HBM,
        scratch_shapes=spreading + [
            pltpu.VMEM((seq, rows, 2 * channels), jnp.bfloat16), pltpu.SemaphoreType.DMA,
        ],
        compiler_params=params_of(16),
    )(own_params, x, stale_cache[0, 1])

    other_params = swap(own_params)
    own_in, own_out, other_params, packed = lax.optimization_barrier(
        (own_in, own_out, other_params, packed)
    )
    other_in = swap(own_in)
    other_out = swap(own_out)
    params = [jnp.where(core == turn, own_params, other_params) for turn in range(2)]
    gain_rows = [p[3, : 2 * head_size].reshape(2, head_size) for p in params]
    blocks_shape = bf16(seq, rows, width)

    def norm(x, turn):
        return pl.pallas_call(
            norm_kernel, out_shape=blocks_shape, in_specs=[VMEM] * 2, out_specs=HBM,
            scratch_shapes=spreading, compiler_params=params_of(16),
        )(params[turn], x)

    flat = lambda blocks: blocks.reshape(tokens, blocks.shape[2])
    apart = lambda values: values.reshape(seq, rows, values.shape[1])

    def block(blocks, far, turn, caches=()):
        total = width + 2 * channels * len(caches)
        side = (2, tokens, channels) if far.ndim == 3 else (tokens, 2 * channels)
        out, pair = pl.pallas_call(
            functools.partial(block_kernel, turn, head_size, planes),
            out_shape=(bf16(tokens, total), bf16(2, tokens, channels)),
            in_specs=[VMEM] + [HBM] * 4 + [ANY] * 2 + [VMEM] * len(caches),
            out_specs=(HBM, VMEM),
            scratch_shapes=[
                pltpu.VMEM((tokens, width), jnp.bfloat16),
                pltpu.VMEM(side, jnp.bfloat16),
                pltpu.VMEM(own_in.shape, jnp.bfloat16),
                pltpu.VMEM(own_out.shape[1:], jnp.bfloat16),
                pltpu.VMEM((tokens, total), jnp.bfloat16),
                pltpu.VMEM((tokens, channels), jnp.bfloat16),
                pltpu.SemaphoreType.DMA((3, 2)),
                pltpu.SemaphoreType.DMA((3,)),
                pltpu.SemaphoreType.DMA((5,)),
            ],
            compiler_params=params_of(32),
        )(
            gain_rows[turn], own_in, other_in, own_out, other_out, flat(blocks), far, *caches
        )
        return apart(out), pair

    def finish(x, parts, turn, onward):
        shapes = (bf16(rows, width),) + (blocks_shape,) * onward
        return pl.pallas_call(
            finish_kernel, out_shape=shapes, in_specs=[VMEM] * 4,
            out_specs=(VMEM,) + (HBM,) * onward,
            scratch_shapes=spreading * onward, compiler_params=params_of(16),
        )(params[turn], params[1 - turn], x, parts)

    early = core == 0
    either = lambda on_early, on_late: lax.cond(early, on_early, on_late)

    def first_early():
        return across(packed), blank(bf16(tokens, 2 * channels))[0]

    def first_late():
        return blank(bf16(*packed.shape))[0], flat(across(packed[:, :, width:]))

    received, stale = either(first_early, first_late)
    stales = [flat(received), swap(stale)]
    pair_shape, block_shape = bf16(2, tokens, channels), bf16(rows, width)
    late_pair = None
    early_x, late_x = x, x
    blocks_out, sources = {}, {}
    for layer in range(sections):
        turn, level = layer % 2, layer // 2
        crossing = layer > 0 and turn == 0

        def early_scatter():
            parts, fresh = block(received, stales[turn], turn)
            return parts, fresh, blank(block_shape)[0]

        def late_gather():
            old = late_pair if turn else blank(pair_shape)[0]
            if turn == 0:
                return norm(late_x, turn), old, blank(block_shape)[0]
            result, normed = finish(late_x, received, 1 - turn, 1)
            return normed, old, result

        if crossing:
            late_x = either(
                lambda: blank(block_shape)[0], lambda: finish(late_x, received, 1 - turn, 0)[0]
            )
            blocks_out[layer - 1, 1] = late_x
            late_x = upward(late_x, level - 1, 1)
        payload, pair, result = either(early_scatter, late_gather)
        if turn:
            late_x = blocks_out[layer - 1, 1] = result
        sources[layer, 0] = pair
        got = swap(pair)
        sources[layer, 2] = got
        received = across(payload)
        if layer == sections - 1:
            break

        crossing = turn == 1

        def early_gather():
            if crossing:
                return norm(early_x, 1 - turn), blank(pair_shape)[0], blank(block_shape)[0]
            if level:
                result = finish(early_x, received, turn, 0)[0]
                return norm(result, 1 - turn), blank(pair_shape)[0], result
            result, normed = finish(early_x, received, turn, 1)
            return normed, blank(pair_shape)[0], result

        def late_scatter():
            parts, fresh = block(received, got, turn)
            return parts, fresh, blank(block_shape)[0]

        if crossing:
            early_x = either(
                lambda: finish(early_x, received, turn, 0)[0], lambda: blank(block_shape)[0]
            )
            blocks_out[layer, 0] = early_x
            early_x = upward(early_x, level, 0)
        payload, late_pair, result = either(early_gather, late_scatter)
        if not crossing:
            early_x = blocks_out[layer, 0] = result
        sources[layer, 1] = late_pair
        if crossing:
            active = pipe == jnp.where(early, 2 * level + 2, 2 * level + 1)
            received = lax.cond(active, across, lambda _: blank(blocks_shape)[0], payload)
        else:
            received = across(payload)

    def by_plane(values):
        chosen = values[0]
        for level in range(1, planes):
            chosen = jnp.where(plane == level, values[level], chosen)
        return chosen

    last = sections - 1
    first_cache = by_plane(
        [jnp.where(early, sources[2 * m, 0], sources[2 * m + 1, 2]) for m in range(planes)]
    )
    second_cache = by_plane(
        [
            jnp.where(early, sources[2 * m + 1, 2], sources[2 * m + 1, int(m < planes - 1)])
            for m in range(planes)
        ]
    )

    cache_shape = bf16(2, rows, 2, seq * channels)

    def last_early():
        result = finish(early_x, received, last % 2, 0)[0]
        packed = pl.pallas_call(
            cache_kernel, out_shape=bf16(tokens, 4 * channels),
            in_specs=[VMEM] * 2, out_specs=VMEM, compiler_params=params_of(16),
        )(first_cache, second_cache)
        cache = pl.pallas_call(
            place_kernel, out_shape=cache_shape, in_specs=[VMEM], out_specs=VMEM,
            compiler_params=params_of(16),
        )(across(apart(packed)))
        return result, cache

    def last_late():
        parts, _ = block(received, got, last % 2, (first_cache, second_cache))
        return tuple(
            pl.pallas_call(
                last_kernel, out_shape=(block_shape, cache_shape),
                in_specs=[VMEM] * 3, out_specs=(VMEM,) * 2, compiler_params=params_of(16),
            )(params[last % 2], late_x, across(parts))
        )

    x, cache = either(last_early, last_late)
    blocks_out[last, 0] = blocks_out[last, 1] = x
    mine = by_plane(
        [jnp.where(early, blocks_out[2 * m, 0], blocks_out[2 * m + 1, 1]) for m in range(planes)]
    )
    theirs = swap(
        by_plane(
            [jnp.where(early, blocks_out[2 * m + 1, 0], blocks_out[2 * m, 1]) for m in range(planes)]
        )
    )
    block_output = pl.pallas_call(
        pair_kernel, out_shape=bf16(2, rows, width), in_specs=[VMEM] * 2, out_specs=VMEM,
        compiler_params=params_of(16),
    )(mine, theirs)
    return block_output[None], cache[None]


def solution(mesh):
    in_specs = (
        P(None, "seq", None),
        P("pipe", None),
        P("pipe", None),
        P("pipe", None),
        P("pipe", None, None),
        P("pipe", None, None, "seq"),
        P("pipe", "seq", None),
        P("pipe", None, "seq", None, None),
    )
    out_specs = (P("pipe", None, "seq", None), P("pipe", None, "seq", None, None))
    return jax.shard_map(body, mesh=mesh, in_specs=in_specs, out_specs=out_specs, check_vma=False)
```

```python
import functools
import math

import jax
import jax.numpy as jnp
from jax import lax
from jax.experimental import pallas as pl
from jax.experimental.pallas import tpu as pltpu
from jax.sharding import PartitionSpec as P

AXES = ("pipe", "seq")
VMEM = pl.BlockSpec(memory_space=pltpu.VMEM)
ANY = pl.BlockSpec(memory_space=pl.ANY)
HBM = pl.BlockSpec(memory_space=pltpu.HBM)


def normalise(values, params_ref):
    centered = values - jnp.mean(values, axis=-1, keepdims=True)
    spread = jnp.mean(centered * centered, axis=-1, keepdims=True)
    return (
        centered * lax.rsqrt(spread + 1e-06) * (1.0 + params_ref[1:2, :]) + params_ref[0:1, :]
    ).astype(jnp.bfloat16)


def spread_block(block, buffer, out_ref, sems):
    width = buffer.shape[1]
    buffer[...] = block
    copies = [
        pltpu.make_async_copy(buffer, out_ref.at[shard, :, :width], sems.at[shard])
        for shard in range(out_ref.shape[0])
    ]
    for copy in copies:
        copy.start()
    return copies


def norm_kernel(params_ref, x_ref, out_ref, buffer, sems):
    block = normalise(x_ref[...].astype(jnp.float32), params_ref)
    for copy in spread_block(block, buffer, out_ref, sems):
        copy.wait()


def pack_kernel(params_ref, x_ref, cache_ref, out_ref, buffer, sems, sides, sem):
    count, _, total = sides.shape
    width = x_ref.shape[1]
    channels = total // 2
    block = normalise(x_ref[...].astype(jnp.float32), params_ref)
    copies = spread_block(block, buffer, out_ref, sems)
    for kind in range(2):
        rows = cache_ref[:, kind, :]
        for shard in range(count):
            sides[shard, :, kind * channels : (kind + 1) * channels] = rows[
                :, shard * channels : (shard + 1) * channels
            ]
    copies.append(pltpu.make_async_copy(sides, out_ref.at[:, :, width:], sem))
    copies[-1].start()
    for copy in copies:
        copy.wait()


def attention(head_size, q_ref, kv_ref, far_ref):
    factor = 1.0 / math.sqrt(head_size)
    channels = q_ref.shape[1]
    heads = []
    across = (((1,), (1,)), ((), ()))

    def far_of(kind, start):
        if len(far_ref.shape) == 3:
            return far_ref[kind, :, start : start + head_size]
        return far_ref[:, kind * channels + start : kind * channels + start + head_size]

    for start in range(0, channels, head_size):
        cut = slice(start, start + head_size)
        query = q_ref[:, cut]
        near = lax.dot_general(query, kv_ref[0, :, cut], across, preferred_element_type=jnp.float32)
        far = lax.dot_general(query, far_of(0, start), across, preferred_element_type=jnp.float32)
        near = jnp.exp(near * factor)
        far = jnp.exp(far * factor)
        total = jnp.sum(near, axis=-1, keepdims=True) + jnp.sum(far, axis=-1, keepdims=True)
        near = (near / total).astype(jnp.bfloat16)
        far = (far / total).astype(jnp.bfloat16)
        mixed = jnp.dot(near, kv_ref[1, :, cut], preferred_element_type=jnp.float32)
        mixed = mixed + jnp.dot(far, far_of(1, start), preferred_element_type=jnp.float32)
        heads.append(mixed.astype(jnp.bfloat16))
    return jnp.concatenate(heads, axis=1)


def put_cache(caches, out_ref, offset):
    channels = caches[0].shape[2]
    for patch, cache in enumerate(caches):
        for kind in range(2):
            begin = offset + (2 * patch + kind) * channels
            out_ref[:, begin : begin + channels] = cache[kind]


def cache_kernel(*refs):
    put_cache(refs[:-1], refs[-1], 0)


def block_kernel(
    turn, head_size, planes, gain_ref, own_in, other_in, own_out, other_out, blocks_ref, far_ref, *refs
):
    caches, refs = refs[:-11], refs[-11:]
    out_ref, kv_ref, blocks, far, w_in, w_out, parts, q_ref, in_sems, sems, part_sems = refs
    width = blocks.shape[1]
    channels = w_out.shape[0]
    pieces = in_sems.shape[1]
    depth = width // pieces
    mine = lax.rem(lax.axis_index("pipe"), 2) == turn

    def weight_copies(source_in, source_out):
        for part in (1, 2, 0):
            for piece in range(pieces):
                cut = pl.ds(piece * depth, depth)
                pltpu.make_async_copy(
                    source_in.at[part, cut], w_in.at[part, cut], in_sems.at[part, piece]
                ).start()
        pltpu.make_async_copy(source_out.at[0], w_out, sems.at[1]).start()

    fetch = pltpu.make_async_copy(blocks_ref.at[:, :width], blocks, sems.at[0])
    fetch.start()
    if len(far.shape) == 3:
        fetch_far = pltpu.make_async_copy(far_ref, far, sems.at[2])
    else:
        begin = far_ref.shape[1] - far.shape[1]
        fetch_far = pltpu.make_async_copy(far_ref.at[:, begin:], far, sems.at[2])
    fetch_far.start()

    @pl.when(mine)
    def _():
        weight_copies(own_in, own_out)

    @pl.when(jnp.logical_not(mine))
    def _():
        weight_copies(other_in, other_out)

    fetch.wait()
    tokens = blocks[...]
    for part in (1, 2, 0):
        for piece in range(pieces):
            cut = pl.ds(piece * depth, depth)
            pltpu.make_async_copy(
                own_in.at[part, cut], w_in.at[part, cut], in_sems.at[part, piece]
            ).wait()
        projected = jnp.dot(tokens, w_in[part], preferred_element_type=jnp.float32)
        if part == 2:
            kv_ref[1] = projected.astype(jnp.bfloat16)
            continue
        for start in range(0, channels, head_size):
            head = projected[:, start : start + head_size]
            square = jnp.mean(head * head, axis=-1, keepdims=True)
            head = (head * lax.rsqrt(square + 1e-06) * gain_ref[part : part + 1, :]).astype(
                jnp.bfloat16
            )
            if part == 0:
                q_ref[:, start : start + head_size] = head
            else:
                kv_ref[0, :, start : start + head_size] = head

    fetch_far.wait()
    sent = []

    def send(begin, size, sem):
        cut = pl.ds(begin, size)
        sent.append(
            pltpu.make_async_copy(parts.at[:, cut], out_ref.at[:, cut], part_sems.at[sem])
        )
        sent[-1].start()

    steps = part_sems.shape[0] - 1
    if caches:
        last = lax.axis_index("pipe") // 2 == planes - 1
        first, second = caches
        put_cache((first, jnp.where(last, kv_ref[...], second[...])), parts, width)
        send(width, 4 * channels, steps)
    attended = attention(head_size, q_ref, kv_ref, far)
    pltpu.make_async_copy(own_out.at[0], w_out, sems.at[1]).wait()
    tile = width // steps
    for step in range(steps):
        cut = slice(step * tile, (step + 1) * tile)
        update = jnp.dot(attended, w_out[:, cut], preferred_element_type=jnp.float32)
        parts[:, cut] = update.astype(jnp.bfloat16)
        send(step * tile, tile, step)
    for copy in sent:
        copy.wait()


def place_cache(caches, out_ref, offset):
    channels = (caches.shape[2] - offset) // 4
    for patch in range(2):
        for shard in range(caches.shape[0]):
            begin = offset + 2 * patch * channels
            sides = [
                caches[shard, :, begin + kind * channels : begin + (kind + 1) * channels].astype(
                    jnp.float32
                )
                for kind in range(2)
            ]
            out_ref[patch, :, :, shard * channels : (shard + 1) * channels] = jnp.stack(
                sides, axis=1
            ).astype(jnp.bfloat16)


def place_kernel(caches_ref, out_ref):
    place_cache(caches_ref, out_ref, 0)


def last_kernel(params_ref, x_ref, parts_ref, out_ref, cache_ref):
    width = x_ref.shape[1]
    update = jnp.sum(parts_ref[:, :, :width].astype(jnp.float32), axis=0)
    out_ref[...] = (x_ref[...].astype(jnp.float32) + params_ref[2:3, :] * update).astype(
        jnp.bfloat16
    )
    place_cache(parts_ref, cache_ref, width)


def pair_kernel(mine_ref, theirs_ref, out_ref):
    mine, theirs = mine_ref[...], theirs_ref[...]
    early = lax.rem(lax.axis_index("pipe"), 2) == 0
    out_ref[0] = jnp.where(early, mine, theirs)
    out_ref[1] = jnp.where(early, theirs, mine)


def finish_kernel(params_ref, next_ref, x_ref, parts_ref, out_ref, *rest):
    width = x_ref.shape[1]
    update = jnp.sum(parts_ref[:, :, :width].astype(jnp.float32), axis=0)
    result = (x_ref[...].astype(jnp.float32) + params_ref[2:3, :] * update).astype(jnp.bfloat16)
    out_ref[...] = result
    if rest:
        blocks_ref, buffer, sems = rest
        block = normalise(result.astype(jnp.float32), next_ref)
        for copy in spread_block(block, buffer, blocks_ref, sems):
            copy.wait()


def blank_kernel(*refs):
    pass


def params_of(limit):
    return pltpu.CompilerParams(vmem_limit_bytes=limit << 20)


def body(hidden, mod_shift, mod_scale, mod_gate, norm_gain, input_proj, output_proj, stale_cache):
    sections = lax.axis_size("pipe")
    planes = sections // 2
    seq = lax.axis_size("seq")
    pipe = lax.axis_index("pipe")
    core = lax.rem(pipe, 2)
    plane = pipe // 2
    rows, width = hidden.shape[1:]
    head_size = norm_gain.shape[2]
    channels = input_proj.shape[3]
    tokens = rows * seq
    bf16 = lambda *shape: jax.ShapeDtypeStruct(shape, jnp.bfloat16)

    place = lambda row, position: row * seq + position

    def swap(value):
        pairs = [(place(row, s), place(row ^ 1, s)) for row in range(sections) for s in range(seq)]
        return lax.ppermute(value, AXES, pairs)

    def upward(value, level, side):
        row = 2 * level + side
        return lax.ppermute(value, AXES, [(place(row, s), place(row + 2, s)) for s in range(seq)])

    def across(blocks):
        return lax.all_to_all(blocks, "seq", split_axis=0, concat_axis=0, tiled=True)

    def blank(*shapes):
        return pl.pallas_call(blank_kernel, out_shape=shapes, out_specs=(ANY,) * len(shapes))()

    gains = jnp.pad(norm_gain[0].reshape(1, -1), ((0, 0), (0, width - 2 * head_size)))
    own_params = jnp.concatenate([mod_shift, mod_scale, mod_gate, gains], axis=0)
    own_in = jnp.transpose(input_proj[0], (1, 0, 2))
    own_out = output_proj
    x = lax.dynamic_index_in_dim(hidden, core, 0, keepdims=False)
    spreading = [pltpu.VMEM((rows, width), jnp.bfloat16), pltpu.SemaphoreType.DMA((seq,))]
    packed = pl.pallas_call(
        pack_kernel, out_shape=bf16(seq, rows, width + 2 * channels),
        in_specs=[VMEM] * 3, out_specs=HBM,
        scratch_shapes=spreading + [
            pltpu.VMEM((seq, rows, 2 * channels), jnp.bfloat16), pltpu.SemaphoreType.DMA,
        ],
        compiler_params=params_of(16),
    )(own_params, x, stale_cache[0, 1])

    other_params = swap(own_params)
    own_in, own_out, other_params, packed = lax.optimization_barrier(
        (own_in, own_out, other_params, packed)
    )
    other_in = swap(own_in)
    other_out = swap(own_out)
    params = [jnp.where(core == turn, own_params, other_params) for turn in range(2)]
    gain_rows = [p[3, : 2 * head_size].reshape(2, head_size) for p in params]
    blocks_shape = bf16(seq, rows, width)

    def norm(x, turn):
        return pl.pallas_call(
            norm_kernel, out_shape=blocks_shape, in_specs=[VMEM] * 2, out_specs=HBM,
            scratch_shapes=spreading, compiler_params=params_of(16),
        )(params[turn], x)

    flat = lambda blocks: blocks.reshape(tokens, blocks.shape[2])
    apart = lambda values: values.reshape(seq, rows, values.shape[1])

    def block(blocks, far, turn, caches=()):
        total = width + 2 * channels * len(caches)
        side = (2, tokens, channels) if far.ndim == 3 else (tokens, 2 * channels)
        out, pair = pl.pallas_call(
            functools.partial(block_kernel, turn, head_size, planes),
            out_shape=(bf16(tokens, total), bf16(2, tokens, channels)),
            in_specs=[VMEM] + [HBM] * 4 + [ANY] * 2 + [VMEM] * len(caches),
            out_specs=(HBM, VMEM),
            scratch_shapes=[
                pltpu.VMEM((tokens, width), jnp.bfloat16),
                pltpu.VMEM(side, jnp.bfloat16),
                pltpu.VMEM(own_in.shape, jnp.bfloat16),
                pltpu.VMEM(own_out.shape[1:], jnp.bfloat16),
                pltpu.VMEM((tokens, total), jnp.bfloat16),
                pltpu.VMEM((tokens, channels), jnp.bfloat16),
                pltpu.SemaphoreType.DMA((3, 2)),
                pltpu.SemaphoreType.DMA((3,)),
                pltpu.SemaphoreType.DMA((5,)),
            ],
            compiler_params=params_of(32),
        )(
            gain_rows[turn], own_in, other_in, own_out, other_out, flat(blocks), far, *caches
        )
        return apart(out), pair

    def finish(x, parts, turn, onward):
        shapes = (bf16(rows, width),) + (blocks_shape,) * onward
        return pl.pallas_call(
            finish_kernel, out_shape=shapes, in_specs=[VMEM] * 4,
            out_specs=(VMEM,) + (HBM,) * onward,
            scratch_shapes=spreading * onward, compiler_params=params_of(16),
        )(params[turn], params[1 - turn], x, parts)

    early = core == 0
    either = lambda on_early, on_late: lax.cond(early, on_early, on_late)

    def first_early():
        return across(packed), blank(bf16(tokens, 2 * channels))[0]

    def first_late():
        return blank(bf16(*packed.shape))[0], flat(across(packed[:, :, width:]))

    received, stale = either(first_early, first_late)
    stales = [flat(received), swap(stale)]
    pair_shape, block_shape = bf16(2, tokens, channels), bf16(rows, width)
    late_pair = None
    early_x, late_x = x, x
    blocks_out, sources = {}, {}
    for layer in range(sections):
        turn, level = layer % 2, layer // 2
        crossing = layer > 0 and turn == 0

        def early_scatter():
            parts, fresh = block(received, stales[turn], turn)
            return parts, fresh, blank(block_shape)[0]

        def late_gather():
            old = late_pair if turn else blank(pair_shape)[0]
            if turn == 0:
                return norm(late_x, turn), old, blank(block_shape)[0]
            result, normed = finish(late_x, received, 1 - turn, 1)
            return normed, old, result

        if crossing:
            late_x = either(
                lambda: blank(block_shape)[0], lambda: finish(late_x, received, 1 - turn, 0)[0]
            )
            blocks_out[layer - 1, 1] = late_x
            late_x = upward(late_x, level - 1, 1)
        payload, pair, result = either(early_scatter, late_gather)
        if turn:
            late_x = blocks_out[layer - 1, 1] = result
        sources[layer, 0] = pair
        got = swap(pair)
        sources[layer, 2] = got
        received = across(payload)
        if layer == sections - 1:
            break

        crossing = turn == 1

        def early_gather():
            if crossing:
                return norm(early_x, 1 - turn), blank(pair_shape)[0], blank(block_shape)[0]
            if level:
                result = finish(early_x, received, turn, 0)[0]
                return norm(result, 1 - turn), blank(pair_shape)[0], result
            result, normed = finish(early_x, received, turn, 1)
            return normed, blank(pair_shape)[0], result

        def late_scatter():
            parts, fresh = block(received, got, turn)
            return parts, fresh, blank(block_shape)[0]

        if crossing:
            early_x = either(
                lambda: finish(early_x, received, turn, 0)[0], lambda: blank(block_shape)[0]
            )
            blocks_out[layer, 0] = early_x
            early_x = upward(early_x, level, 0)
        payload, late_pair, result = either(early_gather, late_scatter)
        if not crossing:
            early_x = blocks_out[layer, 0] = result
        sources[layer, 1] = late_pair
        if crossing:
            active = pipe == jnp.where(early, 2 * level + 2, 2 * level + 1)
            received = lax.cond(active, across, lambda _: blank(blocks_shape)[0], payload)
        else:
            received = across(payload)

    def by_plane(values):
        chosen = values[0]
        for level in range(1, planes):
            chosen = jnp.where(plane == level, values[level], chosen)
        return chosen

    last = sections - 1
    first_cache = by_plane(
        [jnp.where(early, sources[2 * m, 0], sources[2 * m + 1, 2]) for m in range(planes)]
    )
    second_cache = by_plane(
        [
            jnp.where(early, sources[2 * m + 1, 2], sources[2 * m + 1, int(m < planes - 1)])
            for m in range(planes)
        ]
    )

    cache_shape = bf16(2, rows, 2, seq * channels)

    def cache_alone():
        packed = pl.pallas_call(
            cache_kernel, out_shape=bf16(tokens, 4 * channels),
            in_specs=[VMEM] * 2, out_specs=VMEM, compiler_params=params_of(16),
        )(first_cache, second_cache)
        return pl.pallas_call(
            place_kernel, out_shape=cache_shape, in_specs=[VMEM], out_specs=VMEM,
            compiler_params=params_of(16),
        )(across(apart(packed)))

    def last_block():
        parts, _ = block(received, got, last % 2, (first_cache, second_cache))
        return tuple(
            pl.pallas_call(
                last_kernel, out_shape=(block_shape, cache_shape),
                in_specs=[VMEM] * 3, out_specs=(VMEM,) * 2, compiler_params=params_of(16),
            )(params[last % 2], late_x, across(parts))
        )

    def last_early():
        return finish(early_x, received, last % 2, 0)[0], cache_alone()

    def last_late():
        return lax.cond(
            plane == planes - 1, last_block, lambda: (blank(block_shape)[0], cache_alone())
        )

    x, cache = either(last_early, last_late)
    blocks_out[last, 0] = blocks_out[last, 1] = x
    mine = by_plane(
        [jnp.where(early, blocks_out[2 * m, 0], blocks_out[2 * m + 1, 1]) for m in range(planes)]
    )
    theirs = swap(
        by_plane(
            [jnp.where(early, blocks_out[2 * m + 1, 0], blocks_out[2 * m, 1]) for m in range(planes)]
        )
    )
    block_output = pl.pallas_call(
        pair_kernel, out_shape=bf16(2, rows, width), in_specs=[VMEM] * 2, out_specs=VMEM,
        compiler_params=params_of(16),
    )(mine, theirs)
    return block_output[None], cache[None]


def solution(mesh):
    in_specs = (
        P(None, "seq", None),
        P("pipe", None),
        P("pipe", None),
        P("pipe", None),
        P("pipe", None, None),
        P("pipe", None, None, "seq"),
        P("pipe", "seq", None),
        P("pipe", None, "seq", None, None),
    )
    out_specs = (P("pipe", None, "seq", None), P("pipe", None, "seq", None, None))
    return jax.shard_map(body, mesh=mesh, in_specs=in_specs, out_specs=out_specs, check_vma=False)
```

```python
import functools
import math

import jax
import jax.numpy as jnp
from jax import lax
from jax.experimental import pallas as pl
from jax.experimental.pallas import tpu as pltpu
from jax.sharding import PartitionSpec as P

AXES = ("pipe", "seq")
VMEM = pl.BlockSpec(memory_space=pltpu.VMEM)
ANY = pl.BlockSpec(memory_space=pl.ANY)
HBM = pl.BlockSpec(memory_space=pltpu.HBM)


def normalise(values, params_ref):
    centered = values - jnp.mean(values, axis=-1, keepdims=True)
    spread = jnp.mean(centered * centered, axis=-1, keepdims=True)
    return (
        centered * lax.rsqrt(spread + 1e-06) * (1.0 + params_ref[1:2, :]) + params_ref[0:1, :]
    ).astype(jnp.bfloat16)


def spread_block(block, buffer, out_ref, sems):
    width = buffer.shape[1]
    buffer[...] = block
    copies = [
        pltpu.make_async_copy(buffer, out_ref.at[shard, :, :width], sems.at[shard])
        for shard in range(out_ref.shape[0])
    ]
    for copy in copies:
        copy.start()
    return copies


def norm_kernel(params_ref, x_ref, out_ref, buffer, sems):
    block = normalise(x_ref[...].astype(jnp.float32), params_ref)
    for copy in spread_block(block, buffer, out_ref, sems):
        copy.wait()


def pack_kernel(params_ref, x_ref, cache_ref, out_ref, buffer, sems, sides, sem):
    count, _, total = sides.shape
    width = x_ref.shape[1]
    channels = total // 2
    block = normalise(x_ref[...].astype(jnp.float32), params_ref)
    copies = spread_block(block, buffer, out_ref, sems)
    for kind in range(2):
        rows = cache_ref[:, kind, :]
        for shard in range(count):
            sides[shard, :, kind * channels : (kind + 1) * channels] = rows[
                :, shard * channels : (shard + 1) * channels
            ]
    copies.append(pltpu.make_async_copy(sides, out_ref.at[:, :, width:], sem))
    copies[-1].start()
    for copy in copies:
        copy.wait()


def attention(head_size, q_ref, kv_ref, far_ref):
    factor = 1.0 / math.sqrt(head_size)
    channels = q_ref.shape[1]
    heads = []
    across = (((1,), (1,)), ((), ()))

    def far_of(kind, start):
        if len(far_ref.shape) == 3:
            return far_ref[kind, :, start : start + head_size]
        return far_ref[:, kind * channels + start : kind * channels + start + head_size]

    for start in range(0, channels, head_size):
        cut = slice(start, start + head_size)
        query = q_ref[:, cut]
        near = lax.dot_general(query, kv_ref[0, :, cut], across, preferred_element_type=jnp.float32)
        far = lax.dot_general(query, far_of(0, start), across, preferred_element_type=jnp.float32)
        near = jnp.exp(near * factor)
        far = jnp.exp(far * factor)
        total = jnp.sum(near, axis=-1, keepdims=True) + jnp.sum(far, axis=-1, keepdims=True)
        near = (near / total).astype(jnp.bfloat16)
        far = (far / total).astype(jnp.bfloat16)
        mixed = jnp.dot(near, kv_ref[1, :, cut], preferred_element_type=jnp.float32)
        mixed = mixed + jnp.dot(far, far_of(1, start), preferred_element_type=jnp.float32)
        heads.append(mixed.astype(jnp.bfloat16))
    return jnp.concatenate(heads, axis=1)


def put_cache(caches, out_ref, offset):
    channels = caches[0].shape[2]
    for patch, cache in enumerate(caches):
        for kind in range(2):
            begin = offset + (2 * patch + kind) * channels
            out_ref[:, begin : begin + channels] = cache[kind]


def cache_kernel(*refs):
    put_cache(refs[:-1], refs[-1], 0)


def block_kernel(
    turn, head_size, planes, gain_ref, own_in, other_in, own_out, other_out, blocks_ref, far_ref, *refs
):
    caches, refs = refs[:-11], refs[-11:]
    out_ref, kv_ref, blocks, far, w_in, w_out, parts, q_ref, in_sems, sems, part_sems = refs
    width = blocks.shape[1]
    channels = w_out.shape[0]
    pieces = in_sems.shape[1]
    depth = width // pieces
    mine = lax.rem(lax.axis_index("pipe"), 2) == turn

    def weight_copies(source_in, source_out):
        for part in (1, 2, 0):
            for piece in range(pieces):
                cut = pl.ds(piece * depth, depth)
                pltpu.make_async_copy(
                    source_in.at[part, cut], w_in.at[part, cut], in_sems.at[part, piece]
                ).start()
        pltpu.make_async_copy(source_out.at[0], w_out, sems.at[1]).start()

    fetch = pltpu.make_async_copy(blocks_ref.at[:, :width], blocks, sems.at[0])
    fetch.start()
    if len(far.shape) == 3:
        fetch_far = pltpu.make_async_copy(far_ref, far, sems.at[2])
    else:
        begin = far_ref.shape[1] - far.shape[1]
        fetch_far = pltpu.make_async_copy(far_ref.at[:, begin:], far, sems.at[2])
    fetch_far.start()

    @pl.when(mine)
    def _():
        weight_copies(own_in, own_out)

    @pl.when(jnp.logical_not(mine))
    def _():
        weight_copies(other_in, other_out)

    fetch.wait()
    tokens = blocks[...]
    for part in (1, 2, 0):
        for piece in range(pieces):
            cut = pl.ds(piece * depth, depth)
            pltpu.make_async_copy(
                own_in.at[part, cut], w_in.at[part, cut], in_sems.at[part, piece]
            ).wait()
        projected = jnp.dot(tokens, w_in[part], preferred_element_type=jnp.float32)
        if part == 2:
            kv_ref[1] = projected.astype(jnp.bfloat16)
            continue
        for start in range(0, channels, head_size):
            head = projected[:, start : start + head_size]
            square = jnp.mean(head * head, axis=-1, keepdims=True)
            head = (head * lax.rsqrt(square + 1e-06) * gain_ref[part : part + 1, :]).astype(
                jnp.bfloat16
            )
            if part == 0:
                q_ref[:, start : start + head_size] = head
            else:
                kv_ref[0, :, start : start + head_size] = head

    fetch_far.wait()
    sent = []

    def send(begin, size, sem):
        cut = pl.ds(begin, size)
        sent.append(
            pltpu.make_async_copy(parts.at[:, cut], out_ref.at[:, cut], part_sems.at[sem])
        )
        sent[-1].start()

    steps = part_sems.shape[0] - 1
    if caches:
        last = lax.axis_index("pipe") // 2 == planes - 1
        first, second = caches
        put_cache((first, jnp.where(last, kv_ref[...], second[...])), parts, width)
        send(width, 4 * channels, steps)
    attended = attention(head_size, q_ref, kv_ref, far)
    pltpu.make_async_copy(own_out.at[0], w_out, sems.at[1]).wait()
    tile = width // steps
    for step in range(steps):
        cut = slice(step * tile, (step + 1) * tile)
        update = jnp.dot(attended, w_out[:, cut], preferred_element_type=jnp.float32)
        parts[:, cut] = update.astype(jnp.bfloat16)
        send(step * tile, tile, step)
    for copy in sent:
        copy.wait()


def place_cache(caches, out_ref, offset):
    channels = (caches.shape[2] - offset) // 4
    for patch in range(2):
        for shard in range(caches.shape[0]):
            begin = offset + 2 * patch * channels
            sides = [
                caches[shard, :, begin + kind * channels : begin + (kind + 1) * channels].astype(
                    jnp.float32
                )
                for kind in range(2)
            ]
            out_ref[patch, :, :, shard * channels : (shard + 1) * channels] = jnp.stack(
                sides, axis=1
            ).astype(jnp.bfloat16)


def place_kernel(caches_ref, out_ref):
    place_cache(caches_ref, out_ref, 0)


def last_kernel(params_ref, x_ref, parts_ref, out_ref, cache_ref):
    width = x_ref.shape[1]
    update = jnp.sum(parts_ref[:, :, :width].astype(jnp.float32), axis=0)
    out_ref[...] = (x_ref[...].astype(jnp.float32) + params_ref[2:3, :] * update).astype(
        jnp.bfloat16
    )
    place_cache(parts_ref, cache_ref, width)


def pair_kernel(mine_ref, theirs_ref, out_ref):
    mine, theirs = mine_ref[...], theirs_ref[...]
    early = lax.rem(lax.axis_index("pipe"), 2) == 0
    out_ref[0] = jnp.where(early, mine, theirs)
    out_ref[1] = jnp.where(early, theirs, mine)


def finish_kernel(params_ref, next_ref, x_ref, parts_ref, out_ref, *rest):
    width = x_ref.shape[1]
    update = jnp.sum(parts_ref[:, :, :width].astype(jnp.float32), axis=0)
    result = (x_ref[...].astype(jnp.float32) + params_ref[2:3, :] * update).astype(jnp.bfloat16)
    out_ref[...] = result
    if rest:
        blocks_ref, buffer, sems = rest
        block = normalise(result.astype(jnp.float32), next_ref)
        for copy in spread_block(block, buffer, blocks_ref, sems):
            copy.wait()


def blank_kernel(*refs):
    pass


def params_of(limit):
    return pltpu.CompilerParams(vmem_limit_bytes=limit << 20)


def body(hidden, mod_shift, mod_scale, mod_gate, norm_gain, input_proj, output_proj, stale_cache):
    sections = lax.axis_size("pipe")
    planes = sections // 2
    seq = lax.axis_size("seq")
    pipe = lax.axis_index("pipe")
    core = lax.rem(pipe, 2)
    plane = pipe // 2
    rows, width = hidden.shape[1:]
    head_size = norm_gain.shape[2]
    channels = input_proj.shape[3]
    tokens = rows * seq
    bf16 = lambda *shape: jax.ShapeDtypeStruct(shape, jnp.bfloat16)

    place = lambda row, position: row * seq + position

    def swap(value):
        pairs = [(place(row, s), place(row ^ 1, s)) for row in range(sections) for s in range(seq)]
        return lax.ppermute(value, AXES, pairs)

    def upward(value, level, side):
        row = 2 * level + side
        return lax.ppermute(value, AXES, [(place(row, s), place(row + 2, s)) for s in range(seq)])

    def across(blocks):
        return lax.all_to_all(blocks, "seq", split_axis=0, concat_axis=0, tiled=True)

    def blank(*shapes):
        return pl.pallas_call(blank_kernel, out_shape=shapes, out_specs=(ANY,) * len(shapes))()

    gains = jnp.pad(norm_gain[0].reshape(1, -1), ((0, 0), (0, width - 2 * head_size)))
    own_params = jnp.concatenate([mod_shift, mod_scale, mod_gate, gains], axis=0)
    own_in = jnp.transpose(input_proj[0], (1, 0, 2))
    own_out = output_proj
    x = lax.dynamic_index_in_dim(hidden, core, 0, keepdims=False)
    spreading = [pltpu.VMEM((rows, width), jnp.bfloat16), pltpu.SemaphoreType.DMA((seq,))]
    packed = pl.pallas_call(
        pack_kernel, out_shape=bf16(seq, rows, width + 2 * channels),
        in_specs=[VMEM] * 3, out_specs=HBM,
        scratch_shapes=spreading + [
            pltpu.VMEM((seq, rows, 2 * channels), jnp.bfloat16), pltpu.SemaphoreType.DMA,
        ],
        compiler_params=params_of(16),
    )(own_params, x, stale_cache[0, 1])

    other_params = swap(own_params)
    own_in, own_out, other_params, packed = lax.optimization_barrier(
        (own_in, own_out, other_params, packed)
    )
    other_in = swap(own_in)
    other_out = swap(own_out)
    params = [jnp.where(core == turn, own_params, other_params) for turn in range(2)]
    gain_rows = [p[3, : 2 * head_size].reshape(2, head_size) for p in params]
    blocks_shape = bf16(seq, rows, width)

    def norm(x, turn):
        return pl.pallas_call(
            norm_kernel, out_shape=blocks_shape, in_specs=[VMEM] * 2, out_specs=HBM,
            scratch_shapes=spreading, compiler_params=params_of(16),
        )(params[turn], x)

    flat = lambda blocks: blocks.reshape(tokens, blocks.shape[2])
    apart = lambda values: values.reshape(seq, rows, values.shape[1])

    def block(blocks, far, turn, caches=()):
        total = width + 2 * channels * len(caches)
        side = (2, tokens, channels) if far.ndim == 3 else (tokens, 2 * channels)
        out, pair = pl.pallas_call(
            functools.partial(block_kernel, turn, head_size, planes),
            out_shape=(bf16(tokens, total), bf16(2, tokens, channels)),
            in_specs=[VMEM] + [HBM] * 4 + [ANY] * 2 + [VMEM] * len(caches),
            out_specs=(HBM, VMEM),
            scratch_shapes=[
                pltpu.VMEM((tokens, width), jnp.bfloat16),
                pltpu.VMEM(side, jnp.bfloat16),
                pltpu.VMEM(own_in.shape, jnp.bfloat16),
                pltpu.VMEM(own_out.shape[1:], jnp.bfloat16),
                pltpu.VMEM((tokens, total), jnp.bfloat16),
                pltpu.VMEM((tokens, channels), jnp.bfloat16),
                pltpu.SemaphoreType.DMA((3, 2)),
                pltpu.SemaphoreType.DMA((3,)),
                pltpu.SemaphoreType.DMA((5,)),
            ],
            compiler_params=params_of(32),
        )(
            gain_rows[turn], own_in, other_in, own_out, other_out, flat(blocks), far, *caches
        )
        return apart(out), pair

    def finish(x, parts, turn, onward):
        shapes = (bf16(rows, width),) + (blocks_shape,) * onward
        return pl.pallas_call(
            finish_kernel, out_shape=shapes, in_specs=[VMEM] * 4,
            out_specs=(VMEM,) + (HBM,) * onward,
            scratch_shapes=spreading * onward, compiler_params=params_of(16),
        )(params[turn], params[1 - turn], x, parts)

    early = core == 0
    either = lambda on_early, on_late: lax.cond(early, on_early, on_late)

    def first_early():
        return across(packed), blank(bf16(tokens, 2 * channels))[0]

    def first_late():
        return blank(bf16(*packed.shape))[0], flat(across(packed[:, :, width:]))

    received, stale = either(first_early, first_late)
    stales = [flat(received), swap(stale)]
    pair_shape, block_shape = bf16(2, tokens, channels), bf16(rows, width)
    late_pair = None
    early_x, late_x = x, x
    blocks_out, sources = {}, {}
    for layer in range(sections):
        turn, level = layer % 2, layer // 2
        crossing = layer > 0 and turn == 0

        def early_scatter():
            parts, fresh = block(received, stales[turn], turn)
            return parts, fresh, blank(block_shape)[0]

        def late_gather():
            old = late_pair if turn else blank(pair_shape)[0]
            if turn == 0:
                return norm(late_x, turn), old, blank(block_shape)[0]
            result, normed = finish(late_x, received, 1 - turn, 1)
            return normed, old, result

        if crossing:
            late_x = either(
                lambda: blank(block_shape)[0], lambda: finish(late_x, received, 1 - turn, 0)[0]
            )
            blocks_out[layer - 1, 1] = late_x
            late_x = upward(late_x, level - 1, 1)
        payload, pair, result = either(early_scatter, late_gather)
        if turn:
            late_x = blocks_out[layer - 1, 1] = result
        sources[layer, 0] = pair
        got = swap(pair)
        sources[layer, 2] = got
        received = across(payload)
        if layer == sections - 1:
            break

        crossing = turn == 1

        def early_gather():
            if crossing:
                return norm(early_x, 1 - turn), blank(pair_shape)[0], blank(block_shape)[0]
            if level:
                result = finish(early_x, received, turn, 0)[0]
                return norm(result, 1 - turn), blank(pair_shape)[0], result
            result, normed = finish(early_x, received, turn, 1)
            return normed, blank(pair_shape)[0], result

        def late_scatter():
            parts, fresh = block(received, got, turn)
            return parts, fresh, blank(block_shape)[0]

        if crossing:
            early_x = either(
                lambda: finish(early_x, received, turn, 0)[0], lambda: blank(block_shape)[0]
            )
            blocks_out[layer, 0] = early_x
            early_x = upward(early_x, level, 0)
        payload, late_pair, result = either(early_gather, late_scatter)
        if not crossing:
            early_x = blocks_out[layer, 0] = result
        sources[layer, 1] = late_pair
        if crossing:
            active = pipe == jnp.where(early, 2 * level + 2, 2 * level + 1)
            received = lax.cond(active, across, lambda _: blank(blocks_shape)[0], payload)
        else:
            received = across(payload)

    def by_plane(values):
        chosen = values[0]
        for level in range(1, planes):
            chosen = jnp.where(plane == level, values[level], chosen)
        return chosen

    last = sections - 1
    first_cache = by_plane(
        [jnp.where(early, sources[2 * m, 0], sources[2 * m + 1, 2]) for m in range(planes)]
    )
    second_cache = by_plane(
        [
            jnp.where(early, sources[2 * m + 1, 2], sources[2 * m + 1, int(m < planes - 1)])
            for m in range(planes)
        ]
    )

    cache_shape = bf16(2, rows, 2, seq * channels)

    def cache_alone():
        packed = pl.pallas_call(
            cache_kernel, out_shape=bf16(tokens, 4 * channels),
            in_specs=[VMEM] * 2, out_specs=VMEM, compiler_params=params_of(16),
        )(first_cache, second_cache)
        return pl.pallas_call(
            place_kernel, out_shape=cache_shape, in_specs=[VMEM], out_specs=VMEM,
            compiler_params=params_of(16),
        )(across(apart(packed)))

    def last_block():
        parts, _ = block(received, got, last % 2, (first_cache, second_cache))
        return tuple(
            pl.pallas_call(
                last_kernel, out_shape=(block_shape, cache_shape),
                in_specs=[VMEM] * 3, out_specs=(VMEM,) * 2, compiler_params=params_of(16),
            )(params[last % 2], late_x, across(parts))
        )

    rest = range(planes - 1)
    below = lambda at, side: by_plane(
        [blocks_out[2 * m + at, side] for m in rest] + [blocks_out[0, 0]]
    )
    first_done = by_plane([blocks_out[2 * m, 0] for m in range(planes)])
    first_sent = by_plane([blocks_out[2 * m, 1] for m in range(planes)])
    second_done, second_sent = below(1, 1), below(1, 0)

    def last_early():
        result = finish(early_x, received, last % 2, 0)[0]
        return first_done, jnp.where(plane == planes - 1, result, second_sent), cache_alone()

    def last_late():
        result, cache = lax.cond(
            plane == planes - 1, last_block, lambda: (second_done, cache_alone())
        )
        return result, first_sent, cache

    mine, theirs, cache = either(last_early, last_late)
    theirs = swap(theirs)
    block_output = pl.pallas_call(
        pair_kernel, out_shape=bf16(2, rows, width), in_specs=[VMEM] * 2, out_specs=VMEM,
        compiler_params=params_of(16),
    )(mine, theirs)
    return block_output[None], cache[None]


def solution(mesh):
    in_specs = (
        P(None, "seq", None),
        P("pipe", None),
        P("pipe", None),
        P("pipe", None),
        P("pipe", None, None),
        P("pipe", None, None, "seq"),
        P("pipe", "seq", None),
        P("pipe", None, "seq", None, None),
    )
    out_specs = (P("pipe", None, "seq", None), P("pipe", None, "seq", None, None))
    return jax.shard_map(body, mesh=mesh, in_specs=in_specs, out_specs=out_specs, check_vma=False)
```

```python
import functools
import math

import jax
import jax.numpy as jnp
from jax import lax
from jax.experimental import pallas as pl
from jax.experimental.pallas import tpu as pltpu
from jax.sharding import PartitionSpec as P

AXES = ("pipe", "seq")
VMEM = pl.BlockSpec(memory_space=pltpu.VMEM)
ANY = pl.BlockSpec(memory_space=pl.ANY)
HBM = pl.BlockSpec(memory_space=pltpu.HBM)


def normalise(values, params_ref):
    centered = values - jnp.mean(values, axis=-1, keepdims=True)
    spread = jnp.mean(centered * centered, axis=-1, keepdims=True)
    return (
        centered * lax.rsqrt(spread + 1e-06) * (1.0 + params_ref[1:2, :]) + params_ref[0:1, :]
    ).astype(jnp.bfloat16)


def spread_block(block, buffer, out_ref, sems):
    width = buffer.shape[1]
    buffer[...] = block
    copies = [
        pltpu.make_async_copy(buffer, out_ref.at[shard, :, :width], sems.at[shard])
        for shard in range(out_ref.shape[0])
    ]
    for copy in copies:
        copy.start()
    return copies


def norm_kernel(params_ref, x_ref, out_ref, buffer, sems):
    block = normalise(x_ref[...].astype(jnp.float32), params_ref)
    for copy in spread_block(block, buffer, out_ref, sems):
        copy.wait()


def pack_kernel(params_ref, x_ref, cache_ref, out_ref, buffer, sems, sides, sem):
    count, _, total = sides.shape
    width = x_ref.shape[1]
    channels = total // 2
    block = normalise(x_ref[...].astype(jnp.float32), params_ref)
    copies = spread_block(block, buffer, out_ref, sems)
    for kind in range(2):
        rows = cache_ref[:, kind, :]
        for shard in range(count):
            sides[shard, :, kind * channels : (kind + 1) * channels] = rows[
                :, shard * channels : (shard + 1) * channels
            ]
    copies.append(pltpu.make_async_copy(sides, out_ref.at[:, :, width:], sem))
    copies[-1].start()
    for copy in copies:
        copy.wait()


def attention(head_size, q_ref, kv_ref, far_ref):
    factor = 1.0 / math.sqrt(head_size)
    channels = q_ref.shape[1]
    heads = []
    across = (((1,), (1,)), ((), ()))

    def far_of(kind, start):
        if len(far_ref.shape) == 3:
            return far_ref[kind, :, start : start + head_size]
        return far_ref[:, kind * channels + start : kind * channels + start + head_size]

    for start in range(0, channels, head_size):
        cut = slice(start, start + head_size)
        query = q_ref[:, cut]
        near = lax.dot_general(query, kv_ref[0, :, cut], across, preferred_element_type=jnp.float32)
        far = lax.dot_general(query, far_of(0, start), across, preferred_element_type=jnp.float32)
        near = jnp.exp(near * factor)
        far = jnp.exp(far * factor)
        total = jnp.sum(near, axis=-1, keepdims=True) + jnp.sum(far, axis=-1, keepdims=True)
        near = (near / total).astype(jnp.bfloat16)
        far = (far / total).astype(jnp.bfloat16)
        mixed = jnp.dot(near, kv_ref[1, :, cut], preferred_element_type=jnp.float32)
        mixed = mixed + jnp.dot(far, far_of(1, start), preferred_element_type=jnp.float32)
        heads.append(mixed.astype(jnp.bfloat16))
    return jnp.concatenate(heads, axis=1)


def put_cache(caches, out_ref, offset):
    channels = caches[0].shape[2]
    for patch, cache in enumerate(caches):
        for kind in range(2):
            begin = offset + (2 * patch + kind) * channels
            out_ref[:, begin : begin + channels] = cache[kind]


def cache_kernel(*refs):
    put_cache(refs[:-1], refs[-1], 0)


def block_kernel(
    turn, head_size, planes, gain_ref, own_in, other_in, own_out, other_out, blocks_ref, far_ref, *refs
):
    caches, refs = refs[:-11], refs[-11:]
    out_ref, kv_ref, blocks, far, w_in, w_out, parts, q_ref, in_sems, sems, part_sems = refs
    width = blocks.shape[1]
    channels = w_out.shape[0]
    pieces = in_sems.shape[1]
    depth = width // pieces
    mine = lax.rem(lax.axis_index("pipe"), 2) == turn

    def weight_copies(source_in, source_out):
        for part in (1, 2, 0):
            for piece in range(pieces):
                cut = pl.ds(piece * depth, depth)
                pltpu.make_async_copy(
                    source_in.at[part, cut], w_in.at[part, cut], in_sems.at[part, piece]
                ).start()
        pltpu.make_async_copy(source_out.at[0], w_out, sems.at[1]).start()

    fetch = pltpu.make_async_copy(blocks_ref.at[:, :width], blocks, sems.at[0])
    fetch.start()
    if len(far.shape) == 3:
        fetch_far = pltpu.make_async_copy(far_ref, far, sems.at[2])
    else:
        begin = far_ref.shape[1] - far.shape[1]
        fetch_far = pltpu.make_async_copy(far_ref.at[:, begin:], far, sems.at[2])
    fetch_far.start()

    @pl.when(mine)
    def _():
        weight_copies(own_in, own_out)

    @pl.when(jnp.logical_not(mine))
    def _():
        weight_copies(other_in, other_out)

    fetch.wait()
    tokens = blocks[...]
    for part in (1, 2, 0):
        for piece in range(pieces):
            cut = pl.ds(piece * depth, depth)
            pltpu.make_async_copy(
                own_in.at[part, cut], w_in.at[part, cut], in_sems.at[part, piece]
            ).wait()
        projected = jnp.dot(tokens, w_in[part], preferred_element_type=jnp.float32)
        if part == 2:
            kv_ref[1] = projected.astype(jnp.bfloat16)
            continue
        for start in range(0, channels, head_size):
            head = projected[:, start : start + head_size]
            square = jnp.mean(head * head, axis=-1, keepdims=True)
            head = (head * lax.rsqrt(square + 1e-06) * gain_ref[part : part + 1, :]).astype(
                jnp.bfloat16
            )
            if part == 0:
                q_ref[:, start : start + head_size] = head
            else:
                kv_ref[0, :, start : start + head_size] = head

    fetch_far.wait()
    sent = []

    def send(begin, size, sem):
        cut = pl.ds(begin, size)
        sent.append(
            pltpu.make_async_copy(parts.at[:, cut], out_ref.at[:, cut], part_sems.at[sem])
        )
        sent[-1].start()

    steps = part_sems.shape[0] - 1
    if caches:
        last = lax.axis_index("pipe") // 2 == planes - 1
        first, second = caches
        put_cache((first, jnp.where(last, kv_ref[...], second[...])), parts, width)
        send(width, 4 * channels, steps)
    attended = attention(head_size, q_ref, kv_ref, far)
    pltpu.make_async_copy(own_out.at[0], w_out, sems.at[1]).wait()
    tile = width // steps
    for step in range(steps):
        cut = slice(step * tile, (step + 1) * tile)
        update = jnp.dot(attended, w_out[:, cut], preferred_element_type=jnp.float32)
        parts[:, cut] = update.astype(jnp.bfloat16)
        send(step * tile, tile, step)
    for copy in sent:
        copy.wait()


def place_cache(caches, out_ref, offset):
    channels = (caches.shape[2] - offset) // 4
    for patch in range(2):
        for shard in range(caches.shape[0]):
            begin = offset + 2 * patch * channels
            sides = [
                caches[shard, :, begin + kind * channels : begin + (kind + 1) * channels].astype(
                    jnp.float32
                )
                for kind in range(2)
            ]
            out_ref[patch, :, :, shard * channels : (shard + 1) * channels] = jnp.stack(
                sides, axis=1
            ).astype(jnp.bfloat16)


def place_kernel(caches_ref, out_ref):
    place_cache(caches_ref, out_ref, 0)


def last_kernel(params_ref, x_ref, parts_ref, out_ref, cache_ref):
    width = x_ref.shape[1]
    update = jnp.sum(parts_ref[:, :, :width].astype(jnp.float32), axis=0)
    out_ref[...] = (x_ref[...].astype(jnp.float32) + params_ref[2:3, :] * update).astype(
        jnp.bfloat16
    )
    place_cache(parts_ref, cache_ref, width)


def pair_kernel(mine_ref, theirs_ref, out_ref):
    mine, theirs = mine_ref[...], theirs_ref[...]
    early = lax.rem(lax.axis_index("pipe"), 2) == 0
    out_ref[0] = jnp.where(early, mine, theirs)
    out_ref[1] = jnp.where(early, theirs, mine)


def finish_kernel(params_ref, next_ref, x_ref, parts_ref, out_ref, *rest):
    width = x_ref.shape[1]
    update = jnp.sum(parts_ref[:, :, :width].astype(jnp.float32), axis=0)
    result = (x_ref[...].astype(jnp.float32) + params_ref[2:3, :] * update).astype(jnp.bfloat16)
    out_ref[...] = result
    if rest:
        blocks_ref, buffer, sems = rest
        block = normalise(result.astype(jnp.float32), next_ref)
        for copy in spread_block(block, buffer, blocks_ref, sems):
            copy.wait()


def blank_kernel(*refs):
    pass


def params_of(limit):
    return pltpu.CompilerParams(vmem_limit_bytes=limit << 20)


def body(hidden, mod_shift, mod_scale, mod_gate, norm_gain, input_proj, output_proj, stale_cache):
    sections = lax.axis_size("pipe")
    planes = sections // 2
    seq = lax.axis_size("seq")
    pipe = lax.axis_index("pipe")
    core = lax.rem(pipe, 2)
    plane = pipe // 2
    rows, width = hidden.shape[1:]
    head_size = norm_gain.shape[2]
    channels = input_proj.shape[3]
    tokens = rows * seq
    bf16 = lambda *shape: jax.ShapeDtypeStruct(shape, jnp.bfloat16)

    place = lambda row, position: row * seq + position

    def swap(value):
        pairs = [(place(row, s), place(row ^ 1, s)) for row in range(sections) for s in range(seq)]
        return lax.ppermute(value, AXES, pairs)

    def upward(value, level, side):
        row = 2 * level + side
        return lax.ppermute(value, AXES, [(place(row, s), place(row + 2, s)) for s in range(seq)])

    def across(blocks):
        return lax.all_to_all(blocks, "seq", split_axis=0, concat_axis=0, tiled=True)

    def blank(*shapes):
        return pl.pallas_call(blank_kernel, out_shape=shapes, out_specs=(ANY,) * len(shapes))()

    gains = jnp.pad(norm_gain[0].reshape(1, -1), ((0, 0), (0, width - 2 * head_size)))
    own_params = jnp.concatenate([mod_shift, mod_scale, mod_gate, gains], axis=0)
    own_in = jnp.transpose(input_proj[0], (1, 0, 2))
    own_out = output_proj
    x = lax.dynamic_index_in_dim(hidden, core, 0, keepdims=False)
    spreading = [pltpu.VMEM((rows, width), jnp.bfloat16), pltpu.SemaphoreType.DMA((seq,))]
    packed = pl.pallas_call(
        pack_kernel, out_shape=bf16(seq, rows, width + 2 * channels),
        in_specs=[VMEM] * 3, out_specs=HBM,
        scratch_shapes=spreading + [
            pltpu.VMEM((seq, rows, 2 * channels), jnp.bfloat16), pltpu.SemaphoreType.DMA,
        ],
        compiler_params=params_of(16),
    )(own_params, x, stale_cache[0, 1])

    other_params = swap(own_params)
    own_in, own_out, other_params, packed = lax.optimization_barrier(
        (own_in, own_out, other_params, packed)
    )
    other_in = swap(own_in)
    other_out = swap(own_out)
    params = [jnp.where(core == turn, own_params, other_params) for turn in range(2)]
    gain_rows = [p[3, : 2 * head_size].reshape(2, head_size) for p in params]
    blocks_shape = bf16(seq, rows, width)

    def norm(x, turn):
        return pl.pallas_call(
            norm_kernel, out_shape=blocks_shape, in_specs=[VMEM] * 2, out_specs=HBM,
            scratch_shapes=spreading, compiler_params=params_of(16),
        )(params[turn], x)

    flat = lambda blocks: blocks.reshape(tokens, blocks.shape[2])
    apart = lambda values: values.reshape(seq, rows, values.shape[1])

    def block(blocks, far, turn, caches=()):
        total = width + 2 * channels * len(caches)
        side = (2, tokens, channels) if far.ndim == 3 else (tokens, 2 * channels)
        out, pair = pl.pallas_call(
            functools.partial(block_kernel, turn, head_size, planes),
            out_shape=(bf16(tokens, total), bf16(2, tokens, channels)),
            in_specs=[VMEM] + [HBM] * 4 + [ANY] * 2 + [VMEM] * len(caches),
            out_specs=(HBM, VMEM),
            scratch_shapes=[
                pltpu.VMEM((tokens, width), jnp.bfloat16),
                pltpu.VMEM(side, jnp.bfloat16),
                pltpu.VMEM(own_in.shape, jnp.bfloat16),
                pltpu.VMEM(own_out.shape[1:], jnp.bfloat16),
                pltpu.VMEM((tokens, total), jnp.bfloat16),
                pltpu.VMEM((tokens, channels), jnp.bfloat16),
                pltpu.SemaphoreType.DMA((3, 4)),
                pltpu.SemaphoreType.DMA((3,)),
                pltpu.SemaphoreType.DMA((5,)),
            ],
            compiler_params=params_of(32),
        )(
            gain_rows[turn], own_in, other_in, own_out, other_out, flat(blocks), far, *caches
        )
        return apart(out), pair

    def finish(x, parts, turn, onward):
        shapes = (bf16(rows, width),) + (blocks_shape,) * onward
        return pl.pallas_call(
            finish_kernel, out_shape=shapes, in_specs=[VMEM] * 4,
            out_specs=(VMEM,) + (HBM,) * onward,
            scratch_shapes=spreading * onward, compiler_params=params_of(16),
        )(params[turn], params[1 - turn], x, parts)

    early = core == 0
    either = lambda on_early, on_late: lax.cond(early, on_early, on_late)

    def first_early():
        return across(packed), blank(bf16(tokens, 2 * channels))[0]

    def first_late():
        return blank(bf16(*packed.shape))[0], flat(across(packed[:, :, width:]))

    received, stale = either(first_early, first_late)
    stales = [flat(received), swap(stale)]
    pair_shape, block_shape = bf16(2, tokens, channels), bf16(rows, width)
    late_pair = None
    early_x, late_x = x, x
    blocks_out, sources = {}, {}
    for layer in range(sections):
        turn, level = layer % 2, layer // 2
        crossing = layer > 0 and turn == 0

        def early_scatter():
            parts, fresh = block(received, stales[turn], turn)
            return parts, fresh, blank(block_shape)[0]

        def late_gather():
            old = late_pair if turn else blank(pair_shape)[0]
            if turn == 0:
                return norm(late_x, turn), old, blank(block_shape)[0]
            result, normed = finish(late_x, received, 1 - turn, 1)
            return normed, old, result

        if crossing:
            late_x = either(
                lambda: blank(block_shape)[0], lambda: finish(late_x, received, 1 - turn, 0)[0]
            )
            blocks_out[layer - 1, 1] = late_x
            late_x = upward(late_x, level - 1, 1)
        payload, pair, result = either(early_scatter, late_gather)
        if turn:
            late_x = blocks_out[layer - 1, 1] = result
        sources[layer, 0] = pair
        got = swap(pair)
        sources[layer, 2] = got
        received = across(payload)
        if layer == sections - 1:
            break

        crossing = turn == 1

        def early_gather():
            if crossing:
                return norm(early_x, 1 - turn), blank(pair_shape)[0], blank(block_shape)[0]
            if level:
                result = finish(early_x, received, turn, 0)[0]
                return norm(result, 1 - turn), blank(pair_shape)[0], result
            result, normed = finish(early_x, received, turn, 1)
            return normed, blank(pair_shape)[0], result

        def late_scatter():
            parts, fresh = block(received, got, turn)
            return parts, fresh, blank(block_shape)[0]

        if crossing:
            early_x = either(
                lambda: finish(early_x, received, turn, 0)[0], lambda: blank(block_shape)[0]
            )
            blocks_out[layer, 0] = early_x
            early_x = upward(early_x, level, 0)
        payload, late_pair, result = either(early_gather, late_scatter)
        if not crossing:
            early_x = blocks_out[layer, 0] = result
        sources[layer, 1] = late_pair
        if crossing:
            active = pipe == jnp.where(early, 2 * level + 2, 2 * level + 1)
            received = lax.cond(active, across, lambda _: blank(blocks_shape)[0], payload)
        else:
            received = across(payload)

    def by_plane(values):
        chosen = values[0]
        for level in range(1, planes):
            chosen = jnp.where(plane == level, values[level], chosen)
        return chosen

    last = sections - 1
    first_cache = by_plane(
        [jnp.where(early, sources[2 * m, 0], sources[2 * m + 1, 2]) for m in range(planes)]
    )
    second_cache = by_plane(
        [
            jnp.where(early, sources[2 * m + 1, 2], sources[2 * m + 1, int(m < planes - 1)])
            for m in range(planes)
        ]
    )

    cache_shape = bf16(2, rows, 2, seq * channels)

    def cache_alone():
        packed = pl.pallas_call(
            cache_kernel, out_shape=bf16(tokens, 4 * channels),
            in_specs=[VMEM] * 2, out_specs=VMEM, compiler_params=params_of(16),
        )(first_cache, second_cache)
        return pl.pallas_call(
            place_kernel, out_shape=cache_shape, in_specs=[VMEM], out_specs=VMEM,
            compiler_params=params_of(16),
        )(across(apart(packed)))

    def last_block():
        parts, _ = block(received, got, last % 2, (first_cache, second_cache))
        return tuple(
            pl.pallas_call(
                last_kernel, out_shape=(block_shape, cache_shape),
                in_specs=[VMEM] * 3, out_specs=(VMEM,) * 2, compiler_params=params_of(16),
            )(params[last % 2], late_x, across(parts))
        )

    def last_early():
        return finish(early_x, received, last % 2, 0)[0], cache_alone()

    def last_late():
        return lax.cond(
            plane == planes - 1, last_block, lambda: (blank(block_shape)[0], cache_alone())
        )

    x, cache = either(last_early, last_late)
    blocks_out[last, 0] = blocks_out[last, 1] = x
    mine = by_plane(
        [jnp.where(early, blocks_out[2 * m, 0], blocks_out[2 * m + 1, 1]) for m in range(planes)]
    )
    theirs = swap(
        by_plane(
            [jnp.where(early, blocks_out[2 * m + 1, 0], blocks_out[2 * m, 1]) for m in range(planes)]
        )
    )
    block_output = pl.pallas_call(
        pair_kernel, out_shape=bf16(2, rows, width), in_specs=[VMEM] * 2, out_specs=VMEM,
        compiler_params=params_of(16),
    )(mine, theirs)
    return block_output[None], cache[None]


def solution(mesh):
    in_specs = (
        P(None, "seq", None),
        P("pipe", None),
        P("pipe", None),
        P("pipe", None),
        P("pipe", None, None),
        P("pipe", None, None, "seq"),
        P("pipe", "seq", None),
        P("pipe", None, "seq", None, None),
    )
    out_specs = (P("pipe", None, "seq", None), P("pipe", None, "seq", None, None))
    return jax.shard_map(body, mesh=mesh, in_specs=in_specs, out_specs=out_specs, check_vma=False)
```
